32 devices in a mesh: groups: 2 (over x), leaf: 16 (over z, y, core).
Axes of the slice: x: 2, y: 2, z: 4, core: 2. Of those that a mesh axis runs over, the one named last changes fastest.
Arguments:
- queries: bfloat16 [8192, 2560], P(('groups', 'leaf')), parts along dimension 0, may hold values from -5 to 5
- keys: bfloat16 [8192, 512], P(('groups', 'leaf')), parts along dimension 0, may hold values from -5 to 5
- values: bfloat16 [8192, 512], P(('groups', 'leaf')), parts along dimension 0, may hold values from -6 to 6
- saved_out: bfloat16 [8192, 2560], P(('groups', 'leaf')), parts along dimension 0, may hold values from -3 to 3
- grad_out: bfloat16 [8192, 2560], P(('groups', 'leaf')), parts along dimension 0, may hold values from -60 to 60
- parents: int32 [32], P('groups'), parts along dimension 0, may hold values from -1 to 15, as said below
- assignment: int32 [32], P('groups'), parts along dimension 0, may hold values from 0 to 15, each once
- lengths: int32 [32], P('groups'), parts along dimension 0, may hold values from 64 to 256, as said below
Outputs:
- query_grad: bfloat16 [8192, 2560], P(('groups', 'leaf')), parts along dimension 0
- key_grad: bfloat16 [8192, 512], P(('groups', 'leaf')), parts along dimension 0
- value_grad: bfloat16 [8192, 512], P(('groups', 'leaf')), parts along dimension 0
The draws below stay inside these ranges and needn't reach their ends.
There are 2 independent parts, one for each index of `groups`. The reference program is written for one: setup_inputs(seed, part) draws one part's arguments, and reference() takes and returns one part's arrays. A program takes and returns all parts, laid end to end along the dimension named above; each array names one. Nothing has to cross between parts.
Inputs may be any that keep to these rules, and one draw needn't show every extreme that they name: parents[s] is the segment that segment s continues, -1 for segment 0 alone; segments 0 to 1 are the root prompt, each continuing the one before; every chain of ancestors holds at most 5 segments, and some segment's holds exactly that many. lengths[s] counts the live tokens of segment s from its start; the root prompt's segments are full.
All inputs are finite; a program needn't handle non-finite values.
Results may differ from the reference program's by a relative error of at most 0.0052.
Values may be sent and summed in bfloat16 or wider, within the bound.
No kernel may reach another device: no remote copies, remote signals or barrier semaphores. Data moves between devices by JAX's collectives and lax.ppermute only.
A program may use at most 128 MiB of HBM per device.

```python
import math
import jax
import jax.numpy as jnp
from jax import lax

HQ = 20
HK = 4
DH = 128
SEG = 256
ROOT_SEGS = 2
LEVELS = 4
ANCESTORS = 5
TOKENS = 4096
N_LEAF = 16


def draw_queries(key, part):
    key = jax.random.fold_in(key, 3)
    return jnp.clip(jax.random.normal(key, (TOKENS, HQ * DH), jnp.float32), -5.0, 5.0).astype(jnp.bfloat16)


def draw_keys(key, part):
    key = jax.random.fold_in(key, 5)
    return jnp.clip(jax.random.normal(key, (TOKENS, HK * DH), jnp.float32), -5.0, 5.0).astype(jnp.bfloat16)


def draw_parents(key, part):
    key = jax.random.fold_in(key, 7)
    count = TOKENS // SEG
    index = jnp.arange(count, dtype=jnp.int32)
    level_key, score_key = jax.random.split(key)
    drawn = jax.random.randint(level_key, (count,), 1, LEVELS + 1, dtype=jnp.int32)
    chain_mid = (index >= ROOT_SEGS) & (index <= ROOT_SEGS + LEVELS - 2)
    level = jnp.where(index < ROOT_SEGS, index - (ROOT_SEGS - 1), drawn)
    level = jnp.where(chain_mid, index - ROOT_SEGS + 2, level)
    level = jnp.where(index == count - 1, 1, level)
    scores = jax.random.randint(score_key, (count,), 0, 1 << 20, dtype=jnp.int32) * count + index
    allowed = level[None, :] == level[:, None] - 1
    ranked = jnp.where(allowed, scores[None, :], -1)
    chosen = jnp.argmax(ranked, axis=1).astype(jnp.int32)
    parent = jnp.where(jnp.any(allowed, axis=1), chosen, -1)
    forced = jnp.where(index == ROOT_SEGS, count - 1, index - 1)
    return jnp.where(chain_mid, forced, parent).astype(jnp.int32)


def draw_lengths(key, part):
    key = jax.random.fold_in(key, 9)
    count = TOKENS // SEG
    index = jnp.arange(count, dtype=jnp.int32)
    drawn = jax.random.randint(key, (count,), SEG // 4, SEG + 1, dtype=jnp.int32)
    drawn = jnp.where(index < ROOT_SEGS, SEG, drawn)
    return jnp.where(index == ROOT_SEGS, SEG // 4, drawn).astype(jnp.int32)


def shard_levels(rng, dims, cuts, smallest, top_value):
    gain, own = 1.0, jax.random.fold_in(rng, 6)
    for axis_at, blocks in cuts:
        steps = jnp.exp(jax.random.uniform(jax.random.fold_in(own, axis_at), (blocks,), jnp.float32, smallest / len(cuts), top_value / len(cuts)))
        gain = gain * jnp.repeat(steps, dims[axis_at] // blocks).reshape([-1 if axis == axis_at else 1 for axis in range(len(dims))])
    return gain


def bell_draw(own_key, dims, width, most, cuts=(), kind=jnp.bfloat16):
    values = width * jax.random.normal(own_key, dims, jnp.float32)
    if cuts:
        values = values * shard_levels(own_key, dims, cuts, -0.22, 0.18)
    return jnp.clip(values, -most, most).astype(kind)


def setup_inputs(seed: int = 0, part: int = 0) -> dict:
    streams_of = jax.random.split(jax.random.key(seed), 9)
    part_keys = jax.random.split(jax.random.fold_in(streams_of[8], part), 9)
    queries = draw_queries(jax.random.fold_in(jax.random.fold_in(streams_of[8], part), 71), part)
    keys = draw_keys(jax.random.fold_in(jax.random.fold_in(streams_of[8], part), 71), part)
    values = bell_draw(part_keys[2], (TOKENS, HK * DH), 1.0, 6.0, ((0, 16),))
    saved_out = bell_draw(part_keys[3], (TOKENS, HQ * DH), 0.5, 3.0, ((0, 16),))
    grad_out = bell_draw(part_keys[4], (TOKENS, HQ * DH), 10.0, 60.0, ((0, 16),))
    parents = draw_parents(jax.random.fold_in(jax.random.fold_in(streams_of[8], part), 71), part)
    assignment = jax.random.permutation(part_keys[6], N_LEAF).astype(jnp.int32)
    lengths = draw_lengths(jax.random.fold_in(jax.random.fold_in(streams_of[8], part), 71), part)
    return {"queries": queries, "keys": keys, "values": values, "saved_out": saved_out, "grad_out": grad_out, "parents": parents, "assignment": assignment, "lengths": lengths}


def pick(table, index):
    hits = index[..., None] == jnp.arange(table.shape[0], dtype=jnp.int32)
    return lax.optimization_barrier(jnp.sum(jnp.where(hits, table, 0), axis=-1)).astype(jnp.int32)

def pick_rows(table, index):
    hits = index[:, None] == jnp.arange(table.shape[0], dtype=jnp.int32)[None, :]
    return lax.optimization_barrier(jnp.sum(jnp.where(hits[:, :, None], table[None, :, :], 0), axis=1)).astype(jnp.int32)

def tree_tables(parents, assignment, lengths):
    count = parents.shape[0]
    iota = jnp.arange(count, dtype=jnp.int32)
    owner = lax.optimization_barrier(jnp.sum(jnp.where(assignment[None, :] == iota[:, None], iota[None, :], 0), axis=1)).astype(jnp.int32)
    links = [iota]
    for step in range(ANCESTORS):
        before = links[-1]
        above = pick(parents, jnp.maximum(before, 0))
        links.append(jnp.where(before >= 0, above, -1).astype(jnp.int32))
    stacked = jnp.stack(links)
    depth = lax.optimization_barrier(jnp.sum((stacked[1:] >= 0).astype(jnp.int32), axis=0)).astype(jnp.int32)
    steps_up = jnp.arange(ANCESTORS + 1, dtype=jnp.int32)
    slot_ids = jnp.arange(ANCESTORS, dtype=jnp.int32)
    hits = steps_up[:, None, None] == depth[None, None, :] - slot_ids[None, :, None]
    ancestor = lax.optimization_barrier(jnp.sum(jnp.where(hits, stacked[:, None, :], 0), axis=0)).T.astype(jnp.int32)
    valid = (slot_ids[None, :] < depth[:, None]).astype(jnp.int32)
    ancestor = jnp.where(valid > 0, ancestor, 0).astype(jnp.int32)
    holder = pick(owner, ancestor)
    reach = pick(lengths, ancestor)
    return (owner, pick_rows(holder, assignment), pick_rows(valid, assignment), pick_rows(reach, assignment), pick(lengths, assignment), pick(depth, assignment))

def build_mask(block_rows, usable, extent):
    position = jnp.arange(block_rows, dtype=jnp.int32)
    own_part = position[None, :] <= position[:, None]
    far_part = (usable[:, None] > 0) & (position[None, :] < extent[:, None])
    far_part = jnp.broadcast_to(far_part[None], (block_rows, ANCESTORS, block_rows))
    joined = jnp.concatenate([own_part[:, None, :], far_part], axis=1)
    return joined.reshape(block_rows, (ANCESTORS + 1) * block_rows)

def slot_grads(query, key_rows, value_rows, grad_rows, saved_rows, allowed):
    block_rows = query.shape[0]
    key_count = key_rows.shape[0]
    per_group = HQ // HK
    factor = 1.0 / math.sqrt(DH)
    query_heads = query.reshape(block_rows, HK, per_group, DH).transpose(1, 2, 0, 3)
    key_heads = key_rows.reshape(key_count, HK, DH).transpose(1, 0, 2)
    value_heads = value_rows.reshape(key_count, HK, DH).transpose(1, 0, 2)
    grad_heads = grad_rows.reshape(block_rows, HK, per_group, DH).transpose(1, 2, 0, 3)
    saved_heads = saved_rows.reshape(block_rows, HK, per_group, DH).transpose(1, 2, 0, 3)

    def one_group(pieces):
        query_part, key_part, value_part, grad_part, saved_part = pieces
        query_wide = query_part.astype(jnp.float32)
        key_wide = key_part.astype(jnp.float32)
        value_wide = value_part.astype(jnp.float32)
        grad_wide = grad_part.astype(jnp.float32)
        saved_wide = saved_part.astype(jnp.float32)
        scores = jnp.einsum('gid,kd->gik', query_wide, key_wide) * factor
        scores = jnp.where(allowed[None], scores, -1e+30)
        highest = lax.optimization_barrier(jnp.max(scores, axis=-1, keepdims=True))
        weights = jnp.exp(scores - highest)
        attention = weights / lax.optimization_barrier(jnp.sum(weights, axis=-1, keepdims=True))
        attention_half = lax.optimization_barrier(attention.astype(jnp.bfloat16))
        prob_grad = jnp.einsum('gid,kd->gik', grad_wide, value_wide)
        row_delta = lax.optimization_barrier(jnp.sum(grad_wide * saved_wide, axis=-1, keepdims=True))
        score_grad = lax.optimization_barrier((attention * (prob_grad - row_delta)).astype(jnp.bfloat16))
        score_wide = score_grad.astype(jnp.float32)
        query_terms = jnp.einsum('gik,kd->gid', score_wide, key_wide) * factor
        key_terms = jnp.einsum('gik,gid->kd', score_wide, query_wide) * factor
        value_terms = jnp.einsum('gik,gid->kd', attention_half.astype(jnp.float32), grad_wide)
        return (query_terms, key_terms, value_terms)
    query_terms, key_terms, value_terms = lax.map(one_group, (query_heads, key_heads, value_heads, grad_heads, saved_heads))
    query_terms = query_terms.transpose(2, 0, 1, 3).reshape(block_rows, HQ * DH)
    key_terms = key_terms.transpose(1, 0, 2).reshape(key_count, HK * DH)
    value_terms = value_terms.transpose(1, 0, 2).reshape(key_count, HK * DH)
    return (query_terms, key_terms, value_terms)

def reference(queries, keys, values, saved_out, grad_out, parents, assignment, lengths):
    devices = parents.shape[0]
    block_rows = queries.shape[0] // devices
    columns = keys.shape[1]
    owner, holder, valid, reach, own_length, own_depth = tree_tables(parents, assignment, lengths)
    query_blocks = queries.reshape(devices, block_rows, HQ * DH)
    saved_blocks = saved_out.reshape(devices, block_rows, HQ * DH)
    grad_blocks = grad_out.reshape(devices, block_rows, HQ * DH)
    key_blocks = keys.reshape(devices, block_rows, columns)
    value_blocks = values.reshape(devices, block_rows, columns)
    position = jnp.arange(block_rows, dtype=jnp.int32)

    def visit(carry, inputs):
        key_total, value_total = carry
        slot, query, saved, grad, hold, usable, extent, length = inputs
        masked = jnp.where((position < length)[:, None], grad, jnp.zeros_like(grad))
        key_rows = jnp.concatenate([key_blocks[slot][None], key_blocks[hold]], axis=0).reshape(-1, columns)
        value_rows = jnp.concatenate([value_blocks[slot][None], value_blocks[hold]], axis=0).reshape(-1, columns)
        allowed = build_mask(block_rows, usable, extent)
        query_terms, key_terms, value_terms = slot_grads(query, key_rows, value_rows, masked, saved, allowed)
        key_terms = key_terms.reshape(ANCESTORS + 1, block_rows, columns)
        value_terms = value_terms.reshape(ANCESTORS + 1, block_rows, columns)
        weight = usable.astype(key_terms.dtype)[:, None, None]
        key_total = key_total.at[slot].add(key_terms[0]).at[hold].add(key_terms[1:] * weight)
        value_total = value_total.at[slot].add(value_terms[0]).at[hold].add(value_terms[1:] * weight)
        return ((key_total, value_total), query_terms.astype(jnp.bfloat16))
    zeros = jnp.zeros((devices, block_rows, columns), jnp.float32)
    slot_list = jnp.arange(devices, dtype=jnp.int32)
    (key_total, value_total), query_grads = lax.scan(visit, (zeros, zeros), (slot_list, query_blocks, saved_blocks, grad_blocks, holder, valid, reach, own_length))
    query_grad = query_grads.reshape(devices * block_rows, HQ * DH)
    key_grad = key_total.reshape(devices * block_rows, columns).astype(jnp.bfloat16)
    value_grad = value_total.reshape(devices * block_rows, columns).astype(jnp.bfloat16)
    return (query_grad, key_grad, value_grad)
```

```python
import functools
import math

import jax
import jax.numpy as jnp
from jax import lax
from jax.experimental import pallas as pl
from jax.experimental.pallas import tpu as pltpu
from jax.sharding import PartitionSpec as P

HQ = 20
HK = 4
DH = 128
PER = HQ // HK
ANCESTORS = 5
SLOTS = ANCESTORS + 1
SCALE = 1.0 / math.sqrt(DH)
EXP_SCALE = SCALE / math.log(2.0)
NT = (((1,), (1,)), ((), ()))
NN = (((1,), (0,)), ((), ()))


def dot(a, b, dims):
    return lax.dot_general(a, b, dims, preferred_element_type=jnp.float32)


def walk(me_ref, parents, assignment, lengths, owner, holder, reach):
    devices = parents.shape[0]
    me = me_ref[0]

    def invert(d, carry):
        owner[assignment[d]] = d
        return carry

    lax.fori_loop(0, devices, invert, 0)
    segment = assignment[me]
    holder[0] = me
    reach[0] = lengths[segment]
    depth = jnp.int32(0)
    up = parents[segment]
    for slot in range(1, SLOTS):
        usable = up >= 0
        at = jnp.maximum(up, 0)
        holder[slot] = owner[at]
        reach[slot] = lengths[at]
        depth = depth + usable.astype(jnp.int32)
        up = jnp.where(usable, parents[at], -1)
    holder[SLOTS] = depth


def kernel(me_ref, parents, assignment, lengths, q_ref, g_ref, o_ref, k_ref, v_ref,
           dq_ref, dk_ref, dv_ref,
           owner, holder, reach, s_ref, gm_ref, kt_ref, dqt_ref):
    rows = q_ref.shape[0]

    @pl.when(pl.program_id(0) == 0)
    def _():
        walk(me_ref, parents, assignment, lengths, owner, holder, reach)

    slots = holder[SLOTS] + 1
    dk_ref[...] = jnp.zeros_like(dk_ref)
    dv_ref[...] = jnp.zeros_like(dv_ref)
    row_at = lax.broadcasted_iota(jnp.int32, (rows, 1), 0)
    lane_at = lax.broadcasted_iota(jnp.int32, (1, rows), 1)
    key_at = lax.broadcasted_iota(jnp.int32, (rows, rows), 0)
    delta = []
    for h in range(PER):
        cols = slice(h * DH, (h + 1) * DH)
        masked = jnp.where(row_at < reach[0], g_ref[:, cols], jnp.zeros((), g_ref.dtype))
        gm_ref[:, cols] = masked
        terms = masked.astype(jnp.float32) * o_ref[:, cols].astype(jnp.float32)
        delta.append(jnp.sum(terms.T, axis=0, keepdims=True))

    def scores(slot, highest):
        held = holder[slot]
        k = k_ref[held]
        kt_ref[slot] = k.T
        limit = jnp.where(slot == 0, lane_at, reach[slot] - 1)
        allowed = key_at <= limit
        out = []
        for h in range(PER):
            s = dot(k, q_ref[:, h * DH:(h + 1) * DH], NT)
            s = jnp.where(allowed, s, -1e30)
            s_ref[slot, :, h * rows:(h + 1) * rows] = s
            out.append(jnp.maximum(highest[h], jnp.max(s, axis=0, keepdims=True)))
        return tuple(out)

    start = tuple(jnp.full((1, rows), -1e30, jnp.float32) for _ in range(PER))
    highest = lax.fori_loop(0, slots, scores, start)

    def weigh(slot, total):
        out = []
        for h in range(PER):
            at = (slot, slice(None), slice(h * rows, (h + 1) * rows))
            w = jnp.exp2((s_ref[at] - highest[h]) * EXP_SCALE)
            s_ref[at] = w
            out.append(total[h] + jnp.sum(w, axis=0, keepdims=True))
        return tuple(out)

    start = tuple(jnp.zeros((1, rows), jnp.float32) for _ in range(PER))
    total = lax.fori_loop(0, slots, weigh, start)
    inverse = [1.0 / t for t in total]
    dqt_ref[...] = jnp.zeros_like(dqt_ref)

    def grads(slot, carry):
        held = holder[slot]
        v = v_ref[held]
        kt = kt_ref[slot]
        dk = jnp.zeros((rows, DH), jnp.float32)
        dv = jnp.zeros((rows, DH), jnp.float32)
        for h in range(PER):
            cols = slice(h * DH, (h + 1) * DH)
            p = s_ref[slot, :, h * rows:(h + 1) * rows] * inverse[h]
            gm = gm_ref[:, cols]
            dp = dot(v, gm, NT)
            ds = (p * (dp - delta[h])).astype(jnp.bfloat16)
            dv = dv + dot(p.astype(jnp.bfloat16), gm, NN)
            dk = dk + dot(ds, q_ref[:, cols], NN)
            dqt_ref[h] += dot(kt, ds, NN)
        dk_ref[held] = (dk * SCALE).astype(dk_ref.dtype)
        dv_ref[held] = dv.astype(dv_ref.dtype)
        return carry

    lax.fori_loop(0, slots, grads, 0)
    for h in range(PER):
        dq_ref[:, h * DH:(h + 1) * DH] = (dqt_ref[h].T * SCALE).astype(dq_ref.dtype)


def attend(me, parents, assignment, lengths, queries, grad_out, saved_out, keys, values):
    rows = queries.shape[0]
    devices = keys.shape[0]
    smem = pl.BlockSpec(memory_space=pltpu.SMEM)
    wide = pl.BlockSpec((rows, PER * DH), lambda g: (0, g))
    held = pl.BlockSpec((devices, rows, DH), lambda g: (0, 0, g))
    return pl.pallas_call(
        kernel,
        grid=(HK,),
        in_specs=[smem] * 4 + [wide] * 3 + [held] * 2,
        out_specs=[wide, held, held],
        out_shape=[
            jax.ShapeDtypeStruct(queries.shape, jnp.bfloat16),
            jax.ShapeDtypeStruct(keys.shape, jnp.bfloat16),
            jax.ShapeDtypeStruct(values.shape, jnp.bfloat16),
        ],
        scratch_shapes=[
            pltpu.SMEM((devices,), jnp.int32),
            pltpu.SMEM((SLOTS + 1,), jnp.int32),
            pltpu.SMEM((SLOTS,), jnp.int32),
            pltpu.VMEM((SLOTS, rows, PER * rows), jnp.float32),
            pltpu.VMEM((rows, PER * DH), jnp.bfloat16),
            pltpu.VMEM((SLOTS, DH, rows), jnp.bfloat16),
            pltpu.VMEM((PER, DH, rows), jnp.float32),
        ],
        compiler_params=pltpu.CompilerParams(vmem_limit_bytes=56 * 1024 * 1024),
    )(me, parents, assignment, lengths, queries, grad_out, saved_out, keys, values)


def local(queries, keys, values, saved_out, grad_out, parents, assignment, lengths):
    rows, columns = keys.shape
    me = lax.axis_index("leaf").astype(jnp.int32).reshape(1)
    all_keys = lax.all_gather(keys, "leaf")
    all_values = lax.all_gather(values, "leaf")
    dq, dk, dv = attend(
        me, parents, assignment, lengths, queries, grad_out, saved_out, all_keys, all_values
    )
    key_grad = lax.psum_scatter(dk, "leaf", scatter_dimension=0)
    value_grad = lax.psum_scatter(dv, "leaf", scatter_dimension=0)
    return (dq, key_grad, value_grad)


def solution(mesh):
    tokens = P(("groups", "leaf"), None)
    tables = P("groups")
    return jax.shard_map(
        local,
        mesh=mesh,
        in_specs=(tokens,) * 5 + (tables,) * 3,
        out_specs=(tokens,) * 3,
        check_vma=False,
    )
```

```python
import functools
import math

import jax
import jax.numpy as jnp
from jax import lax
from jax.experimental import pallas as pl
from jax.experimental.pallas import tpu as pltpu
from jax.sharding import PartitionSpec as P

HQ = 20
HK = 4
DH = 128
PER = HQ // HK
HALF = HK // 2
WIDE = PER * DH
ANCESTORS = 5
SLOTS = ANCESTORS + 1
SCALE = 1.0 / math.sqrt(DH)
EXP_SCALE = SCALE / math.log(2.0)
NT = (((1,), (1,)), ((), ()))
NN = (((1,), (0,)), ((), ()))


def dot(a, b, dims):
    return lax.dot_general(a, b, dims, preferred_element_type=jnp.float32)


def ring_order(chips):
    if chips == 8:
        return [0, 2, 4, 6, 7, 5, 3, 1]
    return list(range(chips))


def walk(device, me, places, parents, assignment, lengths, owner, block, reach, side):
    chips = places.shape[0]
    here = places[me // 2]

    def place(held):
        ahead = places[held // 2] - here
        ahead = jnp.where(ahead < 0, ahead + chips, ahead)
        return ahead * 2 + jnp.where(held % 2 == me % 2, 0, 1)

    segment = assignment[device]
    block[side, 0] = place(device)
    reach[side, 0] = lengths[segment]
    depth = jnp.int32(0)
    up = parents[segment]
    for slot in range(1, SLOTS):
        usable = up >= 0
        at = jnp.maximum(up, 0)
        block[side, slot] = place(owner[at])
        reach[side, slot] = lengths[at]
        depth = depth + usable.astype(jnp.int32)
        up = jnp.where(usable, parents[at], -1)
    block[side, SLOTS] = depth + 1


def kernel(chips, head, me_ref, places, parents, assignment, lengths, *refs):
    mine, refs = refs[:3], refs[3:]
    other, refs = refs[:3], refs[3:]
    k_in, refs = refs[:chips], refs[chips:]
    v_in, refs = refs[:chips], refs[chips:]
    dk_ref, dv_ref, dq_mine, dq_other = refs[:4]
    (owner, block, reach, q_ref, g_ref, o_ref, k_ref, v_ref, dk_sum, dv_sum,
     s_ref, kt_ref, dqt_ref, sems) = refs[4:]
    rows = dq_mine.shape[0]
    me = me_ref[0]

    copies = []
    for at, (ours, theirs, held) in enumerate(zip(mine, other, (q_ref, g_ref, o_ref))):
        column = pl.multiple_of((me % 2 * HALF + head) * WIDE, WIDE)
        copies.append(pltpu.make_async_copy(ours.at[:, pl.ds(column, WIDE)], held.at[0], sems.at[at]))
        copies.append(pltpu.make_async_copy(theirs.at[:, head * WIDE:(head + 1) * WIDE], held.at[1], sems.at[3 + at]))
    for at in range(chips):
        copies.append(pltpu.make_async_copy(k_in[at], k_ref.at[at], sems.at[6 + at]))
        copies.append(pltpu.make_async_copy(v_in[at], v_ref.at[at], sems.at[6 + chips + at]))
    for copy in copies:
        copy.start()

    def invert(d, carry):
        owner[assignment[d]] = d
        return carry

    lax.fori_loop(0, assignment.shape[0], invert, 0)
    walk(me, me, places, parents, assignment, lengths, owner, block, reach, 0)
    walk(me + 1 - me % 2 * 2, me, places, parents, assignment, lengths, owner, block, reach, 1)
    dk_sum[...] = jnp.zeros_like(dk_sum)
    dv_sum[...] = jnp.zeros_like(dv_sum)
    row_at = lax.broadcasted_iota(jnp.int32, (rows, 1), 0)
    lane_at = lax.broadcasted_iota(jnp.int32, (1, rows), 1)
    key_at = lax.broadcasted_iota(jnp.int32, (rows, rows), 0)
    for copy in copies:
        copy.wait()

    for side, dq_ref in enumerate((dq_mine, dq_other)):
        slots = block[side, SLOTS]
        delta = []
        for h in range(PER):
            cols = slice(h * DH, (h + 1) * DH)
            live = row_at < reach[side, 0]
            masked = jnp.where(live, g_ref[side, :, cols], jnp.zeros((), g_ref.dtype))
            g_ref[side, :, cols] = masked
            terms = masked.astype(jnp.float32) * o_ref[side, :, cols].astype(jnp.float32)
            delta.append(jnp.sum(terms.T, axis=0, keepdims=True))

        def key_rows(ref, slot):
            at = block[side, slot]
            first = pl.multiple_of(at % 2 * rows, rows)
            return ref.at[at // 2, pl.ds(first, rows), :]

        def scores(slot, highest):
            k = key_rows(k_ref, slot)[...]
            kt_ref[slot] = k.T
            limit = jnp.where(slot == 0, lane_at, reach[side, slot] - 1)
            allowed = key_at <= limit
            out = []
            for h in range(PER):
                s = dot(k, q_ref[side, :, h * DH:(h + 1) * DH], NT)
                s = jnp.where(allowed, s, -1e30)
                s_ref[slot, :, h * rows:(h + 1) * rows] = s
                out.append(jnp.maximum(highest[h], jnp.max(s, axis=0, keepdims=True)))
            return tuple(out)

        start = tuple(jnp.full((1, rows), -1e30, jnp.float32) for _ in range(PER))
        highest = lax.fori_loop(0, slots, scores, start)

        def weigh(slot, total):
            out = []
            for h in range(PER):
                at = (slot, slice(None), slice(h * rows, (h + 1) * rows))
                w = jnp.exp2((s_ref[at] - highest[h]) * EXP_SCALE)
                s_ref[at] = w
                out.append(total[h] + jnp.sum(w, axis=0, keepdims=True))
            return tuple(out)

        start = tuple(jnp.zeros((1, rows), jnp.float32) for _ in range(PER))
        total = lax.fori_loop(0, slots, weigh, start)
        inverse = [1.0 / t for t in total]
        dqt_ref[...] = jnp.zeros_like(dqt_ref)

        def grads(slot, carry):
            v = key_rows(v_ref, slot)[...]
            kt = kt_ref[slot]
            dk = jnp.zeros((rows, DH), jnp.float32)
            dv = jnp.zeros((rows, DH), jnp.float32)
            for h in range(PER):
                cols = slice(h * DH, (h + 1) * DH)
                p = s_ref[slot, :, h * rows:(h + 1) * rows] * inverse[h]
                gm = g_ref[side, :, cols]
                dp = dot(v, gm, NT)
                ds = (p * (dp - delta[h])).astype(jnp.bfloat16)
                dv = dv + dot(p.astype(jnp.bfloat16), gm, NN)
                dk = dk + dot(ds, q_ref[side, :, cols], NN)
                dqt_ref[h] += dot(kt, ds, NN)
            key_rows(dk_sum, slot)[...] += dk
            key_rows(dv_sum, slot)[...] += dv
            return carry

        lax.fori_loop(0, slots, grads, 0)
        for h in range(PER):
            dq_ref[:, h * DH:(h + 1) * DH] = (dqt_ref[h].T * SCALE).astype(dq_ref.dtype)
    dk_ref[...] = (dk_sum[...] * SCALE).astype(dk_ref.dtype)
    dv_ref[...] = dv_sum[...].astype(dv_ref.dtype)


def attend(head, tables, mine, other, keys, values):
    rows = mine[0].shape[0]
    chips = len(keys)
    devices = 2 * chips
    smem = pl.BlockSpec(memory_space=pltpu.SMEM)
    hbm = pl.BlockSpec(memory_space=pl.ANY)
    vmem = pl.BlockSpec(memory_space=pltpu.VMEM)
    dense = jax.ShapeDtypeStruct((chips, 2 * rows, DH), jnp.bfloat16)
    narrow = jax.ShapeDtypeStruct((rows, WIDE), jnp.bfloat16)
    work = 2 * 5 * 5 * PER * rows * rows * DH * 2
    return pl.pallas_call(
        functools.partial(kernel, chips, head),
        in_specs=[smem] * 5 + [hbm] * (6 + 2 * chips),
        out_specs=[vmem] * 4,
        out_shape=[dense, dense, narrow, narrow],
        scratch_shapes=[
            pltpu.SMEM((devices,), jnp.int32),
            pltpu.SMEM((2, SLOTS + 1), jnp.int32),
            pltpu.SMEM((2, SLOTS), jnp.int32),
            pltpu.VMEM((2, rows, WIDE), jnp.bfloat16),
            pltpu.VMEM((2, rows, WIDE), jnp.bfloat16),
            pltpu.VMEM((2, rows, WIDE), jnp.bfloat16),
            pltpu.VMEM((chips, 2 * rows, DH), jnp.bfloat16),
            pltpu.VMEM((chips, 2 * rows, DH), jnp.bfloat16),
            pltpu.VMEM((chips, 2 * rows, DH), jnp.float32),
            pltpu.VMEM((chips, 2 * rows, DH), jnp.float32),
            pltpu.VMEM((SLOTS, rows, PER * rows), jnp.float32),
            pltpu.VMEM((SLOTS, DH, rows), jnp.bfloat16),
            pltpu.VMEM((PER, DH, rows), jnp.float32),
            pltpu.SemaphoreType.DMA((6 + 2 * chips,)),
        ],
        compiler_params=pltpu.CompilerParams(vmem_limit_bytes=56 * 1024 * 1024),
        cost_estimate=pl.CostEstimate(flops=work, bytes_accessed=8 << 20, transcendentals=0),
    )(*tables, *mine, *other, *keys, *values)


def spread(block, right, left, steps_right, steps_left):
    chips = 1 + steps_right + steps_left
    got = [block] + [None] * (chips - 1)
    up = down = block
    for step in range(1, max(steps_right, steps_left) + 1):
        if step <= steps_right:
            up = lax.ppermute(up, "leaf", right)
            got[chips - step] = up
        if step <= steps_left:
            down = lax.ppermute(down, "leaf", left)
            got[step] = down
    return got


def add(a, b):
    return (a.astype(jnp.float32) + b.astype(jnp.float32)).astype(jnp.bfloat16)


def collect(terms, right, left, steps_right, steps_left):
    chips = terms.shape[0]
    up = terms[steps_right]
    down = terms[chips - steps_left]
    for step in range(max(steps_right, steps_left), 0, -1):
        if step <= steps_right:
            up = lax.ppermute(up, "leaf", right)
            if step > 1:
                up = add(up, terms[step - 1])
        if step <= steps_left:
            down = lax.ppermute(down, "leaf", left)
            if step > 1:
                down = add(down, terms[chips - step + 1])
    total = terms[0].astype(jnp.float32) + up.astype(jnp.float32) + down.astype(jnp.float32)
    return total.astype(jnp.bfloat16)


def local(queries, keys, values, saved_out, grad_out, parents, assignment, lengths):
    rows = keys.shape[0]
    chips = lax.axis_size("leaf") // 2
    order = ring_order(chips)
    ahead = [(order[i], order[(i + 1) % chips]) for i in range(chips)]
    right = [(2 * a + c, 2 * b + c) for a, b in ahead for c in range(2)]
    left = [(b, a) for a, b in right]
    swap = [(2 * a + c, 2 * a + 1 - c) for a in range(chips) for c in range(2)]
    places = jnp.asarray([order.index(chip) for chip in range(chips)], jnp.int32)
    index = lax.axis_index("leaf").astype(jnp.int32)
    core = index % 2
    tables = (index.reshape(1), places, parents, assignment, lengths)
    far, near = chips // 2, chips - 1 - chips // 2

    def part(array, which, width):
        return lax.dynamic_slice(array, (0, which * width), (rows, width))

    def chip_block(array, head):
        kept = part(array, core * HALF + head, DH)
        sent = part(array, (1 - core) * HALF + head, DH)
        return jnp.concatenate([kept, lax.ppermute(sent, "leaf", swap)], axis=0)

    gathered = []
    for head in range(HALF):
        gathered.append((
            spread(chip_block(keys, head), right, left, far, near),
            spread(chip_block(values, head), right, left, near, far),
        ))
    mine = (queries, grad_out, saved_out)
    other = tuple(
        lax.ppermute(part(array, 1 - core, HALF * WIDE), "leaf", swap) for array in mine
    )
    key_sums, value_sums, ours, theirs = [], [], [], []
    for head in range(HALF):
        dk, dv, dq_mine, dq_other = attend(head, tables, mine, other, *gathered[head])
        key_sums.append(collect(dk, right, left, far, near))
        value_sums.append(collect(dv, right, left, near, far))
        ours.append(dq_mine)
        theirs.append(lax.ppermute(dq_other, "leaf", swap))

    def whole(kept, got):
        low = jnp.concatenate([jnp.where(core == 0, a, b) for a, b in zip(kept, got)], axis=1)
        high = jnp.concatenate([jnp.where(core == 0, b, a) for a, b in zip(kept, got)], axis=1)
        return jnp.concatenate([low, high], axis=1)

    def owned(sums):
        kept = [total[:rows] for total in sums]
        got = [lax.ppermute(total[rows:], "leaf", swap) for total in sums]
        return whole(kept, got)

    return (whole(ours, theirs), owned(key_sums), owned(value_sums))


def solution(mesh):
    tokens = P(("groups", "leaf"), None)
    tables = P("groups")
    return jax.shard_map(
        local,
        mesh=mesh,
        in_specs=(tokens,) * 5 + (tables,) * 3,
        out_specs=(tokens,) * 3,
        check_vma=False,
    )
```

```python
import functools
import math

import jax
import jax.numpy as jnp
from jax import lax
from jax.experimental import pallas as pl
from jax.experimental.pallas import tpu as pltpu
from jax.sharding import PartitionSpec as P

HQ = 20
HK = 4
DH = 128
PER = HQ // HK
HALF = HK // 2
WIDE = PER * DH
ANCESTORS = 5
SLOTS = ANCESTORS + 1
SCALE = 1.0 / math.sqrt(DH)
EXP_SCALE = SCALE / math.log(2.0)
NN = (((1,), (0,)), ((), ()))


def dot(a, b):
    return lax.dot_general(a, b, NN, preferred_element_type=jnp.float32)


def ring_order(chips):
    if chips == 8:
        return [0, 2, 4, 6, 7, 5, 3, 1]
    return list(range(chips))


def walk(device, me, places, parents, assignment, lengths, owner, block, reach, side):
    chips = places.shape[0]
    here = places[me // 2]

    def place(held):
        ahead = places[held // 2] - here
        ahead = jnp.where(ahead < 0, ahead + chips, ahead)
        return ahead * 2 + jnp.where(held % 2 == me % 2, 0, 1)

    segment = assignment[device]
    block[side, 0] = place(device)
    reach[side, 0] = lengths[segment]
    depth = jnp.int32(0)
    up = parents[segment]
    for slot in range(1, SLOTS):
        usable = up >= 0
        at = jnp.maximum(up, 0)
        block[side, slot] = place(owner[at])
        reach[side, slot] = lengths[at]
        depth = depth + usable.astype(jnp.int32)
        up = jnp.where(usable, parents[at], -1)
    block[side, SLOTS] = depth + 1


def kernel(chips, head, me_ref, places, parents, assignment, lengths, *refs):
    mine, refs = refs[:3], refs[3:]
    other_ref, refs = refs[0], refs[1:]
    kv_in, refs = refs[:chips + 1], refs[chips + 1:]
    sum_ref, up_ref, down_ref, dq_mine, dq_other = refs[:5]
    (owner, block, reach, q_ref, g_ref, o_ref, qt_ref, gt_ref, kv_ref, total_ref,
     s_ref, kt_ref, dqt_ref, sems) = refs[5:]
    rows = dq_mine.shape[0]
    far = chips // 2
    me = me_ref[0]

    copies = []
    for at, held in enumerate((q_ref, g_ref, o_ref)):
        for h in range(PER):
            column = pl.multiple_of(((me % 2 * HALF + head) * PER + h) * DH, DH)
            copies.append((mine[at].at[:, pl.ds(column, DH)], held.at[0, h]))
            column = ((at * HALF + head) * PER + h) * DH
            copies.append((other_ref.at[:, column:column + DH], held.at[1, h]))
    blocks = [at for at in range(chips) if at != far]
    for at, held in zip(blocks, kv_in):
        copies.append((held, kv_ref.at[at]))
    copies.append((kv_in[chips - 1], kv_ref.at[far, :rows]))
    copies.append((kv_in[chips], kv_ref.at[far, rows:]))
    copies = [pltpu.make_async_copy(a, b, sems.at[i]) for i, (a, b) in enumerate(copies)]
    for copy in copies:
        copy.start()

    def invert(d, carry):
        owner[assignment[d]] = d
        return carry

    lax.fori_loop(0, assignment.shape[0], invert, 0)
    walk(me, me, places, parents, assignment, lengths, owner, block, reach, 0)
    walk(me + 1 - me % 2 * 2, me, places, parents, assignment, lengths, owner, block, reach, 1)

    def clear(at, carry):
        total_ref[at] = jnp.zeros(total_ref.shape[1:], total_ref.dtype)
        return carry

    lax.fori_loop(0, chips, clear, 0)
    row_at = lax.broadcasted_iota(jnp.int32, (rows, 1), 0)
    lane_at = lax.broadcasted_iota(jnp.int32, (1, PER * rows), 1) % rows
    key_at = lax.broadcasted_iota(jnp.int32, (rows, 1), 0)
    for copy in copies:
        copy.wait()

    for side, dq_ref in enumerate((dq_mine, dq_other)):
        slots = block[side, SLOTS]
        delta = []
        for h in range(PER):
            masked = jnp.where(row_at < reach[side, 0], g_ref[side, h], jnp.zeros((), g_ref.dtype))
            g_ref[side, h] = masked
            gt_ref[:, h * rows:(h + 1) * rows] = masked.T
            qt_ref[:, h * rows:(h + 1) * rows] = q_ref[side, h].T
            terms = masked.astype(jnp.float32) * o_ref[side, h].astype(jnp.float32)
            delta.append(jnp.sum(terms.T, axis=0, keepdims=True))
        delta = jnp.concatenate(delta, axis=1)

        def key_rows(ref, slot):
            at = block[side, slot]
            first = pl.multiple_of(at % 2 * rows, rows)
            return ref.at[at // 2, pl.ds(first, rows)]

        def fold(x, op):
            return op(x.reshape(rows // 8, 8, PER * rows), axis=0)

        def scores(slot, highest):
            k = key_rows(kv_ref, slot)[:, :DH]
            kt_ref[slot] = k.T
            limit = jnp.where(slot == 0, lane_at, reach[side, slot] - 1)
            s = jnp.where(key_at <= limit, dot(k, qt_ref[...]), -1e30)
            s_ref[slot] = s
            return jnp.maximum(highest, fold(s, jnp.max))

        highest = jnp.full((8, PER * rows), -1e30, jnp.float32)
        highest = lax.fori_loop(0, slots, scores, highest)
        highest = jnp.max(highest, axis=0, keepdims=True)

        def weigh(slot, total):
            w = jnp.exp2((s_ref[slot] - highest) * EXP_SCALE)
            s_ref[slot] = w
            return total + fold(w, jnp.sum)

        total = jnp.zeros((8, PER * rows), jnp.float32)
        total = lax.fori_loop(0, slots, weigh, total)
        inverse = 1.0 / jnp.sum(total, axis=0, keepdims=True)
        dqt_ref[...] = jnp.zeros_like(dqt_ref)

        def grads(slot, carry):
            v = key_rows(kv_ref, slot)[:, DH:]
            p = s_ref[slot] * inverse
            ds = (p * (dot(v, gt_ref[...]) - delta)).astype(jnp.bfloat16)
            into = key_rows(total_ref, slot)
            into[:, DH:] += dot(p.astype(jnp.bfloat16), g_ref[side].reshape(PER * rows, DH))
            into[:, :DH] += dot(ds, q_ref[side].reshape(PER * rows, DH))
            dqt_ref[...] += dot(kt_ref[slot], ds)
            return carry

        lax.fori_loop(0, slots, grads, 0)
        for h in range(PER):
            dq = dqt_ref[:, h * rows:(h + 1) * rows].T * SCALE
            dq_ref[:, h * DH:(h + 1) * DH] = dq.astype(dq_ref.dtype)

    def finish(at, carry):
        sum_ref[at, :, :DH] = (total_ref[at, :, :DH] * SCALE).astype(sum_ref.dtype)
        sum_ref[at, :, DH:] = total_ref[at, :, DH:].astype(sum_ref.dtype)
        return carry

    lax.fori_loop(0, chips, finish, 0)
    up_ref[...] = sum_ref[far, :rows]
    down_ref[...] = sum_ref[far, rows:]


def attend(head, tables, mine, other, blocks):
    rows = other.shape[0]
    chips = len(blocks) - 1
    devices = 2 * chips
    smem = pl.BlockSpec(memory_space=pltpu.SMEM)
    hbm = pl.BlockSpec(memory_space=pl.ANY)
    vmem = pl.BlockSpec(memory_space=pltpu.VMEM)
    bf16, f32 = jnp.bfloat16, jnp.float32
    work = 2 * 5 * 5 * PER * rows * rows * DH * 2
    return pl.pallas_call(
        functools.partial(kernel, chips, head),
        in_specs=[smem] * 5 + [hbm] * (4 + chips + 1),
        out_specs=[vmem] * 5,
        out_shape=[
            jax.ShapeDtypeStruct((chips, 2 * rows, 2 * DH), bf16),
            jax.ShapeDtypeStruct((rows, 2 * DH), bf16),
            jax.ShapeDtypeStruct((rows, 2 * DH), bf16),
            jax.ShapeDtypeStruct((rows, WIDE), bf16),
            jax.ShapeDtypeStruct((rows, WIDE), bf16),
        ],
        scratch_shapes=[
            pltpu.SMEM((devices,), jnp.int32),
            pltpu.SMEM((2, SLOTS + 1), jnp.int32),
            pltpu.SMEM((2, SLOTS), jnp.int32),
            pltpu.VMEM((2, PER, rows, DH), bf16),
            pltpu.VMEM((2, PER, rows, DH), bf16),
            pltpu.VMEM((2, PER, rows, DH), bf16),
            pltpu.VMEM((DH, PER * rows), bf16),
            pltpu.VMEM((DH, PER * rows), bf16),
            pltpu.VMEM((chips, 2 * rows, 2 * DH), bf16),
            pltpu.VMEM((chips, 2 * rows, 2 * DH), f32),
            pltpu.VMEM((SLOTS, rows, PER * rows), f32),
            pltpu.VMEM((SLOTS, DH, rows), bf16),
            pltpu.VMEM((DH, PER * rows), f32),
            pltpu.SemaphoreType.DMA((6 * PER + chips + 1,)),
        ],
        compiler_params=pltpu.CompilerParams(vmem_limit_bytes=56 * 1024 * 1024),
        cost_estimate=pl.CostEstimate(flops=work, bytes_accessed=8 << 20, transcendentals=0),
    )(*tables, *mine, other, *blocks)


def spread(block, right, left, chips):
    far, rows = chips // 2, block.shape[0] // 2
    got = {0: block}
    up = down = block
    for step in range(1, far):
        up = got[chips - step] = lax.ppermute(up, "leaf", right)
        down = got[step] = lax.ppermute(down, "leaf", left)
    up = lax.ppermute(up[:rows], "leaf", right)
    down = lax.ppermute(down[rows:], "leaf", left)
    return [got[at] for at in range(chips) if at != far] + [up, down]


def wide(x):
    return x.astype(jnp.float32)


def collect(terms, up, down, right, left):
    chips, rows = terms.shape[0], up.shape[0]
    up = lax.ppermute(up, "leaf", right)
    down = lax.ppermute(down, "leaf", left)
    up = jnp.pad(wide(up), ((0, rows), (0, 0)))
    down = jnp.pad(wide(down), ((rows, 0), (0, 0)))
    for step in range(chips // 2 - 1, 0, -1):
        up = wide(lax.ppermute((up + wide(terms[step])).astype(terms.dtype), "leaf", right))
        down = wide(lax.ppermute((down + wide(terms[chips - step])).astype(terms.dtype), "leaf", left))
    return (wide(terms[0]) + up + down).astype(terms.dtype)


def local(queries, keys, values, saved_out, grad_out, parents, assignment, lengths):
    rows = keys.shape[0]
    chips = lax.axis_size("leaf") // 2
    order = ring_order(chips)
    ahead = [(order[i], order[(i + 1) % chips]) for i in range(chips)]
    right = [(2 * a + c, 2 * b + c) for a, b in ahead for c in range(2)]
    left = [(b, a) for a, b in right]
    swap = [(2 * a + c, 2 * a + 1 - c) for a in range(chips) for c in range(2)]
    places = jnp.asarray([order.index(chip) for chip in range(chips)], jnp.int32)
    index = lax.axis_index("leaf").astype(jnp.int32)
    core = index % 2
    tables = (index.reshape(1), places, parents, assignment, lengths)

    def part(array, which, width):
        return lax.dynamic_slice(array, (0, which * width), (rows, width))

    def heads_of(which):
        pieces = [part(array, which * HALF + head, DH) for head in range(HALF) for array in (keys, values)]
        return jnp.concatenate(pieces, axis=1)

    kept = heads_of(core)
    got = lax.ppermute(heads_of(1 - core), "leaf", swap)
    gathered = []
    for head in range(HALF):
        cols = slice(head * 2 * DH, (head + 1) * 2 * DH)
        block = jnp.concatenate([kept[:, cols], got[:, cols]], axis=0)
        gathered.append(spread(block, right, left, chips))
    mine = (queries, grad_out, saved_out)
    other = jnp.concatenate([part(array, 1 - core, HALF * WIDE) for array in mine], axis=1)
    other = lax.ppermute(other, "leaf", swap)
    sums, ours, theirs = [], [], []
    for head in range(HALF):
        terms, up, down, dq_mine, dq_other = attend(head, tables, mine, other, gathered[head])
        sums.append(collect(terms, up, down, right, left))
        ours.append(dq_mine)
        theirs.append(lax.ppermute(dq_other, "leaf", swap))

    def whole(kept, got):
        low = [jnp.where(core == 0, a, b) for a, b in zip(kept, got)]
        high = [jnp.where(core == 0, b, a) for a, b in zip(kept, got)]
        return jnp.concatenate(low + high, axis=1)

    sums = jnp.concatenate(sums, axis=1)
    kept, got = sums[:rows], lax.ppermute(sums[rows:], "leaf", swap)

    def owned(first):
        columns = [slice((2 * head + first) * DH, (2 * head + first + 1) * DH) for head in range(HALF)]
        return whole([kept[:, c] for c in columns], [got[:, c] for c in columns])

    return (whole(ours, theirs), owned(0), owned(1))


def solution(mesh):
    tokens = P(("groups", "leaf"), None)
    tables = P("groups")
    return jax.shard_map(
        local,
        mesh=mesh,
        in_specs=(tokens,) * 5 + (tables,) * 3,
        out_specs=(tokens,) * 3,
        check_vma=False,
    )
```

```python
import functools
import math

import jax
import jax.numpy as jnp
from jax import lax
from jax.experimental import pallas as pl
from jax.experimental.pallas import tpu as pltpu
from jax.sharding import PartitionSpec as P

HQ = 20
HK = 4
DH = 128
PER = HQ // HK
HALF = HK // 2
WIDE = PER * DH
ANCESTORS = 5
SLOTS = ANCESTORS + 1
SCALE = 1.0 / math.sqrt(DH)
EXP_SCALE = SCALE / math.log(2.0)
NN = (((1,), (0,)), ((), ()))


def dot(a, b):
    return lax.dot_general(a, b, NN, preferred_element_type=jnp.float32)


def ring_order(chips):
    if chips == 8:
        return [0, 2, 4, 6, 7, 5, 3, 1]
    return list(range(chips))


def walk(device, me, places, parents, assignment, lengths, owner, block, reach, side, turn):
    chips = places.shape[0]

    def place(held):
        at = places[held // 2] - turn
        at = jnp.where(at < 0, at + chips, at)
        return at * 2 + jnp.where(held % 2 == me % 2, 0, 1)

    segment = assignment[device]
    block[side, 0] = place(device)
    reach[side, 0] = lengths[segment]
    depth = jnp.int32(0)
    up = parents[segment]
    for slot in range(1, SLOTS):
        usable = up >= 0
        at = jnp.maximum(up, 0)
        block[side, slot] = place(owner[at])
        reach[side, slot] = lengths[at]
        depth = depth + usable.astype(jnp.int32)
        up = jnp.where(usable, parents[at], -1)
    block[side, SLOTS] = depth + 1


def kernel(chips, head, ring_in, ring_out, me_ref, places, parents, assignment, lengths, *refs):
    mine, refs = refs[:3], refs[3:]
    other_ref, refs = refs[0], refs[1:]
    count = chips + 1 if ring_in else 1
    kv_in, refs = refs[:count], refs[count:]
    count = 3 if ring_out else 1
    sums, refs = refs[:count], refs[count:]
    sum_ref = sums[0]
    dq_mine, dq_other = refs[:2]
    (owner, block, reach, q_ref, g_ref, o_ref, qt_ref, gt_ref, kv_ref, total_ref,
     s_ref, kt_ref, dqt_ref, sems) = refs[2:]
    rows = dq_mine.shape[0]
    far = chips // 2
    me = me_ref[0]

    copies = []
    for at, held in enumerate((q_ref, g_ref, o_ref)):
        for h in range(PER):
            column = pl.multiple_of(((me % 2 * HALF + head) * PER + h) * DH, DH)
            copies.append((mine[at].at[:, pl.ds(column, DH)], held.at[0, h]))
            column = ((at * HALF + head) * PER + h) * DH
            copies.append((other_ref.at[:, column:column + DH], held.at[1, h]))
    if ring_in:
        blocks = [at for at in range(chips) if at != far]
        for at, held in zip(blocks, kv_in):
            copies.append((held, kv_ref.at[at]))
        copies.append((kv_in[chips - 1], kv_ref.at[far, :rows]))
        copies.append((kv_in[chips], kv_ref.at[far, rows:]))
    else:
        copies.append((kv_in[0], kv_ref))
    copies = [pltpu.make_async_copy(a, b, sems.at[i]) for i, (a, b) in enumerate(copies)]
    for copy in copies:
        copy.start()

    def invert(d, carry):
        owner[assignment[d]] = d
        return carry

    lax.fori_loop(0, assignment.shape[0], invert, 0)
    here = places[me // 2]
    turn_in = here if ring_in else 0
    turn_out = (here if ring_in else 0) - (here if ring_out else 0)
    walk(me, me, places, parents, assignment, lengths, owner, block, reach, 0, turn_in)
    walk(me + 1 - me % 2 * 2, me, places, parents, assignment, lengths, owner, block, reach, 1, turn_in)

    def clear(at, carry):
        total_ref[at] = jnp.zeros(total_ref.shape[1:], total_ref.dtype)
        return carry

    lax.fori_loop(0, chips, clear, 0)
    row_at = lax.broadcasted_iota(jnp.int32, (rows, 1), 0)
    lane_at = lax.broadcasted_iota(jnp.int32, (1, PER * rows), 1) % rows
    key_at = lax.broadcasted_iota(jnp.int32, (rows, 1), 0)
    for copy in copies:
        copy.wait()

    for side, dq_ref in enumerate((dq_mine, dq_other)):
        slots = block[side, SLOTS]
        delta = []
        for h in range(PER):
            masked = jnp.where(row_at < reach[side, 0], g_ref[side, h], jnp.zeros((), g_ref.dtype))
            g_ref[side, h] = masked
            gt_ref[:, h * rows:(h + 1) * rows] = masked.T
            qt_ref[:, h * rows:(h + 1) * rows] = q_ref[side, h].T
            terms = masked.astype(jnp.float32) * o_ref[side, h].astype(jnp.float32)
            delta.append(jnp.sum(terms.T, axis=0, keepdims=True))
        delta = jnp.concatenate(delta, axis=1)

        def key_rows(ref, slot, turn=0):
            at = block[side, slot]
            first = pl.multiple_of(at % 2 * rows, rows)
            chip = at // 2 + turn
            chip = jnp.where(chip < 0, chip + chips, jnp.where(chip >= chips, chip - chips, chip))
            return ref.at[chip, pl.ds(first, rows)]

        def fold(x, op):
            return op(x.reshape(rows // 8, 8, PER * rows), axis=0)

        def scores(slot, highest):
            k = key_rows(kv_ref, slot)[:, :DH]
            kt_ref[slot] = k.T
            limit = jnp.where(slot == 0, lane_at, reach[side, slot] - 1)
            s = jnp.where(key_at <= limit, dot(k, qt_ref[...]), -1e30)
            s_ref[slot] = s
            return jnp.maximum(highest, fold(s, jnp.max))

        highest = jnp.full((8, PER * rows), -1e30, jnp.float32)
        highest = lax.fori_loop(0, slots, scores, highest)
        highest = jnp.max(highest, axis=0, keepdims=True)

        def weigh(slot, total):
            w = jnp.exp2((s_ref[slot] - highest) * EXP_SCALE)
            s_ref[slot] = w
            return total + fold(w, jnp.sum)

        total = jnp.zeros((8, PER * rows), jnp.float32)
        total = lax.fori_loop(0, slots, weigh, total)
        inverse = 1.0 / jnp.sum(total, axis=0, keepdims=True)
        dqt_ref[...] = jnp.zeros_like(dqt_ref)

        def grads(slot, carry):
            v = key_rows(kv_ref, slot)[:, DH:]
            p = s_ref[slot] * inverse
            ds = (p * (dot(v, gt_ref[...]) - delta)).astype(jnp.bfloat16)
            into = key_rows(total_ref, slot, turn_out)
            into[:, DH:] += dot(p.astype(jnp.bfloat16), g_ref[side].reshape(PER * rows, DH))
            into[:, :DH] += dot(ds, q_ref[side].reshape(PER * rows, DH))
            dqt_ref[...] += dot(kt_ref[slot], ds)
            return carry

        lax.fori_loop(0, slots, grads, 0)
        for h in range(PER):
            dq = dqt_ref[:, h * rows:(h + 1) * rows].T * SCALE
            dq_ref[:, h * DH:(h + 1) * DH] = dq.astype(dq_ref.dtype)

    def finish(at, carry):
        sum_ref[at, :, :DH] = (total_ref[at, :, :DH] * SCALE).astype(sum_ref.dtype)
        sum_ref[at, :, DH:] = total_ref[at, :, DH:].astype(sum_ref.dtype)
        return carry

    lax.fori_loop(0, chips, finish, 0)
    if ring_out:
        sums[1][...] = sum_ref[far, :rows]
        sums[2][...] = sum_ref[far, rows:]


def attend(head, ring_out, tables, mine, other, blocks):
    rows = other.shape[0]
    chips = tables[1].shape[0]
    ring_in = len(blocks) > 1
    devices = 2 * chips
    smem = pl.BlockSpec(memory_space=pltpu.SMEM)
    hbm = pl.BlockSpec(memory_space=pl.ANY)
    vmem = pl.BlockSpec(memory_space=pltpu.VMEM)
    bf16, f32 = jnp.bfloat16, jnp.float32
    outs = [jax.ShapeDtypeStruct((chips, 2 * rows, 2 * DH), bf16)]
    if ring_out:
        outs += [jax.ShapeDtypeStruct((rows, 2 * DH), bf16)] * 2
    outs += [jax.ShapeDtypeStruct((rows, WIDE), bf16)] * 2
    work = 2 * 5 * 5 * PER * rows * rows * DH * 2
    return pl.pallas_call(
        functools.partial(kernel, chips, head, ring_in, ring_out),
        in_specs=[smem] * 5 + [hbm] * (4 + len(blocks)),
        out_specs=[vmem] * len(outs),
        out_shape=outs,
        scratch_shapes=[
            pltpu.SMEM((devices,), jnp.int32),
            pltpu.SMEM((2, SLOTS + 1), jnp.int32),
            pltpu.SMEM((2, SLOTS), jnp.int32),
            pltpu.VMEM((2, PER, rows, DH), bf16),
            pltpu.VMEM((2, PER, rows, DH), bf16),
            pltpu.VMEM((2, PER, rows, DH), bf16),
            pltpu.VMEM((DH, PER * rows), bf16),
            pltpu.VMEM((DH, PER * rows), bf16),
            pltpu.VMEM((chips, 2 * rows, 2 * DH), bf16),
            pltpu.VMEM((chips, 2 * rows, 2 * DH), f32),
            pltpu.VMEM((SLOTS, rows, PER * rows), f32),
            pltpu.VMEM((SLOTS, DH, rows), bf16),
            pltpu.VMEM((DH, PER * rows), f32),
            pltpu.SemaphoreType.DMA((6 * PER + chips + 1,)),
        ],
        compiler_params=pltpu.CompilerParams(vmem_limit_bytes=56 * 1024 * 1024),
        cost_estimate=pl.CostEstimate(flops=work, bytes_accessed=8 << 20, transcendentals=0),
    )(*tables, *mine, other, *blocks)


def spread(block, right, left, chips):
    far, rows = chips // 2, block.shape[0] // 2
    got = {0: block}
    up = down = block
    for step in range(1, far):
        up = got[chips - step] = lax.ppermute(up, "leaf", right)
        down = got[step] = lax.ppermute(down, "leaf", left)
    up = lax.ppermute(up[:rows], "leaf", right)
    down = lax.ppermute(down[rows:], "leaf", left)
    return [got[at] for at in range(chips) if at != far] + [up, down]


def wide(x):
    return x.astype(jnp.float32)


def collect(terms, up, down, right, left):
    chips, rows = terms.shape[0], up.shape[0]
    up = lax.ppermute(up, "leaf", right)
    down = lax.ppermute(down, "leaf", left)
    up = jnp.pad(wide(up), ((0, rows), (0, 0)))
    down = jnp.pad(wide(down), ((rows, 0), (0, 0)))
    for step in range(chips // 2 - 1, 0, -1):
        up = wide(lax.ppermute((up + wide(terms[step])).astype(terms.dtype), "leaf", right))
        down = wide(lax.ppermute((down + wide(terms[chips - step])).astype(terms.dtype), "leaf", left))
    return (wide(terms[0]) + up + down).astype(terms.dtype)


def local(queries, keys, values, saved_out, grad_out, parents, assignment, lengths):
    rows = keys.shape[0]
    chips = lax.axis_size("leaf") // 2
    order = ring_order(chips)
    ahead = [(order[i], order[(i + 1) % chips]) for i in range(chips)]
    right = [(2 * a + c, 2 * b + c) for a, b in ahead for c in range(2)]
    left = [(b, a) for a, b in right]
    swap = [(2 * a + c, 2 * a + 1 - c) for a in range(chips) for c in range(2)]
    rings = [[2 * chip + c for chip in order] for c in range(2)]
    places = jnp.asarray([order.index(chip) for chip in range(chips)], jnp.int32)
    index = lax.axis_index("leaf").astype(jnp.int32)
    core = index % 2
    tables = (index.reshape(1), places, parents, assignment, lengths)

    def part(array, which, width):
        return lax.dynamic_slice(array, (0, which * width), (rows, width))

    def heads_of(which):
        pieces = [part(array, which * HALF + head, DH) for head in range(HALF) for array in (keys, values)]
        return jnp.concatenate(pieces, axis=1)

    kept = heads_of(core)
    got = lax.ppermute(heads_of(1 - core), "leaf", swap)
    gathered = []
    for head in range(HALF):
        cols = slice(head * 2 * DH, (head + 1) * 2 * DH)
        block = jnp.concatenate([kept[:, cols], got[:, cols]], axis=0)
        if head == 0:
            gathered.append(spread(block, right, left, chips))
        else:
            gathered.append([lax.all_gather(block, "leaf", axis_index_groups=rings)])
    mine = (queries, grad_out, saved_out)
    other = jnp.concatenate([part(array, 1 - core, HALF * WIDE) for array in mine], axis=1)
    other = lax.ppermute(other, "leaf", swap)
    sums, ours, theirs = [], [], []
    for head in range(HALF):
        *terms, dq_mine, dq_other = attend(head, head > 0, tables, mine, other, gathered[head])
        if head > 0:
            sums.append(collect(*terms, right, left))
        else:
            total = lax.psum_scatter(terms[0], "leaf", axis_index_groups=rings)
            sums.append(total)
        ours.append(dq_mine)
        theirs.append(lax.ppermute(dq_other, "leaf", swap))

    def whole(kept, got):
        low = [jnp.where(core == 0, a, b) for a, b in zip(kept, got)]
        high = [jnp.where(core == 0, b, a) for a, b in zip(kept, got)]
        return jnp.concatenate(low + high, axis=1)

    sums = jnp.concatenate(sums, axis=1)
    kept, got = sums[:rows], lax.ppermute(sums[rows:], "leaf", swap)

    def owned(first):
        columns = [slice((2 * head + first) * DH, (2 * head + first + 1) * DH) for head in range(HALF)]
        return whole([kept[:, c] for c in columns], [got[:, c] for c in columns])

    return (whole(ours, theirs), owned(0), owned(1))


def solution(mesh):
    tokens = P(("groups", "leaf"), None)
    tables = P("groups")
    return jax.shard_map(
        local,
        mesh=mesh,
        in_specs=(tokens,) * 5 + (tables,) * 3,
        out_specs=(tokens,) * 3,
        check_vma=False,
    )
```

```python
import functools
import math

import jax
import jax.numpy as jnp
from jax import lax
from jax.experimental import pallas as pl
from jax.experimental.pallas import tpu as pltpu
from jax.sharding import PartitionSpec as P

HQ = 20
HK = 4
DH = 128
PER = HQ // HK
HALF = HK // 2
WIDE = PER * DH
ANCESTORS = 5
SLOTS = ANCESTORS + 1
REACH = 8
PLAN = 16
SCALE = 1.0 / math.sqrt(DH)
EXP_SCALE = SCALE / math.log(2.0)
NN = (((1,), (0,)), ((), ()))
SMEM = pl.BlockSpec(memory_space=pltpu.SMEM)
HBM = pl.BlockSpec(memory_space=pl.ANY)
VMEM = pl.BlockSpec(memory_space=pltpu.VMEM)
PARAMS = pltpu.CompilerParams(vmem_limit_bytes=56 * 1024 * 1024)


def dot(a, b):
    return lax.dot_general(a, b, NN, preferred_element_type=jnp.float32)


def ring_order(chips):
    if chips == 8:
        return [0, 2, 4, 6, 7, 5, 3, 1]
    return list(range(chips))


def walk(device, me, places, parents, assignment, lengths, owner, plan, side):
    chips = places.shape[0]
    here = places[me // 2]

    def place(held):
        at = places[held // 2] - here
        at = jnp.where(at < 0, at + chips, at)
        return at * 2 + jnp.where(held % 2 == me % 2, 0, 1)

    first = side * PLAN
    segment = assignment[device]
    plan[first] = place(device)
    plan[first + REACH] = lengths[segment]
    depth = jnp.int32(0)
    up = parents[segment]
    for slot in range(1, SLOTS):
        usable = up >= 0
        at = jnp.maximum(up, 0)
        plan[first + slot] = place(owner[at])
        plan[first + REACH + slot] = lengths[at]
        depth = depth + usable.astype(jnp.int32)
        up = jnp.where(usable, parents[at], -1)
    plan[first + SLOTS] = depth + 1


def run_copies(pairs, sems):
    copies = [pltpu.make_async_copy(a, b, sems.at[i]) for i, (a, b) in enumerate(pairs)]
    for copy in copies:
        copy.start()
    return copies


def column_of(me, head, h):
    return pl.multiple_of(((me % 2 * HALF + head) * PER + h) * DH, DH)


def prepare_kernel(me_ref, places, parents, assignment, lengths, queries, grads, saved, other,
                   plan, qt_ref, gt_ref, gm_ref, delta_ref, owner, q_ref, g_ref, o_ref, sems):
    rows = queries.shape[0]
    me = me_ref[0]
    width = HALF * WIDE
    column = pl.multiple_of(me % 2 * width, width)
    pairs = []
    for at, (array, held) in enumerate(zip((queries, grads, saved), (q_ref, g_ref, o_ref))):
        pairs.append((array.at[:, pl.ds(column, width)], held.at[0]))
        pairs.append((other.at[:, at * width:(at + 1) * width], held.at[1]))
    copies = run_copies(pairs, sems)

    def invert(d, carry):
        owner[assignment[d]] = d
        return carry

    lax.fori_loop(0, assignment.shape[0], invert, 0)
    walk(me, me, places, parents, assignment, lengths, owner, plan, 0)
    walk(me + 1 - me % 2 * 2, me, places, parents, assignment, lengths, owner, plan, 1)
    row_at = lax.broadcasted_iota(jnp.int32, (rows, 1), 0)
    for copy in copies:
        copy.wait()
    for side in range(2):
        live = row_at < plan[side * PLAN + REACH]
        for head in range(HALF):
            for h in range(PER):
                lanes = slice(h * rows, (h + 1) * rows)
                cols = slice((head * PER + h) * DH, (head * PER + h + 1) * DH)
                masked = jnp.where(live, g_ref[side, :, cols], jnp.zeros((), g_ref.dtype))
                gm_ref[head, side, h] = masked
                gt_ref[head, side, :, lanes] = masked.T
                qt_ref[head, side, :, lanes] = q_ref[side, :, cols].T
                terms = masked.astype(jnp.float32) * o_ref[side, :, cols].astype(jnp.float32)
                delta_ref[head, side, :, lanes] = jnp.sum(terms.T, axis=0, keepdims=True)


def prepare(tables, mine, other):
    rows = other.shape[0]
    bf16, f32 = jnp.bfloat16, jnp.float32
    return pl.pallas_call(
        prepare_kernel,
        in_specs=[SMEM] * 5 + [HBM] * 4,
        out_specs=[SMEM] + [VMEM] * 4,
        out_shape=[
            jax.ShapeDtypeStruct((2 * PLAN,), jnp.int32),
            jax.ShapeDtypeStruct((HALF, 2, DH, PER * rows), bf16),
            jax.ShapeDtypeStruct((HALF, 2, DH, PER * rows), bf16),
            jax.ShapeDtypeStruct((HALF, 2, PER, rows, DH), bf16),
            jax.ShapeDtypeStruct((HALF, 2, 1, PER * rows), f32),
        ],
        scratch_shapes=[pltpu.SMEM(tables[3].shape, jnp.int32)]
        + [pltpu.VMEM((2, rows, HALF * WIDE), bf16)] * 3
        + [pltpu.SemaphoreType.DMA((6,))],
        compiler_params=PARAMS,
        cost_estimate=pl.CostEstimate(flops=0, bytes_accessed=16 << 20, transcendentals=0),
    )(*tables, *mine, other)


def kernel(chips, head, side, add, me_ref, plan, delta_in, qt_in, gt_in, gm_in, q_in, *refs):
    kv_in, refs = refs[:chips + 1], refs[chips + 1:]
    sum_in = None
    if add:
        sum_in, refs = refs[0], refs[1:]
    outs = 4 if add else 2
    scratch = refs[-9:]
    sum_ref, dq_ref, *halves = refs[-9 - outs:-9]
    q_ref, gm_ref, qt_ref, gt_ref, delta_ref, kv_ref, s_ref, dqt_ref, sems = scratch
    rows = dq_ref.shape[0]
    far = chips // 2

    pairs = []
    for h in range(PER):
        if side == 0:
            pairs.append((q_in.at[:, pl.ds(column_of(me_ref[0], head, h), DH)], q_ref.at[h]))
        else:
            column = (head * PER + h) * DH
            pairs.append((q_in.at[:, column:column + DH], q_ref.at[h]))
    pairs.append((gm_in.at[head, side], gm_ref))
    pairs.append((qt_in.at[head, side], qt_ref))
    pairs.append((gt_in.at[head, side], gt_ref))
    pairs.append((delta_in.at[head, side], delta_ref))
    blocks = [at for at in range(chips) if at != far]
    for at, held in zip(blocks, kv_in):
        pairs.append((held, kv_ref.at[at]))
    pairs.append((kv_in[chips - 1], kv_ref.at[far, :rows]))
    pairs.append((kv_in[chips], kv_ref.at[far, rows:]))
    if add:
        pairs.append((sum_in, sum_ref))
    copies = run_copies(pairs, sems)

    first = side * PLAN
    slots = plan[first + SLOTS]
    lane_at = lax.broadcasted_iota(jnp.int32, (1, PER * rows), 1) % rows
    key_at = lax.broadcasted_iota(jnp.int32, (rows, 1), 0)
    dqt_ref[...] = jnp.zeros_like(dqt_ref)
    if not add:
        def clear(at, carry):
            sum_ref[at] = jnp.zeros(sum_ref.shape[1:], sum_ref.dtype)
            return carry

        lax.fori_loop(0, chips, clear, 0)
    for copy in copies:
        copy.wait()

    def key_rows(ref, slot):
        at = plan[first + slot]
        return ref.at[at // 2, pl.ds(pl.multiple_of(at % 2 * rows, rows), rows)]

    def fold(x, op):
        return op(x.reshape(rows // 8, 8, PER * rows), axis=0)

    def scores(slot, highest):
        k = key_rows(kv_ref, slot)[:, :DH]
        limit = jnp.where(slot == 0, lane_at, plan[first + REACH + slot] - 1)
        s = jnp.where(key_at <= limit, dot(k, qt_ref[...]), -1e30)
        s_ref[slot] = s
        return jnp.maximum(highest, fold(s, jnp.max))

    highest = jnp.full((8, PER * rows), -1e30, jnp.float32)
    highest = lax.fori_loop(0, slots, scores, highest)
    highest = jnp.max(highest, axis=0, keepdims=True)

    def weigh(slot, total):
        w = jnp.exp2((s_ref[slot] - highest) * EXP_SCALE)
        s_ref[slot] = w
        return total + fold(w, jnp.sum)

    total = jnp.zeros((8, PER * rows), jnp.float32)
    total = lax.fori_loop(0, slots, weigh, total)
    inverse = 1.0 / jnp.sum(total, axis=0, keepdims=True)

    def grads(slot, carry):
        kv = key_rows(kv_ref, slot)
        p = s_ref[slot] * inverse
        ds = (p * (dot(kv[:, DH:], gt_ref[...]) - delta_ref[...])).astype(jnp.bfloat16)
        dv = dot(p.astype(jnp.bfloat16), gm_ref[...].reshape(PER * rows, DH))
        dk = dot(ds, q_ref[...].reshape(PER * rows, DH)) * SCALE
        dqt_ref[...] += dot(kv[:, :DH].T, ds)
        into = key_rows(sum_ref, slot)
        if add:
            dk = dk + into[:, :DH].astype(jnp.float32)
            dv = dv + into[:, DH:].astype(jnp.float32)
        into[:, :DH] = dk.astype(into.dtype)
        into[:, DH:] = dv.astype(into.dtype)
        return carry

    lax.fori_loop(0, slots, grads, 0)
    for h in range(PER):
        dq = dqt_ref[:, h * rows:(h + 1) * rows].T * SCALE
        dq_ref[:, h * DH:(h + 1) * DH] = dq.astype(dq_ref.dtype)
    if add:
        halves[0][...] = sum_ref[far, :rows]
        halves[1][...] = sum_ref[far, rows:]


def attend(head, side, me, prepared, query, blocks, before, after):
    rows = query.shape[0]
    chips = len(blocks) - 1
    bf16, f32 = jnp.bfloat16, jnp.float32
    add = before is not None
    plan, qt, gt, gm, delta = prepared
    outs = [
        jax.ShapeDtypeStruct((chips, 2 * rows, 2 * DH), bf16),
        jax.ShapeDtypeStruct((rows, WIDE), bf16),
    ]
    if add:
        outs += [jax.ShapeDtypeStruct((rows, 2 * DH), bf16)] * 2
    arrays = (delta, qt, gt, gm, query, *blocks, *([before] if add else []), *after)
    work = 4 * 5 * 5 * PER * rows * rows * DH * 2
    return pl.pallas_call(
        functools.partial(kernel, chips, head, side, add),
        in_specs=[SMEM] * 2 + [HBM] * len(arrays),
        out_specs=[VMEM] * len(outs),
        out_shape=outs,
        scratch_shapes=[
            pltpu.VMEM((PER, rows, DH), bf16),
            pltpu.VMEM((PER, rows, DH), bf16),
            pltpu.VMEM((DH, PER * rows), bf16),
            pltpu.VMEM((DH, PER * rows), bf16),
            pltpu.VMEM((1, PER * rows), f32),
            pltpu.VMEM((chips, 2 * rows, 2 * DH), bf16),
            pltpu.VMEM((SLOTS, rows, PER * rows), f32),
            pltpu.VMEM((DH, PER * rows), f32),
            pltpu.SemaphoreType.DMA((PER + chips + 6,)),
        ],
        compiler_params=PARAMS,
        cost_estimate=pl.CostEstimate(flops=work, bytes_accessed=8 << 20, transcendentals=0),
    )(me, plan, *arrays)


def spread(block, right, left, chips):
    far, rows = chips // 2, block.shape[0] // 2
    got = {0: block}
    steps = []
    up = down = block
    for step in range(1, far):
        up = got[chips - step] = lax.ppermute(up, "leaf", right)
        down = got[step] = lax.ppermute(down, "leaf", left)
        steps.append([up, down])
    up = lax.ppermute(up[:rows], "leaf", right)
    down = lax.ppermute(down[rows:], "leaf", left)
    steps.append([up, down])
    return [got[at] for at in range(chips) if at != far] + [up, down], steps


def wide(x):
    return x.astype(jnp.float32)


def collect_first(terms, up, down, right, left):
    chips, rows = terms.shape[0], up.shape[0]
    up = jnp.pad(wide(lax.ppermute(up, "leaf", right)), ((0, rows), (0, 0)))
    down = jnp.pad(wide(lax.ppermute(down, "leaf", left)), ((rows, 0), (0, 0)))
    near = chips // 2 - 1
    return (
        (up + wide(terms[near])).astype(terms.dtype),
        (down + wide(terms[chips - near])).astype(terms.dtype),
    )


def collect_rest(terms, up, down, right, left):
    chips = terms.shape[0]
    for step in range(chips // 2 - 1, 0, -1):
        up = wide(lax.ppermute(up, "leaf", right))
        down = wide(lax.ppermute(down, "leaf", left))
        if step > 1:
            up = (up + wide(terms[step - 1])).astype(terms.dtype)
            down = (down + wide(terms[chips - step + 1])).astype(terms.dtype)
    return (wide(terms[0]) + up + down).astype(terms.dtype)


def local(queries, keys, values, saved_out, grad_out, parents, assignment, lengths):
    rows = keys.shape[0]
    chips = lax.axis_size("leaf") // 2
    order = ring_order(chips)
    ahead = [(order[i], order[(i + 1) % chips]) for i in range(chips)]
    right = [(2 * a + c, 2 * b + c) for a, b in ahead for c in range(2)]
    left = [(b, a) for a, b in right]
    swap = [(2 * a + c, 2 * a + 1 - c) for a in range(chips) for c in range(2)]
    places = jnp.asarray([order.index(chip) for chip in range(chips)], jnp.int32)
    index = lax.axis_index("leaf").astype(jnp.int32)
    core = index % 2
    me = index.reshape(1)
    tables = (me, places, parents, assignment, lengths)

    def part(array, which, width):
        return lax.dynamic_slice(array, (0, which * width), (rows, width))

    def heads_of(which):
        pieces = [part(array, which * HALF + head, DH) for head in range(HALF) for array in (keys, values)]
        return jnp.concatenate(pieces, axis=1)

    kept = heads_of(core)
    got = lax.ppermute(heads_of(1 - core), "leaf", swap)
    mine = (queries, grad_out, saved_out)
    other = jnp.concatenate([part(array, 1 - core, HALF * WIDE) for array in mine], axis=1)
    other = lax.ppermute(other, "leaf", swap)
    prepared = prepare(tables, mine, other)
    present = prepared[0][REACH] > 0
    gathered, steps = [], []
    for head in range(HALF):
        cols = slice(head * 2 * DH, (head + 1) * 2 * DH)
        block = jnp.concatenate([kept[:, cols], got[:, cols]], axis=0)
        if head > 0:
            block = jnp.where(present, block, steps[0][1][0])
        blocks, arrivals = spread(block, right, left, chips)
        gathered.append(blocks)
        steps.append(arrivals)

    ours, theirs, kept, got = [], [], [], []
    after = [steps[1][-3], steps[1][-2]]
    returned = []
    for head in range(HALF):
        common = (me, prepared)
        terms, dq = attend(head, 1, *common, other, gathered[head], None, after[0])
        theirs.append(lax.ppermute(dq, "leaf", swap))
        if head > 0:
            after[1] = returned[-1][1:]
        terms, dq, up, down = attend(head, 0, *common, queries, gathered[head], terms, after[1])
        ours.append(dq)
        returned.append((terms, *collect_first(terms, up, down, right, left)))
        after = [[], []]
    for parts in returned:
        total = collect_rest(*parts, right, left)
        kept.append(total[:rows])
        got.append(lax.ppermute(total[rows:], "leaf", swap))

    def whole(kept, got):
        low = [jnp.where(core == 0, a, b) for a, b in zip(kept, got)]
        high = [jnp.where(core == 0, b, a) for a, b in zip(kept, got)]
        return jnp.concatenate(low + high, axis=1)

    key_grad = whole([a[:, :DH] for a in kept], [a[:, :DH] for a in got])
    value_grad = whole([a[:, DH:] for a in kept], [a[:, DH:] for a in got])
    return (whole(ours, theirs), key_grad, value_grad)


def solution(mesh):
    tokens = P(("groups", "leaf"), None)
    tables = P("groups")
    return jax.shard_map(
        local,
        mesh=mesh,
        in_specs=(tokens,) * 5 + (tables,) * 3,
        out_specs=(tokens,) * 3,
        check_vma=False,
    )
```

```python
import functools
import math

import jax
import jax.numpy as jnp
from jax import lax
from jax.experimental import pallas as pl
from jax.experimental.pallas import tpu as pltpu
from jax.sharding import PartitionSpec as P

HQ = 20
HK = 4
DH = 128
PER = HQ // HK
HALF = HK // 2
WIDE = PER * DH
ANCESTORS = 5
SLOTS = ANCESTORS + 1
OWN = 1 << 20
SCALE = 1.0 / math.sqrt(DH)
EXP_SCALE = SCALE / math.log(2.0)
NN = (((1,), (0,)), ((), ()))
SMEM = pl.BlockSpec(memory_space=pltpu.SMEM)
HBM = pl.BlockSpec(memory_space=pl.ANY)
VMEM = pl.BlockSpec(memory_space=pltpu.VMEM)


def dot(a, b):
    return lax.dot_general(a, b, NN, preferred_element_type=jnp.float32)


def ring_order(chips):
    if chips == 8:
        return [0, 2, 4, 6, 7, 5, 3, 1]
    return list(range(chips))


def walk(device, me, places, parents, assignment, lengths, owner, plan, side):
    chips = places.shape[0]
    here = places[me // 2]

    def place(held):
        at = places[held // 2] - here
        at = jnp.where(at < 0, at + chips, at)
        return side * 2 * chips + at * 2 + jnp.where(held % 2 == me % 2, 0, 1)

    def clear(at, carry):
        plan[side * 2 * chips + at] = 0
        return carry

    lax.fori_loop(0, 2 * chips, clear, 0)
    segment = assignment[device]
    plan[place(device)] = OWN
    up = parents[segment]
    for _ in range(ANCESTORS):
        at = jnp.maximum(up, 0)

        @pl.when(up >= 0)
        def _():
            plan[place(owner[at])] = lengths[at]

        up = jnp.where(up >= 0, parents[at], -1)


def run_copies(pairs, sems):
    copies = [pltpu.make_async_copy(a, b, sems.at[i]) for i, (a, b) in enumerate(pairs)]
    for copy in copies:
        copy.start()
    return copies


def column_of(me, head, h):
    return pl.multiple_of(((me % 2 * HALF + head) * PER + h) * DH, DH)


def masked_scores(keys, queries, sees):
    rows = keys.shape[0]
    lane_at = lax.broadcasted_iota(jnp.int32, (1, PER * rows), 1) % rows
    key_at = lax.broadcasted_iota(jnp.int32, (rows, 1), 0)
    seen = key_at <= jnp.where(sees == OWN, lane_at, sees - 1)
    return dot(keys, queries), seen


def measure_block(sees, keys, queries, top_ref, sum_ref, at):
    rows = keys.shape[0]
    s, seen = masked_scores(keys, queries, sees)
    s = jnp.where(seen, s, -1e30)
    old = top_ref[at]
    top = jnp.maximum(old, jnp.max(s, axis=0, keepdims=True))
    w = jnp.exp2((s - top) * EXP_SCALE)
    top_ref[at] = top
    total = jnp.sum(w.reshape(rows // 8, 8, PER * rows), axis=0)
    sum_ref[at] = sum_ref[at] * jnp.exp2((old - top) * EXP_SCALE) + jnp.sum(total, axis=0, keepdims=True)


def measure_blocks(plan, offsets, kv_ref, qt_ref, top_ref, sum_ref):
    rows = kv_ref.shape[2] // 2
    chips = plan.shape[0] // 4
    for slot, offset in enumerate(offsets):
        def visit(i, carry):
            half, side = i // 2, i % 2
            sees = plan[side * 2 * chips + offset * 2 + half]

            @pl.when(sees > 0)
            def _():
                for head in range(HALF):
                    keys = kv_ref[slot, head, pl.ds(pl.multiple_of(half * rows, rows), rows), :DH]
                    measure_block(sees, keys, qt_ref[head, side], top_ref, sum_ref, (head, side))

            return carry

        lax.fori_loop(0, 4, visit, 0)


def prepare_kernel(me_ref, places, parents, assignment, lengths, queries, grads, saved, other, *refs):
    blocks, refs = refs[:HALF], refs[HALF:]
    (plan, qt_ref, gt_ref, gm_ref, qm_ref, delta_ref, top_ref, sum_ref,
     owner, q_ref, g_ref, o_ref, kv_ref, sems) = refs
    rows = queries.shape[0]
    me = me_ref[0]
    width = HALF * WIDE
    column = pl.multiple_of(me % 2 * width, width)
    pairs = []
    for at, (array, held) in enumerate(zip((queries, grads, saved), (q_ref, g_ref, o_ref))):
        pairs.append((array.at[:, pl.ds(column, width)], held.at[0]))
        pairs.append((other.at[:, at * width:(at + 1) * width], held.at[1]))
    for head in range(HALF):
        pairs.append((blocks[head], kv_ref.at[0, head]))
    copies = run_copies(pairs, sems)

    def invert(d, carry):
        owner[assignment[d]] = d
        return carry

    lax.fori_loop(0, assignment.shape[0], invert, 0)
    walk(me, me, places, parents, assignment, lengths, owner, plan, 0)
    walk(me + 1 - me % 2 * 2, me, places, parents, assignment, lengths, owner, plan, 1)
    row_at = lax.broadcasted_iota(jnp.int32, (rows, 1), 0)
    top_ref[...] = jnp.full(top_ref.shape, -1e30, top_ref.dtype)
    sum_ref[...] = jnp.zeros_like(sum_ref)
    for copy in copies:
        copy.wait()
    for side, device in enumerate((me, me + 1 - me % 2 * 2)):
        live = row_at < lengths[assignment[device]]
        for head in range(HALF):
            for h in range(PER):
                lanes = slice(h * rows, (h + 1) * rows)
                cols = slice((head * PER + h) * DH, (head * PER + h + 1) * DH)
                masked = jnp.where(live, g_ref[side, :, cols], jnp.zeros((), g_ref.dtype))
                query = q_ref[side, :, cols]
                gm_ref[head, side, lanes, :] = masked
                qm_ref[head, side, lanes, :] = query
                gt_ref[head, side, :, lanes] = masked.T
                qt_ref[head, side, :, lanes] = query.T
                terms = masked.astype(jnp.float32) * o_ref[side, :, cols].astype(jnp.float32)
                delta_ref[head, side, :, lanes] = jnp.sum(terms.T, axis=0, keepdims=True)
    measure_blocks(plan, [0], kv_ref, qt_ref, top_ref, sum_ref)


def row_stats(rows):
    return jax.ShapeDtypeStruct((HALF, 2, 1, PER * rows), jnp.float32)


def prepare(tables, mine, other, blocks):
    rows = other.shape[0]
    chips = tables[1].shape[0]
    bf16 = jnp.bfloat16
    return pl.pallas_call(
        prepare_kernel,
        in_specs=[SMEM] * 5 + [HBM] * (4 + HALF),
        out_specs=[SMEM] + [VMEM] * 7,
        out_shape=[
            jax.ShapeDtypeStruct((4 * chips,), jnp.int32),
            jax.ShapeDtypeStruct((HALF, 2, DH, PER * rows), bf16),
            jax.ShapeDtypeStruct((HALF, 2, DH, PER * rows), bf16),
            jax.ShapeDtypeStruct((HALF, 2, PER * rows, DH), bf16),
            jax.ShapeDtypeStruct((HALF, 2, PER * rows, DH), bf16),
            row_stats(rows),
            row_stats(rows),
            row_stats(rows),
        ],
        scratch_shapes=[pltpu.SMEM(tables[3].shape, jnp.int32)]
        + [pltpu.VMEM((2, rows, HALF * WIDE), bf16)] * 3
        + [pltpu.VMEM((1, HALF, 2 * rows, 2 * DH), bf16), pltpu.SemaphoreType.DMA((6 + HALF,))],
        compiler_params=pltpu.CompilerParams(vmem_limit_bytes=28 << 20),
        cost_estimate=pl.CostEstimate(flops=0, bytes_accessed=24 << 20, transcendentals=0),
    )(*tables, *mine, other, *blocks)


def measure_kernel(offsets, plan, qt_in, top_in, sum_in, *refs):
    count = len(offsets) * HALF
    blocks, (top_ref, sum_ref, qt_ref, kv_ref, sems) = refs[:count], refs[count:]
    pairs = [(qt_in, qt_ref), (top_in, top_ref), (sum_in, sum_ref)]
    pairs += [(held, kv_ref.at[i // HALF, i % HALF]) for i, held in enumerate(blocks)]
    for copy in run_copies(pairs, sems):
        copy.wait()
    measure_blocks(plan, offsets, kv_ref, qt_ref, top_ref, sum_ref)


def measure(offsets, plan, qt, top, total, blocks):
    rows = blocks[0].shape[0] // 2
    return pl.pallas_call(
        functools.partial(measure_kernel, offsets),
        in_specs=[SMEM] + [HBM] * (3 + len(blocks)),
        out_specs=[VMEM] * 2,
        out_shape=[row_stats(rows)] * 2,
        scratch_shapes=[
            pltpu.VMEM(qt.shape, qt.dtype),
            pltpu.VMEM((len(offsets), HALF, 2 * rows, 2 * DH), jnp.bfloat16),
            pltpu.SemaphoreType.DMA((3 + len(blocks),)),
        ],
        compiler_params=pltpu.CompilerParams(vmem_limit_bytes=20 << 20),
        cost_estimate=pl.CostEstimate(flops=0, bytes_accessed=12 << 20, transcendentals=0),
    )(plan, qt, top, total, *blocks)


def grads_kernel(chips, plan, qt_in, gt_in, gm_in, qm_in, delta_in, top_in, sum_in, *refs):
    count = HALF * (chips + 1)
    blocks, refs = refs[:count], refs[count:]
    terms, ups, downs = refs[:HALF], refs[HALF:2 * HALF], refs[2 * HALF:3 * HALF]
    (dq_mine, dq_other, qt_ref, gt_ref, gm_ref, qm_ref, delta_ref, top_ref, sum_ref, kv_ref,
     acc_ref, stage_ref, dqt_ref, sems, kv_sems, out_sems) = refs[3 * HALF:]
    rows = dq_mine.shape[0]
    far = chips // 2
    pairs = []
    for head in range(HALF):
        pairs.append((blocks[head * (chips + 1) + chips - 1], kv_ref.at[far, head, :rows]))
        pairs.append((blocks[head * (chips + 1) + chips], kv_ref.at[far, head, rows:]))
    shared = zip((qt_in, gt_in, gm_in, qm_in, delta_in, top_in, sum_in),
                 (qt_ref, gt_ref, gm_ref, qm_ref, delta_ref, top_ref, sum_ref))
    copies = run_copies(pairs + list(shared), sems)
    rest = [at for at in range(chips) if at != far]
    for slot, at in enumerate(rest):
        for head in range(HALF):
            pltpu.make_async_copy(
                blocks[head * (chips + 1) + slot], kv_ref.at[at, head], kv_sems.at[at, head]
            ).start()
    dqt_ref[...] = jnp.zeros_like(dqt_ref)
    for copy in copies:
        copy.wait()
    measure_blocks(plan, [far], kv_ref.at[pl.ds(far, 1)], qt_ref, top_ref, sum_ref)
    top_ref[...] = top_ref[...] * EXP_SCALE + jnp.log2(sum_ref[...])

    def out_copy(slot, head, target):
        return pltpu.make_async_copy(stage_ref.at[slot, head], target, out_sems.at[slot, head])

    def visit(i, carry):
        step = i // 2
        half = i % 2
        offset = jnp.where(step % 2 == 1, far + (step + 1) // 2, far - step // 2)
        offset = jnp.where(offset >= chips, offset - chips, offset)
        slot = i % 2
        here = pl.ds(pl.multiple_of(half * rows, rows), rows)

        @pl.when((half == 0) & (offset != far))
        def _():
            for head in range(HALF):
                pltpu.make_async_copy(
                    blocks[0], kv_ref.at[offset, head], kv_sems.at[offset, head]
                ).wait()

        @pl.when(i >= 2)
        def _():
            for head in range(HALF):
                out_copy(slot, head, ups[0]).wait()

        acc_ref[...] = jnp.zeros_like(acc_ref)

        def look(side, carry):
            sees = plan[side * 2 * chips + offset * 2 + half]

            @pl.when(sees > 0)
            def _():
                for head in range(HALF):
                    at = (head, side)
                    k = kv_ref[offset, head, here, :DH]
                    v = kv_ref[offset, head, here, DH:]
                    s, seen = masked_scores(k, qt_ref[at], sees)
                    p = jnp.where(seen, jnp.exp2(s * EXP_SCALE - top_ref[at]), 0.0)
                    ds = (p * (dot(v, gt_ref[at]) - delta_ref[at])).astype(jnp.bfloat16)
                    acc_ref[head, :, DH:] += dot(p.astype(jnp.bfloat16), gm_ref[at])
                    acc_ref[head, :, :DH] += dot(ds, qm_ref[at])
                    dqt_ref[at] += dot(k.T, ds)

            return carry

        lax.fori_loop(0, 2, look, 0)
        for head in range(HALF):
            stage_ref[slot, head, :, :DH] = (acc_ref[head, :, :DH] * SCALE).astype(stage_ref.dtype)
            stage_ref[slot, head, :, DH:] = acc_ref[head, :, DH:].astype(stage_ref.dtype)

        for head in range(HALF):
            @pl.when(offset != far)
            def _():
                out_copy(slot, head, terms[head].at[offset, here]).start()

            @pl.when((offset == far) & (half == 0))
            def _():
                out_copy(slot, head, ups[head]).start()

            @pl.when((offset == far) & (half == 1))
            def _():
                out_copy(slot, head, downs[head]).start()

        return carry

    lax.fori_loop(0, 2 * chips, visit, 0)
    for side, dq_ref in enumerate((dq_mine, dq_other)):
        for head in range(HALF):
            for h in range(PER):
                dq = dqt_ref[head, side, :, h * rows:(h + 1) * rows].T * SCALE
                dq_ref[:, (head * PER + h) * DH:(head * PER + h + 1) * DH] = dq.astype(dq_ref.dtype)
    for slot in range(2):
        for head in range(HALF):
            out_copy(slot, head, ups[0]).wait()


def gradients(prepared, top, total, gathered):
    plan, qt, gt, gm, qm, delta = prepared[:6]
    chips = plan.shape[0] // 4
    rows = gm.shape[2] // PER
    bf16, f32 = jnp.bfloat16, jnp.float32
    blocks = [block for head in gathered for block in head]
    shared = (qt, gt, gm, qm, delta, top, total)
    dense = jax.ShapeDtypeStruct((chips, 2 * rows, 2 * DH), bf16)
    piece = jax.ShapeDtypeStruct((rows, 2 * DH), bf16)
    query = jax.ShapeDtypeStruct((rows, HALF * WIDE), bf16)
    return pl.pallas_call(
        functools.partial(grads_kernel, chips),
        in_specs=[SMEM] + [HBM] * (len(shared) + len(blocks)),
        out_specs=[HBM] * (3 * HALF) + [VMEM] * 2,
        out_shape=[dense] * HALF + [piece] * (2 * HALF) + [query] * 2,
        scratch_shapes=[pltpu.VMEM(array.shape, array.dtype) for array in shared]
        + [
            pltpu.VMEM((chips, HALF, 2 * rows, 2 * DH), bf16),
            pltpu.VMEM((HALF, rows, 2 * DH), f32),
            pltpu.VMEM((2, HALF, rows, 2 * DH), bf16),
            pltpu.VMEM((HALF, 2, DH, PER * rows), f32),
            pltpu.SemaphoreType.DMA((2 * HALF + len(shared),)),
            pltpu.SemaphoreType.DMA((chips, HALF)),
            pltpu.SemaphoreType.DMA((2, HALF)),
        ],
        compiler_params=pltpu.CompilerParams(vmem_limit_bytes=(32 << 20) + (chips << 19)),
        cost_estimate=pl.CostEstimate(flops=20 << 30, bytes_accessed=16 << 20, transcendentals=0),
    )(plan, *shared, *blocks)


def spread(block, right, left, chips):
    far, rows = chips // 2, block.shape[0] // 2
    got = {0: block}
    up = down = block
    for step in range(1, far):
        up = got[chips - step] = lax.ppermute(up, "leaf", right)
        down = got[step] = lax.ppermute(down, "leaf", left)
    up = lax.ppermute(up[:rows], "leaf", right)
    down = lax.ppermute(down[rows:], "leaf", left)
    return [got[at] for at in range(chips) if at != far] + [up, down]


def wide(x):
    return x.astype(jnp.float32)


def collect(terms, up, down, right, left):
    chips, rows = terms.shape[0], up.shape[0]
    up = lax.ppermute(up, "leaf", right)
    down = lax.ppermute(down, "leaf", left)
    up = jnp.pad(wide(up), ((0, rows), (0, 0)))
    down = jnp.pad(wide(down), ((rows, 0), (0, 0)))
    for step in range(chips // 2 - 1, 0, -1):
        up = wide(lax.ppermute((up + wide(terms[step])).astype(terms.dtype), "leaf", right))
        down = wide(lax.ppermute((down + wide(terms[chips - step])).astype(terms.dtype), "leaf", left))
    return (wide(terms[0]) + up + down).astype(terms.dtype)


def local(queries, keys, values, saved_out, grad_out, parents, assignment, lengths):
    rows = keys.shape[0]
    chips = lax.axis_size("leaf") // 2
    order = ring_order(chips)
    ahead = [(order[i], order[(i + 1) % chips]) for i in range(chips)]
    right = [(2 * a + c, 2 * b + c) for a, b in ahead for c in range(2)]
    left = [(b, a) for a, b in right]
    swap = [(2 * a + c, 2 * a + 1 - c) for a in range(chips) for c in range(2)]
    places = jnp.asarray([order.index(chip) for chip in range(chips)], jnp.int32)
    index = lax.axis_index("leaf").astype(jnp.int32)
    core = index % 2
    me = index.reshape(1)
    tables = (me, places, parents, assignment, lengths)

    def part(array, which, width):
        return lax.dynamic_slice(array, (0, which * width), (rows, width))

    def heads_of(which):
        pieces = [part(array, which * HALF + head, DH) for head in range(HALF) for array in (keys, values)]
        return jnp.concatenate(pieces, axis=1)

    kept = heads_of(core)
    got = lax.ppermute(heads_of(1 - core), "leaf", swap)
    gathered = []
    for head in range(HALF):
        cols = slice(head * 2 * DH, (head + 1) * 2 * DH)
        block = jnp.concatenate([kept[:, cols], got[:, cols]], axis=0)
        gathered.append(spread(block, right, left, chips))
    mine = (queries, grad_out, saved_out)
    late = lax.optimization_barrier((*mine, got))[:3]
    other = jnp.concatenate([part(array, 1 - core, HALF * WIDE) for array in late], axis=1)
    other = lax.ppermute(other, "leaf", swap)
    prepared = prepare(tables, mine, other, [blocks[0] for blocks in gathered])
    plan, qt, top, total = prepared[0], prepared[1], prepared[6], prepared[7]
    far = chips // 2
    for step in range(1, far):
        arrived = [blocks[at] for at in (step, chips - step - 1) for blocks in gathered]
        top, total = measure((step, chips - step), plan, qt, top, total, arrived)
    *terms, ours, theirs = gradients(prepared, top, total, gathered)
    theirs = lax.ppermute(theirs, "leaf", swap)
    kept, got = [], []
    for head in range(HALF):
        summed = collect(*terms[head::HALF], right, left)
        kept.append(summed[:rows])
        got.append(lax.ppermute(summed[rows:], "leaf", swap))

    def whole(kept, got):
        low = [jnp.where(core == 0, a, b) for a, b in zip(kept, got)]
        high = [jnp.where(core == 0, b, a) for a, b in zip(kept, got)]
        return jnp.concatenate(low + high, axis=1)

    key_grad = whole([a[:, :DH] for a in kept], [a[:, :DH] for a in got])
    value_grad = whole([a[:, DH:] for a in kept], [a[:, DH:] for a in got])
    return (whole([ours], [theirs]), key_grad, value_grad)


def solution(mesh):
    tokens = P(("groups", "leaf"), None)
    tables = P("groups")
    return jax.shard_map(
        local,
        mesh=mesh,
        in_specs=(tokens,) * 5 + (tables,) * 3,
        out_specs=(tokens,) * 3,
        check_vma=False,
    )
```

```python
import functools
import math

import jax
import jax.numpy as jnp
from jax import lax
from jax.experimental import pallas as pl
from jax.experimental.pallas import tpu as pltpu
from jax.sharding import PartitionSpec as P

HQ = 20
HK = 4
DH = 128
PER = HQ // HK
HALF = HK // 2
WIDE = PER * DH
ANCESTORS = 5
SLOTS = ANCESTORS + 1
OWN = 1 << 20
SCALE = 1.0 / math.sqrt(DH)
EXP_SCALE = SCALE / math.log(2.0)
NN = (((1,), (0,)), ((), ()))
SMEM = pl.BlockSpec(memory_space=pltpu.SMEM)
HBM = pl.BlockSpec(memory_space=pl.ANY)
VMEM = pl.BlockSpec(memory_space=pltpu.VMEM)


def dot(a, b):
    return lax.dot_general(a, b, NN, preferred_element_type=jnp.float32)


def ring_order(chips):
    if chips == 8:
        return [0, 2, 4, 6, 7, 5, 3, 1]
    return list(range(chips))


def walk(device, me, places, parents, assignment, lengths, owner, plan, side):
    chips = places.shape[0]
    here = places[me // 2]

    def place(held):
        at = places[held // 2] - here
        at = jnp.where(at < 0, at + chips, at)
        return side * 2 * chips + at * 2 + jnp.where(held % 2 == me % 2, 0, 1)

    def clear(at, carry):
        plan[side * 2 * chips + at] = 0
        return carry

    lax.fori_loop(0, 2 * chips, clear, 0)
    segment = assignment[device]
    plan[place(device)] = OWN
    up = parents[segment]
    for _ in range(ANCESTORS):
        at = jnp.maximum(up, 0)

        @pl.when(up >= 0)
        def _():
            plan[place(owner[at])] = lengths[at]

        up = jnp.where(up >= 0, parents[at], -1)


def run_copies(pairs, sems):
    copies = [pltpu.make_async_copy(a, b, sems.at[i]) for i, (a, b) in enumerate(pairs)]
    for copy in copies:
        copy.start()
    return copies


def column_of(me, head, h):
    return pl.multiple_of(((me % 2 * HALF + head) * PER + h) * DH, DH)


def masked_scores(keys, queries, sees):
    rows = keys.shape[0]
    lane_at = lax.broadcasted_iota(jnp.int32, (1, PER * rows), 1) % rows
    key_at = lax.broadcasted_iota(jnp.int32, (rows, 1), 0)
    seen = key_at <= jnp.where(sees == OWN, lane_at, sees - 1)
    return dot(keys, queries), seen


def measure_block(sees, keys, queries, top_ref, sum_ref, at):
    rows = keys.shape[0]
    s, seen = masked_scores(keys, queries, sees)
    s = jnp.where(seen, s, -1e30)
    old = top_ref[at]
    top = jnp.maximum(old, jnp.max(s, axis=0, keepdims=True))
    w = jnp.exp2((s - top) * EXP_SCALE)
    top_ref[at] = top
    total = jnp.sum(w.reshape(rows // 8, 8, PER * rows), axis=0)
    sum_ref[at] = sum_ref[at] * jnp.exp2((old - top) * EXP_SCALE) + jnp.sum(total, axis=0, keepdims=True)


def measure_blocks(plan, offsets, kv_ref, qt_ref, top_ref, sum_ref):
    rows = kv_ref.shape[2] // 2
    chips = plan.shape[0] // 4
    for slot, offset in enumerate(offsets):
        def visit(i, carry):
            half, side = i // 2, i % 2
            sees = plan[side * 2 * chips + offset * 2 + half]

            @pl.when(sees > 0)
            def _():
                for head in range(HALF):
                    keys = kv_ref[slot, head, pl.ds(pl.multiple_of(half * rows, rows), rows), :DH]
                    measure_block(sees, keys, qt_ref[head, side], top_ref, sum_ref, (head, side))

            return carry

        lax.fori_loop(0, 4, visit, 0)


def prepare_kernel(me_ref, places, parents, assignment, lengths, queries, grads, saved, other, *refs):
    blocks, refs = refs[:HALF], refs[HALF:]
    (plan, qt_ref, gt_ref, gm_ref, qm_ref, delta_ref, top_ref, sum_ref,
     owner, q_ref, g_ref, o_ref, kv_ref, sems) = refs
    rows = queries.shape[0]
    me = me_ref[0]
    width = HALF * WIDE
    column = pl.multiple_of(me % 2 * width, width)
    pairs = []
    for at, (array, held) in enumerate(zip((queries, grads, saved), (q_ref, g_ref, o_ref))):
        pairs.append((array.at[:, pl.ds(column, width)], held.at[0]))
        pairs.append((other.at[:, at * width:(at + 1) * width], held.at[1]))
    for head in range(HALF):
        pairs.append((blocks[head], kv_ref.at[0, head]))
    copies = run_copies(pairs, sems)

    def invert(d, carry):
        owner[assignment[d]] = d
        return carry

    lax.fori_loop(0, assignment.shape[0], invert, 0)
    walk(me, me, places, parents, assignment, lengths, owner, plan, 0)
    walk(me + 1 - me % 2 * 2, me, places, parents, assignment, lengths, owner, plan, 1)
    row_at = lax.broadcasted_iota(jnp.int32, (rows, 1), 0)
    top_ref[...] = jnp.full(top_ref.shape, -1e30, top_ref.dtype)
    sum_ref[...] = jnp.zeros_like(sum_ref)
    for copy in copies:
        copy.wait()
    for side, device in enumerate((me, me + 1 - me % 2 * 2)):
        live = row_at < lengths[assignment[device]]
        for head in range(HALF):
            for h in range(PER):
                lanes = slice(h * rows, (h + 1) * rows)
                cols = slice((head * PER + h) * DH, (head * PER + h + 1) * DH)
                masked = jnp.where(live, g_ref[side, :, cols], jnp.zeros((), g_ref.dtype))
                query = q_ref[side, :, cols]
                gm_ref[head, side, lanes, :] = masked
                qm_ref[head, side, lanes, :] = query
                gt_ref[head, side, :, lanes] = masked.T
                qt_ref[head, side, :, lanes] = query.T
                terms = masked.astype(jnp.float32) * o_ref[side, :, cols].astype(jnp.float32)
                delta_ref[head, side, :, lanes] = jnp.sum(terms.T, axis=0, keepdims=True)
    measure_blocks(plan, [0], kv_ref, qt_ref, top_ref, sum_ref)


def row_stats(rows):
    return jax.ShapeDtypeStruct((HALF, 2, 1, PER * rows), jnp.float32)


def prepare(tables, mine, other, blocks):
    rows = other.shape[0]
    chips = tables[1].shape[0]
    bf16 = jnp.bfloat16
    return pl.pallas_call(
        prepare_kernel,
        in_specs=[SMEM] * 5 + [HBM] * (4 + HALF),
        out_specs=[SMEM] + [VMEM] * 7,
        out_shape=[
            jax.ShapeDtypeStruct((4 * chips,), jnp.int32),
            jax.ShapeDtypeStruct((HALF, 2, DH, PER * rows), bf16),
            jax.ShapeDtypeStruct((HALF, 2, DH, PER * rows), bf16),
            jax.ShapeDtypeStruct((HALF, 2, PER * rows, DH), bf16),
            jax.ShapeDtypeStruct((HALF, 2, PER * rows, DH), bf16),
            row_stats(rows),
            row_stats(rows),
            row_stats(rows),
        ],
        scratch_shapes=[pltpu.SMEM(tables[3].shape, jnp.int32)]
        + [pltpu.VMEM((2, rows, HALF * WIDE), bf16)] * 3
        + [pltpu.VMEM((1, HALF, 2 * rows, 2 * DH), bf16), pltpu.SemaphoreType.DMA((6 + HALF,))],
        compiler_params=pltpu.CompilerParams(vmem_limit_bytes=28 << 20),
        cost_estimate=pl.CostEstimate(flops=0, bytes_accessed=24 << 20, transcendentals=0),
    )(*tables, *mine, other, *blocks)


def measure_kernel(offsets, plan, qt_in, top_in, sum_in, *refs):
    count = len(offsets) * HALF
    blocks, (top_ref, sum_ref, qt_ref, kv_ref, sems) = refs[:count], refs[count:]
    pairs = [(qt_in, qt_ref), (top_in, top_ref), (sum_in, sum_ref)]
    pairs += [(held, kv_ref.at[i // HALF, i % HALF]) for i, held in enumerate(blocks)]
    for copy in run_copies(pairs, sems):
        copy.wait()
    measure_blocks(plan, offsets, kv_ref, qt_ref, top_ref, sum_ref)


def measure(offsets, plan, qt, top, total, blocks):
    rows = blocks[0].shape[0] // 2
    return pl.pallas_call(
        functools.partial(measure_kernel, offsets),
        in_specs=[SMEM] + [HBM] * (3 + len(blocks)),
        out_specs=[VMEM] * 2,
        out_shape=[row_stats(rows)] * 2,
        scratch_shapes=[
            pltpu.VMEM(qt.shape, qt.dtype),
            pltpu.VMEM((len(offsets), HALF, 2 * rows, 2 * DH), jnp.bfloat16),
            pltpu.SemaphoreType.DMA((3 + len(blocks),)),
        ],
        compiler_params=pltpu.CompilerParams(vmem_limit_bytes=20 << 20),
        cost_estimate=pl.CostEstimate(flops=0, bytes_accessed=12 << 20, transcendentals=0),
    )(plan, qt, top, total, *blocks)


def grads_kernel(chips, offsets, first, last, plan, *refs):
    far = chips // 2
    count = HALF * (len(offsets) + first)
    shared, refs = refs[:6 + first], refs[6 + first:]
    blocks, refs = refs[:count], refs[count:]
    carried = None
    if not first:
        carried, refs = refs[0], refs[1:]
    terms, refs = refs[:HALF], refs[HALF:]
    if first:
        ups, downs, refs = refs[:HALF], refs[HALF:2 * HALF], refs[2 * HALF:]
        lse_out, refs = refs[0], refs[1:]
    outs, refs = refs[:2 if last else 1], refs[2 if last else 1:]
    held, refs = refs[:6 + first], refs[6 + first:]
    qt_ref, gt_ref, gm_ref, qm_ref, delta_ref, lse_ref = held[:6]
    kv_ref, acc_ref, stage_ref, zero_ref, dqt_ref, offset_ref, sems, kv_sems, out_sems = refs
    rows = acc_ref.shape[1]

    pairs = []
    for slot, offset in enumerate(offsets):
        offset_ref[slot] = offset
        for head in range(HALF):
            at = head * (len(offsets) + first)
            if offset == far:
                pairs.append((blocks[at], kv_ref.at[slot, head, :rows]))
                pairs.append((blocks[at + 1], kv_ref.at[slot, head, rows:]))
            else:
                pltpu.make_async_copy(
                    blocks[at + slot + first], kv_ref.at[slot, head], kv_sems.at[slot, head]
                ).start()
    pairs += list(zip(shared, held))
    if carried is not None:
        pairs.append((carried, dqt_ref))
    copies = run_copies(pairs, sems)
    zero_ref[...] = jnp.zeros_like(zero_ref)
    if first:
        dqt_ref[...] = jnp.zeros_like(dqt_ref)
    for copy in copies:
        copy.wait()
    if first:
        sum_ref = held[6]
        measure_blocks(plan, [far], kv_ref, qt_ref, lse_ref, sum_ref)
        lse_ref[...] = lse_ref[...] * EXP_SCALE + jnp.log2(sum_ref[...])
        lse_out[...] = lse_ref[...]

    def out_copy(source, slot, head, target):
        return pltpu.make_async_copy(source, target, out_sems.at[slot, head])

    def visit(i, carry):
        at_block = i // 2
        half = i % 2
        offset = offset_ref[at_block]
        slot = i % 2
        here = pl.ds(pl.multiple_of(half * rows, rows), rows)
        seen_by = [plan[side * 2 * chips + offset * 2 + half] for side in range(2)]
        any_seen = (seen_by[0] > 0) | (seen_by[1] > 0)

        @pl.when((half == 0) & (offset != far))
        def _():
            for head in range(HALF):
                pltpu.make_async_copy(
                    blocks[-1], kv_ref.at[at_block, head], kv_sems.at[at_block, head]
                ).wait()

        @pl.when(i >= 2)
        def _():
            for head in range(HALF):
                out_copy(zero_ref, slot, head, terms[0].at[0, :rows]).wait()

        def send(sources):
            for head in range(HALF):
                if first:
                    @pl.when(offset != far)
                    def _():
                        out_copy(sources[head], slot, head, terms[head].at[at_block, here]).start()

                    @pl.when((offset == far) & (half == 0))
                    def _():
                        out_copy(sources[head], slot, head, ups[head]).start()

                    @pl.when((offset == far) & (half == 1))
                    def _():
                        out_copy(sources[head], slot, head, downs[head]).start()
                else:
                    out_copy(sources[head], slot, head, terms[head].at[at_block, here]).start()

        def look(side, carry):
            sees = plan[side * 2 * chips + offset * 2 + half]

            @pl.when(sees > 0)
            def _():
                for head in range(HALF):
                    at = (head, side)
                    k = kv_ref[at_block, head, here, :DH]
                    v = kv_ref[at_block, head, here, DH:]
                    s, seen = masked_scores(k, qt_ref[at], sees)
                    p = jnp.where(seen, jnp.exp2(s * EXP_SCALE - lse_ref[at]), 0.0)
                    ds = (p * (dot(v, gt_ref[at]) - delta_ref[at])).astype(jnp.bfloat16)
                    acc_ref[head, :, DH:] += dot(p.astype(jnp.bfloat16), gm_ref[at])
                    acc_ref[head, :, :DH] += dot(ds, qm_ref[at])
                    dqt_ref[at] += dot(k.T, ds)

            return carry

        @pl.when(any_seen)
        def _():
            acc_ref[...] = jnp.zeros_like(acc_ref)
            lax.fori_loop(0, 2, look, 0)
            for head in range(HALF):
                stage_ref[slot, head, :, :DH] = (acc_ref[head, :, :DH] * SCALE).astype(stage_ref.dtype)
                stage_ref[slot, head, :, DH:] = acc_ref[head, :, DH:].astype(stage_ref.dtype)
            send([stage_ref.at[slot, head] for head in range(HALF)])

        @pl.when(jnp.logical_not(any_seen))
        def _():
            send([zero_ref] * HALF)

        return carry

    lax.fori_loop(0, 2 * len(offsets), visit, 0)
    if last:
        for side, dq_ref in enumerate(outs):
            for head in range(HALF):
                for h in range(PER):
                    dq = (dqt_ref[head, side, :, h * rows:(h + 1) * rows] * SCALE).astype(dq_ref.dtype)
                    dq_ref[:, (head * PER + h) * DH:(head * PER + h + 1) * DH] = dq.T
    else:
        copy = pltpu.make_async_copy(dqt_ref, outs[0], sems.at[0])
        copy.start()
        copy.wait()
    for slot in range(2):
        for head in range(HALF):
            out_copy(zero_ref, slot, head, terms[0].at[0, :rows]).wait()


def gradients(prepared, stats, offsets, blocks, carried, last):
    plan, qt, gt, gm, qm, delta = prepared[:6]
    chips = plan.shape[0] // 4
    rows = gm.shape[2] // PER
    first = carried is None
    bf16, f32 = jnp.bfloat16, jnp.float32
    shared = (qt, gt, gm, qm, delta, *stats)
    arrays = [*shared, *blocks] + ([] if first else [carried])
    dense = jax.ShapeDtypeStruct((len(offsets), 2 * rows, 2 * DH), bf16)
    piece = jax.ShapeDtypeStruct((rows, 2 * DH), bf16)
    query = jax.ShapeDtypeStruct((rows, HALF * WIDE), bf16)
    sums = jax.ShapeDtypeStruct((HALF, 2, DH, PER * rows), f32)
    out_shape, out_specs = [dense] * HALF, [HBM] * HALF
    if first:
        out_shape += [piece] * (2 * HALF) + [row_stats(rows)]
        out_specs += [HBM] * (2 * HALF) + [VMEM]
    out_shape += [query] * 2 if last else [sums]
    out_specs += [VMEM] * 2 if last else [HBM]
    return pl.pallas_call(
        functools.partial(grads_kernel, chips, tuple(offsets), first, last),
        in_specs=[SMEM] + [HBM] * len(arrays),
        out_specs=out_specs,
        out_shape=out_shape,
        scratch_shapes=[pltpu.VMEM(array.shape, array.dtype) for array in shared]
        + [
            pltpu.VMEM((len(offsets), HALF, 2 * rows, 2 * DH), bf16),
            pltpu.VMEM((HALF, rows, 2 * DH), f32),
            pltpu.VMEM((2, HALF, rows, 2 * DH), bf16),
            pltpu.VMEM((rows, 2 * DH), bf16),
            pltpu.VMEM((HALF, 2, DH, PER * rows), f32),
            pltpu.SMEM((len(offsets),), jnp.int32),
            pltpu.SemaphoreType.DMA((2 * HALF + 8,)),
            pltpu.SemaphoreType.DMA((len(offsets), HALF)),
            pltpu.SemaphoreType.DMA((2, HALF)),
        ],
        compiler_params=pltpu.CompilerParams(vmem_limit_bytes=(30 << 20) + (len(offsets) << 19)),
        cost_estimate=pl.CostEstimate(flops=8 << 30, bytes_accessed=16 << 20, transcendentals=0),
    )(plan, *arrays)


def wide(x):
    return x.astype(jnp.float32)


def local(queries, keys, values, saved_out, grad_out, parents, assignment, lengths):
    rows = keys.shape[0]
    chips = lax.axis_size("leaf") // 2
    order = ring_order(chips)
    ahead = [(order[i], order[(i + 1) % chips]) for i in range(chips)]
    right = [(2 * a + c, 2 * b + c) for a, b in ahead for c in range(2)]
    left = [(b, a) for a, b in right]
    swap = [(2 * a + c, 2 * a + 1 - c) for a in range(chips) for c in range(2)]
    places = jnp.asarray([order.index(chip) for chip in range(chips)], jnp.int32)
    index = lax.axis_index("leaf").astype(jnp.int32)
    core = index % 2
    me = index.reshape(1)
    tables = (me, places, parents, assignment, lengths)

    def part(array, which, width):
        return lax.dynamic_slice(array, (0, which * width), (rows, width))

    def heads_of(which):
        pieces = [part(array, which * HALF + head, DH) for head in range(HALF) for array in (keys, values)]
        return jnp.concatenate(pieces, axis=1)

    kept = heads_of(core)
    got = lax.ppermute(heads_of(1 - core), "leaf", swap)
    own = []
    for head in range(HALF):
        cols = slice(head * 2 * DH, (head + 1) * 2 * DH)
        own.append(jnp.concatenate([kept[:, cols], got[:, cols]], axis=0))
    mine = (queries, grad_out, saved_out)
    late = lax.optimization_barrier((*mine, got))[:3]
    other = jnp.concatenate([part(array, 1 - core, HALF * WIDE) for array in late], axis=1)
    other = lax.ppermute(other, "leaf", swap)

    def shift(arrays, ring):
        return [lax.ppermute(array, "leaf", ring) for array in arrays]

    far = chips // 2
    blocks = {0: own}
    ups, downs = own, own
    prepared = stats = None
    for step in range(1, far):
        ups, downs = shift(ups, right), shift(downs, left)
        blocks[chips - step], blocks[step] = ups, downs
        if step == 1:
            prepared = prepare(tables, mine, other, own)
            stats = prepared[6:]
        else:
            seen = (step - 1, chips - step + 1)
            stats = measure(seen, prepared[0], prepared[1], *stats, [b for at in seen for b in blocks[at]])
        stats, held = lax.optimization_barrier((stats, (ups[1:], downs[1:])))
        ups, downs = ups[:1] + held[0], downs[:1] + held[1]
    halves = shift([a[:rows] for a in ups], right), shift([a[rows:] for a in downs], left)
    seen = (far - 1, far + 1)
    stats = measure(seen, prepared[0], prepared[1], *stats, [b for at in seen for b in blocks[at]])

    offsets = [far]
    for step in range(1, far - 1):
        offsets += [far + step, far - step]
    arrays = []
    for head in range(HALF):
        arrays += [halves[0][head], halves[1][head]] + [blocks[at][head] for at in offsets[1:]]
    *terms, lse, carried = gradients(prepared, stats, offsets, arrays, None, False)
    by_offset = {at: [terms[head][slot] for head in range(HALF)] for slot, at in enumerate(offsets)}
    ups = [jnp.pad(wide(a), ((0, rows), (0, 0))) for a in shift(terms[HALF:2 * HALF], right)]
    downs = [jnp.pad(wide(a), ((rows, 0), (0, 0))) for a in shift(terms[2 * HALF:], left)]

    def add(sums, at):
        return [(a + wide(b)).astype(jnp.bfloat16) for a, b in zip(sums, by_offset[at])]

    later = {far - 1: [chips - 1, 1], max(far - 2, 1): [0]}
    ours = theirs = None
    for step in range(far - 1, 0, -1):
        ups, downs = add(ups, step), add(downs, chips - step)
        if step in later:
            last = 0 in later[step]
            (lse, carried), ups, downs = lax.optimization_barrier(((lse, carried), ups, downs))
            arrays = [blocks[at][head] for head in range(HALF) for at in later[step]]
            *terms, lead = gradients(prepared, (lse,), later[step], arrays, carried, last)
            for slot, at in enumerate(later[step]):
                by_offset[at] = [terms[head][slot] for head in range(HALF)]
            if last:
                ours, theirs = terms[HALF], lax.ppermute(lead, "leaf", swap)
            else:
                carried = lead
        ups = [wide(a) for a in shift(ups, right)]
        downs = [wide(a) for a in shift(downs, left)]
    kept, got = [], []
    for head in range(HALF):
        summed = (wide(by_offset[0][head]) + ups[head] + downs[head]).astype(jnp.bfloat16)
        kept.append(summed[:rows])
        got.append(lax.ppermute(summed[rows:], "leaf", swap))

    def whole(kept, got):
        low = [jnp.where(core == 0, a, b) for a, b in zip(kept, got)]
        high = [jnp.where(core == 0, b, a) for a, b in zip(kept, got)]
        return jnp.concatenate(low + high, axis=1)

    key_grad = whole([a[:, :DH] for a in kept], [a[:, :DH] for a in got])
    value_grad = whole([a[:, DH:] for a in kept], [a[:, DH:] for a in got])
    return (whole([ours], [theirs]), key_grad, value_grad)


def solution(mesh):
    tokens = P(("groups", "leaf"), None)
    tables = P("groups")
    return jax.shard_map(
        local,
        mesh=mesh,
        in_specs=(tokens,) * 5 + (tables,) * 3,
        out_specs=(tokens,) * 3,
        check_vma=False,
    )
```

```python
import functools
import math

import jax
import jax.numpy as jnp
from jax import lax
from jax.experimental import pallas as pl
from jax.experimental.pallas import tpu as pltpu
from jax.sharding import PartitionSpec as P

HQ = 20
HK = 4
DH = 128
PER = HQ // HK
HALF = HK // 2
WIDE = PER * DH
ANCESTORS = 5
SLOTS = ANCESTORS + 1
OWN = 1 << 20
SCALE = 1.0 / math.sqrt(DH)
EXP_SCALE = SCALE / math.log(2.0)
NN = (((1,), (0,)), ((), ()))
SMEM = pl.BlockSpec(memory_space=pltpu.SMEM)
HBM = pl.BlockSpec(memory_space=pl.ANY)
VMEM = pl.BlockSpec(memory_space=pltpu.VMEM)


def dot(a, b):
    return lax.dot_general(a, b, NN, preferred_element_type=jnp.float32)


def ring_order(chips):
    if chips == 8:
        return [0, 2, 4, 6, 7, 5, 3, 1]
    return list(range(chips))


def walk(device, me, places, parents, assignment, lengths, owner, plan, side):
    chips = places.shape[0]
    here = places[me // 2]

    def place(held):
        at = places[held // 2] - here
        at = jnp.where(at < 0, at + chips, at)
        return side * 2 * chips + at * 2 + jnp.where(held % 2 == me % 2, 0, 1)

    def clear(at, carry):
        plan[side * 2 * chips + at] = 0
        return carry

    lax.fori_loop(0, 2 * chips, clear, 0)
    segment = assignment[device]
    plan[place(device)] = OWN
    up = parents[segment]
    for _ in range(ANCESTORS):
        at = jnp.maximum(up, 0)

        @pl.when(up >= 0)
        def _():
            plan[place(owner[at])] = lengths[at]

        up = jnp.where(up >= 0, parents[at], -1)


def run_copies(pairs, sems):
    copies = [pltpu.make_async_copy(a, b, sems.at[i]) for i, (a, b) in enumerate(pairs)]
    for copy in copies:
        copy.start()
    return copies


def column_of(me, head, h):
    return pl.multiple_of(((me % 2 * HALF + head) * PER + h) * DH, DH)


def seen_keys(rows, sees):
    lane_at = lax.broadcasted_iota(jnp.int32, (1, rows), 1)
    key_at = lax.broadcasted_iota(jnp.int32, (rows, 1), 0)
    return key_at <= jnp.where(sees == OWN, lane_at, sees - 1)


def measure_blocks(plan, offsets, kv_ref, qt_ref, top_ref, sum_ref):
    rows = kv_ref.shape[1] // 2
    chips = plan.shape[0] // 4
    for slot, offset in enumerate(offsets):
        def visit(i, carry):
            half, side = i // 2, i % 2
            sees = plan[side * 2 * chips + offset * 2 + half]

            @pl.when(sees > 0)
            def _():
                seen = seen_keys(rows, sees)
                keys = kv_ref[slot, pl.ds(pl.multiple_of(half * rows, rows), rows), :DH]
                for h in range(PER):
                    at = (side, slice(None), slice(h * rows, (h + 1) * rows))
                    s = jnp.where(seen, dot(keys, qt_ref[at]), -1e30)
                    old = top_ref[at]
                    top = jnp.maximum(old, jnp.max(s, axis=0, keepdims=True))
                    total = jnp.sum(jnp.exp2((s - top) * EXP_SCALE), axis=0, keepdims=True)
                    top_ref[at] = top
                    sum_ref[at] = sum_ref[at] * jnp.exp2((old - top) * EXP_SCALE) + total

            return carry

        lax.fori_loop(0, 4, visit, 0)


def prepare_kernel(head, me_ref, places, parents, assignment, lengths, queries, grads, saved, other, block, *refs):
    (plan, qt_ref, gt_ref, gm_ref, qm_ref, delta_ref, top_ref, sum_ref,
     owner, q_ref, g_ref, o_ref, kv_ref, sems) = refs
    rows = queries.shape[0]
    me = me_ref[0]
    column = pl.multiple_of((me % 2 * HALF + head) * WIDE, WIDE)
    pairs = [(block, kv_ref.at[0])]
    for at, (array, held) in enumerate(zip((queries, grads, saved), (q_ref, g_ref, o_ref))):
        pairs.append((array.at[:, pl.ds(column, WIDE)], held.at[0]))
        first = (at * HALF + head) * WIDE
        pairs.append((other.at[:, first:first + WIDE], held.at[1]))
    copies = run_copies(pairs, sems)

    def invert(d, carry):
        owner[assignment[d]] = d
        return carry

    lax.fori_loop(0, assignment.shape[0], invert, 0)
    walk(me, me, places, parents, assignment, lengths, owner, plan, 0)
    walk(me + 1 - me % 2 * 2, me, places, parents, assignment, lengths, owner, plan, 1)
    row_at = lax.broadcasted_iota(jnp.int32, (rows, 1), 0)
    top_ref[...] = jnp.full(top_ref.shape, -1e30, top_ref.dtype)
    sum_ref[...] = jnp.zeros_like(sum_ref)
    for copy in copies:
        copy.wait()
    for side, device in enumerate((me, me + 1 - me % 2 * 2)):
        live = row_at < lengths[assignment[device]]
        for h in range(PER):
            lanes = slice(h * rows, (h + 1) * rows)
            cols = slice(h * DH, (h + 1) * DH)
            masked = jnp.where(live, g_ref[side, :, cols], jnp.zeros((), g_ref.dtype))
            query = q_ref[side, :, cols]
            gm_ref[side, lanes, :] = masked
            qm_ref[side, lanes, :] = query
            gt_ref[side, :, lanes] = masked.T
            qt_ref[side, :, lanes] = query.T
            terms = masked.astype(jnp.float32) * o_ref[side, :, cols].astype(jnp.float32)
            delta_ref[side, :, lanes] = jnp.sum(terms.T, axis=0, keepdims=True)
    measure_blocks(plan, [0], kv_ref, qt_ref, top_ref, sum_ref)


def row_stats(rows):
    return jax.ShapeDtypeStruct((2, 1, PER * rows), jnp.float32)


def prepare(head, tables, mine, other, block):
    rows = other.shape[0]
    chips = tables[1].shape[0]
    bf16 = jnp.bfloat16
    return pl.pallas_call(
        functools.partial(prepare_kernel, head),
        in_specs=[SMEM] * 5 + [HBM] * 5,
        out_specs=[SMEM] + [VMEM] * 7,
        out_shape=[
            jax.ShapeDtypeStruct((4 * chips,), jnp.int32),
            jax.ShapeDtypeStruct((2, DH, PER * rows), bf16),
            jax.ShapeDtypeStruct((2, DH, PER * rows), bf16),
            jax.ShapeDtypeStruct((2, PER * rows, DH), bf16),
            jax.ShapeDtypeStruct((2, PER * rows, DH), bf16),
            row_stats(rows),
            row_stats(rows),
            row_stats(rows),
        ],
        scratch_shapes=[pltpu.SMEM(tables[3].shape, jnp.int32)]
        + [pltpu.VMEM((2, rows, WIDE), bf16)] * 3
        + [pltpu.VMEM((1, 2 * rows, 2 * DH), bf16), pltpu.SemaphoreType.DMA((7,))],
        compiler_params=pltpu.CompilerParams(vmem_limit_bytes=16 << 20),
        cost_estimate=pl.CostEstimate(flops=0, bytes_accessed=12 << 20, transcendentals=0),
    )(*tables, *mine, other, block)


def measure_kernel(offsets, plan, qt_in, top_in, sum_in, *refs):
    count = len(offsets)
    blocks, (top_ref, sum_ref, qt_ref, kv_ref, sems) = refs[:count], refs[count:]
    pairs = [(qt_in, qt_ref), (top_in, top_ref), (sum_in, sum_ref)]
    pairs += [(held, kv_ref.at[i]) for i, held in enumerate(blocks)]
    for copy in run_copies(pairs, sems):
        copy.wait()
    measure_blocks(plan, offsets, kv_ref, qt_ref, top_ref, sum_ref)


def measure(offsets, prepared, stats, blocks):
    rows = blocks[0].shape[0] // 2
    plan, qt = prepared[:2]
    return pl.pallas_call(
        functools.partial(measure_kernel, offsets),
        in_specs=[SMEM] + [HBM] * (3 + len(blocks)),
        out_specs=[VMEM] * 2,
        out_shape=[row_stats(rows)] * 2,
        scratch_shapes=[
            pltpu.VMEM(qt.shape, qt.dtype),
            pltpu.VMEM((len(offsets), 2 * rows, 2 * DH), jnp.bfloat16),
            pltpu.SemaphoreType.DMA((3 + len(blocks),)),
        ],
        compiler_params=pltpu.CompilerParams(vmem_limit_bytes=12 << 20),
        cost_estimate=pl.CostEstimate(flops=0, bytes_accessed=8 << 20, transcendentals=0),
    )(plan, qt, *stats, *blocks)


def grads_kernel(chips, offsets, first, last, plan, *refs):
    far = chips // 2
    shared = []
    for head in range(HALF):
        shared.append(refs[:6 + first])
        refs = refs[6 + first:]
    blocks = []
    for head in range(HALF):
        blocks.append(refs[:len(offsets) + first])
        refs = refs[len(offsets) + first:]
    carried = None
    if not first:
        carried, refs = refs[0], refs[1:]
    terms, refs = refs[:HALF], refs[HALF:]
    if first:
        ups, downs, refs = refs[:HALF], refs[HALF:2 * HALF], refs[2 * HALF:]
        lse_out, refs = refs[:HALF], refs[HALF:]
    outs, refs = refs[:2 if last else 1], refs[2 if last else 1:]
    held, refs = refs[:6 + first], refs[6 + first:]
    qt_ref, gt_ref, gm_ref, qm_ref, delta_ref, lse_ref = held[:6]
    (kv_ref, acc_ref, stage_ref, zero_ref, p_ref, ds_ref, dqt_ref, offset_ref,
     sems, kv_sems, out_sems, zero_sems) = refs
    rows = acc_ref.shape[1]
    slots = stage_ref.shape[0]

    pairs = []
    for head in range(HALF):
        for slot, offset in enumerate(offsets):
            offset_ref[slot] = offset
            if offset == far:
                pairs.append((blocks[head][0], kv_ref.at[slot, head, :rows]))
                pairs.append((blocks[head][1], kv_ref.at[slot, head, rows:]))
            else:
                pltpu.make_async_copy(
                    blocks[head][slot + first], kv_ref.at[slot, head], kv_sems.at[slot, head]
                ).start()
        pairs += [(array, ref.at[head]) for array, ref in zip(shared[head], held)]
    if carried is not None:
        pairs.append((carried, dqt_ref))
    copies = run_copies(pairs, sems)
    zero_ref[...] = jnp.zeros_like(zero_ref)

    def sees(side, i):
        return plan[side * 2 * chips + offset_ref[i // 2] * 2 + i % 2]

    def seen(i):
        return (sees(0, i) > 0) | (sees(1, i) > 0)

    def send(i, sources, sem_of):
        at_block, half = i // 2, i % 2
        here = pl.ds(pl.multiple_of(half * rows, rows), rows)
        for head in range(HALF):
            def put(target):
                pltpu.make_async_copy(sources[head], target, sem_of(head)).start()

            if not first:
                put(terms[head].at[at_block, here])
                continue

            @pl.when(i >= 2)
            def _():
                put(terms[head].at[at_block, here])

            @pl.when(i == 0)
            def _():
                put(ups[head])

            @pl.when(i == 1)
            def _():
                put(downs[head])

    def sent(sem_of):
        for head in range(HALF):
            pltpu.make_async_copy(zero_ref, terms[head].at[0, :rows], sem_of(head)).wait()

    def send_zeros(i, carry):
        @pl.when(jnp.logical_not(seen(i)))
        def _():
            send(i, [zero_ref] * HALF, lambda head: zero_sems.at[i, head])

        return carry

    lax.fori_loop(0, 2 * len(offsets), send_zeros, 0)
    if first:
        dqt_ref[...] = jnp.zeros_like(dqt_ref)
    for copy in copies:
        copy.wait()
    if first:
        for head in range(HALF):
            measure_blocks(
                plan, [far], kv_ref.at[:, head], qt_ref.at[head], lse_ref.at[head], held[6].at[head]
            )
            lse_ref[head] = lse_ref[head] * EXP_SCALE + jnp.log2(held[6][head])
            lse_out[head][...] = lse_ref[head]

    def visit(i, done):
        at_block, half = i // 2, i % 2
        here = pl.ds(pl.multiple_of(half * rows, rows), rows)

        @pl.when((half == 0) & (offset_ref[at_block] != far))
        def _():
            for head in range(HALF):
                pltpu.make_async_copy(
                    blocks[head][-1], kv_ref.at[at_block, head], kv_sems.at[at_block, head]
                ).wait()

        def look(side, carry):
            @pl.when(sees(side, i) > 0)
            def _():
                allowed = seen_keys(rows, sees(side, i))
                for head in range(HALF):
                    at = (head, side)
                    k = kv_ref[at_block, head, here, :DH]
                    v = kv_ref[at_block, head, here, DH:]
                    for h in range(PER):
                        lanes = slice(h * rows, (h + 1) * rows)
                        part = (head, side, slice(None), lanes)
                        s = dot(k, qt_ref[part]) * EXP_SCALE - lse_ref[part]
                        p = jnp.where(allowed, jnp.exp2(s), 0.0)
                        ds = p * (dot(v, gt_ref[part]) - delta_ref[part])
                        p_ref[head, :, lanes] = p.astype(p_ref.dtype)
                        ds_ref[head, :, lanes] = ds.astype(ds_ref.dtype)
                    acc_ref[head, :, DH:] += dot(p_ref[head], gm_ref[at])
                    acc_ref[head, :, :DH] += dot(ds_ref[head], qm_ref[at])
                    dqt_ref[at] += dot(k.T, ds_ref[head])

            return carry

        @pl.when(seen(i))
        def _():
            slot = done % slots

            @pl.when(done >= slots)
            def _():
                sent(lambda head: out_sems.at[slot, head])

            acc_ref[...] = jnp.zeros_like(acc_ref)
            lax.fori_loop(0, 2, look, 0)
            for head in range(HALF):
                stage_ref[slot, head, :, :DH] = (acc_ref[head, :, :DH] * SCALE).astype(stage_ref.dtype)
                stage_ref[slot, head, :, DH:] = acc_ref[head, :, DH:].astype(stage_ref.dtype)
            send(i, [stage_ref.at[slot, head] for head in range(HALF)], lambda head: out_sems.at[slot, head])

        return done + seen(i).astype(jnp.int32)

    done = lax.fori_loop(0, 2 * len(offsets), visit, jnp.int32(0))
    if last:
        for side, dq_ref in enumerate(outs):
            for head in range(HALF):
                for h in range(PER):
                    dq = (dqt_ref[head, side, :, h * rows:(h + 1) * rows] * SCALE).astype(dq_ref.dtype)
                    dq_ref[:, (head * PER + h) * DH:(head * PER + h + 1) * DH] = dq.T
    else:
        copy = pltpu.make_async_copy(dqt_ref, outs[0], sems.at[0])
        copy.start()
        copy.wait()

    def zeros_sent(i, carry):
        @pl.when(jnp.logical_not(seen(i)))
        def _():
            sent(lambda head: zero_sems.at[i, head])

        return carry

    lax.fori_loop(0, 2 * len(offsets), zeros_sent, 0)
    for slot in range(slots):
        @pl.when(done > slot)
        def _():
            sent(lambda head: out_sems.at[slot, head])


def gradients(prepared, stats, offsets, blocks, carried, last):
    plan = prepared[0][0]
    chips = plan.shape[0] // 4
    rows = blocks[0][-1].shape[0] // 2
    first = carried is None
    bf16, f32 = jnp.bfloat16, jnp.float32
    shared = [(*prepared[head][1:6], *stats[head]) for head in range(HALF)]
    arrays = [a for head in shared for a in head] + [a for head in blocks for a in head]
    arrays += [] if first else [carried]
    dense = jax.ShapeDtypeStruct((len(offsets), 2 * rows, 2 * DH), bf16)
    piece = jax.ShapeDtypeStruct((rows, 2 * DH), bf16)
    query = jax.ShapeDtypeStruct((rows, HALF * WIDE), bf16)
    sums = jax.ShapeDtypeStruct((HALF, 2, DH, PER * rows), f32)
    out_shape, out_specs = [dense] * HALF, [HBM] * HALF
    if first:
        out_shape += [piece] * (2 * HALF) + [row_stats(rows)] * HALF
        out_specs += [HBM] * (2 * HALF) + [VMEM] * HALF
    out_shape += [query] * 2 if last else [sums]
    out_specs += [VMEM] * 2 if last else [HBM]
    return pl.pallas_call(
        functools.partial(grads_kernel, chips, tuple(offsets), first, last),
        in_specs=[SMEM] + [HBM] * len(arrays),
        out_specs=out_specs,
        out_shape=out_shape,
        scratch_shapes=[pltpu.VMEM((HALF, *array.shape), array.dtype) for array in shared[0]]
        + [
            pltpu.VMEM((len(offsets), HALF, 2 * rows, 2 * DH), bf16),
            pltpu.VMEM((HALF, rows, 2 * DH), f32),
            pltpu.VMEM((4, HALF, rows, 2 * DH), bf16),
            pltpu.VMEM((rows, 2 * DH), bf16),
            pltpu.VMEM((HALF, rows, PER * rows), bf16),
            pltpu.VMEM((HALF, rows, PER * rows), bf16),
            pltpu.VMEM((HALF, 2, DH, PER * rows), f32),
            pltpu.SMEM((len(offsets),), jnp.int32),
            pltpu.SemaphoreType.DMA((HALF * (8 + first) + 1,)),
            pltpu.SemaphoreType.DMA((len(offsets), HALF)),
            pltpu.SemaphoreType.DMA((4, HALF)),
            pltpu.SemaphoreType.DMA((2 * len(offsets), HALF)),
        ],
        compiler_params=pltpu.CompilerParams(vmem_limit_bytes=(26 << 20) + (len(offsets) << 19)),
        cost_estimate=pl.CostEstimate(flops=8 << 30, bytes_accessed=16 << 20, transcendentals=0),
    )(plan, *arrays)


def wide(x):
    return x.astype(jnp.float32)


def local(queries, keys, values, saved_out, grad_out, parents, assignment, lengths):
    rows = keys.shape[0]
    chips = lax.axis_size("leaf") // 2
    order = ring_order(chips)
    ahead = [(order[i], order[(i + 1) % chips]) for i in range(chips)]
    right = [(2 * a + c, 2 * b + c) for a, b in ahead for c in range(2)]
    left = [(b, a) for a, b in right]
    swap = [(2 * a + c, 2 * a + 1 - c) for a in range(chips) for c in range(2)]
    places = jnp.asarray([order.index(chip) for chip in range(chips)], jnp.int32)
    index = lax.axis_index("leaf").astype(jnp.int32)
    core = index % 2
    me = index.reshape(1)
    tables = (me, places, parents, assignment, lengths)

    def part(array, which, width):
        return lax.dynamic_slice(array, (0, which * width), (rows, width))

    def heads_of(which):
        pieces = [part(array, which * HALF + head, DH) for head in range(HALF) for array in (keys, values)]
        return jnp.concatenate(pieces, axis=1)

    kept = heads_of(core)
    got = lax.ppermute(heads_of(1 - core), "leaf", swap)
    own = []
    for head in range(HALF):
        cols = slice(head * 2 * DH, (head + 1) * 2 * DH)
        own.append(jnp.concatenate([kept[:, cols], got[:, cols]], axis=0))
    mine = (queries, grad_out, saved_out)
    late = lax.optimization_barrier((*mine, got))[:3]
    other = jnp.concatenate([part(array, 1 - core, HALF * WIDE) for array in late], axis=1)
    other = lax.ppermute(other, "leaf", swap)

    def shift(arrays, ring):
        return [lax.ppermute(array, "leaf", ring) for array in arrays]

    far = chips // 2
    prepared, stats = [None] * HALF, [None] * HALF
    blocks, halves = [], []
    streams = [(block, block) for block in own]
    blocks = [{0: block} for block in own]
    for step in range(1, far):
        for head in range(HALF):
            up, down = streams[head]
            up, down = lax.ppermute(up, "leaf", right), lax.ppermute(down, "leaf", left)
            blocks[head][chips - step], blocks[head][step] = up, down
            if step == 1:
                prepared[head] = prepare(head, tables, mine, other, own[head])
                stats[head] = prepared[head][6:]
            else:
                met = (step - 1, chips - step + 1)
                stats[head] = measure(met, prepared[head], stats[head], [blocks[head][at] for at in met])
            stats[head], streams[head] = lax.optimization_barrier((stats[head], (up, down)))
    for head in range(HALF):
        up, down = streams[head]
        halves.append([lax.ppermute(up[:rows], "leaf", right), lax.ppermute(down[rows:], "leaf", left)])
        met = (far - 1, far + 1)
        stats[head] = measure(met, prepared[head], stats[head], [blocks[head][at] for at in met])

    offsets = [far]
    for step in range(1, far - 1):
        offsets += [far + step, far - step]
    arrays = [halves[head] + [blocks[head][at] for at in offsets[1:]] for head in range(HALF)]
    *terms, carried = gradients(prepared, stats, offsets, arrays, None, False)
    lse = [[a] for a in terms[3 * HALF:]]
    by_offset = {at: [terms[head][slot] for head in range(HALF)] for slot, at in enumerate(offsets)}
    ups = [jnp.pad(wide(a), ((0, rows), (0, 0))) for a in shift(terms[HALF:2 * HALF], right)]
    downs = [jnp.pad(wide(a), ((rows, 0), (0, 0))) for a in shift(terms[2 * HALF:3 * HALF], left)]

    def add(sums, at):
        return [(a + wide(b)).astype(jnp.bfloat16) for a, b in zip(sums, by_offset[at])]

    later = {far - 1: [chips - 1, 1], max(far - 2, 1): [0]}
    ours = theirs = None
    for step in range(far - 1, 0, -1):
        ups, downs = add(ups, step), add(downs, chips - step)
        if step in later:
            last = 0 in later[step]
            (lse, carried), ups, downs = lax.optimization_barrier(((lse, carried), ups, downs))
            arrays = [[blocks[head][at] for at in later[step]] for head in range(HALF)]
            *terms, lead = gradients(prepared, lse, later[step], arrays, carried, last)
            for slot, at in enumerate(later[step]):
                by_offset[at] = [terms[head][slot] for head in range(HALF)]
            if last:
                ours, theirs = terms[HALF], lax.ppermute(lead, "leaf", swap)
            else:
                carried = lead
        ups = [wide(a) for a in shift(ups, right)]
        downs = [wide(a) for a in shift(downs, left)]
    kept, got = [], []
    for head in range(HALF):
        summed = (wide(by_offset[0][head]) + ups[head] + downs[head]).astype(jnp.bfloat16)
        kept.append(summed[:rows])
        got.append(lax.ppermute(summed[rows:], "leaf", swap))

    def whole(kept, got):
        low = [jnp.where(core == 0, a, b) for a, b in zip(kept, got)]
        high = [jnp.where(core == 0, b, a) for a, b in zip(kept, got)]
        return jnp.concatenate(low + high, axis=1)

    key_grad = whole([a[:, :DH] for a in kept], [a[:, :DH] for a in got])
    value_grad = whole([a[:, DH:] for a in kept], [a[:, DH:] for a in got])
    return (whole([ours], [theirs]), key_grad, value_grad)


def solution(mesh):
    tokens = P(("groups", "leaf"), None)
    tables = P("groups")
    return jax.shard_map(
        local,
        mesh=mesh,
        in_specs=(tokens,) * 5 + (tables,) * 3,
        out_specs=(tokens,) * 3,
        check_vma=False,
    )
```

```python
import functools
import math

import jax
import jax.numpy as jnp
from jax import lax
from jax.experimental import pallas as pl
from jax.experimental.pallas import tpu as pltpu
from jax.sharding import PartitionSpec as P

HQ = 20
HK = 4
DH = 128
PER = HQ // HK
HALF = HK // 2
WIDE = PER * DH
ANCESTORS = 5
SLOTS = ANCESTORS + 1
OWN = 1 << 20
SCALE = 1.0 / math.sqrt(DH)
EXP_SCALE = SCALE / math.log(2.0)
NN = (((1,), (0,)), ((), ()))
SMEM = pl.BlockSpec(memory_space=pltpu.SMEM)
HBM = pl.BlockSpec(memory_space=pl.ANY)
VMEM = pl.BlockSpec(memory_space=pltpu.VMEM)


def dot(a, b):
    return lax.dot_general(a, b, NN, preferred_element_type=jnp.float32)


def ring_order(chips):
    if chips == 8:
        return [0, 2, 4, 6, 7, 5, 3, 1]
    return list(range(chips))


def walk(device, me, places, parents, assignment, lengths, owner, plan, side):
    chips = places.shape[0]
    here = places[me // 2]

    def place(held):
        at = places[held // 2] - here
        at = jnp.where(at < 0, at + chips, at)
        return side * 2 * chips + at * 2 + jnp.where(held % 2 == me % 2, 0, 1)

    def clear(at, carry):
        plan[side * 2 * chips + at] = 0
        return carry

    lax.fori_loop(0, 2 * chips, clear, 0)
    segment = assignment[device]
    plan[place(device)] = OWN
    up = parents[segment]
    for _ in range(ANCESTORS):
        at = jnp.maximum(up, 0)

        @pl.when(up >= 0)
        def _():
            plan[place(owner[at])] = lengths[at]

        up = jnp.where(up >= 0, parents[at], -1)


def run_copies(pairs, sems):
    copies = [pltpu.make_async_copy(a, b, sems.at[i]) for i, (a, b) in enumerate(pairs)]
    for copy in copies:
        copy.start()
    return copies


def column_of(me, head, h):
    return pl.multiple_of(((me % 2 * HALF + head) * PER + h) * DH, DH)


def seen_keys(rows, sees):
    lane_at = lax.broadcasted_iota(jnp.int32, (1, rows), 1)
    key_at = lax.broadcasted_iota(jnp.int32, (rows, 1), 0)
    return key_at <= jnp.where(sees == OWN, lane_at, sees - 1)


def measure_blocks(plan, offsets, kv_ref, qt_ref, top_ref, sum_ref):
    rows = kv_ref.shape[1] // 2
    chips = plan.shape[0] // 4
    for slot, offset in enumerate(offsets):
        def visit(i, carry):
            half, side = i // 2, i % 2
            sees = plan[side * 2 * chips + offset * 2 + half]

            @pl.when(sees > 0)
            def _():
                seen = seen_keys(rows, sees)
                keys = kv_ref[slot, pl.ds(pl.multiple_of(half * rows, rows), rows), :DH]
                for h in range(PER):
                    at = (side, slice(None), slice(h * rows, (h + 1) * rows))
                    s = jnp.where(seen, dot(keys, qt_ref[at]), -1e30)
                    old = top_ref[at]
                    top = jnp.maximum(old, jnp.max(s, axis=0, keepdims=True))
                    total = jnp.sum(jnp.exp2((s - top) * EXP_SCALE), axis=0, keepdims=True)
                    top_ref[at] = top
                    sum_ref[at] = sum_ref[at] * jnp.exp2((old - top) * EXP_SCALE) + total

            return carry

        lax.fori_loop(0, 4, visit, 0)


def prepare_kernel(head, me_ref, places, parents, assignment, lengths, queries, grads, saved, other, block, *refs):
    (plan, qt_ref, gt_ref, gm_ref, qm_ref, delta_ref, top_ref, sum_ref,
     owner, q_ref, g_ref, o_ref, kv_ref, sems) = refs
    rows = queries.shape[0]
    me = me_ref[0]
    column = pl.multiple_of((me % 2 * HALF + head) * WIDE, WIDE)
    pairs = [(block, kv_ref.at[0])]
    for at, (array, held) in enumerate(zip((queries, grads, saved), (q_ref, g_ref, o_ref))):
        pairs.append((array.at[:, pl.ds(column, WIDE)], held.at[0]))
        first = (at * HALF + head) * WIDE
        pairs.append((other.at[:, first:first + WIDE], held.at[1]))
    copies = run_copies(pairs, sems)

    def invert(d, carry):
        owner[assignment[d]] = d
        return carry

    lax.fori_loop(0, assignment.shape[0], invert, 0)
    walk(me, me, places, parents, assignment, lengths, owner, plan, 0)
    walk(me + 1 - me % 2 * 2, me, places, parents, assignment, lengths, owner, plan, 1)
    row_at = lax.broadcasted_iota(jnp.int32, (rows, 1), 0)
    top_ref[...] = jnp.full(top_ref.shape, -1e30, top_ref.dtype)
    sum_ref[...] = jnp.zeros_like(sum_ref)
    for copy in copies:
        copy.wait()
    for side, device in enumerate((me, me + 1 - me % 2 * 2)):
        live = row_at < lengths[assignment[device]]
        for h in range(PER):
            lanes = slice(h * rows, (h + 1) * rows)
            cols = slice(h * DH, (h + 1) * DH)
            masked = jnp.where(live, g_ref[side, :, cols], jnp.zeros((), g_ref.dtype))
            query = q_ref[side, :, cols]
            gm_ref[side, lanes, :] = masked
            qm_ref[side, lanes, :] = query
            gt_ref[side, :, lanes] = masked.T
            qt_ref[side, :, lanes] = query.T
            terms = masked.astype(jnp.float32) * o_ref[side, :, cols].astype(jnp.float32)
            delta_ref[side, :, lanes] = jnp.sum(terms.T, axis=0, keepdims=True)
    measure_blocks(plan, [0], kv_ref, qt_ref, top_ref, sum_ref)


def row_stats(rows):
    return jax.ShapeDtypeStruct((2, 1, PER * rows), jnp.float32)


def prepare(head, tables, mine, other, block):
    rows = other.shape[0]
    chips = tables[1].shape[0]
    bf16 = jnp.bfloat16
    return pl.pallas_call(
        functools.partial(prepare_kernel, head),
        in_specs=[SMEM] * 5 + [HBM] * 5,
        out_specs=[SMEM] + [VMEM] * 7,
        out_shape=[
            jax.ShapeDtypeStruct((4 * chips,), jnp.int32),
            jax.ShapeDtypeStruct((2, DH, PER * rows), bf16),
            jax.ShapeDtypeStruct((2, DH, PER * rows), bf16),
            jax.ShapeDtypeStruct((2, PER * rows, DH), bf16),
            jax.ShapeDtypeStruct((2, PER * rows, DH), bf16),
            row_stats(rows),
            row_stats(rows),
            row_stats(rows),
        ],
        scratch_shapes=[pltpu.SMEM(tables[3].shape, jnp.int32)]
        + [pltpu.VMEM((2, rows, WIDE), bf16)] * 3
        + [pltpu.VMEM((1, 2 * rows, 2 * DH), bf16), pltpu.SemaphoreType.DMA((7,))],
        compiler_params=pltpu.CompilerParams(vmem_limit_bytes=16 << 20),
        cost_estimate=pl.CostEstimate(flops=0, bytes_accessed=12 << 20, transcendentals=0),
    )(*tables, *mine, other, block)


def measure_kernel(offsets, plan, qt_ref, top_in, sum_in, *refs):
    count = len(offsets)
    blocks, (top_ref, sum_ref, kv_ref, sems) = refs[:count], refs[count:]
    copies = run_copies([(held, kv_ref.at[i]) for i, held in enumerate(blocks)], sems)
    top_ref[...] = top_in[...]
    sum_ref[...] = sum_in[...]
    for copy in copies:
        copy.wait()
    measure_blocks(plan, offsets, kv_ref, qt_ref, top_ref, sum_ref)


def measure(offsets, prepared, stats, blocks):
    rows = blocks[0].shape[0] // 2
    plan, qt = prepared[:2]
    return pl.pallas_call(
        functools.partial(measure_kernel, offsets),
        in_specs=[SMEM] + [VMEM] * 3 + [HBM] * len(blocks),
        out_specs=[VMEM] * 2,
        out_shape=[row_stats(rows)] * 2,
        scratch_shapes=[
            pltpu.VMEM((len(offsets), 2 * rows, 2 * DH), jnp.bfloat16),
            pltpu.SemaphoreType.DMA((len(blocks),)),
        ],
        compiler_params=pltpu.CompilerParams(vmem_limit_bytes=12 << 20),
        cost_estimate=pl.CostEstimate(flops=0, bytes_accessed=8 << 20, transcendentals=0),
    )(plan, qt, *stats, *blocks)


def grads_kernel(chips, offsets, first, last, plan, *refs):
    far = chips // 2
    shared = []
    for head in range(HALF):
        shared.append(refs[:6 + first])
        refs = refs[6 + first:]
    blocks = []
    for head in range(HALF):
        blocks.append(refs[:len(offsets) + first])
        refs = refs[len(offsets) + first:]
    carried = None
    if not first:
        carried, refs = refs[0], refs[1:]
    terms, refs = refs[:HALF], refs[HALF:]
    if first:
        ups, downs, refs = refs[:HALF], refs[HALF:2 * HALF], refs[2 * HALF:]
        lse_out, refs = refs[:HALF], refs[HALF:]
    outs, refs = refs[:2 if last else 1], refs[2 if last else 1:]
    (kv_ref, acc_ref, stage_ref, zero_ref, p_ref, ds_ref, sum_ref, dqt_ref, offset_ref,
     sems, kv_sems, out_sems, zero_sems) = refs
    lse_ref = lse_out if first else [head[5] for head in shared]
    if not last:
        dqt_ref = outs[0]
    rows = acc_ref.shape[1]
    slots = stage_ref.shape[0]

    pairs = []
    for head in range(HALF):
        for slot, offset in enumerate(offsets):
            offset_ref[slot] = offset
            if offset == far:
                pairs.append((blocks[head][0], kv_ref.at[slot, head, :rows]))
                pairs.append((blocks[head][1], kv_ref.at[slot, head, rows:]))
            else:
                pltpu.make_async_copy(
                    blocks[head][slot + first], kv_ref.at[slot, head], kv_sems.at[slot, head]
                ).start()
    copies = run_copies(pairs, sems)
    zero_ref[...] = jnp.zeros_like(zero_ref)

    def sees(side, i):
        return plan[side * 2 * chips + offset_ref[i // 2] * 2 + i % 2]

    def seen(i):
        return (sees(0, i) > 0) | (sees(1, i) > 0)

    def send(i, sources, sem_of):
        at_block, half = i // 2, i % 2
        here = pl.ds(pl.multiple_of(half * rows, rows), rows)
        for head in range(HALF):
            def put(target):
                pltpu.make_async_copy(sources[head], target, sem_of(head)).start()

            if not first:
                put(terms[head].at[at_block, here])
                continue

            @pl.when(i >= 2)
            def _():
                put(terms[head].at[at_block, here])

            @pl.when(i == 0)
            def _():
                put(ups[head])

            @pl.when(i == 1)
            def _():
                put(downs[head])

    def sent(sem_of):
        for head in range(HALF):
            pltpu.make_async_copy(zero_ref, terms[head].at[0, :rows], sem_of(head)).wait()

    def send_zeros(i, carry):
        @pl.when(jnp.logical_not(seen(i)))
        def _():
            send(i, [zero_ref] * HALF, lambda head: zero_sems.at[i, head])

        return carry

    lax.fori_loop(0, 2 * len(offsets), send_zeros, 0)
    dqt_ref[...] = jnp.zeros_like(dqt_ref) if first else carried[...]
    for copy in copies:
        copy.wait()
    if first:
        for head in range(HALF):
            top_ref, total_ref = lse_out[head], sum_ref.at[head]
            top_ref[...] = shared[head][5][...]
            total_ref[...] = shared[head][6][...]
            measure_blocks(plan, [far], kv_ref.at[:, head], shared[head][0], top_ref, total_ref)
            top_ref[...] = top_ref[...] * EXP_SCALE + jnp.log2(total_ref[...])

    def visit(i, done):
        at_block, half = i // 2, i % 2
        here = pl.ds(pl.multiple_of(half * rows, rows), rows)

        @pl.when((half == 0) & (offset_ref[at_block] != far))
        def _():
            for head in range(HALF):
                pltpu.make_async_copy(
                    blocks[head][-1], kv_ref.at[at_block, head], kv_sems.at[at_block, head]
                ).wait()

        def look(side, carry):
            @pl.when(sees(side, i) > 0)
            def _():
                allowed = seen_keys(rows, sees(side, i))
                for head in range(HALF):
                    qt_ref, gt_ref, gm_ref, qm_ref, delta_ref = shared[head][:5]
                    k = kv_ref[at_block, head, here, :DH]
                    v = kv_ref[at_block, head, here, DH:]
                    for h in range(PER):
                        lanes = slice(h * rows, (h + 1) * rows)
                        part = (side, slice(None), lanes)
                        s = dot(k, qt_ref[part]) * EXP_SCALE - lse_ref[head][part]
                        p = jnp.where(allowed, jnp.exp2(s), 0.0)
                        ds = p * (dot(v, gt_ref[part]) - delta_ref[part])
                        p_ref[head, :, lanes] = p.astype(p_ref.dtype)
                        ds_ref[head, :, lanes] = ds.astype(ds_ref.dtype)
                    acc_ref[head, :, DH:] += dot(p_ref[head], gm_ref[side])
                    acc_ref[head, :, :DH] += dot(ds_ref[head], qm_ref[side])
                    dqt_ref[head, side] += dot(k.T, ds_ref[head])

            return carry

        @pl.when(seen(i))
        def _():
            slot = done % slots

            @pl.when(done >= slots)
            def _():
                sent(lambda head: out_sems.at[slot, head])

            acc_ref[...] = jnp.zeros_like(acc_ref)
            lax.fori_loop(0, 2, look, 0)
            for head in range(HALF):
                stage_ref[slot, head, :, :DH] = (acc_ref[head, :, :DH] * SCALE).astype(stage_ref.dtype)
                stage_ref[slot, head, :, DH:] = acc_ref[head, :, DH:].astype(stage_ref.dtype)
            send(i, [stage_ref.at[slot, head] for head in range(HALF)], lambda head: out_sems.at[slot, head])

        return done + seen(i).astype(jnp.int32)

    done = lax.fori_loop(0, 2 * len(offsets), visit, jnp.int32(0))
    if last:
        for side, dq_ref in enumerate(outs):
            for head in range(HALF):
                for h in range(PER):
                    dq = (dqt_ref[head, side, :, h * rows:(h + 1) * rows] * SCALE).astype(dq_ref.dtype)
                    dq_ref[:, (head * PER + h) * DH:(head * PER + h + 1) * DH] = dq.T

    def zeros_sent(i, carry):
        @pl.when(jnp.logical_not(seen(i)))
        def _():
            sent(lambda head: zero_sems.at[i, head])

        return carry

    lax.fori_loop(0, 2 * len(offsets), zeros_sent, 0)
    for slot in range(slots):
        @pl.when(done > slot)
        def _():
            sent(lambda head: out_sems.at[slot, head])


def gradients(prepared, stats, offsets, blocks, carried, last):
    plan = prepared[0][0]
    chips = plan.shape[0] // 4
    rows = blocks[0][-1].shape[0] // 2
    first = carried is None
    bf16, f32 = jnp.bfloat16, jnp.float32
    shared = [(*prepared[head][1:6], *stats[head]) for head in range(HALF)]
    arrays = [a for head in shared for a in head] + [a for head in blocks for a in head]
    arrays += [] if first else [carried]
    dense = jax.ShapeDtypeStruct((len(offsets), 2 * rows, 2 * DH), bf16)
    piece = jax.ShapeDtypeStruct((rows, 2 * DH), bf16)
    query = jax.ShapeDtypeStruct((rows, HALF * WIDE), bf16)
    sums = jax.ShapeDtypeStruct((HALF, 2, DH, PER * rows), f32)
    out_shape, out_specs = [dense] * HALF, [HBM] * HALF
    if first:
        out_shape += [piece] * (2 * HALF) + [row_stats(rows)] * HALF
        out_specs += [HBM] * (2 * HALF) + [VMEM] * HALF
    out_shape += [query] * 2 if last else [sums]
    out_specs += [VMEM] * (2 if last else 1)
    flat = sum(len(head) for head in shared)
    in_specs = [SMEM] + [VMEM] * flat + [HBM] * (len(arrays) - flat)
    if not first:
        in_specs[-1] = VMEM
    return pl.pallas_call(
        functools.partial(grads_kernel, chips, tuple(offsets), first, last),
        in_specs=in_specs,
        out_specs=out_specs,
        out_shape=out_shape,
        scratch_shapes=[
            pltpu.VMEM((len(offsets), HALF, 2 * rows, 2 * DH), bf16),
            pltpu.VMEM((HALF, rows, 2 * DH), f32),
            pltpu.VMEM((4, HALF, rows, 2 * DH), bf16),
            pltpu.VMEM((rows, 2 * DH), bf16),
            pltpu.VMEM((HALF, rows, PER * rows), bf16),
            pltpu.VMEM((HALF, rows, PER * rows), bf16),
            pltpu.VMEM((HALF, 2, 1, PER * rows), f32),
            pltpu.VMEM((HALF, 2, DH, PER * rows) if last else (8, DH), f32),
            pltpu.SMEM((len(offsets),), jnp.int32),
            pltpu.SemaphoreType.DMA((2 * HALF,)),
            pltpu.SemaphoreType.DMA((len(offsets), HALF)),
            pltpu.SemaphoreType.DMA((4, HALF)),
            pltpu.SemaphoreType.DMA((2 * len(offsets), HALF)),
        ],
        compiler_params=pltpu.CompilerParams(vmem_limit_bytes=(24 << 20) + (len(offsets) << 19)),
        cost_estimate=pl.CostEstimate(flops=8 << 30, bytes_accessed=16 << 20, transcendentals=0),
    )(plan, *arrays)


def wide(x):
    return x.astype(jnp.float32)


def local(queries, keys, values, saved_out, grad_out, parents, assignment, lengths):
    rows = keys.shape[0]
    chips = lax.axis_size("leaf") // 2
    order = ring_order(chips)
    ahead = [(order[i], order[(i + 1) % chips]) for i in range(chips)]
    right = [(2 * a + c, 2 * b + c) for a, b in ahead for c in range(2)]
    left = [(b, a) for a, b in right]
    swap = [(2 * a + c, 2 * a + 1 - c) for a in range(chips) for c in range(2)]
    places = jnp.asarray([order.index(chip) for chip in range(chips)], jnp.int32)
    index = lax.axis_index("leaf").astype(jnp.int32)
    core = index % 2
    me = index.reshape(1)
    tables = (me, places, parents, assignment, lengths)

    def part(array, which, width):
        return lax.dynamic_slice(array, (0, which * width), (rows, width))

    def heads_of(which):
        pieces = [part(array, which * HALF + head, DH) for head in range(HALF) for array in (keys, values)]
        return jnp.concatenate(pieces, axis=1)

    kept = heads_of(core)
    got = lax.ppermute(heads_of(1 - core), "leaf", swap)
    own = []
    for head in range(HALF):
        cols = slice(head * 2 * DH, (head + 1) * 2 * DH)
        own.append(jnp.concatenate([kept[:, cols], got[:, cols]], axis=0))
    mine = (queries, grad_out, saved_out)
    late = lax.optimization_barrier((*mine, got))[:3]
    other = jnp.concatenate([part(array, 1 - core, HALF * WIDE) for array in late], axis=1)
    other = lax.ppermute(other, "leaf", swap)

    def shift(arrays, ring):
        return [lax.ppermute(array, "leaf", ring) for array in arrays]

    far = chips // 2
    prepared, stats = [None] * HALF, [None] * HALF
    blocks, halves = [], []
    streams = [(block, block) for block in own]
    blocks = [{0: block} for block in own]
    for step in range(1, far):
        for head in range(HALF):
            up, down = streams[head]
            up, down = lax.ppermute(up, "leaf", right), lax.ppermute(down, "leaf", left)
            blocks[head][chips - step], blocks[head][step] = up, down
            if step == 1:
                prepared[head] = prepare(head, tables, mine, other, own[head])
                stats[head] = prepared[head][6:]
            else:
                met = (step - 1, chips - step + 1)
                stats[head] = measure(met, prepared[head], stats[head], [blocks[head][at] for at in met])
            stats[head], streams[head] = lax.optimization_barrier((stats[head], (up, down)))
    for head in range(HALF):
        up, down = streams[head]
        halves.append([lax.ppermute(up[:rows], "leaf", right), lax.ppermute(down[rows:], "leaf", left)])
        met = (far - 1, far + 1)
        stats[head] = measure(met, prepared[head], stats[head], [blocks[head][at] for at in met])

    offsets = [far]
    for step in range(1, far - 1):
        offsets += [far + step, far - step]
    arrays = [halves[head] + [blocks[head][at] for at in offsets[1:]] for head in range(HALF)]
    *terms, carried = gradients(prepared, stats, offsets, arrays, None, False)
    lse = [[a] for a in terms[3 * HALF:]]
    by_offset = {at: [terms[head][slot] for head in range(HALF)] for slot, at in enumerate(offsets)}
    ups = [jnp.pad(wide(a), ((0, rows), (0, 0))) for a in shift(terms[HALF:2 * HALF], right)]
    downs = [jnp.pad(wide(a), ((rows, 0), (0, 0))) for a in shift(terms[2 * HALF:3 * HALF], left)]

    def add(sums, at):
        return [(a + wide(b)).astype(jnp.bfloat16) for a, b in zip(sums, by_offset[at])]

    later = {far - 1: [chips - 1, 1], max(far - 2, 1): [0]}
    ours = theirs = None
    for step in range(far - 1, 0, -1):
        ups, downs = add(ups, step), add(downs, chips - step)
        if step in later:
            last = 0 in later[step]
            (lse, carried), ups, downs = lax.optimization_barrier(((lse, carried), ups, downs))
            arrays = [[blocks[head][at] for at in later[step]] for head in range(HALF)]
            *terms, lead = gradients(prepared, lse, later[step], arrays, carried, last)
            for slot, at in enumerate(later[step]):
                by_offset[at] = [terms[head][slot] for head in range(HALF)]
            if last:
                ours, theirs = terms[HALF], lax.ppermute(lead, "leaf", swap)
            else:
                carried = lead
        ups = [wide(a) for a in shift(ups, right)]
        downs = [wide(a) for a in shift(downs, left)]
    kept, got = [], []
    for head in range(HALF):
        summed = (wide(by_offset[0][head]) + ups[head] + downs[head]).astype(jnp.bfloat16)
        kept.append(summed[:rows])
        got.append(lax.ppermute(summed[rows:], "leaf", swap))

    def whole(kept, got):
        low = [jnp.where(core == 0, a, b) for a, b in zip(kept, got)]
        high = [jnp.where(core == 0, b, a) for a, b in zip(kept, got)]
        return jnp.concatenate(low + high, axis=1)

    key_grad = whole([a[:, :DH] for a in kept], [a[:, :DH] for a in got])
    value_grad = whole([a[:, DH:] for a in kept], [a[:, DH:] for a in got])
    return (whole([ours], [theirs]), key_grad, value_grad)


def solution(mesh):
    tokens = P(("groups", "leaf"), None)
    tables = P("groups")
    return jax.shard_map(
        local,
        mesh=mesh,
        in_specs=(tokens,) * 5 + (tables,) * 3,
        out_specs=(tokens,) * 3,
        check_vma=False,
    )
```

```python
import functools
import math

import jax
import jax.numpy as jnp
from jax import lax
from jax.experimental import pallas as pl
from jax.experimental.pallas import tpu as pltpu
from jax.sharding import PartitionSpec as P

HQ = 20
HK = 4
DH = 128
PER = HQ // HK
HALF = HK // 2
WIDE = PER * DH
ANCESTORS = 5
SLOTS = ANCESTORS + 1
OWN = 1 << 20
SCALE = 1.0 / math.sqrt(DH)
EXP_SCALE = SCALE / math.log(2.0)
NN = (((1,), (0,)), ((), ()))
SMEM = pl.BlockSpec(memory_space=pltpu.SMEM)
HBM = pl.BlockSpec(memory_space=pl.ANY)
VMEM = pl.BlockSpec(memory_space=pltpu.VMEM)


def dot(a, b):
    return lax.dot_general(a, b, NN, preferred_element_type=jnp.float32)


def ring_order(chips):
    if chips == 8:
        return [0, 2, 4, 6, 7, 5, 3, 1]
    return list(range(chips))


def walk(device, me, places, parents, assignment, lengths, owner, plan, side):
    chips = places.shape[0]
    here = places[me // 2]

    def place(held):
        at = places[held // 2] - here
        at = jnp.where(at < 0, at + chips, at)
        return side * 2 * chips + at * 2 + jnp.where(held % 2 == me % 2, 0, 1)

    def clear(at, carry):
        plan[side * 2 * chips + at] = 0
        return carry

    lax.fori_loop(0, 2 * chips, clear, 0)
    segment = assignment[device]
    plan[place(device)] = OWN
    up = parents[segment]
    for _ in range(ANCESTORS):
        at = jnp.maximum(up, 0)

        @pl.when(up >= 0)
        def _():
            plan[place(owner[at])] = lengths[at]

        up = jnp.where(up >= 0, parents[at], -1)


def run_copies(pairs, sems):
    copies = [pltpu.make_async_copy(a, b, sems.at[i]) for i, (a, b) in enumerate(pairs)]
    for copy in copies:
        copy.start()
    return copies


def column_of(me, head, h):
    return pl.multiple_of(((me % 2 * HALF + head) * PER + h) * DH, DH)


def seen_keys(rows, sees):
    lane_at = lax.broadcasted_iota(jnp.int32, (1, rows), 1)
    key_at = lax.broadcasted_iota(jnp.int32, (rows, 1), 0)
    return key_at <= jnp.where(sees == OWN, lane_at, sees - 1)


def measure_blocks(plan, offsets, kv_ref, qt_ref, top_ref, sum_ref):
    rows = kv_ref.shape[1] // 2
    chips = plan.shape[0] // 4
    for slot, offset in enumerate(offsets):
        def visit(i, carry):
            half, side = i // 2, i % 2
            sees = plan[side * 2 * chips + offset * 2 + half]

            @pl.when(sees > 0)
            def _():
                seen = seen_keys(rows, sees)
                keys = kv_ref[slot, pl.ds(pl.multiple_of(half * rows, rows), rows), :DH]
                for h in range(PER):
                    at = (side, slice(None), slice(h * rows, (h + 1) * rows))
                    s = jnp.where(seen, dot(keys, qt_ref[at]), -1e30)
                    old = top_ref[at]
                    top = jnp.maximum(old, jnp.max(s, axis=0, keepdims=True))
                    total = jnp.sum(jnp.exp2((s - top) * EXP_SCALE), axis=0, keepdims=True)
                    top_ref[at] = top
                    sum_ref[at] = sum_ref[at] * jnp.exp2((old - top) * EXP_SCALE) + total

            return carry

        lax.fori_loop(0, 4, visit, 0)


def prepare_kernel(head, me_ref, places, parents, assignment, lengths, queries, grads, saved, other, block, *refs):
    (plan, qt_ref, gt_ref, gm_ref, qm_ref, delta_ref, top_ref, sum_ref,
     owner, q_ref, g_ref, o_ref, kv_ref, sems) = refs
    rows = queries.shape[0]
    me = me_ref[0]
    column = pl.multiple_of((me % 2 * HALF + head) * WIDE, WIDE)
    pairs = [(block, kv_ref.at[0])]
    for at, (array, held) in enumerate(zip((queries, grads, saved), (q_ref, g_ref, o_ref))):
        pairs.append((array.at[:, pl.ds(column, WIDE)], held.at[0]))
        first = (at * HALF + head) * WIDE
        pairs.append((other.at[:, first:first + WIDE], held.at[1]))
    copies = run_copies(pairs, sems)

    def invert(d, carry):
        owner[assignment[d]] = d
        return carry

    lax.fori_loop(0, assignment.shape[0], invert, 0)
    walk(me, me, places, parents, assignment, lengths, owner, plan, 0)
    walk(me + 1 - me % 2 * 2, me, places, parents, assignment, lengths, owner, plan, 1)
    row_at = lax.broadcasted_iota(jnp.int32, (rows, 1), 0)
    top_ref[...] = jnp.full(top_ref.shape, -1e30, top_ref.dtype)
    sum_ref[...] = jnp.zeros_like(sum_ref)
    for copy in copies:
        copy.wait()
    for side, device in enumerate((me, me + 1 - me % 2 * 2)):
        live = row_at < lengths[assignment[device]]
        for h in range(PER):
            lanes = slice(h * rows, (h + 1) * rows)
            cols = slice(h * DH, (h + 1) * DH)
            masked = jnp.where(live, g_ref[side, :, cols], jnp.zeros((), g_ref.dtype))
            query = q_ref[side, :, cols]
            gm_ref[side, lanes, :] = masked
            qm_ref[side, lanes, :] = query
            gt_ref[side, :, lanes] = masked.T
            qt_ref[side, :, lanes] = query.T
            terms = masked.astype(jnp.float32) * o_ref[side, :, cols].astype(jnp.float32)
            delta_ref[side, :, lanes] = jnp.sum(terms.T, axis=0, keepdims=True)
    measure_blocks(plan, [0], kv_ref, qt_ref, top_ref, sum_ref)


def row_stats(rows):
    return jax.ShapeDtypeStruct((2, 1, PER * rows), jnp.float32)


def prepare(head, tables, mine, other, block):
    rows = other.shape[0]
    chips = tables[1].shape[0]
    bf16 = jnp.bfloat16
    return pl.pallas_call(
        functools.partial(prepare_kernel, head),
        in_specs=[SMEM] * 5 + [HBM] * 5,
        out_specs=[SMEM] + [VMEM] * 7,
        out_shape=[
            jax.ShapeDtypeStruct((4 * chips,), jnp.int32),
            jax.ShapeDtypeStruct((2, DH, PER * rows), bf16),
            jax.ShapeDtypeStruct((2, DH, PER * rows), bf16),
            jax.ShapeDtypeStruct((2, PER * rows, DH), bf16),
            jax.ShapeDtypeStruct((2, PER * rows, DH), bf16),
            row_stats(rows),
            row_stats(rows),
            row_stats(rows),
        ],
        scratch_shapes=[pltpu.SMEM(tables[3].shape, jnp.int32)]
        + [pltpu.VMEM((2, rows, WIDE), bf16)] * 3
        + [pltpu.VMEM((1, 2 * rows, 2 * DH), bf16), pltpu.SemaphoreType.DMA((7,))],
        compiler_params=pltpu.CompilerParams(vmem_limit_bytes=16 << 20),
        cost_estimate=pl.CostEstimate(flops=0, bytes_accessed=12 << 20, transcendentals=0),
    )(*tables, *mine, other, block)


def measure_kernel(offsets, plan, qt_ref, top_in, sum_in, *refs):
    count = len(offsets)
    blocks, (top_ref, sum_ref, kv_ref, sems) = refs[:count], refs[count:]
    copies = run_copies([(held, kv_ref.at[i]) for i, held in enumerate(blocks)], sems)
    top_ref[...] = top_in[...]
    sum_ref[...] = sum_in[...]
    for copy in copies:
        copy.wait()
    measure_blocks(plan, offsets, kv_ref, qt_ref, top_ref, sum_ref)


def measure(offsets, prepared, stats, blocks):
    rows = blocks[0].shape[0] // 2
    plan, qt = prepared[:2]
    return pl.pallas_call(
        functools.partial(measure_kernel, offsets),
        in_specs=[SMEM] + [VMEM] * 3 + [HBM] * len(blocks),
        out_specs=[VMEM] * 2,
        out_shape=[row_stats(rows)] * 2,
        scratch_shapes=[
            pltpu.VMEM((len(offsets), 2 * rows, 2 * DH), jnp.bfloat16),
            pltpu.SemaphoreType.DMA((len(blocks),)),
        ],
        compiler_params=pltpu.CompilerParams(vmem_limit_bytes=12 << 20),
        cost_estimate=pl.CostEstimate(flops=0, bytes_accessed=8 << 20, transcendentals=0),
    )(plan, qt, *stats, *blocks)


def grads_kernel(chips, offsets, first, last, plan, *refs):
    far = chips // 2
    shared = []
    for head in range(HALF):
        shared.append(refs[:6 + first])
        refs = refs[6 + first:]
    blocks = []
    for head in range(HALF):
        blocks.append(refs[:len(offsets) + first])
        refs = refs[len(offsets) + first:]
    carried = None
    if not first:
        carried, refs = refs[0], refs[1:]
    terms, refs = refs[:HALF], refs[HALF:]
    if first:
        ups, downs, refs = refs[:HALF], refs[HALF:2 * HALF], refs[2 * HALF:]
        lse_out, refs = refs[:HALF], refs[HALF:]
    outs, refs = refs[:2 if last else 1], refs[2 if last else 1:]
    (kv_ref, acc_ref, stage_ref, zero_ref, p_ref, ds_ref, sum_ref, dqt_ref, offset_ref,
     sems, kv_sems, out_sems, zero_sems) = refs
    lse_ref = lse_out if first else [head[5] for head in shared]
    if not last:
        dqt_ref = outs[0]
    rows = acc_ref.shape[1]
    slots = stage_ref.shape[0]

    pairs = []
    for head in range(HALF):
        for slot, offset in enumerate(offsets):
            offset_ref[slot] = offset
            if offset == far:
                pairs.append((blocks[head][0], kv_ref.at[slot, head, :rows]))
                pairs.append((blocks[head][1], kv_ref.at[slot, head, rows:]))
            else:
                pltpu.make_async_copy(
                    blocks[head][slot + first], kv_ref.at[slot, head], kv_sems.at[slot, head]
                ).start()
    copies = run_copies(pairs, sems)
    zero_ref[...] = jnp.zeros_like(zero_ref)

    def sees(side, i):
        return plan[side * 2 * chips + offset_ref[i // 2] * 2 + i % 2]

    def seen(i):
        return (sees(0, i) > 0) | (sees(1, i) > 0)

    def send(i, sources, sem_of):
        at_block, half = i // 2, i % 2
        here = pl.ds(pl.multiple_of(half * rows, rows), rows)
        for head in range(HALF):
            def put(target):
                pltpu.make_async_copy(sources[head], target, sem_of(head)).start()

            if not first:
                put(terms[head].at[at_block, here])
                continue

            @pl.when(i >= 2)
            def _():
                put(terms[head].at[at_block, here])

            @pl.when(i == 0)
            def _():
                put(ups[head])

            @pl.when(i == 1)
            def _():
                put(downs[head])

    def sent(sem_of):
        for head in range(HALF):
            pltpu.make_async_copy(zero_ref, terms[head].at[0, :rows], sem_of(head)).wait()

    def send_zeros(i, carry):
        @pl.when(jnp.logical_not(seen(i)))
        def _():
            send(i, [zero_ref] * HALF, lambda head: zero_sems.at[i, head])

        return carry

    lax.fori_loop(0, 2 * len(offsets), send_zeros, 0)
    dqt_ref[...] = jnp.zeros_like(dqt_ref) if first else carried[...]
    for copy in copies:
        copy.wait()
    if first:
        for head in range(HALF):
            top_ref, total_ref = lse_out[head], sum_ref.at[head]
            top_ref[...] = shared[head][5][...]
            total_ref[...] = shared[head][6][...]
            measure_blocks(plan, [far], kv_ref.at[:, head], shared[head][0], top_ref, total_ref)
            top_ref[...] = top_ref[...] * EXP_SCALE + jnp.log2(total_ref[...])

    def visit(i, done):
        at_block, half = i // 2, i % 2
        here = pl.ds(pl.multiple_of(half * rows, rows), rows)

        @pl.when((half == 0) & (offset_ref[at_block] != far))
        def _():
            for head in range(HALF):
                pltpu.make_async_copy(
                    blocks[head][-1], kv_ref.at[at_block, head], kv_sems.at[at_block, head]
                ).wait()

        def look(side, carry):
            @pl.when(sees(side, i) > 0)
            def _():
                allowed = seen_keys(rows, sees(side, i))
                for head in range(HALF):
                    qt_ref, gt_ref, gm_ref, qm_ref, delta_ref = shared[head][:5]
                    k = kv_ref[at_block, head, here, :DH]
                    v = kv_ref[at_block, head, here, DH:]
                    for h in range(PER):
                        lanes = slice(h * rows, (h + 1) * rows)
                        part = (side, slice(None), lanes)
                        s = dot(k, qt_ref[part]) * EXP_SCALE - lse_ref[head][part]
                        p = jnp.where(allowed, jnp.exp2(s), 0.0)
                        ds = p * (dot(v, gt_ref[part]) - delta_ref[part])
                        p_ref[head, :, lanes] = p.astype(p_ref.dtype)
                        ds_ref[head, :, lanes] = ds.astype(ds_ref.dtype)
                    acc_ref[head, :, DH:] += dot(p_ref[head], gm_ref[side])
                    acc_ref[head, :, :DH] += dot(ds_ref[head], qm_ref[side])
                    dqt_ref[head, side] += dot(k.T, ds_ref[head])

            return carry

        @pl.when(seen(i))
        def _():
            slot = done % slots

            @pl.when(done >= slots)
            def _():
                sent(lambda head: out_sems.at[slot, head])

            acc_ref[...] = jnp.zeros_like(acc_ref)
            lax.fori_loop(0, 2, look, 0)
            for head in range(HALF):
                stage_ref[slot, head, :, :DH] = (acc_ref[head, :, :DH] * SCALE).astype(stage_ref.dtype)
                stage_ref[slot, head, :, DH:] = acc_ref[head, :, DH:].astype(stage_ref.dtype)
            send(i, [stage_ref.at[slot, head] for head in range(HALF)], lambda head: out_sems.at[slot, head])

        return done + seen(i).astype(jnp.int32)

    done = lax.fori_loop(0, 2 * len(offsets), visit, jnp.int32(0))
    if last:
        for side, dq_ref in enumerate(outs):
            for head in range(HALF):
                for h in range(PER):
                    dq = (dqt_ref[head, side, :, h * rows:(h + 1) * rows] * SCALE).astype(dq_ref.dtype)
                    dq_ref[:, (head * PER + h) * DH:(head * PER + h + 1) * DH] = dq.T

    def zeros_sent(i, carry):
        @pl.when(jnp.logical_not(seen(i)))
        def _():
            sent(lambda head: zero_sems.at[i, head])

        return carry

    lax.fori_loop(0, 2 * len(offsets), zeros_sent, 0)
    for slot in range(slots):
        @pl.when(done > slot)
        def _():
            sent(lambda head: out_sems.at[slot, head])


def gradients(prepared, stats, offsets, blocks, carried, last):
    plan = prepared[0][0]
    chips = plan.shape[0] // 4
    rows = blocks[0][-1].shape[0] // 2
    first = carried is None
    bf16, f32 = jnp.bfloat16, jnp.float32
    shared = [(*prepared[head][1:6], *stats[head]) for head in range(HALF)]
    arrays = [a for head in shared for a in head] + [a for head in blocks for a in head]
    arrays += [] if first else [carried]
    dense = jax.ShapeDtypeStruct((len(offsets), 2 * rows, 2 * DH), bf16)
    piece = jax.ShapeDtypeStruct((rows, 2 * DH), bf16)
    query = jax.ShapeDtypeStruct((rows, HALF * WIDE), bf16)
    sums = jax.ShapeDtypeStruct((HALF, 2, DH, PER * rows), f32)
    out_shape, out_specs = [dense] * HALF, [HBM] * HALF
    if first:
        out_shape += [piece] * (2 * HALF) + [row_stats(rows)] * HALF
        out_specs += [HBM] * (2 * HALF) + [VMEM] * HALF
    out_shape += [query] * 2 if last else [sums]
    out_specs += [VMEM] * (2 if last else 1)
    flat = sum(len(head) for head in shared)
    in_specs = [SMEM] + [VMEM] * flat + [HBM] * (len(arrays) - flat)
    if not first:
        in_specs[-1] = VMEM
    return pl.pallas_call(
        functools.partial(grads_kernel, chips, tuple(offsets), first, last),
        in_specs=in_specs,
        out_specs=out_specs,
        out_shape=out_shape,
        scratch_shapes=[
            pltpu.VMEM((len(offsets), HALF, 2 * rows, 2 * DH), bf16),
            pltpu.VMEM((HALF, rows, 2 * DH), f32),
            pltpu.VMEM((4, HALF, rows, 2 * DH), bf16),
            pltpu.VMEM((rows, 2 * DH), bf16),
            pltpu.VMEM((HALF, rows, PER * rows), bf16),
            pltpu.VMEM((HALF, rows, PER * rows), bf16),
            pltpu.VMEM((HALF, 2, 1, PER * rows), f32),
            pltpu.VMEM((HALF, 2, DH, PER * rows) if last else (8, DH), f32),
            pltpu.SMEM((len(offsets),), jnp.int32),
            pltpu.SemaphoreType.DMA((2 * HALF,)),
            pltpu.SemaphoreType.DMA((len(offsets), HALF)),
            pltpu.SemaphoreType.DMA((4, HALF)),
            pltpu.SemaphoreType.DMA((2 * len(offsets), HALF)),
        ],
        compiler_params=pltpu.CompilerParams(vmem_limit_bytes=(24 << 20) + (len(offsets) << 19)),
        cost_estimate=pl.CostEstimate(flops=8 << 30, bytes_accessed=16 << 20, transcendentals=0),
    )(plan, *arrays)


def wide(x):
    return x.astype(jnp.float32)


def local(queries, keys, values, saved_out, grad_out, parents, assignment, lengths):
    rows = keys.shape[0]
    chips = lax.axis_size("leaf") // 2
    order = ring_order(chips)
    ahead = [(order[i], order[(i + 1) % chips]) for i in range(chips)]
    right = [(2 * a + c, 2 * b + c) for a, b in ahead for c in range(2)]
    left = [(b, a) for a, b in right]
    swap = [(2 * a + c, 2 * a + 1 - c) for a in range(chips) for c in range(2)]
    places = jnp.asarray([order.index(chip) for chip in range(chips)], jnp.int32)
    index = lax.axis_index("leaf").astype(jnp.int32)
    core = index % 2
    me = index.reshape(1)
    tables = (me, places, parents, assignment, lengths)

    def part(array, which, width):
        return lax.dynamic_slice(array, (0, which * width), (rows, width))

    def heads_of(which):
        pieces = [part(array, which * HALF + head, DH) for head in range(HALF) for array in (keys, values)]
        return jnp.concatenate(pieces, axis=1)

    kept = heads_of(core)
    got = lax.ppermute(heads_of(1 - core), "leaf", swap)
    own = []
    for head in range(HALF):
        cols = slice(head * 2 * DH, (head + 1) * 2 * DH)
        own.append(jnp.concatenate([kept[:, cols], got[:, cols]], axis=0))
    mine = (queries, grad_out, saved_out)
    late = lax.optimization_barrier((*mine, got))[:3]
    other = jnp.concatenate([part(array, 1 - core, HALF * WIDE) for array in late], axis=1)
    other = lax.ppermute(other, "leaf", swap)

    def shift(arrays, ring):
        return [lax.ppermute(array, "leaf", ring) for array in arrays]

    far = chips // 2
    prepared, stats = [None] * HALF, [None] * HALF
    blocks, halves = [], []
    streams = [(block, block) for block in own]
    blocks = [{0: block} for block in own]
    for step in range(1, far):
        for head in range(HALF):
            up, down = streams[head]
            up, down = lax.ppermute(up, "leaf", right), lax.ppermute(down, "leaf", left)
            blocks[head][chips - step], blocks[head][step] = up, down
            if step == 1:
                prepared[head] = prepare(head, tables, mine, other, own[head])
                stats[head] = prepared[head][6:]
            else:
                met = (step - 1, chips - step + 1)
                stats[head] = measure(met, prepared[head], stats[head], [blocks[head][at] for at in met])
            stats[head], streams[head] = lax.optimization_barrier((stats[head], (up, down)))
    for head in range(HALF):
        up, down = streams[head]
        halves.append([lax.ppermute(up[:rows], "leaf", right), lax.ppermute(down[rows:], "leaf", left)])
        met = (far - 1, far + 1)
        stats[head] = measure(met, prepared[head], stats[head], [blocks[head][at] for at in met])

    offsets = [far]
    for step in range(1, far - 2):
        offsets += [far + step, far - step]
    arrays = [halves[head] + [blocks[head][at] for at in offsets[1:]] for head in range(HALF)]
    *terms, carried = gradients(prepared, stats, offsets, arrays, None, False)
    lse = [[a] for a in terms[3 * HALF:]]
    by_offset = {at: [terms[head][slot] for head in range(HALF)] for slot, at in enumerate(offsets)}
    ups = [jnp.pad(wide(a), ((0, rows), (0, 0))) for a in shift(terms[HALF:2 * HALF], right)]
    downs = [jnp.pad(wide(a), ((rows, 0), (0, 0))) for a in shift(terms[2 * HALF:3 * HALF], left)]

    def add(sums, at):
        return [(a + wide(b)).astype(jnp.bfloat16) for a, b in zip(sums, by_offset[at])]

    later = {3: [chips - 2, 2], 2: [chips - 1, 1], 1: [0]}
    ours = theirs = None
    for step in range(far - 1, 0, -1):
        ups, downs = add(ups, step), add(downs, chips - step)
        if step in later:
            last = 0 in later[step]
            (lse, carried), held = lax.optimization_barrier(((lse, carried), (ups[1:], downs[1:])))
            ups, downs = ups[:1] + held[0], downs[:1] + held[1]
            arrays = [[blocks[head][at] for at in later[step]] for head in range(HALF)]
            *terms, lead = gradients(prepared, lse, later[step], arrays, carried, last)
            for slot, at in enumerate(later[step]):
                by_offset[at] = [terms[head][slot] for head in range(HALF)]
            if last:
                ours, theirs = terms[HALF], lax.ppermute(lead, "leaf", swap)
            else:
                carried = lead
        ups = [wide(a) for a in shift(ups, right)]
        downs = [wide(a) for a in shift(downs, left)]
    kept, got = [], []
    for head in range(HALF):
        summed = (wide(by_offset[0][head]) + ups[head] + downs[head]).astype(jnp.bfloat16)
        kept.append(summed[:rows])
        got.append(lax.ppermute(summed[rows:], "leaf", swap))

    def whole(kept, got):
        low = [jnp.where(core == 0, a, b) for a, b in zip(kept, got)]
        high = [jnp.where(core == 0, b, a) for a, b in zip(kept, got)]
        return jnp.concatenate(low + high, axis=1)

    key_grad = whole([a[:, :DH] for a in kept], [a[:, :DH] for a in got])
    value_grad = whole([a[:, DH:] for a in kept], [a[:, DH:] for a in got])
    return (whole([ours], [theirs]), key_grad, value_grad)


def solution(mesh):
    tokens = P(("groups", "leaf"), None)
    tables = P("groups")
    return jax.shard_map(
        local,
        mesh=mesh,
        in_specs=(tokens,) * 5 + (tables,) * 3,
        out_specs=(tokens,) * 3,
        check_vma=False,
    )
```

```python
import functools
import math

import jax
import jax.numpy as jnp
from jax import lax
from jax.experimental import pallas as pl
from jax.experimental.pallas import tpu as pltpu
from jax.sharding import PartitionSpec as P

HQ = 20
HK = 4
DH = 128
PER = HQ // HK
HALF = HK // 2
WIDE = PER * DH
ANCESTORS = 5
SLOTS = ANCESTORS + 1
OWN = 1 << 20
SCALE = 1.0 / math.sqrt(DH)
EXP_SCALE = SCALE / math.log(2.0)
NN = (((1,), (0,)), ((), ()))
SMEM = pl.BlockSpec(memory_space=pltpu.SMEM)
HBM = pl.BlockSpec(memory_space=pl.ANY)
VMEM = pl.BlockSpec(memory_space=pltpu.VMEM)


def dot(a, b):
    return lax.dot_general(a, b, NN, preferred_element_type=jnp.float32)


def ring_order(chips):
    if chips == 8:
        return [0, 2, 4, 6, 7, 5, 3, 1]
    return list(range(chips))


def walk(device, me, places, parents, assignment, lengths, owner, plan, side):
    chips = places.shape[0]
    here = places[me // 2]

    def place(held):
        at = places[held // 2] - here
        at = jnp.where(at < 0, at + chips, at)
        return side * 2 * chips + at * 2 + jnp.where(held % 2 == me % 2, 0, 1)

    def clear(at, carry):
        plan[side * 2 * chips + at] = 0
        return carry

    lax.fori_loop(0, 2 * chips, clear, 0)
    segment = assignment[device]
    plan[place(device)] = OWN
    up = parents[segment]
    for _ in range(ANCESTORS):
        at = jnp.maximum(up, 0)

        @pl.when(up >= 0)
        def _():
            plan[place(owner[at])] = lengths[at]

        up = jnp.where(up >= 0, parents[at], -1)


def run_copies(pairs, sems):
    copies = [pltpu.make_async_copy(a, b, sems.at[i]) for i, (a, b) in enumerate(pairs)]
    for copy in copies:
        copy.start()
    return copies


def column_of(me, head, h):
    return pl.multiple_of(((me % 2 * HALF + head) * PER + h) * DH, DH)


def seen_keys(rows, sees):
    lane_at = lax.broadcasted_iota(jnp.int32, (1, rows), 1)
    key_at = lax.broadcasted_iota(jnp.int32, (rows, 1), 0)
    return key_at <= jnp.where(sees == OWN, lane_at, sees - 1)


def measure_blocks(plan, offsets, kv_ref, qt_ref, top_ref, sum_ref):
    rows = kv_ref.shape[1] // 2
    chips = plan.shape[0] // 4
    for slot, offset in enumerate(offsets):
        def visit(i, carry):
            half, side = i // 2, i % 2
            sees = plan[side * 2 * chips + offset * 2 + half]

            @pl.when(sees > 0)
            def _():
                seen = seen_keys(rows, sees)
                keys = kv_ref[slot, pl.ds(pl.multiple_of(half * rows, rows), rows), :DH]
                for h in range(PER):
                    at = (side, slice(None), slice(h * rows, (h + 1) * rows))
                    s = jnp.where(seen, dot(keys, qt_ref[at]), -1e30)
                    old = top_ref[at]
                    top = jnp.maximum(old, jnp.max(s, axis=0, keepdims=True))
                    total = jnp.sum(jnp.exp2((s - top) * EXP_SCALE), axis=0, keepdims=True)
                    top_ref[at] = top
                    sum_ref[at] = sum_ref[at] * jnp.exp2((old - top) * EXP_SCALE) + total

            return carry

        lax.fori_loop(0, 4, visit, 0)


def prepare_kernel(head, me_ref, places, parents, assignment, lengths, queries, grads, saved, other, block, *refs):
    (plan, qt_ref, gt_ref, gm_ref, qm_ref, delta_ref, top_ref, sum_ref,
     owner, q_ref, g_ref, o_ref, kv_ref, sems) = refs
    rows = queries.shape[0]
    me = me_ref[0]
    column = pl.multiple_of((me % 2 * HALF + head) * WIDE, WIDE)
    pairs = [(block, kv_ref.at[0])]
    for at, (array, held) in enumerate(zip((queries, grads, saved), (q_ref, g_ref, o_ref))):
        pairs.append((array.at[:, pl.ds(column, WIDE)], held.at[0]))
        first = (at * HALF + head) * WIDE
        pairs.append((other.at[:, first:first + WIDE], held.at[1]))
    copies = run_copies(pairs, sems)

    def invert(d, carry):
        owner[assignment[d]] = d
        return carry

    lax.fori_loop(0, assignment.shape[0], invert, 0)
    walk(me, me, places, parents, assignment, lengths, owner, plan, 0)
    walk(me + 1 - me % 2 * 2, me, places, parents, assignment, lengths, owner, plan, 1)
    row_at = lax.broadcasted_iota(jnp.int32, (rows, 1), 0)
    top_ref[...] = jnp.full(top_ref.shape, -1e30, top_ref.dtype)
    sum_ref[...] = jnp.zeros_like(sum_ref)
    for copy in copies:
        copy.wait()
    for side, device in enumerate((me, me + 1 - me % 2 * 2)):
        live = row_at < lengths[assignment[device]]
        for h in range(PER):
            lanes = slice(h * rows, (h + 1) * rows)
            cols = slice(h * DH, (h + 1) * DH)
            masked = jnp.where(live, g_ref[side, :, cols], jnp.zeros((), g_ref.dtype))
            query = q_ref[side, :, cols]
            gm_ref[side, lanes, :] = masked
            qm_ref[side, lanes, :] = query
            gt_ref[side, :, lanes] = masked.T
            qt_ref[side, :, lanes] = query.T
            terms = masked.astype(jnp.float32) * o_ref[side, :, cols].astype(jnp.float32)
            delta_ref[side, :, lanes] = jnp.sum(terms.T, axis=0, keepdims=True)
    measure_blocks(plan, [0], kv_ref, qt_ref, top_ref, sum_ref)


def row_stats(rows):
    return jax.ShapeDtypeStruct((2, 1, PER * rows), jnp.float32)


def prepare(head, tables, mine, other, block):
    rows = other.shape[0]
    chips = tables[1].shape[0]
    bf16 = jnp.bfloat16
    return pl.pallas_call(
        functools.partial(prepare_kernel, head),
        in_specs=[SMEM] * 5 + [HBM] * 5,
        out_specs=[SMEM] + [VMEM] * 7,
        out_shape=[
            jax.ShapeDtypeStruct((4 * chips,), jnp.int32),
            jax.ShapeDtypeStruct((2, DH, PER * rows), bf16),
            jax.ShapeDtypeStruct((2, DH, PER * rows), bf16),
            jax.ShapeDtypeStruct((2, PER * rows, DH), bf16),
            jax.ShapeDtypeStruct((2, PER * rows, DH), bf16),
            row_stats(rows),
            row_stats(rows),
            row_stats(rows),
        ],
        scratch_shapes=[pltpu.SMEM(tables[3].shape, jnp.int32)]
        + [pltpu.VMEM((2, rows, WIDE), bf16)] * 3
        + [pltpu.VMEM((1, 2 * rows, 2 * DH), bf16), pltpu.SemaphoreType.DMA((7,))],
        compiler_params=pltpu.CompilerParams(vmem_limit_bytes=8 << 20),
        cost_estimate=pl.CostEstimate(flops=0, bytes_accessed=12 << 20, transcendentals=0),
    )(*tables, *mine, other, block)


def measure_kernel(offsets, plan, qt_ref, top_in, sum_in, *refs):
    count = len(offsets)
    blocks, (top_ref, sum_ref, kv_ref, sems) = refs[:count], refs[count:]
    copies = run_copies([(held, kv_ref.at[i]) for i, held in enumerate(blocks)], sems)
    top_ref[...] = top_in[...]
    sum_ref[...] = sum_in[...]
    for copy in copies:
        copy.wait()
    measure_blocks(plan, offsets, kv_ref, qt_ref, top_ref, sum_ref)


def measure(offsets, prepared, stats, blocks):
    rows = blocks[0].shape[0] // 2
    plan, qt = prepared[:2]
    return pl.pallas_call(
        functools.partial(measure_kernel, offsets),
        in_specs=[SMEM] + [VMEM] * 3 + [HBM] * len(blocks),
        out_specs=[VMEM] * 2,
        out_shape=[row_stats(rows)] * 2,
        scratch_shapes=[
            pltpu.VMEM((len(offsets), 2 * rows, 2 * DH), jnp.bfloat16),
            pltpu.SemaphoreType.DMA((len(blocks),)),
        ],
        compiler_params=pltpu.CompilerParams(vmem_limit_bytes=6 << 20),
        cost_estimate=pl.CostEstimate(flops=0, bytes_accessed=8 << 20, transcendentals=0),
    )(plan, qt, *stats, *blocks)


def grads_kernel(chips, offsets, first, last, plan, *refs):
    far = chips // 2
    shared = []
    for head in range(HALF):
        shared.append(refs[:6 + first])
        refs = refs[6 + first:]
    blocks = []
    for head in range(HALF):
        blocks.append(refs[:len(offsets) + first])
        refs = refs[len(offsets) + first:]
    carried = None
    if not first:
        carried, refs = refs[0], refs[1:]
    terms, refs = refs[:HALF], refs[HALF:]
    if first:
        ups, downs, refs = refs[:HALF], refs[HALF:2 * HALF], refs[2 * HALF:]
        lse_out, refs = refs[:HALF], refs[HALF:]
    outs, refs = refs[:2 if last else 1], refs[2 if last else 1:]
    (kv_ref, acc_ref, stage_ref, zero_ref, p_ref, ds_ref, sum_ref, dqt_ref, offset_ref,
     sems, kv_sems, out_sems, zero_sems) = refs
    lse_ref = lse_out if first else [head[5] for head in shared]
    if not last:
        dqt_ref = outs[0]
    rows = acc_ref.shape[1]
    slots = stage_ref.shape[0]

    pairs = []
    for head in range(HALF):
        for slot, offset in enumerate(offsets):
            offset_ref[slot] = offset
            if offset == far:
                pairs.append((blocks[head][0], kv_ref.at[slot, head, :rows]))
                pairs.append((blocks[head][1], kv_ref.at[slot, head, rows:]))
            else:
                pltpu.make_async_copy(
                    blocks[head][slot + first], kv_ref.at[slot, head], kv_sems.at[slot, head]
                ).start()
    copies = run_copies(pairs, sems)
    zero_ref[...] = jnp.zeros_like(zero_ref)

    def sees(side, i):
        return plan[side * 2 * chips + offset_ref[i // 2] * 2 + i % 2]

    def seen(i):
        return (sees(0, i) > 0) | (sees(1, i) > 0)

    def send(i, sources, sem_of):
        at_block, half = i // 2, i % 2
        here = pl.ds(pl.multiple_of(half * rows, rows), rows)
        for head in range(HALF):
            def put(target):
                pltpu.make_async_copy(sources[head], target, sem_of(head)).start()

            if not first:
                put(terms[head].at[at_block, here])
                continue

            @pl.when(i >= 2)
            def _():
                put(terms[head].at[at_block, here])

            @pl.when(i == 0)
            def _():
                put(ups[head])

            @pl.when(i == 1)
            def _():
                put(downs[head])

    def sent(sem_of):
        for head in range(HALF):
            pltpu.make_async_copy(zero_ref, terms[head].at[0, :rows], sem_of(head)).wait()

    def send_zeros(i, carry):
        @pl.when(jnp.logical_not(seen(i)))
        def _():
            send(i, [zero_ref] * HALF, lambda head: zero_sems.at[i, head])

        return carry

    lax.fori_loop(0, 2 * len(offsets), send_zeros, 0)
    dqt_ref[...] = jnp.zeros_like(dqt_ref) if first else carried[...]
    for copy in copies:
        copy.wait()
    if first:
        for head in range(HALF):
            top_ref, total_ref = lse_out[head], sum_ref.at[head]
            top_ref[...] = shared[head][5][...]
            total_ref[...] = shared[head][6][...]
            measure_blocks(plan, [far], kv_ref.at[:, head], shared[head][0], top_ref, total_ref)
            top_ref[...] = top_ref[...] * EXP_SCALE + jnp.log2(total_ref[...])

    def visit(i, done):
        at_block, half = i // 2, i % 2
        here = pl.ds(pl.multiple_of(half * rows, rows), rows)

        @pl.when((half == 0) & (offset_ref[at_block] != far))
        def _():
            for head in range(HALF):
                pltpu.make_async_copy(
                    blocks[head][-1], kv_ref.at[at_block, head], kv_sems.at[at_block, head]
                ).wait()

        def look(side, carry):
            @pl.when(sees(side, i) > 0)
            def _():
                allowed = seen_keys(rows, sees(side, i))
                for head in range(HALF):
                    qt_ref, gt_ref, gm_ref, qm_ref, delta_ref = shared[head][:5]
                    k = kv_ref[at_block, head, here, :DH]
                    v = kv_ref[at_block, head, here, DH:]
                    for h in range(PER):
                        lanes = slice(h * rows, (h + 1) * rows)
                        part = (side, slice(None), lanes)
                        s = dot(k, qt_ref[part]) * EXP_SCALE - lse_ref[head][part]
                        p = jnp.where(allowed, jnp.exp2(s), 0.0)
                        ds = p * (dot(v, gt_ref[part]) - delta_ref[part])
                        p_ref[head, :, lanes] = p.astype(p_ref.dtype)
                        ds_ref[head, :, lanes] = ds.astype(ds_ref.dtype)
                    acc_ref[head, :, DH:] += dot(p_ref[head], gm_ref[side])
                    acc_ref[head, :, :DH] += dot(ds_ref[head], qm_ref[side])
                    dqt_ref[head, side] += dot(k.T, ds_ref[head])

            return carry

        @pl.when(seen(i))
        def _():
            slot = done % slots

            @pl.when(done >= slots)
            def _():
                sent(lambda head: out_sems.at[slot, head])

            acc_ref[...] = jnp.zeros_like(acc_ref)
            lax.fori_loop(0, 2, look, 0)
            for head in range(HALF):
                stage_ref[slot, head, :, :DH] = (acc_ref[head, :, :DH] * SCALE).astype(stage_ref.dtype)
                stage_ref[slot, head, :, DH:] = acc_ref[head, :, DH:].astype(stage_ref.dtype)
            send(i, [stage_ref.at[slot, head] for head in range(HALF)], lambda head: out_sems.at[slot, head])

        return done + seen(i).astype(jnp.int32)

    done = lax.fori_loop(0, 2 * len(offsets), visit, jnp.int32(0))
    if last:
        for side, dq_ref in enumerate(outs):
            for head in range(HALF):
                for h in range(PER):
                    dq = (dqt_ref[head, side, :, h * rows:(h + 1) * rows] * SCALE).astype(dq_ref.dtype)
                    dq_ref[:, (head * PER + h) * DH:(head * PER + h + 1) * DH] = dq.T

    def zeros_sent(i, carry):
        @pl.when(jnp.logical_not(seen(i)))
        def _():
            sent(lambda head: zero_sems.at[i, head])

        return carry

    lax.fori_loop(0, 2 * len(offsets), zeros_sent, 0)
    for slot in range(slots):
        @pl.when(done > slot)
        def _():
            sent(lambda head: out_sems.at[slot, head])


def gradients(prepared, stats, offsets, blocks, carried, last):
    plan = prepared[0][0]
    chips = plan.shape[0] // 4
    rows = blocks[0][-1].shape[0] // 2
    first = carried is None
    bf16, f32 = jnp.bfloat16, jnp.float32
    shared = [(*prepared[head][1:6], *stats[head]) for head in range(HALF)]
    arrays = [a for head in shared for a in head] + [a for head in blocks for a in head]
    arrays += [] if first else [carried]
    dense = jax.ShapeDtypeStruct((len(offsets), 2 * rows, 2 * DH), bf16)
    piece = jax.ShapeDtypeStruct((rows, 2 * DH), bf16)
    query = jax.ShapeDtypeStruct((rows, HALF * WIDE), bf16)
    sums = jax.ShapeDtypeStruct((HALF, 2, DH, PER * rows), f32)
    out_shape, out_specs = [dense] * HALF, [HBM] * HALF
    if first:
        out_shape += [piece] * (2 * HALF) + [row_stats(rows)] * HALF
        out_specs += [HBM] * (2 * HALF) + [VMEM] * HALF
    out_shape += [query] * 2 if last else [sums]
    out_specs += [VMEM] * (2 if last else 1)
    flat = sum(len(head) for head in shared)
    in_specs = [SMEM] + [VMEM] * flat + [HBM] * (len(arrays) - flat)
    if not first:
        in_specs[-1] = VMEM
    return pl.pallas_call(
        functools.partial(grads_kernel, chips, tuple(offsets), first, last),
        in_specs=in_specs,
        out_specs=out_specs,
        out_shape=out_shape,
        scratch_shapes=[
            pltpu.VMEM((len(offsets), HALF, 2 * rows, 2 * DH), bf16),
            pltpu.VMEM((HALF, rows, 2 * DH), f32),
            pltpu.VMEM((4, HALF, rows, 2 * DH), bf16),
            pltpu.VMEM((rows, 2 * DH), bf16),
            pltpu.VMEM((HALF, rows, PER * rows), bf16),
            pltpu.VMEM((HALF, rows, PER * rows), bf16),
            pltpu.VMEM((HALF, 2, 1, PER * rows), f32),
            pltpu.VMEM((HALF, 2, DH, PER * rows) if last else (8, DH), f32),
            pltpu.SMEM((len(offsets),), jnp.int32),
            pltpu.SemaphoreType.DMA((2 * HALF,)),
            pltpu.SemaphoreType.DMA((len(offsets), HALF)),
            pltpu.SemaphoreType.DMA((4, HALF)),
            pltpu.SemaphoreType.DMA((2 * len(offsets), HALF)),
        ],
        compiler_params=pltpu.CompilerParams(vmem_limit_bytes=(13 << 20) + (len(offsets) << 19)),
        cost_estimate=pl.CostEstimate(flops=8 << 30, bytes_accessed=16 << 20, transcendentals=0),
    )(plan, *arrays)


def wide(x):
    return x.astype(jnp.float32)


def local(queries, keys, values, saved_out, grad_out, parents, assignment, lengths):
    rows = keys.shape[0]
    chips = lax.axis_size("leaf") // 2
    order = ring_order(chips)
    ahead = [(order[i], order[(i + 1) % chips]) for i in range(chips)]
    right = [(2 * a + c, 2 * b + c) for a, b in ahead for c in range(2)]
    left = [(b, a) for a, b in right]
    swap = [(2 * a + c, 2 * a + 1 - c) for a in range(chips) for c in range(2)]
    places = jnp.asarray([order.index(chip) for chip in range(chips)], jnp.int32)
    index = lax.axis_index("leaf").astype(jnp.int32)
    core = index % 2
    me = index.reshape(1)
    tables = (me, places, parents, assignment, lengths)

    def part(array, which, width):
        return lax.dynamic_slice(array, (0, which * width), (rows, width))

    def heads_of(which):
        pieces = [part(array, which * HALF + head, DH) for head in range(HALF) for array in (keys, values)]
        return jnp.concatenate(pieces, axis=1)

    kept = heads_of(core)
    got = lax.ppermute(heads_of(1 - core), "leaf", swap)
    own = []
    for head in range(HALF):
        cols = slice(head * 2 * DH, (head + 1) * 2 * DH)
        own.append(jnp.concatenate([kept[:, cols], got[:, cols]], axis=0))
    mine = (queries, grad_out, saved_out)
    late = lax.optimization_barrier((*mine, got))[:3]
    other = jnp.concatenate([part(array, 1 - core, HALF * WIDE) for array in late], axis=1)
    other = lax.ppermute(other, "leaf", swap)

    def shift(arrays, ring):
        return [lax.ppermute(array, "leaf", ring) for array in arrays]

    far = chips // 2
    prepared, stats = [None] * HALF, [None] * HALF
    blocks, halves = [], []
    streams = [(block, block) for block in own]
    blocks = [{0: block} for block in own]
    for step in range(1, far):
        for head in range(HALF):
            up, down = streams[head]
            up, down = lax.ppermute(up, "leaf", right), lax.ppermute(down, "leaf", left)
            blocks[head][chips - step], blocks[head][step] = up, down
            if step == 1:
                prepared[head] = prepare(head, tables, mine, other, own[head])
                stats[head] = prepared[head][6:]
            else:
                met = (step - 1, chips - step + 1)
                stats[head] = measure(met, prepared[head], stats[head], [blocks[head][at] for at in met])
            stats[head], streams[head] = lax.optimization_barrier((stats[head], (up, down)))
    for head in range(HALF):
        up, down = streams[head]
        halves.append([lax.ppermute(up[:rows], "leaf", right), lax.ppermute(down[rows:], "leaf", left)])
        met = (far - 1, far + 1)
        stats[head] = measure(met, prepared[head], stats[head], [blocks[head][at] for at in met])

    offsets = [far]
    for step in range(1, far - 2):
        offsets += [far + step, far - step]
    arrays = [halves[head] + [blocks[head][at] for at in offsets[1:]] for head in range(HALF)]
    *terms, carried = gradients(prepared, stats, offsets, arrays, None, False)
    lse = [[a] for a in terms[3 * HALF:]]
    by_offset = {at: [terms[head][slot] for head in range(HALF)] for slot, at in enumerate(offsets)}
    ups = [jnp.pad(wide(a), ((0, rows), (0, 0))) for a in shift(terms[HALF:2 * HALF], right)]
    downs = [jnp.pad(wide(a), ((rows, 0), (0, 0))) for a in shift(terms[2 * HALF:3 * HALF], left)]

    def add(sums, at):
        return [(a + wide(b)).astype(jnp.bfloat16) for a, b in zip(sums, by_offset[at])]

    later = {3: [chips - 2, 2], 2: [chips - 1, 1], 1: [0]}
    ours = theirs = None
    for step in range(far - 1, 0, -1):
        ups, downs = add(ups, step), add(downs, chips - step)
        if step in later:
            last = 0 in later[step]
            (lse, carried), held = lax.optimization_barrier(((lse, carried), (ups[1:], downs[1:])))
            ups, downs = ups[:1] + held[0], downs[:1] + held[1]
            arrays = [[blocks[head][at] for at in later[step]] for head in range(HALF)]
            *terms, lead = gradients(prepared, lse, later[step], arrays, carried, last)
            for slot, at in enumerate(later[step]):
                by_offset[at] = [terms[head][slot] for head in range(HALF)]
            if last:
                ours, theirs = terms[HALF], lax.ppermute(lead, "leaf", swap)
            else:
                carried = lead
        ups = [wide(a) for a in shift(ups, right)]
        downs = [wide(a) for a in shift(downs, left)]
    kept, got = [], []
    for head in range(HALF):
        summed = (wide(by_offset[0][head]) + ups[head] + downs[head]).astype(jnp.bfloat16)
        kept.append(summed[:rows])
        got.append(lax.ppermute(summed[rows:], "leaf", swap))

    def whole(kept, got):
        low = [jnp.where(core == 0, a, b) for a, b in zip(kept, got)]
        high = [jnp.where(core == 0, b, a) for a, b in zip(kept, got)]
        return jnp.concatenate(low + high, axis=1)

    key_grad = whole([a[:, :DH] for a in kept], [a[:, :DH] for a in got])
    value_grad = whole([a[:, DH:] for a in kept], [a[:, DH:] for a in got])
    return (whole([ours], [theirs]), key_grad, value_grad)


def solution(mesh):
    tokens = P(("groups", "leaf"), None)
    tables = P("groups")
    return jax.shard_map(
        local,
        mesh=mesh,
        in_specs=(tokens,) * 5 + (tables,) * 3,
        out_specs=(tokens,) * 3,
        check_vma=False,
    )
```

```python
import functools
import math

import jax
import jax.numpy as jnp
from jax import lax
from jax.experimental import pallas as pl
from jax.experimental.pallas import tpu as pltpu
from jax.sharding import PartitionSpec as P

HQ = 20
HK = 4
DH = 128
PER = HQ // HK
HALF = HK // 2
WIDE = PER * DH
ANCESTORS = 5
SLOTS = ANCESTORS + 1
OWN = 1 << 20
SCALE = 1.0 / math.sqrt(DH)
EXP_SCALE = SCALE / math.log(2.0)
NN = (((1,), (0,)), ((), ()))
SMEM = pl.BlockSpec(memory_space=pltpu.SMEM)
HBM = pl.BlockSpec(memory_space=pl.ANY)
VMEM = pl.BlockSpec(memory_space=pltpu.VMEM)


def dot(a, b):
    return lax.dot_general(a, b, NN, preferred_element_type=jnp.float32)


def ring_order(chips):
    if chips == 8:
        return [0, 2, 4, 6, 7, 5, 3, 1]
    return list(range(chips))


def walk(device, me, places, parents, assignment, lengths, owner, plan, side):
    chips = places.shape[0]
    here = places[me // 2]

    def place(held):
        at = places[held // 2] - here
        at = jnp.where(at < 0, at + chips, at)
        return side * 2 * chips + at * 2 + jnp.where(held % 2 == me % 2, 0, 1)

    def clear(at, carry):
        plan[side * 2 * chips + at] = 0
        return carry

    lax.fori_loop(0, 2 * chips, clear, 0)
    segment = assignment[device]
    plan[place(device)] = OWN
    up = parents[segment]
    for _ in range(ANCESTORS):
        at = jnp.maximum(up, 0)

        @pl.when(up >= 0)
        def _():
            plan[place(owner[at])] = lengths[at]

        up = jnp.where(up >= 0, parents[at], -1)


def run_copies(pairs, sems):
    copies = [pltpu.make_async_copy(a, b, sems.at[i]) for i, (a, b) in enumerate(pairs)]
    for copy in copies:
        copy.start()
    return copies


def column_of(me, head, h):
    return pl.multiple_of(((me % 2 * HALF + head) * PER + h) * DH, DH)


def seen_keys(rows, sees):
    lane_at = lax.broadcasted_iota(jnp.int32, (1, rows), 1)
    key_at = lax.broadcasted_iota(jnp.int32, (rows, 1), 0)
    return key_at <= jnp.where(sees == OWN, lane_at, sees - 1)


def measure_blocks(plan, offsets, kv_ref, qt_ref, top_ref, sum_ref):
    rows = kv_ref.shape[1] // 2
    chips = plan.shape[0] // 4
    for slot, offset in enumerate(offsets):
        def visit(i, carry):
            half, side = i // 2, i % 2
            sees = plan[side * 2 * chips + offset * 2 + half]

            @pl.when(sees > 0)
            def _():
                seen = seen_keys(rows, sees)
                keys = kv_ref[slot, pl.ds(pl.multiple_of(half * rows, rows), rows), :DH]
                for h in range(PER):
                    at = (side, slice(None), slice(h * rows, (h + 1) * rows))
                    s = jnp.where(seen, dot(keys, qt_ref[at]), -1e30)
                    old = top_ref[at]
                    top = jnp.maximum(old, jnp.max(s, axis=0, keepdims=True))
                    total = jnp.sum(jnp.exp2((s - top) * EXP_SCALE), axis=0, keepdims=True)
                    top_ref[at] = top
                    sum_ref[at] = sum_ref[at] * jnp.exp2((old - top) * EXP_SCALE) + total

            return carry

        lax.fori_loop(0, 4, visit, 0)


def prepare_kernel(head, me_ref, places, parents, assignment, lengths, queries, grads, saved, other, block, *refs):
    (plan, qt_ref, gt_ref, gm_ref, qm_ref, delta_ref, top_ref, sum_ref,
     owner, q_ref, g_ref, o_ref, kv_ref, sems) = refs
    rows = queries.shape[0]
    me = me_ref[0]
    column = pl.multiple_of((me % 2 * HALF + head) * WIDE, WIDE)
    pairs = [(block, kv_ref.at[0])]
    for at, (array, held) in enumerate(zip((queries, grads, saved), (q_ref, g_ref, o_ref))):
        pairs.append((array.at[:, pl.ds(column, WIDE)], held.at[0]))
        first = (at * HALF + head) * WIDE
        pairs.append((other.at[:, first:first + WIDE], held.at[1]))
    copies = run_copies(pairs, sems)

    def invert(d, carry):
        owner[assignment[d]] = d
        return carry

    lax.fori_loop(0, assignment.shape[0], invert, 0)
    walk(me, me, places, parents, assignment, lengths, owner, plan, 0)
    walk(me + 1 - me % 2 * 2, me, places, parents, assignment, lengths, owner, plan, 1)
    row_at = lax.broadcasted_iota(jnp.int32, (rows, 1), 0)
    top_ref[...] = jnp.full(top_ref.shape, -1e30, top_ref.dtype)
    sum_ref[...] = jnp.zeros_like(sum_ref)
    for copy in copies:
        copy.wait()
    for side, device in enumerate((me, me + 1 - me % 2 * 2)):
        live = row_at < lengths[assignment[device]]
        for h in range(PER):
            lanes = slice(h * rows, (h + 1) * rows)
            cols = slice(h * DH, (h + 1) * DH)
            masked = jnp.where(live, g_ref[side, :, cols], jnp.zeros((), g_ref.dtype))
            query = q_ref[side, :, cols]
            gm_ref[side, lanes, :] = masked
            qm_ref[side, lanes, :] = query
            gt_ref[side, :, lanes] = masked.T
            qt_ref[side, :, lanes] = query.T
            terms = masked.astype(jnp.float32) * o_ref[side, :, cols].astype(jnp.float32)
            delta_ref[side, :, lanes] = jnp.sum(terms.T, axis=0, keepdims=True)
    measure_blocks(plan, [0], kv_ref, qt_ref, top_ref, sum_ref)


def row_stats(rows):
    return jax.ShapeDtypeStruct((2, 1, PER * rows), jnp.float32)


def prepare(head, tables, mine, other, block):
    rows = other.shape[0]
    chips = tables[1].shape[0]
    bf16 = jnp.bfloat16
    return pl.pallas_call(
        functools.partial(prepare_kernel, head),
        in_specs=[SMEM] * 5 + [HBM] * 5,
        out_specs=[SMEM] + [VMEM] * 7,
        out_shape=[
            jax.ShapeDtypeStruct((4 * chips,), jnp.int32),
            jax.ShapeDtypeStruct((2, DH, PER * rows), bf16),
            jax.ShapeDtypeStruct((2, DH, PER * rows), bf16),
            jax.ShapeDtypeStruct((2, PER * rows, DH), bf16),
            jax.ShapeDtypeStruct((2, PER * rows, DH), bf16),
            row_stats(rows),
            row_stats(rows),
            row_stats(rows),
        ],
        scratch_shapes=[pltpu.SMEM(tables[3].shape, jnp.int32)]
        + [pltpu.VMEM((2, rows, WIDE), bf16)] * 3
        + [pltpu.VMEM((1, 2 * rows, 2 * DH), bf16), pltpu.SemaphoreType.DMA((7,))],
        compiler_params=pltpu.CompilerParams(vmem_limit_bytes=8 << 20),
        cost_estimate=pl.CostEstimate(flops=0, bytes_accessed=12 << 20, transcendentals=0),
    )(*tables, *mine, other, block)


def measure_kernel(offsets, plan, qt_ref, top_in, sum_in, *refs):
    count = len(offsets)
    blocks, (top_ref, sum_ref, kv_ref, sems) = refs[:count], refs[count:]
    copies = run_copies([(held, kv_ref.at[i]) for i, held in enumerate(blocks)], sems)
    top_ref[...] = top_in[...]
    sum_ref[...] = sum_in[...]
    for copy in copies:
        copy.wait()
    measure_blocks(plan, offsets, kv_ref, qt_ref, top_ref, sum_ref)


def measure(offsets, prepared, stats, blocks):
    rows = blocks[0].shape[0] // 2
    plan, qt = prepared[:2]
    return pl.pallas_call(
        functools.partial(measure_kernel, offsets),
        in_specs=[SMEM] + [VMEM] * 3 + [HBM] * len(blocks),
        out_specs=[VMEM] * 2,
        out_shape=[row_stats(rows)] * 2,
        scratch_shapes=[
            pltpu.VMEM((len(offsets), 2 * rows, 2 * DH), jnp.bfloat16),
            pltpu.SemaphoreType.DMA((len(blocks),)),
        ],
        compiler_params=pltpu.CompilerParams(vmem_limit_bytes=6 << 20),
        cost_estimate=pl.CostEstimate(flops=0, bytes_accessed=8 << 20, transcendentals=0),
    )(plan, qt, *stats, *blocks)


def grads_kernel(chips, offsets, first, last, plan, *refs):
    far = chips // 2
    shared = []
    for head in range(HALF):
        shared.append(refs[:6 + first])
        refs = refs[6 + first:]
    blocks = []
    for head in range(HALF):
        blocks.append(refs[:len(offsets) + first])
        refs = refs[len(offsets) + first:]
    carried = None
    if not first:
        carried, refs = refs[0], refs[1:]
    terms, refs = refs[:HALF], refs[HALF:]
    if first:
        ups, downs, refs = refs[:HALF], refs[HALF:2 * HALF], refs[2 * HALF:]
        lse_out, refs = refs[:HALF], refs[HALF:]
    outs, refs = refs[:2 if last else 1], refs[2 if last else 1:]
    (kv_ref, acc_ref, stage_ref, zero_ref, p_ref, ds_ref, sum_ref, dqt_ref, offset_ref,
     sems, kv_sems, out_sems, zero_sems) = refs
    lse_ref = lse_out if first else [head[5] for head in shared]
    if not last:
        dqt_ref = outs[0]
    rows = acc_ref.shape[1]
    slots = stage_ref.shape[0]

    pairs = []
    for head in range(HALF):
        for slot, offset in enumerate(offsets):
            offset_ref[slot] = offset
            if offset == far:
                pairs.append((blocks[head][0], kv_ref.at[slot, head, :rows]))
                pairs.append((blocks[head][1], kv_ref.at[slot, head, rows:]))
            else:
                pltpu.make_async_copy(
                    blocks[head][slot + first], kv_ref.at[slot, head], kv_sems.at[slot, head]
                ).start()
    copies = run_copies(pairs, sems)
    zero_ref[...] = jnp.zeros_like(zero_ref)

    def sees(side, i):
        return plan[side * 2 * chips + offset_ref[i // 2] * 2 + i % 2]

    def seen(i):
        return (sees(0, i) > 0) | (sees(1, i) > 0)

    def send(i, sources, sem_of):
        at_block, half = i // 2, i % 2
        here = pl.ds(pl.multiple_of(half * rows, rows), rows)
        for head in range(HALF):
            def put(target):
                pltpu.make_async_copy(sources[head], target, sem_of(head)).start()

            if not first:
                put(terms[head].at[at_block, here])
                continue

            @pl.when(i >= 2)
            def _():
                put(terms[head].at[at_block, here])

            @pl.when(i == 0)
            def _():
                put(ups[head])

            @pl.when(i == 1)
            def _():
                put(downs[head])

    def sent(sem_of):
        for head in range(HALF):
            pltpu.make_async_copy(zero_ref, terms[head].at[0, :rows], sem_of(head)).wait()

    def send_zeros(i, carry):
        @pl.when(jnp.logical_not(seen(i)))
        def _():
            send(i, [zero_ref] * HALF, lambda head: zero_sems.at[i, head])

        return carry

    lax.fori_loop(0, 2 * len(offsets), send_zeros, 0)
    dqt_ref[...] = jnp.zeros_like(dqt_ref) if first else carried[...]
    for copy in copies:
        copy.wait()
    if first:
        for head in range(HALF):
            top_ref, total_ref = lse_out[head], sum_ref.at[head]
            top_ref[...] = shared[head][5][...]
            total_ref[...] = shared[head][6][...]
            measure_blocks(plan, [far], kv_ref.at[:, head], shared[head][0], top_ref, total_ref)
            top_ref[...] = top_ref[...] * EXP_SCALE + jnp.log2(total_ref[...])

    def visit(i, done):
        at_block, half = i // 2, i % 2
        here = pl.ds(pl.multiple_of(half * rows, rows), rows)

        @pl.when((half == 0) & (offset_ref[at_block] != far))
        def _():
            for head in range(HALF):
                pltpu.make_async_copy(
                    blocks[head][-1], kv_ref.at[at_block, head], kv_sems.at[at_block, head]
                ).wait()

        def look(side, carry):
            @pl.when(sees(side, i) > 0)
            def _():
                allowed = seen_keys(rows, sees(side, i))
                for head in range(HALF):
                    qt_ref, gt_ref, gm_ref, qm_ref, delta_ref = shared[head][:5]
                    k = kv_ref[at_block, head, here, :DH]
                    v = kv_ref[at_block, head, here, DH:]
                    for h in range(PER):
                        lanes = slice(h * rows, (h + 1) * rows)
                        part = (side, slice(None), lanes)
                        s = dot(k, qt_ref[part]) * EXP_SCALE - lse_ref[head][part]
                        p = jnp.where(allowed, jnp.exp2(s), 0.0)
                        ds = p * (dot(v, gt_ref[part]) - delta_ref[part])
                        p_ref[head, :, lanes] = p.astype(p_ref.dtype)
                        ds_ref[head, :, lanes] = ds.astype(ds_ref.dtype)
                    acc_ref[head, :, DH:] += dot(p_ref[head], gm_ref[side])
                    acc_ref[head, :, :DH] += dot(ds_ref[head], qm_ref[side])
                    dqt_ref[head, side] += dot(k.T, ds_ref[head])

            return carry

        @pl.when(seen(i))
        def _():
            slot = done % slots

            @pl.when(done >= slots)
            def _():
                sent(lambda head: out_sems.at[slot, head])

            acc_ref[...] = jnp.zeros_like(acc_ref)
            lax.fori_loop(0, 2, look, 0)
            for head in range(HALF):
                stage_ref[slot, head, :, :DH] = (acc_ref[head, :, :DH] * SCALE).astype(stage_ref.dtype)
                stage_ref[slot, head, :, DH:] = acc_ref[head, :, DH:].astype(stage_ref.dtype)
            send(i, [stage_ref.at[slot, head] for head in range(HALF)], lambda head: out_sems.at[slot, head])

        return done + seen(i).astype(jnp.int32)

    done = lax.fori_loop(0, 2 * len(offsets), visit, jnp.int32(0))
    if last:
        for side, dq_ref in enumerate(outs):
            for head in range(HALF):
                for h in range(PER):
                    dq = (dqt_ref[head, side, :, h * rows:(h + 1) * rows] * SCALE).astype(dq_ref.dtype)
                    dq_ref[:, (head * PER + h) * DH:(head * PER + h + 1) * DH] = dq.T

    def zeros_sent(i, carry):
        @pl.when(jnp.logical_not(seen(i)))
        def _():
            sent(lambda head: zero_sems.at[i, head])

        return carry

    lax.fori_loop(0, 2 * len(offsets), zeros_sent, 0)
    for slot in range(slots):
        @pl.when(done > slot)
        def _():
            sent(lambda head: out_sems.at[slot, head])


def gradients(prepared, stats, offsets, blocks, carried, last):
    plan = prepared[0][0]
    chips = plan.shape[0] // 4
    rows = blocks[0][-1].shape[0] // 2
    first = carried is None
    bf16, f32 = jnp.bfloat16, jnp.float32
    shared = [(*prepared[head][1:6], *stats[head]) for head in range(HALF)]
    arrays = [a for head in shared for a in head] + [a for head in blocks for a in head]
    arrays += [] if first else [carried]
    dense = jax.ShapeDtypeStruct((len(offsets), 2 * rows, 2 * DH), bf16)
    piece = jax.ShapeDtypeStruct((rows, 2 * DH), bf16)
    query = jax.ShapeDtypeStruct((rows, HALF * WIDE), bf16)
    sums = jax.ShapeDtypeStruct((HALF, 2, DH, PER * rows), f32)
    out_shape, out_specs = [dense] * HALF, [HBM] * HALF
    if first:
        out_shape += [piece] * (2 * HALF) + [row_stats(rows)] * HALF
        out_specs += [HBM] * (2 * HALF) + [VMEM] * HALF
    out_shape += [query] * 2 if last else [sums]
    out_specs += [VMEM] * (2 if last else 1)
    flat = sum(len(head) for head in shared)
    in_specs = [SMEM] + [VMEM] * flat + [HBM] * (len(arrays) - flat)
    if not first:
        in_specs[-1] = VMEM
    return pl.pallas_call(
        functools.partial(grads_kernel, chips, tuple(offsets), first, last),
        in_specs=in_specs,
        out_specs=out_specs,
        out_shape=out_shape,
        scratch_shapes=[
            pltpu.VMEM((len(offsets), HALF, 2 * rows, 2 * DH), bf16),
            pltpu.VMEM((HALF, rows, 2 * DH), f32),
            pltpu.VMEM((4, HALF, rows, 2 * DH), bf16),
            pltpu.VMEM((rows, 2 * DH), bf16),
            pltpu.VMEM((HALF, rows, PER * rows), bf16),
            pltpu.VMEM((HALF, rows, PER * rows), bf16),
            pltpu.VMEM((HALF, 2, 1, PER * rows), f32),
            pltpu.VMEM((HALF, 2, DH, PER * rows) if last else (8, DH), f32),
            pltpu.SMEM((len(offsets),), jnp.int32),
            pltpu.SemaphoreType.DMA((2 * HALF,)),
            pltpu.SemaphoreType.DMA((len(offsets), HALF)),
            pltpu.SemaphoreType.DMA((4, HALF)),
            pltpu.SemaphoreType.DMA((2 * len(offsets), HALF)),
        ],
        compiler_params=pltpu.CompilerParams(vmem_limit_bytes=(13 << 20) + (len(offsets) << 19)),
        cost_estimate=pl.CostEstimate(flops=8 << 30, bytes_accessed=16 << 20, transcendentals=0),
    )(plan, *arrays)


def wide(x):
    return x.astype(jnp.float32)


def assemble_kernel(me_ref, *refs):
    ours, theirs, refs = refs[0], refs[1], refs[2:]
    kept, got, refs = refs[:HALF], refs[HALF:2 * HALF], refs[2 * HALF:]
    query_grad, key_grad, value_grad, sems = refs
    rows = ours.shape[0]
    core = me_ref[0] % 2
    pairs = []
    for which, query, sums in ((core, ours, kept), (1 - core, theirs, got)):
        column = pl.multiple_of(which * (HALF * WIDE), HALF * WIDE)
        pairs.append((query, query_grad.at[:, pl.ds(column, HALF * WIDE)]))
        for head in range(HALF):
            column = pl.multiple_of((which * HALF + head) * DH, DH)
            for first, out in ((0, key_grad), (DH, value_grad)):
                pairs.append((sums[head].at[:rows, first:first + DH], out.at[:, pl.ds(column, DH)]))
    for copy in run_copies(pairs, sems):
        copy.wait()


def assemble(me, ours, theirs, kept, got):
    rows = ours.shape[0]
    return pl.pallas_call(
        assemble_kernel,
        in_specs=[SMEM] + [HBM] * (2 + 2 * HALF),
        out_specs=[HBM] * 3,
        out_shape=[
            jax.ShapeDtypeStruct((rows, 2 * HALF * WIDE), jnp.bfloat16),
            jax.ShapeDtypeStruct((rows, 2 * HALF * DH), jnp.bfloat16),
            jax.ShapeDtypeStruct((rows, 2 * HALF * DH), jnp.bfloat16),
        ],
        scratch_shapes=[pltpu.SemaphoreType.DMA((2 + 4 * HALF,))],
        compiler_params=pltpu.CompilerParams(vmem_limit_bytes=2 << 20),
        cost_estimate=pl.CostEstimate(flops=0, bytes_accessed=4 << 20, transcendentals=0),
    )(me, ours, theirs, *kept, *got)


def local(queries, keys, values, saved_out, grad_out, parents, assignment, lengths):
    rows = keys.shape[0]
    chips = lax.axis_size("leaf") // 2
    order = ring_order(chips)
    ahead = [(order[i], order[(i + 1) % chips]) for i in range(chips)]
    right = [(2 * a + c, 2 * b + c) for a, b in ahead for c in range(2)]
    left = [(b, a) for a, b in right]
    swap = [(2 * a + c, 2 * a + 1 - c) for a in range(chips) for c in range(2)]
    places = jnp.asarray([order.index(chip) for chip in range(chips)], jnp.int32)
    index = lax.axis_index("leaf").astype(jnp.int32)
    core = index % 2
    me = index.reshape(1)
    tables = (me, places, parents, assignment, lengths)

    def part(array, which, width):
        return lax.dynamic_slice(array, (0, which * width), (rows, width))

    def heads_of(which):
        pieces = [part(array, which * HALF + head, DH) for head in range(HALF) for array in (keys, values)]
        return jnp.concatenate(pieces, axis=1)

    kept = heads_of(core)
    got = lax.ppermute(heads_of(1 - core), "leaf", swap)
    own = []
    for head in range(HALF):
        cols = slice(head * 2 * DH, (head + 1) * 2 * DH)
        own.append(jnp.concatenate([kept[:, cols], got[:, cols]], axis=0))
    mine = (queries, grad_out, saved_out)
    late = lax.optimization_barrier((*mine, got))[:3]
    other = jnp.concatenate([part(array, 1 - core, HALF * WIDE) for array in late], axis=1)
    other = lax.ppermute(other, "leaf", swap)

    def shift(arrays, ring):
        return [lax.ppermute(array, "leaf", ring) for array in arrays]

    far = chips // 2
    prepared, stats = [None] * HALF, [None] * HALF
    blocks, halves = [], []
    streams = [(block, block) for block in own]
    blocks = [{0: block} for block in own]
    for step in range(1, far):
        for head in range(HALF):
            up, down = streams[head]
            up, down = lax.ppermute(up, "leaf", right), lax.ppermute(down, "leaf", left)
            blocks[head][chips - step], blocks[head][step] = up, down
            if step == 1:
                prepared[head] = prepare(head, tables, mine, other, own[head])
                stats[head] = prepared[head][6:]
            else:
                met = (step - 1, chips - step + 1)
                stats[head] = measure(met, prepared[head], stats[head], [blocks[head][at] for at in met])
            stats[head], streams[head] = lax.optimization_barrier((stats[head], (up, down)))
    for head in range(HALF):
        up, down = streams[head]
        halves.append([lax.ppermute(up[:rows], "leaf", right), lax.ppermute(down[rows:], "leaf", left)])
        met = (far - 1, far + 1)
        stats[head] = measure(met, prepared[head], stats[head], [blocks[head][at] for at in met])

    offsets = [far]
    for step in range(1, far - 2):
        offsets += [far + step, far - step]
    arrays = [halves[head] + [blocks[head][at] for at in offsets[1:]] for head in range(HALF)]
    *terms, carried = gradients(prepared, stats, offsets, arrays, None, False)
    lse = [[a] for a in terms[3 * HALF:]]
    by_offset = {at: [terms[head][slot] for head in range(HALF)] for slot, at in enumerate(offsets)}
    ups = [jnp.pad(wide(a), ((0, rows), (0, 0))) for a in shift(terms[HALF:2 * HALF], right)]
    downs = [jnp.pad(wide(a), ((rows, 0), (0, 0))) for a in shift(terms[2 * HALF:3 * HALF], left)]

    def add(sums, at):
        return [(a + wide(b)).astype(jnp.bfloat16) for a, b in zip(sums, by_offset[at])]

    later = {3: [chips - 2, 2], 2: [chips - 1, 1], 1: [0]}
    ours = theirs = None
    for step in range(far - 1, 0, -1):
        ups, downs = add(ups, step), add(downs, chips - step)
        if step in later:
            last = 0 in later[step]
            (lse, carried), held = lax.optimization_barrier(((lse, carried), (ups[1:], downs[1:])))
            ups, downs = ups[:1] + held[0], downs[:1] + held[1]
            arrays = [[blocks[head][at] for at in later[step]] for head in range(HALF)]
            *terms, lead = gradients(prepared, lse, later[step], arrays, carried, last)
            for slot, at in enumerate(later[step]):
                by_offset[at] = [terms[head][slot] for head in range(HALF)]
            if last:
                ours, theirs = terms[HALF], lax.ppermute(lead, "leaf", swap)
            else:
                carried = lead
        ups = [wide(a) for a in shift(ups, right)]
        downs = [wide(a) for a in shift(downs, left)]
    kept, got = [], []
    for head in range(HALF):
        summed = (wide(by_offset[0][head]) + ups[head] + downs[head]).astype(jnp.bfloat16)
        kept.append(summed)
        got.append(lax.ppermute(summed[rows:], "leaf", swap))

    return tuple(assemble(me, ours, theirs, kept, got))


def solution(mesh):
    tokens = P(("groups", "leaf"), None)
    tables = P("groups")
    return jax.shard_map(
        local,
        mesh=mesh,
        in_specs=(tokens,) * 5 + (tables,) * 3,
        out_specs=(tokens,) * 3,
        check_vma=False,
    )
```

```python
import functools
import math

import jax
import jax.numpy as jnp
from jax import lax
from jax.experimental import pallas as pl
from jax.experimental.pallas import tpu as pltpu
from jax.sharding import PartitionSpec as P

HQ = 20
HK = 4
DH = 128
PER = HQ // HK
HALF = HK // 2
WIDE = PER * DH
ANCESTORS = 5
SLOTS = ANCESTORS + 1
OWN = 1 << 20
SCALE = 1.0 / math.sqrt(DH)
EXP_SCALE = SCALE / math.log(2.0)
NN = (((1,), (0,)), ((), ()))
NT = (((1,), (1,)), ((), ()))
SMEM = pl.BlockSpec(memory_space=pltpu.SMEM)
HBM = pl.BlockSpec(memory_space=pl.ANY)
VMEM = pl.BlockSpec(memory_space=pltpu.VMEM)


def dot(a, b, dims=NN):
    return lax.dot_general(a, b, dims, preferred_element_type=jnp.float32)


def ring_order(chips):
    if chips == 8:
        return [0, 2, 4, 6, 7, 5, 3, 1]
    return list(range(chips))


def walk(device, me, places, parents, assignment, lengths, owner, plan, side):
    chips = places.shape[0]
    here = places[me // 2]

    def place(held):
        at = places[held // 2] - here
        at = jnp.where(at < 0, at + chips, at)
        return side * 2 * chips + at * 2 + jnp.where(held % 2 == me % 2, 0, 1)

    def clear(at, carry):
        plan[side * 2 * chips + at] = 0
        return carry

    lax.fori_loop(0, 2 * chips, clear, 0)
    segment = assignment[device]
    plan[place(device)] = OWN
    up = parents[segment]
    for _ in range(ANCESTORS):
        at = jnp.maximum(up, 0)

        @pl.when(up >= 0)
        def _():
            plan[place(owner[at])] = lengths[at]

        up = jnp.where(up >= 0, parents[at], -1)


def run_copies(pairs, sems):
    copies = [pltpu.make_async_copy(a, b, sems.at[i]) for i, (a, b) in enumerate(pairs)]
    for copy in copies:
        copy.start()
    return copies


def column_of(me, head, h):
    return pl.multiple_of(((me % 2 * HALF + head) * PER + h) * DH, DH)


def seen_keys(rows, sees):
    lane_at = lax.broadcasted_iota(jnp.int32, (1, rows), 1)
    key_at = lax.broadcasted_iota(jnp.int32, (rows, 1), 0)
    return key_at <= jnp.where(sees == OWN, lane_at, sees - 1)


def measure_blocks(plan, offsets, kv_ref, qt_ref, top_ref, sum_ref):
    rows = kv_ref.shape[1] // 2
    chips = plan.shape[0] // 4
    for slot, offset in enumerate(offsets):
        def visit(i, carry):
            half, side = i // 2, i % 2
            sees = plan[side * 2 * chips + offset * 2 + half]

            @pl.when(sees > 0)
            def _():
                seen = seen_keys(rows, sees)
                keys = kv_ref[slot, pl.ds(pl.multiple_of(half * rows, rows), rows), :DH]
                for h in range(PER):
                    at = (side, slice(None), slice(h * rows, (h + 1) * rows))
                    s = jnp.where(seen, dot(keys, qt_ref[at]), -1e30)
                    old = top_ref[at]
                    top = jnp.maximum(old, jnp.max(s, axis=0, keepdims=True))
                    total = jnp.sum(jnp.exp2((s - top) * EXP_SCALE), axis=0, keepdims=True)
                    top_ref[at] = top
                    sum_ref[at] = sum_ref[at] * jnp.exp2((old - top) * EXP_SCALE) + total

            return carry

        lax.fori_loop(0, 4, visit, 0)


def prepare_kernel(head, me_ref, places, parents, assignment, lengths, queries, grads, saved, other, block, *refs):
    (plan, qt_ref, gt_ref, gm_ref, qm_ref, delta_ref, top_ref, sum_ref,
     owner, q_ref, g_ref, o_ref, kv_ref, sems) = refs
    rows = queries.shape[0]
    me = me_ref[0]
    column = pl.multiple_of((me % 2 * HALF + head) * WIDE, WIDE)
    pairs = [(block, kv_ref.at[0])]
    for at, (array, held) in enumerate(zip((queries, grads, saved), (q_ref, g_ref, o_ref))):
        pairs.append((array.at[:, pl.ds(column, WIDE)], held.at[0]))
        first = (at * HALF + head) * WIDE
        pairs.append((other.at[:, first:first + WIDE], held.at[1]))
    copies = run_copies(pairs, sems)

    def invert(d, carry):
        owner[assignment[d]] = d
        return carry

    lax.fori_loop(0, assignment.shape[0], invert, 0)
    walk(me, me, places, parents, assignment, lengths, owner, plan, 0)
    walk(me + 1 - me % 2 * 2, me, places, parents, assignment, lengths, owner, plan, 1)
    row_at = lax.broadcasted_iota(jnp.int32, (rows, 1), 0)
    top_ref[...] = jnp.full(top_ref.shape, -1e30, top_ref.dtype)
    sum_ref[...] = jnp.zeros_like(sum_ref)
    for copy in copies:
        copy.wait()
    for side, device in enumerate((me, me + 1 - me % 2 * 2)):
        live = row_at < lengths[assignment[device]]
        for h in range(PER):
            lanes = slice(h * rows, (h + 1) * rows)
            cols = slice(h * DH, (h + 1) * DH)
            masked = jnp.where(live, g_ref[side, :, cols], jnp.zeros((), g_ref.dtype))
            query = q_ref[side, :, cols]
            gm_ref[side, lanes, :] = masked
            qm_ref[side, lanes, :] = query
            gt_ref[side, :, lanes] = masked.T
            qt_ref[side, :, lanes] = query.T
            terms = masked.astype(jnp.float32) * o_ref[side, :, cols].astype(jnp.float32)
            delta = jnp.sum(terms, axis=1, keepdims=True)
            delta_ref[side, lanes, :] = jnp.broadcast_to(delta, (rows, DH))
    measure_blocks(plan, [0], kv_ref, qt_ref, top_ref, sum_ref)


def row_stats(rows):
    return jax.ShapeDtypeStruct((2, 1, PER * rows), jnp.float32)


def wide_stats(rows):
    return jax.ShapeDtypeStruct((2, PER * rows, DH), jnp.float32)


def prepare(head, tables, mine, other, block):
    rows = other.shape[0]
    chips = tables[1].shape[0]
    bf16 = jnp.bfloat16
    return pl.pallas_call(
        functools.partial(prepare_kernel, head),
        in_specs=[SMEM] * 5 + [HBM] * 5,
        out_specs=[SMEM] + [VMEM] * 7,
        out_shape=[
            jax.ShapeDtypeStruct((4 * chips,), jnp.int32),
            jax.ShapeDtypeStruct((2, DH, PER * rows), bf16),
            jax.ShapeDtypeStruct((2, DH, PER * rows), bf16),
            jax.ShapeDtypeStruct((2, PER * rows, DH), bf16),
            jax.ShapeDtypeStruct((2, PER * rows, DH), bf16),
            wide_stats(rows),
            row_stats(rows),
            row_stats(rows),
        ],
        scratch_shapes=[pltpu.SMEM(tables[3].shape, jnp.int32)]
        + [pltpu.VMEM((2, rows, WIDE), bf16)] * 3
        + [pltpu.VMEM((1, 2 * rows, 2 * DH), bf16), pltpu.SemaphoreType.DMA((7,))],
        compiler_params=pltpu.CompilerParams(vmem_limit_bytes=8 << 20),
        cost_estimate=pl.CostEstimate(flops=0, bytes_accessed=12 << 20, transcendentals=0),
    )(*tables, *mine, other, block)


def measure_kernel(offsets, plan, qt_ref, top_in, sum_in, *refs):
    count = len(offsets)
    blocks, (top_ref, sum_ref, kv_ref, sems) = refs[:count], refs[count:]
    copies = run_copies([(held, kv_ref.at[i]) for i, held in enumerate(blocks)], sems)
    top_ref[...] = top_in[...]
    sum_ref[...] = sum_in[...]
    for copy in copies:
        copy.wait()
    measure_blocks(plan, offsets, kv_ref, qt_ref, top_ref, sum_ref)


def measure(offsets, prepared, stats, blocks):
    rows = blocks[0].shape[0] // 2
    plan, qt = prepared[:2]
    return pl.pallas_call(
        functools.partial(measure_kernel, offsets),
        in_specs=[SMEM] + [VMEM] * 3 + [HBM] * len(blocks),
        out_specs=[VMEM] * 2,
        out_shape=[row_stats(rows)] * 2,
        scratch_shapes=[
            pltpu.VMEM((len(offsets), 2 * rows, 2 * DH), jnp.bfloat16),
            pltpu.SemaphoreType.DMA((len(blocks),)),
        ],
        compiler_params=pltpu.CompilerParams(vmem_limit_bytes=6 << 20),
        cost_estimate=pl.CostEstimate(flops=0, bytes_accessed=8 << 20, transcendentals=0),
    )(plan, qt, *stats, *blocks)


def grads_kernel(chips, offsets, first, last, plan, *refs):
    far = chips // 2
    shared = []
    for head in range(HALF):
        shared.append(refs[:6 + first])
        refs = refs[6 + first:]
    blocks = []
    for head in range(HALF):
        blocks.append(refs[:len(offsets) + first])
        refs = refs[len(offsets) + first:]
    carried = None
    if not first:
        carried, refs = refs[0], refs[1:]
    terms, refs = refs[:HALF], refs[HALF:]
    if first:
        ups, downs, refs = refs[:HALF], refs[HALF:2 * HALF], refs[2 * HALF:]
        lse_out, refs = refs[:HALF], refs[HALF:]
    outs, refs = refs[:2 if last else 1], refs[2 if last else 1:]
    (kv_ref, acc_ref, stage_ref, zero_ref, p_ref, ds_ref, top_ref, sum_ref, dq_ref, offset_ref,
     sems, kv_sems, out_sems, zero_sems) = refs
    lse_ref = lse_out if first else [head[5] for head in shared]
    if not last:
        dq_ref = outs[0]
    rows = acc_ref.shape[2]
    slots = stage_ref.shape[0]

    pairs = []
    for head in range(HALF):
        for slot, offset in enumerate(offsets):
            offset_ref[slot] = offset
            if offset == far:
                pairs.append((blocks[head][0], kv_ref.at[slot, head, :rows]))
                pairs.append((blocks[head][1], kv_ref.at[slot, head, rows:]))
            else:
                pltpu.make_async_copy(
                    blocks[head][slot + first], kv_ref.at[slot, head], kv_sems.at[slot, head]
                ).start()
    copies = run_copies(pairs, sems)
    zero_ref[...] = jnp.zeros_like(zero_ref)

    def sees(side, i):
        return plan[side * 2 * chips + offset_ref[i // 2] * 2 + i % 2]

    def seen(i):
        return (sees(0, i) > 0) | (sees(1, i) > 0)

    def send(i, sources, sem_of):
        at_block, half = i // 2, i % 2
        here = pl.ds(pl.multiple_of(half * rows, rows), rows)
        for head in range(HALF):
            def put(target):
                pltpu.make_async_copy(sources[head], target, sem_of(head)).start()

            if not first:
                put(terms[head].at[at_block, here])
                continue

            @pl.when(i >= 2)
            def _():
                put(terms[head].at[at_block, here])

            @pl.when(i == 0)
            def _():
                put(ups[head])

            @pl.when(i == 1)
            def _():
                put(downs[head])

    def sent(sem_of):
        for head in range(HALF):
            pltpu.make_async_copy(zero_ref, terms[head].at[0, :rows], sem_of(head)).wait()

    def send_zeros(i, carry):
        @pl.when(jnp.logical_not(seen(i)))
        def _():
            send(i, [zero_ref] * HALF, lambda head: zero_sems.at[i, head])

        return carry

    lax.fori_loop(0, 2 * len(offsets), send_zeros, 0)
    dq_ref[...] = jnp.zeros_like(dq_ref) if first else carried[...]
    for copy in copies:
        copy.wait()
    if first:
        for head in range(HALF):
            top_ref[...] = shared[head][5][...]
            sum_ref[...] = shared[head][6][...]
            measure_blocks(plan, [far], kv_ref.at[:, head], shared[head][0], top_ref, sum_ref)
            for side in range(2):
                lse = top_ref[side] * EXP_SCALE + jnp.log2(sum_ref[side])
                lse_out[head][side] = jnp.broadcast_to(lse, (DH, lse.shape[1])).T

    def visit(i, done):
        at_block, half = i // 2, i % 2
        here = pl.ds(pl.multiple_of(half * rows, rows), rows)

        @pl.when((half == 0) & (offset_ref[at_block] != far))
        def _():
            for head in range(HALF):
                pltpu.make_async_copy(
                    blocks[head][-1], kv_ref.at[at_block, head], kv_sems.at[at_block, head]
                ).wait()

        def look(side, carry):
            @pl.when(sees(side, i) > 0)
            def _():
                key_at = lax.broadcasted_iota(jnp.int32, (rows, rows), 1)
                row_at = lax.broadcasted_iota(jnp.int32, (rows, rows), 0)
                allowed = key_at <= jnp.where(sees(side, i) == OWN, row_at, sees(side, i) - 1)
                for head in range(HALF):
                    qt_ref, gt_ref, gm_ref, qm_ref, delta_ref = shared[head][:5]
                    k = kv_ref[at_block, head, here, :DH]
                    v = kv_ref[at_block, head, here, DH:]
                    for h in range(PER):
                        span = slice(h * rows, (h + 1) * rows)
                        lse = jnp.concatenate([lse_ref[head][side, span, :]] * (rows // DH), axis=1)
                        delta = jnp.concatenate([delta_ref[side, span, :]] * (rows // DH), axis=1)
                        s = dot(qm_ref[side, span, :], k, NT) * EXP_SCALE - lse
                        p = jnp.where(allowed, jnp.exp2(s), 0.0)
                        ds = p * (dot(gm_ref[side, span, :], v, NT) - delta)
                        p_ref[head, span, :] = p.astype(p_ref.dtype)
                        ds_ref[head, span, :] = ds.astype(ds_ref.dtype)
                    acc_ref[head, DH:, :] += dot(gt_ref[side], p_ref[head])
                    acc_ref[head, :DH, :] += dot(qt_ref[side], ds_ref[head])
                    dq_ref[head, side] += dot(ds_ref[head], k)

            return carry

        @pl.when(seen(i))
        def _():
            slot = done % slots

            @pl.when(done >= slots)
            def _():
                sent(lambda head: out_sems.at[slot, head])

            acc_ref[...] = jnp.zeros_like(acc_ref)
            lax.fori_loop(0, 2, look, 0)
            for head in range(HALF):
                stage_ref[slot, head, :, :DH] = (acc_ref[head, :DH, :] * SCALE).T.astype(stage_ref.dtype)
                stage_ref[slot, head, :, DH:] = acc_ref[head, DH:, :].T.astype(stage_ref.dtype)
            send(i, [stage_ref.at[slot, head] for head in range(HALF)], lambda head: out_sems.at[slot, head])

        return done + seen(i).astype(jnp.int32)

    done = lax.fori_loop(0, 2 * len(offsets), visit, jnp.int32(0))
    if last:
        for side, out_ref in enumerate(outs):
            for head in range(HALF):
                for h in range(PER):
                    cols = slice((head * PER + h) * DH, (head * PER + h + 1) * DH)
                    dq = dq_ref[head, side, h * rows:(h + 1) * rows, :] * SCALE
                    out_ref[:, cols] = dq.astype(out_ref.dtype)

    def zeros_sent(i, carry):
        @pl.when(jnp.logical_not(seen(i)))
        def _():
            sent(lambda head: zero_sems.at[i, head])

        return carry

    lax.fori_loop(0, 2 * len(offsets), zeros_sent, 0)
    for slot in range(slots):
        @pl.when(done > slot)
        def _():
            sent(lambda head: out_sems.at[slot, head])


def gradients(prepared, stats, offsets, blocks, carried, last):
    plan = prepared[0][0]
    chips = plan.shape[0] // 4
    rows = blocks[0][-1].shape[0] // 2
    first = carried is None
    bf16, f32 = jnp.bfloat16, jnp.float32
    shared = [(*prepared[head][1:6], *stats[head]) for head in range(HALF)]
    arrays = [a for head in shared for a in head] + [a for head in blocks for a in head]
    arrays += [] if first else [carried]
    dense = jax.ShapeDtypeStruct((len(offsets), 2 * rows, 2 * DH), bf16)
    piece = jax.ShapeDtypeStruct((rows, 2 * DH), bf16)
    query = jax.ShapeDtypeStruct((rows, HALF * WIDE), bf16)
    sums = jax.ShapeDtypeStruct((HALF, 2, PER * rows, DH), f32)
    out_shape, out_specs = [dense] * HALF, [HBM] * HALF
    if first:
        out_shape += [piece] * (2 * HALF) + [wide_stats(rows)] * HALF
        out_specs += [HBM] * (2 * HALF) + [VMEM] * HALF
    out_shape += [query] * 2 if last else [sums]
    out_specs += [VMEM] * (2 if last else 1)
    flat = sum(len(head) for head in shared)
    in_specs = [SMEM] + [VMEM] * flat + [HBM] * (len(arrays) - flat)
    if not first:
        in_specs[-1] = VMEM
    return pl.pallas_call(
        functools.partial(grads_kernel, chips, tuple(offsets), first, last),
        in_specs=in_specs,
        out_specs=out_specs,
        out_shape=out_shape,
        scratch_shapes=[
            pltpu.VMEM((len(offsets), HALF, 2 * rows, 2 * DH), bf16),
            pltpu.VMEM((HALF, 2 * DH, rows), f32),
            pltpu.VMEM((4, HALF, rows, 2 * DH), bf16),
            pltpu.VMEM((rows, 2 * DH), bf16),
            pltpu.VMEM((HALF, PER * rows, rows), bf16),
            pltpu.VMEM((HALF, PER * rows, rows), bf16),
            pltpu.VMEM((2, 1, PER * rows), f32),
            pltpu.VMEM((2, 1, PER * rows), f32),
            pltpu.VMEM((HALF, 2, PER * rows, DH) if last else (8, DH), f32),
            pltpu.SMEM((len(offsets),), jnp.int32),
            pltpu.SemaphoreType.DMA((2 * HALF,)),
            pltpu.SemaphoreType.DMA((len(offsets), HALF)),
            pltpu.SemaphoreType.DMA((4, HALF)),
            pltpu.SemaphoreType.DMA((2 * len(offsets), HALF)),
        ],
        compiler_params=pltpu.CompilerParams(vmem_limit_bytes=(13 << 20) + (len(offsets) << 19)),
        cost_estimate=pl.CostEstimate(flops=(1 if last else 8) << 30, bytes_accessed=1 << 20, transcendentals=0),
    )(plan, *arrays)


def wide(x):
    return x.astype(jnp.float32)


def assemble_kernel(me_ref, *refs):
    ours, theirs, refs = refs[0], refs[1], refs[2:]
    kept, got, refs = refs[:HALF], refs[HALF:2 * HALF], refs[2 * HALF:]
    query_grad, key_grad, value_grad, sems = refs
    rows = ours.shape[0]
    core = me_ref[0] % 2
    pairs = []
    for which, query, sums in ((core, ours, kept), (1 - core, theirs, got)):
        column = pl.multiple_of(which * (HALF * WIDE), HALF * WIDE)
        pairs.append((query, query_grad.at[:, pl.ds(column, HALF * WIDE)]))
        for head in range(HALF):
            column = pl.multiple_of((which * HALF + head) * DH, DH)
            for first, out in ((0, key_grad), (DH, value_grad)):
                pairs.append((sums[head].at[:rows, first:first + DH], out.at[:, pl.ds(column, DH)]))
    for copy in run_copies(pairs, sems):
        copy.wait()


def assemble(me, ours, theirs, kept, got):
    rows = ours.shape[0]
    return pl.pallas_call(
        assemble_kernel,
        in_specs=[SMEM] + [HBM] * (2 + 2 * HALF),
        out_specs=[HBM] * 3,
        out_shape=[
            jax.ShapeDtypeStruct((rows, 2 * HALF * WIDE), jnp.bfloat16),
            jax.ShapeDtypeStruct((rows, 2 * HALF * DH), jnp.bfloat16),
            jax.ShapeDtypeStruct((rows, 2 * HALF * DH), jnp.bfloat16),
        ],
        scratch_shapes=[pltpu.SemaphoreType.DMA((2 + 4 * HALF,))],
        compiler_params=pltpu.CompilerParams(vmem_limit_bytes=2 << 20),
        cost_estimate=pl.CostEstimate(flops=0, bytes_accessed=4 << 20, transcendentals=0),
    )(me, ours, theirs, *kept, *got)


def local(queries, keys, values, saved_out, grad_out, parents, assignment, lengths):
    rows = keys.shape[0]
    chips = lax.axis_size("leaf") // 2
    order = ring_order(chips)
    ahead = [(order[i], order[(i + 1) % chips]) for i in range(chips)]
    right = [(2 * a + c, 2 * b + c) for a, b in ahead for c in range(2)]
    left = [(b, a) for a, b in right]
    swap = [(2 * a + c, 2 * a + 1 - c) for a in range(chips) for c in range(2)]
    places = jnp.asarray([order.index(chip) for chip in range(chips)], jnp.int32)
    index = lax.axis_index("leaf").astype(jnp.int32)
    core = index % 2
    me = index.reshape(1)
    tables = (me, places, parents, assignment, lengths)

    def part(array, which, width):
        return lax.dynamic_slice(array, (0, which * width), (rows, width))

    def heads_of(which):
        pieces = [part(array, which * HALF + head, DH) for head in range(HALF) for array in (keys, values)]
        return jnp.concatenate(pieces, axis=1)

    kept = heads_of(core)
    got = lax.ppermute(heads_of(1 - core), "leaf", swap)
    own = []
    for head in range(HALF):
        cols = slice(head * 2 * DH, (head + 1) * 2 * DH)
        own.append(jnp.concatenate([kept[:, cols], got[:, cols]], axis=0))
    mine = (queries, grad_out, saved_out)
    late = lax.optimization_barrier((*mine, got))[:3]
    other = jnp.concatenate([part(array, 1 - core, HALF * WIDE) for array in late], axis=1)
    other = lax.ppermute(other, "leaf", swap)

    def shift(arrays, ring):
        return [lax.ppermute(array, "leaf", ring) for array in arrays]

    far = chips // 2
    prepared, stats = [None] * HALF, [None] * HALF
    blocks, halves = [], []
    streams = [(block, block) for block in own]
    blocks = [{0: block} for block in own]
    for step in range(1, far):
        for head in range(HALF):
            up, down = streams[head]
            up, down = lax.ppermute(up, "leaf", right), lax.ppermute(down, "leaf", left)
            blocks[head][chips - step], blocks[head][step] = up, down
            if step == 1:
                prepared[head] = prepare(head, tables, mine, other, own[head])
                stats[head] = prepared[head][6:]
            else:
                met = (step - 1, chips - step + 1)
                stats[head] = measure(met, prepared[head], stats[head], [blocks[head][at] for at in met])
            stats[head], streams[head] = lax.optimization_barrier((stats[head], (up, down)))
    for head in range(HALF):
        up, down = streams[head]
        halves.append([lax.ppermute(up[:rows], "leaf", right), lax.ppermute(down[rows:], "leaf", left)])
        met = (far - 1, far + 1)
        stats[head] = measure(met, prepared[head], stats[head], [blocks[head][at] for at in met])

    offsets = [far]
    for step in range(1, far - 2):
        offsets += [far + step, far - step]
    arrays = [halves[head] + [blocks[head][at] for at in offsets[1:]] for head in range(HALF)]
    *terms, carried = gradients(prepared, stats, offsets, arrays, None, False)
    lse = [[a] for a in terms[3 * HALF:]]
    by_offset = {at: [terms[head][slot] for head in range(HALF)] for slot, at in enumerate(offsets)}
    ups = [jnp.pad(wide(a), ((0, rows), (0, 0))) for a in shift(terms[HALF:2 * HALF], right)]
    downs = [jnp.pad(wide(a), ((rows, 0), (0, 0))) for a in shift(terms[2 * HALF:3 * HALF], left)]

    def add(sums, at):
        return [(a + wide(b)).astype(jnp.bfloat16) for a, b in zip(sums, by_offset[at])]

    later = {3: [chips - 2, 2], 2: [chips - 1, 1], 1: [0]}
    ours = theirs = None
    for step in range(far - 1, 0, -1):
        ups, downs = add(ups, step), add(downs, chips - step)
        if step in later:
            last = 0 in later[step]
            (lse, carried), held = lax.optimization_barrier(((lse, carried), (ups[1:], downs[1:])))
            ups, downs = ups[:1] + held[0], downs[:1] + held[1]
            arrays = [[blocks[head][at] for at in later[step]] for head in range(HALF)]
            *terms, lead = gradients(prepared, lse, later[step], arrays, carried, last)
            for slot, at in enumerate(later[step]):
                by_offset[at] = [terms[head][slot] for head in range(HALF)]
            if last:
                ours, theirs = terms[HALF], lax.ppermute(lead, "leaf", swap)
            else:
                carried = lead
        ups = [wide(a) for a in shift(ups, right)]
        downs = [wide(a) for a in shift(downs, left)]
    kept, got = [], []
    for head in range(HALF):
        summed = (wide(by_offset[0][head]) + ups[head] + downs[head]).astype(jnp.bfloat16)
        kept.append(summed)
        got.append(lax.ppermute(summed[rows:], "leaf", swap))

    return tuple(assemble(me, ours, theirs, kept, got))


def solution(mesh):
    tokens = P(("groups", "leaf"), None)
    tables = P("groups")
    return jax.shard_map(
        local,
        mesh=mesh,
        in_specs=(tokens,) * 5 + (tables,) * 3,
        out_specs=(tokens,) * 3,
        check_vma=False,
    )
```

```python
import functools
import math

import jax
import jax.numpy as jnp
from jax import lax
from jax.experimental import pallas as pl
from jax.experimental.pallas import tpu as pltpu
from jax.sharding import PartitionSpec as P

HQ = 20
HK = 4
DH = 128
PER = HQ // HK
HALF = HK // 2
WIDE = PER * DH
ANCESTORS = 5
SLOTS = ANCESTORS + 1
OWN = 1 << 20
SCALE = 1.0 / math.sqrt(DH)
EXP_SCALE = SCALE / math.log(2.0)
NN = (((1,), (0,)), ((), ()))
SMEM = pl.BlockSpec(memory_space=pltpu.SMEM)
HBM = pl.BlockSpec(memory_space=pl.ANY)
VMEM = pl.BlockSpec(memory_space=pltpu.VMEM)


def dot(a, b):
    return lax.dot_general(a, b, NN, preferred_element_type=jnp.float32)


def ring_order(chips):
    if chips == 8:
        return [0, 2, 4, 6, 7, 5, 3, 1]
    return list(range(chips))


def walk(device, me, places, parents, assignment, lengths, owner, plan, side):
    chips = places.shape[0]
    here = places[me // 2]

    def place(held):
        at = places[held // 2] - here
        at = jnp.where(at < 0, at + chips, at)
        return side * 2 * chips + at * 2 + jnp.where(held % 2 == me % 2, 0, 1)

    def clear(at, carry):
        plan[side * 2 * chips + at] = 0
        return carry

    lax.fori_loop(0, 2 * chips, clear, 0)
    segment = assignment[device]
    plan[place(device)] = OWN
    up = parents[segment]
    for _ in range(ANCESTORS):
        at = jnp.maximum(up, 0)

        @pl.when(up >= 0)
        def _():
            plan[place(owner[at])] = lengths[at]

        up = jnp.where(up >= 0, parents[at], -1)


def run_copies(pairs, sems):
    copies = [pltpu.make_async_copy(a, b, sems.at[i]) for i, (a, b) in enumerate(pairs)]
    for copy in copies:
        copy.start()
    return copies


def column_of(me, head, h):
    return pl.multiple_of(((me % 2 * HALF + head) * PER + h) * DH, DH)


def seen_keys(rows, sees):
    lane_at = lax.broadcasted_iota(jnp.int32, (1, rows), 1)
    key_at = lax.broadcasted_iota(jnp.int32, (rows, 1), 0)
    return key_at <= jnp.where(sees == OWN, lane_at, sees - 1)


def measure_blocks(plan, offsets, kv_ref, qt_ref, top_ref, sum_ref):
    rows = kv_ref.shape[1] // 2
    chips = plan.shape[0] // 4
    for slot, offset in enumerate(offsets):
        def visit(i, carry):
            half, side = i // 2, i % 2
            sees = plan[side * 2 * chips + offset * 2 + half]

            @pl.when(sees > 0)
            def _():
                seen = seen_keys(rows, sees)
                keys = kv_ref[slot, pl.ds(pl.multiple_of(half * rows, rows), rows), :DH]
                for h in range(PER):
                    at = (side, slice(None), slice(h * rows, (h + 1) * rows))
                    s = jnp.where(seen, dot(keys, qt_ref[at]), -1e30)
                    old = top_ref[at]
                    top = jnp.maximum(old, jnp.max(s, axis=0, keepdims=True))
                    total = jnp.sum(jnp.exp2((s - top) * EXP_SCALE), axis=0, keepdims=True)
                    top_ref[at] = top
                    sum_ref[at] = sum_ref[at] * jnp.exp2((old - top) * EXP_SCALE) + total

            return carry

        lax.fori_loop(0, 4, visit, 0)


def prepare_kernel(head, me_ref, places, parents, assignment, lengths, queries, grads, saved, other, block, *refs):
    (plan, qt_ref, gt_ref, gm_ref, qm_ref, delta_ref, top_ref, sum_ref,
     owner, q_ref, g_ref, o_ref, kv_ref, sems) = refs
    rows = queries.shape[0]
    me = me_ref[0]
    column = pl.multiple_of((me % 2 * HALF + head) * WIDE, WIDE)
    pairs = [(block, kv_ref.at[0])]
    for at, (array, held) in enumerate(zip((queries, grads, saved), (q_ref, g_ref, o_ref))):
        pairs.append((array.at[:, pl.ds(column, WIDE)], held.at[0]))
        first = (at * HALF + head) * WIDE
        pairs.append((other.at[:, first:first + WIDE], held.at[1]))
    copies = run_copies(pairs, sems)

    def invert(d, carry):
        owner[assignment[d]] = d
        return carry

    lax.fori_loop(0, assignment.shape[0], invert, 0)
    walk(me, me, places, parents, assignment, lengths, owner, plan, 0)
    walk(me + 1 - me % 2 * 2, me, places, parents, assignment, lengths, owner, plan, 1)
    row_at = lax.broadcasted_iota(jnp.int32, (rows, 1), 0)
    top_ref[...] = jnp.full(top_ref.shape, -1e30, top_ref.dtype)
    sum_ref[...] = jnp.zeros_like(sum_ref)
    for copy in copies:
        copy.wait()
    for side, device in enumerate((me, me + 1 - me % 2 * 2)):
        live = row_at < lengths[assignment[device]]
        for h in range(PER):
            lanes = slice(h * rows, (h + 1) * rows)
            cols = slice(h * DH, (h + 1) * DH)
            masked = jnp.where(live, g_ref[side, :, cols], jnp.zeros((), g_ref.dtype))
            query = q_ref[side, :, cols]
            gm_ref[side, lanes, :] = masked
            qm_ref[side, lanes, :] = query
            gt_ref[side, :, lanes] = masked.T
            qt_ref[side, :, lanes] = query.T
            terms = masked.astype(jnp.float32) * o_ref[side, :, cols].astype(jnp.float32)
            delta_ref[side, :, lanes] = jnp.sum(terms.T, axis=0, keepdims=True)
    measure_blocks(plan, [0], kv_ref, qt_ref, top_ref, sum_ref)


def row_stats(rows):
    return jax.ShapeDtypeStruct((2, 1, PER * rows), jnp.float32)


def prepare(head, tables, mine, other, block):
    rows = other.shape[0]
    chips = tables[1].shape[0]
    bf16 = jnp.bfloat16
    return pl.pallas_call(
        functools.partial(prepare_kernel, head),
        in_specs=[SMEM] * 5 + [HBM] * 5,
        out_specs=[SMEM] + [VMEM] * 7,
        out_shape=[
            jax.ShapeDtypeStruct((4 * chips,), jnp.int32),
            jax.ShapeDtypeStruct((2, DH, PER * rows), bf16),
            jax.ShapeDtypeStruct((2, DH, PER * rows), bf16),
            jax.ShapeDtypeStruct((2, PER * rows, DH), bf16),
            jax.ShapeDtypeStruct((2, PER * rows, DH), bf16),
            row_stats(rows),
            row_stats(rows),
            row_stats(rows),
        ],
        scratch_shapes=[pltpu.SMEM(tables[3].shape, jnp.int32)]
        + [pltpu.VMEM((2, rows, WIDE), bf16)] * 3
        + [pltpu.VMEM((1, 2 * rows, 2 * DH), bf16), pltpu.SemaphoreType.DMA((7,))],
        compiler_params=pltpu.CompilerParams(vmem_limit_bytes=8 << 20),
        cost_estimate=pl.CostEstimate(flops=0, bytes_accessed=12 << 20, transcendentals=0),
    )(*tables, *mine, other, block)


def measure_kernel(offsets, plan, qt_ref, top_in, sum_in, *refs):
    count = len(offsets)
    blocks, (top_ref, sum_ref, kv_ref, sems) = refs[:count], refs[count:]
    copies = run_copies([(held, kv_ref.at[i]) for i, held in enumerate(blocks)], sems)
    top_ref[...] = top_in[...]
    sum_ref[...] = sum_in[...]
    for copy in copies:
        copy.wait()
    measure_blocks(plan, offsets, kv_ref, qt_ref, top_ref, sum_ref)


def measure(offsets, prepared, stats, blocks):
    rows = blocks[0].shape[0] // 2
    plan, qt = prepared[:2]
    return pl.pallas_call(
        functools.partial(measure_kernel, offsets),
        in_specs=[SMEM] + [VMEM] * 3 + [HBM] * len(blocks),
        out_specs=[VMEM] * 2,
        out_shape=[row_stats(rows)] * 2,
        scratch_shapes=[
            pltpu.VMEM((len(offsets), 2 * rows, 2 * DH), jnp.bfloat16),
            pltpu.SemaphoreType.DMA((len(blocks),)),
        ],
        compiler_params=pltpu.CompilerParams(vmem_limit_bytes=6 << 20),
        cost_estimate=pl.CostEstimate(flops=0, bytes_accessed=8 << 20, transcendentals=0),
    )(plan, qt, *stats, *blocks)


def grads_kernel(chips, offsets, first, last, plan, *refs):
    far = chips // 2
    shared = []
    for head in range(HALF):
        shared.append(refs[:6 + first])
        refs = refs[6 + first:]
    blocks = []
    for head in range(HALF):
        blocks.append(refs[:len(offsets) + first])
        refs = refs[len(offsets) + first:]
    carried = None
    if not first:
        carried, refs = refs[0], refs[1:]
    terms, refs = refs[:HALF], refs[HALF:]
    if first:
        ups, downs, refs = refs[:HALF], refs[HALF:2 * HALF], refs[2 * HALF:]
        lse_out, refs = refs[:HALF], refs[HALF:]
    outs, refs = refs[:2 if last else 1], refs[2 if last else 1:]
    (kv_ref, acc_ref, stage_ref, zero_ref, p_ref, ds_ref, sum_ref, dqt_ref, offset_ref,
     sems, kv_sems, out_sems, zero_sems) = refs
    lse_ref = lse_out if first else [head[5] for head in shared]
    if not last:
        dqt_ref = outs[0]
    rows = acc_ref.shape[1]
    slots = stage_ref.shape[0]

    pairs = []
    for head in range(HALF):
        for slot, offset in enumerate(offsets):
            offset_ref[slot] = offset
            if offset == far:
                pairs.append((blocks[head][0], kv_ref.at[slot, head, :rows]))
                pairs.append((blocks[head][1], kv_ref.at[slot, head, rows:]))
            else:
                pltpu.make_async_copy(
                    blocks[head][slot + first], kv_ref.at[slot, head], kv_sems.at[slot, head]
                ).start()
    copies = run_copies(pairs, sems)
    zero_ref[...] = jnp.zeros_like(zero_ref)

    def sees(side, i):
        return plan[side * 2 * chips + offset_ref[i // 2] * 2 + i % 2]

    def seen(i):
        return (sees(0, i) > 0) | (sees(1, i) > 0)

    def send(i, sources, sem_of):
        at_block, half = i // 2, i % 2
        here = pl.ds(pl.multiple_of(half * rows, rows), rows)
        for head in range(HALF):
            def put(target):
                pltpu.make_async_copy(sources[head], target, sem_of(head)).start()

            if not first:
                put(terms[head].at[at_block, here])
                continue

            @pl.when(i >= 2)
            def _():
                put(terms[head].at[at_block, here])

            @pl.when(i == 0)
            def _():
                put(ups[head])

            @pl.when(i == 1)
            def _():
                put(downs[head])

    def sent(sem_of):
        for head in range(HALF):
            pltpu.make_async_copy(zero_ref, terms[head].at[0, :rows], sem_of(head)).wait()

    def send_zeros(i, carry):
        @pl.when(jnp.logical_not(seen(i)))
        def _():
            send(i, [zero_ref] * HALF, lambda head: zero_sems.at[i, head])

        return carry

    lax.fori_loop(0, 2 * len(offsets), send_zeros, 0)
    dqt_ref[...] = jnp.zeros_like(dqt_ref) if first else carried[...]
    for copy in copies:
        copy.wait()
    if first:
        for head in range(HALF):
            top_ref, total_ref = lse_out[head], sum_ref.at[head]
            top_ref[...] = shared[head][5][...]
            total_ref[...] = shared[head][6][...]
            measure_blocks(plan, [far], kv_ref.at[:, head], shared[head][0], top_ref, total_ref)
            top_ref[...] = top_ref[...] * EXP_SCALE + jnp.log2(total_ref[...])

    def visit(i, done):
        at_block, half = i // 2, i % 2
        here = pl.ds(pl.multiple_of(half * rows, rows), rows)

        if len(offsets) > first:
            @pl.when((half == 0) & (offset_ref[at_block] != far))
            def _():
                for head in range(HALF):
                    pltpu.make_async_copy(
                        blocks[head][-1], kv_ref.at[at_block, head], kv_sems.at[at_block, head]
                    ).wait()

        def look(side, carry):
            @pl.when(sees(side, i) > 0)
            def _():
                allowed = seen_keys(rows, sees(side, i))
                for head in range(HALF):
                    qt_ref, gt_ref, gm_ref, qm_ref, delta_ref = shared[head][:5]
                    k = kv_ref[at_block, head, here, :DH]
                    v = kv_ref[at_block, head, here, DH:]
                    for h in range(PER):
                        lanes = slice(h * rows, (h + 1) * rows)
                        part = (side, slice(None), lanes)
                        s = dot(k, qt_ref[part]) * EXP_SCALE - lse_ref[head][part]
                        p = jnp.where(allowed, jnp.exp2(s), 0.0)
                        ds = p * (dot(v, gt_ref[part]) - delta_ref[part])
                        p_ref[head, :, lanes] = p.astype(p_ref.dtype)
                        ds_ref[head, :, lanes] = ds.astype(ds_ref.dtype)
                    acc_ref[head, :, DH:] += dot(p_ref[head], gm_ref[side])
                    acc_ref[head, :, :DH] += dot(ds_ref[head], qm_ref[side])
                    dqt_ref[head, side] += dot(k.T, ds_ref[head])

            return carry

        @pl.when(seen(i))
        def _():
            slot = done % slots

            @pl.when(done >= slots)
            def _():
                sent(lambda head: out_sems.at[slot, head])

            acc_ref[...] = jnp.zeros_like(acc_ref)
            lax.fori_loop(0, 2, look, 0)
            for head in range(HALF):
                stage_ref[slot, head, :, :DH] = (acc_ref[head, :, :DH] * SCALE).astype(stage_ref.dtype)
                stage_ref[slot, head, :, DH:] = acc_ref[head, :, DH:].astype(stage_ref.dtype)
            send(i, [stage_ref.at[slot, head] for head in range(HALF)], lambda head: out_sems.at[slot, head])

        return done + seen(i).astype(jnp.int32)

    done = lax.fori_loop(0, 2 * len(offsets), visit, jnp.int32(0))
    if last:
        for side, dq_ref in enumerate(outs):
            for head in range(HALF):
                for h in range(PER):
                    dq = (dqt_ref[head, side, :, h * rows:(h + 1) * rows] * SCALE).astype(dq_ref.dtype)
                    dq_ref[:, (head * PER + h) * DH:(head * PER + h + 1) * DH] = dq.T

    def zeros_sent(i, carry):
        @pl.when(jnp.logical_not(seen(i)))
        def _():
            sent(lambda head: zero_sems.at[i, head])

        return carry

    lax.fori_loop(0, 2 * len(offsets), zeros_sent, 0)
    for slot in range(slots):
        @pl.when(done > slot)
        def _():
            sent(lambda head: out_sems.at[slot, head])


def gradients(prepared, stats, offsets, blocks, carried, last):
    plan = prepared[0][0]
    chips = plan.shape[0] // 4
    rows = prepared[0][3].shape[1] // PER
    first = carried is None
    bf16, f32 = jnp.bfloat16, jnp.float32
    shared = [(*prepared[head][1:6], *stats[head]) for head in range(HALF)]
    arrays = [a for head in shared for a in head] + [a for head in blocks for a in head]
    arrays += [] if first else [carried]
    dense = jax.ShapeDtypeStruct((len(offsets), 2 * rows, 2 * DH), bf16)
    piece = jax.ShapeDtypeStruct((rows, 2 * DH), bf16)
    query = jax.ShapeDtypeStruct((rows, HALF * WIDE), bf16)
    sums = jax.ShapeDtypeStruct((HALF, 2, DH, PER * rows), f32)
    out_shape, out_specs = [dense] * HALF, [HBM] * HALF
    if first:
        out_shape += [piece] * (2 * HALF) + [row_stats(rows)] * HALF
        out_specs += [HBM] * (2 * HALF) + [VMEM] * HALF
    out_shape += [query] * 2 if last else [sums]
    out_specs += [VMEM] * (2 if last else 1)
    flat = sum(len(head) for head in shared)
    in_specs = [SMEM] + [VMEM] * flat + [HBM] * (len(arrays) - flat)
    if not first:
        in_specs[-1] = VMEM
    return pl.pallas_call(
        functools.partial(grads_kernel, chips, tuple(offsets), first, last),
        in_specs=in_specs,
        out_specs=out_specs,
        out_shape=out_shape,
        scratch_shapes=[
            pltpu.VMEM((len(offsets), HALF, 2 * rows, 2 * DH), bf16),
            pltpu.VMEM((HALF, rows, 2 * DH), f32),
            pltpu.VMEM((4, HALF, rows, 2 * DH), bf16),
            pltpu.VMEM((rows, 2 * DH), bf16),
            pltpu.VMEM((HALF, rows, PER * rows), bf16),
            pltpu.VMEM((HALF, rows, PER * rows), bf16),
            pltpu.VMEM((HALF, 2, 1, PER * rows), f32),
            pltpu.VMEM((HALF, 2, DH, PER * rows) if last else (8, DH), f32),
            pltpu.SMEM((len(offsets),), jnp.int32),
            pltpu.SemaphoreType.DMA((2 * HALF,)),
            pltpu.SemaphoreType.DMA((len(offsets), HALF)),
            pltpu.SemaphoreType.DMA((4, HALF)),
            pltpu.SemaphoreType.DMA((2 * len(offsets), HALF)),
        ],
        compiler_params=pltpu.CompilerParams(vmem_limit_bytes=(13 << 20) + (len(offsets) << 19)),
        cost_estimate=pl.CostEstimate(flops=8 << 30, bytes_accessed=16 << 20, transcendentals=0),
    )(plan, *arrays)


def wide(x):
    return x.astype(jnp.float32)


def assemble_kernel(me_ref, *refs):
    ours, theirs, refs = refs[0], refs[1], refs[2:]
    kept, got, refs = refs[:HALF], refs[HALF:2 * HALF], refs[2 * HALF:]
    query_grad, key_grad, value_grad, sems = refs
    rows = ours.shape[0]
    core = me_ref[0] % 2
    pairs = []
    for which, query, sums in ((core, ours, kept), (1 - core, theirs, got)):
        column = pl.multiple_of(which * (HALF * WIDE), HALF * WIDE)
        pairs.append((query, query_grad.at[:, pl.ds(column, HALF * WIDE)]))
        for head in range(HALF):
            column = pl.multiple_of((which * HALF + head) * DH, DH)
            for first, out in ((0, key_grad), (DH, value_grad)):
                pairs.append((sums[head].at[:rows, first:first + DH], out.at[:, pl.ds(column, DH)]))
    for copy in run_copies(pairs, sems):
        copy.wait()


def assemble(me, ours, theirs, kept, got):
    rows = ours.shape[0]
    return pl.pallas_call(
        assemble_kernel,
        in_specs=[SMEM] + [HBM] * (2 + 2 * HALF),
        out_specs=[HBM] * 3,
        out_shape=[
            jax.ShapeDtypeStruct((rows, 2 * HALF * WIDE), jnp.bfloat16),
            jax.ShapeDtypeStruct((rows, 2 * HALF * DH), jnp.bfloat16),
            jax.ShapeDtypeStruct((rows, 2 * HALF * DH), jnp.bfloat16),
        ],
        scratch_shapes=[pltpu.SemaphoreType.DMA((2 + 4 * HALF,))],
        compiler_params=pltpu.CompilerParams(vmem_limit_bytes=2 << 20),
        cost_estimate=pl.CostEstimate(flops=0, bytes_accessed=4 << 20, transcendentals=0),
    )(me, ours, theirs, *kept, *got)


def local(queries, keys, values, saved_out, grad_out, parents, assignment, lengths):
    rows = keys.shape[0]
    chips = lax.axis_size("leaf") // 2
    order = ring_order(chips)
    ahead = [(order[i], order[(i + 1) % chips]) for i in range(chips)]
    right = [(2 * a + c, 2 * b + c) for a, b in ahead for c in range(2)]
    left = [(b, a) for a, b in right]
    swap = [(2 * a + c, 2 * a + 1 - c) for a in range(chips) for c in range(2)]
    places = jnp.asarray([order.index(chip) for chip in range(chips)], jnp.int32)
    index = lax.axis_index("leaf").astype(jnp.int32)
    core = index % 2
    me = index.reshape(1)
    tables = (me, places, parents, assignment, lengths)

    def part(array, which, width):
        return lax.dynamic_slice(array, (0, which * width), (rows, width))

    def heads_of(which):
        pieces = [part(array, which * HALF + head, DH) for head in range(HALF) for array in (keys, values)]
        return jnp.concatenate(pieces, axis=1)

    kept = heads_of(core)
    got = lax.ppermute(heads_of(1 - core), "leaf", swap)
    own = []
    for head in range(HALF):
        cols = slice(head * 2 * DH, (head + 1) * 2 * DH)
        own.append(jnp.concatenate([kept[:, cols], got[:, cols]], axis=0))
    mine = (queries, grad_out, saved_out)
    late = lax.optimization_barrier((*mine, got))[:3]
    other = jnp.concatenate([part(array, 1 - core, HALF * WIDE) for array in late], axis=1)
    other = lax.ppermute(other, "leaf", swap)

    def shift(arrays, ring):
        return [lax.ppermute(array, "leaf", ring) for array in arrays]

    far = chips // 2
    prepared, stats = [None] * HALF, [None] * HALF
    blocks, halves = [], []
    streams = [(block, block) for block in own]
    blocks = [{0: block} for block in own]
    for step in range(1, far):
        for head in range(HALF):
            up, down = streams[head]
            up, down = lax.ppermute(up, "leaf", right), lax.ppermute(down, "leaf", left)
            blocks[head][chips - step], blocks[head][step] = up, down
            if step == 1:
                prepared[head] = prepare(head, tables, mine, other, own[head])
                stats[head] = prepared[head][6:]
            else:
                met = (step - 1, chips - step + 1)
                stats[head] = measure(met, prepared[head], stats[head], [blocks[head][at] for at in met])
            stats[head], streams[head] = lax.optimization_barrier((stats[head], (up, down)))
    for head in range(HALF):
        up, down = streams[head]
        halves.append([lax.ppermute(up[:rows], "leaf", right), lax.ppermute(down[rows:], "leaf", left)])
        met = (far - 1, far + 1)
        stats[head] = measure(met, prepared[head], stats[head], [blocks[head][at] for at in met])

    offsets = [far]
    for step in range(1, far - 3):
        offsets += [far + step, far - step]
    arrays = [halves[head] + [blocks[head][at] for at in offsets[1:]] for head in range(HALF)]
    *terms, carried = gradients(prepared, stats, offsets, arrays, None, False)
    lse = [[a] for a in terms[3 * HALF:]]
    by_offset = {at: [terms[head][slot] for head in range(HALF)] for slot, at in enumerate(offsets)}
    ups, downs = terms[HALF:2 * HALF], terms[2 * HALF:3 * HALF]

    def add(sums, at):
        return [(a + wide(b)).astype(jnp.bfloat16) for a, b in zip(sums, by_offset[at])]

    later = {4: [chips - 3, 3], 3: [chips - 2, 2], 2: [chips - 1, 1], 1: [0]}
    ours = theirs = None
    for step in range(far, 0, -1):
        if step < far:
            ups, downs = add(ups, step), add(downs, chips - step)
        if step in later:
            last = 0 in later[step]
            (lse, carried), held = lax.optimization_barrier(((lse, carried), (ups[1:], downs[1:])))
            ups, downs = ups[:1] + held[0], downs[:1] + held[1]
            arrays = [[blocks[head][at] for at in later[step]] for head in range(HALF)]
            *terms, lead = gradients(prepared, lse, later[step], arrays, carried, last)
            for slot, at in enumerate(later[step]):
                by_offset[at] = [terms[head][slot] for head in range(HALF)]
            if last:
                ours, theirs = terms[HALF], lax.ppermute(lead, "leaf", swap)
            else:
                carried = lead
        ups = [wide(a) for a in shift(ups, right)]
        downs = [wide(a) for a in shift(downs, left)]
        if step == far:
            ups = [jnp.pad(a, ((0, rows), (0, 0))) for a in ups]
            downs = [jnp.pad(a, ((rows, 0), (0, 0))) for a in downs]
    kept, got = [], []
    for head in range(HALF):
        summed = (wide(by_offset[0][head]) + ups[head] + downs[head]).astype(jnp.bfloat16)
        kept.append(summed)
        got.append(lax.ppermute(summed[rows:], "leaf", swap))

    return tuple(assemble(me, ours, theirs, kept, got))


def solution(mesh):
    tokens = P(("groups", "leaf"), None)
    tables = P("groups")
    return jax.shard_map(
        local,
        mesh=mesh,
        in_specs=(tokens,) * 5 + (tables,) * 3,
        out_specs=(tokens,) * 3,
        check_vma=False,
    )
```

```python
import functools
import math

import jax
import jax.numpy as jnp
from jax import lax
from jax.experimental import pallas as pl
from jax.experimental.pallas import tpu as pltpu
from jax.sharding import PartitionSpec as P

HQ = 20
HK = 4
DH = 128
PER = HQ // HK
HALF = HK // 2
WIDE = PER * DH
ANCESTORS = 5
SLOTS = ANCESTORS + 1
OWN = 1 << 20
SCALE = 1.0 / math.sqrt(DH)
EXP_SCALE = SCALE / math.log(2.0)
NN = (((1,), (0,)), ((), ()))
SMEM = pl.BlockSpec(memory_space=pltpu.SMEM)
HBM = pl.BlockSpec(memory_space=pl.ANY)
VMEM = pl.BlockSpec(memory_space=pltpu.VMEM)


def dot(a, b):
    return lax.dot_general(a, b, NN, preferred_element_type=jnp.float32)


def ring_order(chips):
    if chips == 8:
        return [0, 2, 4, 6, 7, 5, 3, 1]
    return list(range(chips))


def walk(device, me, places, parents, assignment, lengths, owner, plan, side):
    chips = places.shape[0]
    here = places[me // 2]

    def place(held):
        at = places[held // 2] - here
        at = jnp.where(at < 0, at + chips, at)
        return side * 2 * chips + at * 2 + jnp.where(held % 2 == me % 2, 0, 1)

    def clear(at, carry):
        plan[side * 2 * chips + at] = 0
        return carry

    lax.fori_loop(0, 2 * chips, clear, 0)
    segment = assignment[device]
    plan[place(device)] = OWN
    up = parents[segment]
    for _ in range(ANCESTORS):
        at = jnp.maximum(up, 0)

        @pl.when(up >= 0)
        def _():
            plan[place(owner[at])] = lengths[at]

        up = jnp.where(up >= 0, parents[at], -1)


def run_copies(pairs, sems):
    copies = [pltpu.make_async_copy(a, b, sems.at[i]) for i, (a, b) in enumerate(pairs)]
    for copy in copies:
        copy.start()
    return copies


def column_of(me, head, h):
    return pl.multiple_of(((me % 2 * HALF + head) * PER + h) * DH, DH)


def seen_keys(rows, sees):
    lane_at = lax.broadcasted_iota(jnp.int32, (1, rows), 1)
    key_at = lax.broadcasted_iota(jnp.int32, (rows, 1), 0)
    return key_at <= jnp.where(sees == OWN, lane_at, sees - 1)


def measure_blocks(plan, offsets, kv_ref, qt_ref, top_ref, sum_ref):
    rows = kv_ref.shape[1] // 2
    chips = plan.shape[0] // 4
    for slot, offset in enumerate(offsets):
        def visit(i, carry):
            half, side = i // 2, i % 2
            sees = plan[side * 2 * chips + offset * 2 + half]

            @pl.when(sees > 0)
            def _():
                seen = seen_keys(rows, sees)
                keys = kv_ref[slot, pl.ds(pl.multiple_of(half * rows, rows), rows), :DH]
                for h in range(PER):
                    at = (side, slice(None), slice(h * rows, (h + 1) * rows))
                    s = jnp.where(seen, dot(keys, qt_ref[at]), -1e30)
                    old = top_ref[at]
                    top = jnp.maximum(old, jnp.max(s, axis=0, keepdims=True))
                    total = jnp.sum(jnp.exp2((s - top) * EXP_SCALE), axis=0, keepdims=True)
                    top_ref[at] = top
                    sum_ref[at] = sum_ref[at] * jnp.exp2((old - top) * EXP_SCALE) + total

            return carry

        lax.fori_loop(0, 4, visit, 0)


def prepare_kernel(head, me_ref, places, parents, assignment, lengths, queries, grads, saved, other, block, *refs):
    (plan, qt_ref, gt_ref, gm_ref, qm_ref, delta_ref, top_ref, sum_ref,
     owner, q_ref, g_ref, o_ref, kv_ref, sems) = refs
    rows = queries.shape[0]
    me = me_ref[0]
    column = pl.multiple_of((me % 2 * HALF + head) * WIDE, WIDE)
    pairs = [(block, kv_ref.at[0])]
    for at, (array, held) in enumerate(zip((queries, grads, saved), (q_ref, g_ref, o_ref))):
        pairs.append((array.at[:, pl.ds(column, WIDE)], held.at[0]))
        first = (at * HALF + head) * WIDE
        pairs.append((other.at[:, first:first + WIDE], held.at[1]))
    copies = run_copies(pairs, sems)

    def invert(d, carry):
        owner[assignment[d]] = d
        return carry

    lax.fori_loop(0, assignment.shape[0], invert, 0)
    walk(me, me, places, parents, assignment, lengths, owner, plan, 0)
    walk(me + 1 - me % 2 * 2, me, places, parents, assignment, lengths, owner, plan, 1)
    row_at = lax.broadcasted_iota(jnp.int32, (rows, 1), 0)
    top_ref[...] = jnp.full(top_ref.shape, -1e30, top_ref.dtype)
    sum_ref[...] = jnp.zeros_like(sum_ref)
    for copy in copies:
        copy.wait()
    for side, device in enumerate((me, me + 1 - me % 2 * 2)):
        live = row_at < lengths[assignment[device]]
        for h in range(PER):
            lanes = slice(h * rows, (h + 1) * rows)
            cols = slice(h * DH, (h + 1) * DH)
            masked = jnp.where(live, g_ref[side, :, cols], jnp.zeros((), g_ref.dtype))
            query = q_ref[side, :, cols]
            gm_ref[side, lanes, :] = masked
            qm_ref[side, lanes, :] = query
            gt_ref[side, :, lanes] = masked.T
            qt_ref[side, :, lanes] = query.T
            terms = masked.astype(jnp.float32) * o_ref[side, :, cols].astype(jnp.float32)
            delta_ref[side, :, lanes] = jnp.sum(terms.T, axis=0, keepdims=True)
    measure_blocks(plan, [0], kv_ref, qt_ref, top_ref, sum_ref)


def row_stats(rows):
    return jax.ShapeDtypeStruct((2, 1, PER * rows), jnp.float32)


def prepare(head, tables, mine, other, block):
    rows = other.shape[0]
    chips = tables[1].shape[0]
    bf16 = jnp.bfloat16
    return pl.pallas_call(
        functools.partial(prepare_kernel, head),
        in_specs=[SMEM] * 5 + [HBM] * 5,
        out_specs=[SMEM] + [VMEM] * 7,
        out_shape=[
            jax.ShapeDtypeStruct((4 * chips,), jnp.int32),
            jax.ShapeDtypeStruct((2, DH, PER * rows), bf16),
            jax.ShapeDtypeStruct((2, DH, PER * rows), bf16),
            jax.ShapeDtypeStruct((2, PER * rows, DH), bf16),
            jax.ShapeDtypeStruct((2, PER * rows, DH), bf16),
            row_stats(rows),
            row_stats(rows),
            row_stats(rows),
        ],
        scratch_shapes=[pltpu.SMEM(tables[3].shape, jnp.int32)]
        + [pltpu.VMEM((2, rows, WIDE), bf16)] * 3
        + [pltpu.VMEM((1, 2 * rows, 2 * DH), bf16), pltpu.SemaphoreType.DMA((7,))],
        compiler_params=pltpu.CompilerParams(vmem_limit_bytes=8 << 20),
        cost_estimate=pl.CostEstimate(flops=0, bytes_accessed=12 << 20, transcendentals=0),
    )(*tables, *mine, other, block)


def measure_kernel(offsets, plan, qt_ref, top_in, sum_in, *refs):
    count = len(offsets)
    blocks, (top_ref, sum_ref, kv_ref, sems) = refs[:count], refs[count:]
    copies = run_copies([(held, kv_ref.at[i]) for i, held in enumerate(blocks)], sems)
    top_ref[...] = top_in[...]
    sum_ref[...] = sum_in[...]
    for copy in copies:
        copy.wait()
    measure_blocks(plan, offsets, kv_ref, qt_ref, top_ref, sum_ref)


def measure(offsets, prepared, stats, blocks):
    rows = blocks[0].shape[0] // 2
    plan, qt = prepared[:2]
    return pl.pallas_call(
        functools.partial(measure_kernel, offsets),
        in_specs=[SMEM] + [VMEM] * 3 + [HBM] * len(blocks),
        out_specs=[VMEM] * 2,
        out_shape=[row_stats(rows)] * 2,
        scratch_shapes=[
            pltpu.VMEM((len(offsets), 2 * rows, 2 * DH), jnp.bfloat16),
            pltpu.SemaphoreType.DMA((len(blocks),)),
        ],
        compiler_params=pltpu.CompilerParams(vmem_limit_bytes=6 << 20),
        cost_estimate=pl.CostEstimate(flops=0, bytes_accessed=8 << 20, transcendentals=0),
    )(plan, qt, *stats, *blocks)


def grads_kernel(chips, offsets, first, last, plan, *refs):
    far = chips // 2
    shared = []
    for head in range(HALF):
        shared.append(refs[:6 + first])
        refs = refs[6 + first:]
    blocks = []
    for head in range(HALF):
        blocks.append(refs[:len(offsets) + first])
        refs = refs[len(offsets) + first:]
    carried = None
    if not first:
        carried, refs = refs[0], refs[1:]
    terms, refs = refs[:HALF], refs[HALF:]
    if first:
        ups, downs, refs = refs[:HALF], refs[HALF:2 * HALF], refs[2 * HALF:]
        lse_out, refs = refs[:HALF], refs[HALF:]
    outs, refs = refs[:2 if last else 1], refs[2 if last else 1:]
    (kv_ref, acc_ref, stage_ref, zero_ref, p_ref, ds_ref, sum_ref, dqt_ref, offset_ref,
     sems, kv_sems, out_sems, zero_sems) = refs
    lse_ref = lse_out if first else [head[5] for head in shared]
    if not last:
        dqt_ref = outs[0]
    rows = acc_ref.shape[1]
    slots = stage_ref.shape[0]

    pairs = []
    for head in range(HALF):
        for slot, offset in enumerate(offsets):
            offset_ref[slot] = offset
            if offset == far:
                pairs.append((blocks[head][0], kv_ref.at[slot, head, :rows]))
                pairs.append((blocks[head][1], kv_ref.at[slot, head, rows:]))
            else:
                pltpu.make_async_copy(
                    blocks[head][slot + first], kv_ref.at[slot, head], kv_sems.at[slot, head]
                ).start()
    copies = run_copies(pairs, sems)
    zero_ref[...] = jnp.zeros_like(zero_ref)

    def sees(side, i):
        return plan[side * 2 * chips + offset_ref[i // 2] * 2 + i % 2]

    def seen(i):
        return (sees(0, i) > 0) | (sees(1, i) > 0)

    def send(i, sources, sem_of):
        at_block, half = i // 2, i % 2
        here = pl.ds(pl.multiple_of(half * rows, rows), rows)
        for head in range(HALF):
            def put(target):
                pltpu.make_async_copy(sources[head], target, sem_of(head)).start()

            if not first:
                put(terms[head].at[at_block, here])
                continue

            @pl.when(i >= 2)
            def _():
                put(terms[head].at[at_block, here])

            @pl.when(i == 0)
            def _():
                put(ups[head])

            @pl.when(i == 1)
            def _():
                put(downs[head])

    def sent(sem_of):
        for head in range(HALF):
            pltpu.make_async_copy(zero_ref, terms[head].at[0, :rows], sem_of(head)).wait()

    def send_zeros(i, carry):
        @pl.when(jnp.logical_not(seen(i)))
        def _():
            send(i, [zero_ref] * HALF, lambda head: zero_sems.at[i, head])

        return carry

    lax.fori_loop(0, 2 * len(offsets), send_zeros, 0)
    dqt_ref[...] = jnp.zeros_like(dqt_ref) if first else carried[...]
    for copy in copies:
        copy.wait()
    if first:
        for head in range(HALF):
            top_ref, total_ref = lse_out[head], sum_ref.at[head]
            top_ref[...] = shared[head][5][...]
            total_ref[...] = shared[head][6][...]
            measure_blocks(plan, [far], kv_ref.at[:, head], shared[head][0], top_ref, total_ref)
            top_ref[...] = top_ref[...] * EXP_SCALE + jnp.log2(total_ref[...])

    def visit(i, done):
        at_block, half = i // 2, i % 2
        here = pl.ds(pl.multiple_of(half * rows, rows), rows)

        if len(offsets) > first:
            @pl.when((half == 0) & (offset_ref[at_block] != far))
            def _():
                for head in range(HALF):
                    pltpu.make_async_copy(
                        blocks[head][-1], kv_ref.at[at_block, head], kv_sems.at[at_block, head]
                    ).wait()

        def look(side, carry):
            @pl.when(sees(side, i) > 0)
            def _():
                allowed = seen_keys(rows, sees(side, i))
                for head in range(HALF):
                    qt_ref, gt_ref, gm_ref, qm_ref, delta_ref = shared[head][:5]
                    k = kv_ref[at_block, head, here, :DH]
                    v = kv_ref[at_block, head, here, DH:]
                    for h in range(PER):
                        lanes = slice(h * rows, (h + 1) * rows)
                        part = (side, slice(None), lanes)
                        s = dot(k, qt_ref[part]) * EXP_SCALE - lse_ref[head][part]
                        p = jnp.where(allowed, jnp.exp2(s), 0.0)
                        ds = p * (dot(v, gt_ref[part]) - delta_ref[part])
                        p_ref[head, :, lanes] = p.astype(p_ref.dtype)
                        ds_ref[head, :, lanes] = ds.astype(ds_ref.dtype)
                    acc_ref[head, :, DH:] += dot(p_ref[head], gm_ref[side])
                    acc_ref[head, :, :DH] += dot(ds_ref[head], qm_ref[side])
                    dqt_ref[head, side] += dot(k.T, ds_ref[head])

            return carry

        @pl.when(seen(i))
        def _():
            slot = done % slots

            @pl.when(done >= slots)
            def _():
                sent(lambda head: out_sems.at[slot, head])

            acc_ref[...] = jnp.zeros_like(acc_ref)
            lax.fori_loop(0, 2, look, 0)
            for head in range(HALF):
                stage_ref[slot, head, :, :DH] = (acc_ref[head, :, :DH] * SCALE).astype(stage_ref.dtype)
                stage_ref[slot, head, :, DH:] = acc_ref[head, :, DH:].astype(stage_ref.dtype)
            send(i, [stage_ref.at[slot, head] for head in range(HALF)], lambda head: out_sems.at[slot, head])

        return done + seen(i).astype(jnp.int32)

    done = lax.fori_loop(0, 2 * len(offsets), visit, jnp.int32(0))
    if last:
        for side, dq_ref in enumerate(outs):
            for head in range(HALF):
                for h in range(PER):
                    dq = (dqt_ref[head, side, :, h * rows:(h + 1) * rows] * SCALE).astype(dq_ref.dtype)
                    dq_ref[:, (head * PER + h) * DH:(head * PER + h + 1) * DH] = dq.T

    def zeros_sent(i, carry):
        @pl.when(jnp.logical_not(seen(i)))
        def _():
            sent(lambda head: zero_sems.at[i, head])

        return carry

    lax.fori_loop(0, 2 * len(offsets), zeros_sent, 0)
    for slot in range(slots):
        @pl.when(done > slot)
        def _():
            sent(lambda head: out_sems.at[slot, head])


def gradients(prepared, stats, offsets, blocks, carried, last):
    plan = prepared[0][0]
    chips = plan.shape[0] // 4
    rows = prepared[0][3].shape[1] // PER
    first = carried is None
    bf16, f32 = jnp.bfloat16, jnp.float32
    shared = [(*prepared[head][1:6], *stats[head]) for head in range(HALF)]
    arrays = [a for head in shared for a in head] + [a for head in blocks for a in head]
    arrays += [] if first else [carried]
    dense = jax.ShapeDtypeStruct((len(offsets), 2 * rows, 2 * DH), bf16)
    piece = jax.ShapeDtypeStruct((rows, 2 * DH), bf16)
    query = jax.ShapeDtypeStruct((rows, HALF * WIDE), bf16)
    sums = jax.ShapeDtypeStruct((HALF, 2, DH, PER * rows), f32)
    out_shape, out_specs = [dense] * HALF, [HBM] * HALF
    if first:
        out_shape += [piece] * (2 * HALF) + [row_stats(rows)] * HALF
        out_specs += [HBM] * (2 * HALF) + [VMEM] * HALF
    out_shape += [query] * 2 if last else [sums]
    out_specs += [VMEM] * (2 if last else 1)
    flat = sum(len(head) for head in shared)
    in_specs = [SMEM] + [VMEM] * flat + [HBM] * (len(arrays) - flat)
    if not first:
        in_specs[-1] = VMEM
    return pl.pallas_call(
        functools.partial(grads_kernel, chips, tuple(offsets), first, last),
        in_specs=in_specs,
        out_specs=out_specs,
        out_shape=out_shape,
        scratch_shapes=[
            pltpu.VMEM((len(offsets), HALF, 2 * rows, 2 * DH), bf16),
            pltpu.VMEM((HALF, rows, 2 * DH), f32),
            pltpu.VMEM((4, HALF, rows, 2 * DH), bf16),
            pltpu.VMEM((rows, 2 * DH), bf16),
            pltpu.VMEM((HALF, rows, PER * rows), bf16),
            pltpu.VMEM((HALF, rows, PER * rows), bf16),
            pltpu.VMEM((HALF, 2, 1, PER * rows), f32),
            pltpu.VMEM((HALF, 2, DH, PER * rows) if last else (8, DH), f32),
            pltpu.SMEM((len(offsets),), jnp.int32),
            pltpu.SemaphoreType.DMA((2 * HALF,)),
            pltpu.SemaphoreType.DMA((len(offsets), HALF)),
            pltpu.SemaphoreType.DMA((4, HALF)),
            pltpu.SemaphoreType.DMA((2 * len(offsets), HALF)),
        ],
        compiler_params=pltpu.CompilerParams(vmem_limit_bytes=(13 << 20) + (len(offsets) << 19)),
        cost_estimate=pl.CostEstimate(flops=8 << 30, bytes_accessed=16 << 20, transcendentals=0),
    )(plan, *arrays)


def wide(x):
    return x.astype(jnp.float32)


def assemble_kernel(me_ref, *refs):
    ours, theirs, refs = refs[0], refs[1], refs[2:]
    kept, got, refs = refs[:HALF], refs[HALF:2 * HALF], refs[2 * HALF:]
    query_grad, key_grad, value_grad, sems = refs
    rows = ours.shape[0]
    core = me_ref[0] % 2
    pairs = []
    for which, query, sums in ((core, ours, kept), (1 - core, theirs, got)):
        column = pl.multiple_of(which * (HALF * WIDE), HALF * WIDE)
        pairs.append((query, query_grad.at[:, pl.ds(column, HALF * WIDE)]))
        for head in range(HALF):
            column = pl.multiple_of((which * HALF + head) * DH, DH)
            for first, out in ((0, key_grad), (DH, value_grad)):
                pairs.append((sums[head].at[:rows, first:first + DH], out.at[:, pl.ds(column, DH)]))
    for copy in run_copies(pairs, sems):
        copy.wait()


def assemble(me, ours, theirs, kept, got):
    rows = ours.shape[0]
    return pl.pallas_call(
        assemble_kernel,
        in_specs=[SMEM] + [HBM] * (2 + 2 * HALF),
        out_specs=[HBM] * 3,
        out_shape=[
            jax.ShapeDtypeStruct((rows, 2 * HALF * WIDE), jnp.bfloat16),
            jax.ShapeDtypeStruct((rows, 2 * HALF * DH), jnp.bfloat16),
            jax.ShapeDtypeStruct((rows, 2 * HALF * DH), jnp.bfloat16),
        ],
        scratch_shapes=[pltpu.SemaphoreType.DMA((2 + 4 * HALF,))],
        compiler_params=pltpu.CompilerParams(vmem_limit_bytes=2 << 20),
        cost_estimate=pl.CostEstimate(flops=0, bytes_accessed=4 << 20, transcendentals=0),
    )(me, ours, theirs, *kept, *got)


def local(queries, keys, values, saved_out, grad_out, parents, assignment, lengths):
    rows = keys.shape[0]
    chips = lax.axis_size("leaf") // 2
    order = ring_order(chips)
    ahead = [(order[i], order[(i + 1) % chips]) for i in range(chips)]
    right = [(2 * a + c, 2 * b + c) for a, b in ahead for c in range(2)]
    left = [(b, a) for a, b in right]
    swap = [(2 * a + c, 2 * a + 1 - c) for a in range(chips) for c in range(2)]
    places = jnp.asarray([order.index(chip) for chip in range(chips)], jnp.int32)
    index = lax.axis_index("leaf").astype(jnp.int32)
    core = index % 2
    me = index.reshape(1)
    tables = (me, places, parents, assignment, lengths)

    def part(array, which, width):
        return lax.dynamic_slice(array, (0, which * width), (rows, width))

    def heads_of(which):
        pieces = [part(array, which * HALF + head, DH) for head in range(HALF) for array in (keys, values)]
        return jnp.concatenate(pieces, axis=1)

    kept = heads_of(core)
    got = lax.ppermute(heads_of(1 - core), "leaf", swap)
    own = []
    for head in range(HALF):
        cols = slice(head * 2 * DH, (head + 1) * 2 * DH)
        own.append(jnp.concatenate([kept[:, cols], got[:, cols]], axis=0))
    mine = (queries, grad_out, saved_out)
    late = lax.optimization_barrier((*mine, got))[:3]
    other = jnp.concatenate([part(array, 1 - core, HALF * WIDE) for array in late], axis=1)
    other = lax.ppermute(other, "leaf", swap)

    def shift(arrays, ring):
        return [lax.ppermute(array, "leaf", ring) for array in arrays]

    far = chips // 2
    prepared, stats = [None] * HALF, [None] * HALF
    blocks, halves = [], []
    streams = [(block, block) for block in own]
    blocks = [{0: block} for block in own]
    for step in range(1, far):
        for head in range(HALF):
            up, down = streams[head]
            up, down = lax.ppermute(up, "leaf", right), lax.ppermute(down, "leaf", left)
            blocks[head][chips - step], blocks[head][step] = up, down
            if step == 1:
                prepared[head] = prepare(head, tables, mine, other, own[head])
                stats[head] = prepared[head][6:]
            else:
                met = (step - 1, chips - step + 1)
                stats[head] = measure(met, prepared[head], stats[head], [blocks[head][at] for at in met])
            stats[head], streams[head] = lax.optimization_barrier((stats[head], (up, down)))
    for head in range(HALF):
        up, down = streams[head]
        halves.append([lax.ppermute(up[:rows], "leaf", right), lax.ppermute(down[rows:], "leaf", left)])
        met = (far - 1, far + 1)
        stats[head] = measure(met, prepared[head], stats[head], [blocks[head][at] for at in met])

    offsets = [far]
    for step in range(1, far - 3):
        offsets += [far + step, far - step]
    arrays = [halves[head] + [blocks[head][at] for at in offsets[1:]] for head in range(HALF)]
    *terms, carried = gradients(prepared, stats, offsets, arrays, None, False)
    lse = [[a] for a in terms[3 * HALF:]]
    by_offset = {at: [terms[head][slot] for head in range(HALF)] for slot, at in enumerate(offsets)}
    ups, downs = terms[HALF:2 * HALF], terms[2 * HALF:3 * HALF]

    def add(sums, at):
        return [(wide(a) + wide(b)).astype(jnp.bfloat16) for a, b in zip(sums, by_offset[at])]

    later = {4: [chips - 3, 3], 3: [chips - 2, 2], 2: [chips - 1, 1], 1: [0]}
    ours = theirs = None
    for step in range(far, 0, -1):
        if step < far:
            ups, downs = add(ups, step), add(downs, chips - step)
        if step in later:
            last = 0 in later[step]
            (lse, carried), held = lax.optimization_barrier(((lse, carried), (ups[1:], downs[1:])))
            ups, downs = ups[:1] + held[0], downs[:1] + held[1]
            arrays = [[blocks[head][at] for at in later[step]] for head in range(HALF)]
            *terms, lead = gradients(prepared, lse, later[step], arrays, carried, last)
            for slot, at in enumerate(later[step]):
                by_offset[at] = [terms[head][slot] for head in range(HALF)]
            if last:
                ours, theirs = terms[HALF], lead
            else:
                carried = lead
        ups, downs = shift(ups, right), shift(downs, left)
        if step == far:
            ups = [jnp.pad(a, ((0, rows), (0, 0))) for a in ups]
            downs = [jnp.pad(a, ((rows, 0), (0, 0))) for a in downs]
    theirs, ups, downs = lax.optimization_barrier((theirs, ups, downs))
    theirs = lax.ppermute(theirs, "leaf", swap)
    kept, got = [], []
    for head in range(HALF):
        summed = (wide(by_offset[0][head]) + wide(ups[head]) + wide(downs[head])).astype(jnp.bfloat16)
        kept.append(summed)
        got.append(lax.ppermute(summed[rows:], "leaf", swap))

    return tuple(assemble(me, ours, theirs, kept, got))


def solution(mesh):
    tokens = P(("groups", "leaf"), None)
    tables = P("groups")
    return jax.shard_map(
        local,
        mesh=mesh,
        in_specs=(tokens,) * 5 + (tables,) * 3,
        out_specs=(tokens,) * 3,
        check_vma=False,
    )
```

```python
import functools
import math

import jax
import jax.numpy as jnp
from jax import lax
from jax.experimental import pallas as pl
from jax.experimental.pallas import tpu as pltpu
from jax.sharding import PartitionSpec as P

HQ = 20
HK = 4
DH = 128
PER = HQ // HK
HALF = HK // 2
WIDE = PER * DH
ANCESTORS = 5
SLOTS = ANCESTORS + 1
OWN = 1 << 20
CHUNKS = 4
FEWEST = 3
TAIL = 8
SCALE = 1.0 / math.sqrt(DH)
EXP_SCALE = SCALE / math.log(2.0)
NN = (((1,), (0,)), ((), ()))
SMEM = pl.BlockSpec(memory_space=pltpu.SMEM)
HBM = pl.BlockSpec(memory_space=pl.ANY)
VMEM = pl.BlockSpec(memory_space=pltpu.VMEM)


def dot(a, b):
    return lax.dot_general(a, b, NN, preferred_element_type=jnp.float32)


def ring_order(chips):
    if chips == 8:
        return [0, 2, 4, 6, 7, 5, 3, 1]
    return list(range(chips))


def walk(device, me, places, parents, assignment, lengths, owner, plan, side, rows):
    chips = places.shape[0]
    here = places[me // 2]

    def place(held):
        at = places[held // 2] - here
        at = jnp.where(at < 0, at + chips, at)
        return side * 2 * chips + at * 2 + jnp.where(held % 2 == me % 2, 0, 1)

    def clear(at, carry):
        plan[side * 2 * chips + at] = 0
        return carry

    lax.fori_loop(0, 2 * chips, clear, 0)
    segment = assignment[device]
    plan[place(device)] = OWN
    chunk = rows // CHUNKS
    live = (lengths[segment] + chunk - 1) // chunk
    plan[4 * chips + side] = jnp.maximum((live * PER + CHUNKS - 1) // CHUNKS, FEWEST)
    up = parents[segment]
    for _ in range(ANCESTORS):
        at = jnp.maximum(up, 0)

        @pl.when(up >= 0)
        def _():
            plan[place(owner[at])] = lengths[at]

        up = jnp.where(up >= 0, parents[at], -1)


def run_copies(pairs, sems):
    copies = [pltpu.make_async_copy(a, b, sems.at[i]) for i, (a, b) in enumerate(pairs)]
    for copy in copies:
        copy.start()
    return copies


def column_of(me, head, h):
    return pl.multiple_of(((me % 2 * HALF + head) * PER + h) * DH, DH)


def chips_of(plan):
    return (plan.shape[0] - TAIL) // 4


def seen_keys(rows, sees, tile):
    chunk = rows // CHUNKS
    packed = lax.broadcasted_iota(jnp.int32, (1, rows), 1) + tile * rows
    row_at = packed & (chunk - 1)
    for at in range(1, CHUNKS):
        row_at = row_at + jnp.where(packed >= at * PER * chunk, chunk, 0)
    key_at = lax.broadcasted_iota(jnp.int32, (rows, 1), 0)
    return key_at <= jnp.where(sees == OWN, row_at, sees - 1)


def measure_blocks(plan, offsets, kv_ref, qt_ref, top_ref, sum_ref):
    rows = kv_ref.shape[1] // 2
    chips = chips_of(plan)
    for slot, offset in enumerate(offsets):
        def visit(i, carry):
            half, side = i // 2, i % 2
            sees = plan[side * 2 * chips + offset * 2 + half]

            def measure_tiles(tiles):
                keys = kv_ref[slot, pl.ds(pl.multiple_of(half * rows, rows), rows), :DH]
                for tile in range(tiles):
                    at = (side, slice(None), slice(tile * rows, (tile + 1) * rows))
                    s = jnp.where(seen_keys(rows, sees, tile), dot(keys, qt_ref[at]), -1e30)
                    old = top_ref[at]
                    top = jnp.maximum(old, jnp.max(s, axis=0, keepdims=True))
                    total = jnp.sum(jnp.exp2((s - top) * EXP_SCALE), axis=0, keepdims=True)
                    top_ref[at] = top
                    sum_ref[at] = sum_ref[at] * jnp.exp2((old - top) * EXP_SCALE) + total

            for tiles in range(FEWEST, PER + 1):
                @pl.when((sees > 0) & (plan[4 * chips + side] == tiles))
                def _():
                    measure_tiles(tiles)

            return carry

        lax.fori_loop(0, 4, visit, 0)


def prepare_kernel(head, me_ref, places, parents, assignment, lengths, queries, grads, saved, other, block, *refs):
    (plan, qt_ref, gt_ref, gm_ref, qm_ref, delta_ref, top_ref, sum_ref,
     owner, q_ref, g_ref, o_ref, terms_ref, kv_ref, sems) = refs
    rows = queries.shape[0]
    chunk = rows // CHUNKS
    me = me_ref[0]
    column = pl.multiple_of((me % 2 * HALF + head) * WIDE, WIDE)
    pairs = [(block, kv_ref.at[0])]
    for at, (array, held) in enumerate(zip((queries, grads, saved), (q_ref, g_ref, o_ref))):
        pairs.append((array.at[:, pl.ds(column, WIDE)], held.at[0]))
        first = (at * HALF + head) * WIDE
        pairs.append((other.at[:, first:first + WIDE], held.at[1]))
    copies = run_copies(pairs, sems)

    def invert(d, carry):
        owner[assignment[d]] = d
        return carry

    lax.fori_loop(0, assignment.shape[0], invert, 0)
    walk(me, me, places, parents, assignment, lengths, owner, plan, 0, rows)
    walk(me + 1 - me % 2 * 2, me, places, parents, assignment, lengths, owner, plan, 1, rows)
    row_at = lax.broadcasted_iota(jnp.int32, (rows, 1), 0)
    top_ref[...] = jnp.full(top_ref.shape, -1e30, top_ref.dtype)
    sum_ref[...] = jnp.zeros_like(sum_ref)
    for copy in copies:
        copy.wait()
    for side, device in enumerate((me, me + 1 - me % 2 * 2)):
        live = row_at < lengths[assignment[device]]
        for h in range(PER):
            cols = slice(h * DH, (h + 1) * DH)
            masked = jnp.where(live, g_ref[side, :, cols], jnp.zeros((), g_ref.dtype))
            query = q_ref[side, :, cols]
            terms = masked.astype(jnp.float32) * o_ref[side, :, cols].astype(jnp.float32)
            for at in range(CHUNKS):
                here = slice(at * chunk, (at + 1) * chunk)
                there = slice((at * PER + h) * chunk, (at * PER + h + 1) * chunk)
                gm_ref[side, there, :] = masked[here]
                qm_ref[side, there, :] = query[here]
                terms_ref[there, :] = terms[here]
        for tile in range(PER):
            lanes = slice(tile * rows, (tile + 1) * rows)
            gt_ref[side, :, lanes] = gm_ref[side, lanes, :].T
            qt_ref[side, :, lanes] = qm_ref[side, lanes, :].T
            delta_ref[side, :, lanes] = jnp.sum(terms_ref[lanes, :].T, axis=0, keepdims=True)
    measure_blocks(plan, [0], kv_ref, qt_ref, top_ref, sum_ref)


def row_stats(rows):
    return jax.ShapeDtypeStruct((2, 1, PER * rows), jnp.float32)


def prepare(head, tables, mine, other, block):
    rows = other.shape[0]
    chips = tables[1].shape[0]
    bf16 = jnp.bfloat16
    return pl.pallas_call(
        functools.partial(prepare_kernel, head),
        in_specs=[SMEM] * 5 + [HBM] * 5,
        out_specs=[SMEM] + [VMEM] * 7,
        out_shape=[
            jax.ShapeDtypeStruct((4 * chips + TAIL,), jnp.int32),
            jax.ShapeDtypeStruct((2, DH, PER * rows), bf16),
            jax.ShapeDtypeStruct((2, DH, PER * rows), bf16),
            jax.ShapeDtypeStruct((2, PER * rows, DH), bf16),
            jax.ShapeDtypeStruct((2, PER * rows, DH), bf16),
            row_stats(rows),
            row_stats(rows),
            row_stats(rows),
        ],
        scratch_shapes=[pltpu.SMEM(tables[3].shape, jnp.int32)]
        + [pltpu.VMEM((2, rows, WIDE), bf16)] * 3
        + [pltpu.VMEM((PER * rows, DH), jnp.float32)]
        + [pltpu.VMEM((1, 2 * rows, 2 * DH), bf16), pltpu.SemaphoreType.DMA((7,))],
        compiler_params=pltpu.CompilerParams(vmem_limit_bytes=8 << 20),
        cost_estimate=pl.CostEstimate(flops=0, bytes_accessed=12 << 20, transcendentals=0),
    )(*tables, *mine, other, block)


def measure_kernel(offsets, plan, qt_ref, top_in, sum_in, *refs):
    count = len(offsets)
    blocks, (top_ref, sum_ref, kv_ref, sems) = refs[:count], refs[count:]
    copies = run_copies([(held, kv_ref.at[i]) for i, held in enumerate(blocks)], sems)
    top_ref[...] = top_in[...]
    sum_ref[...] = sum_in[...]
    for copy in copies:
        copy.wait()
    measure_blocks(plan, offsets, kv_ref, qt_ref, top_ref, sum_ref)


def measure(offsets, prepared, stats, blocks):
    rows = blocks[0].shape[0] // 2
    plan, qt = prepared[:2]
    return pl.pallas_call(
        functools.partial(measure_kernel, offsets),
        in_specs=[SMEM] + [VMEM] * 3 + [HBM] * len(blocks),
        out_specs=[VMEM] * 2,
        out_shape=[row_stats(rows)] * 2,
        scratch_shapes=[
            pltpu.VMEM((len(offsets), 2 * rows, 2 * DH), jnp.bfloat16),
            pltpu.SemaphoreType.DMA((len(blocks),)),
        ],
        compiler_params=pltpu.CompilerParams(vmem_limit_bytes=6 << 20),
        cost_estimate=pl.CostEstimate(flops=0, bytes_accessed=8 << 20, transcendentals=0),
    )(plan, qt, *stats, *blocks)


def grads_kernel(chips, offsets, first, last, plan, *refs):
    far = chips // 2
    shared = []
    for head in range(HALF):
        shared.append(refs[:6 + first])
        refs = refs[6 + first:]
    blocks = []
    for head in range(HALF):
        blocks.append(refs[:len(offsets) + first])
        refs = refs[len(offsets) + first:]
    carried = None
    if not first:
        carried, refs = refs[0], refs[1:]
    terms, refs = refs[:HALF], refs[HALF:]
    if first:
        ups, downs, refs = refs[:HALF], refs[HALF:2 * HALF], refs[2 * HALF:]
        lse_out, refs = refs[:HALF], refs[HALF:]
    outs, refs = refs[:2 if last else 1], refs[2 if last else 1:]
    (kv_ref, acc_ref, stage_ref, zero_ref, p_ref, ds_ref, sum_ref, dqt_ref, offset_ref,
     sems, kv_sems, out_sems, zero_sems) = refs
    lse_ref = lse_out if first else [head[5] for head in shared]
    if not last:
        dqt_ref = outs[0]
    rows = acc_ref.shape[1]
    slots = stage_ref.shape[0]

    pairs = []
    for head in range(HALF):
        for slot, offset in enumerate(offsets):
            offset_ref[slot] = offset
            if offset == far:
                pairs.append((blocks[head][0], kv_ref.at[slot, head, :rows]))
                pairs.append((blocks[head][1], kv_ref.at[slot, head, rows:]))
            else:
                pltpu.make_async_copy(
                    blocks[head][slot + first], kv_ref.at[slot, head], kv_sems.at[slot, head]
                ).start()
    copies = run_copies(pairs, sems)
    zero_ref[...] = jnp.zeros_like(zero_ref)

    def sees(side, i):
        return plan[side * 2 * chips + offset_ref[i // 2] * 2 + i % 2]

    def seen(i):
        return (sees(0, i) > 0) | (sees(1, i) > 0)

    def send(i, sources, sem_of):
        at_block, half = i // 2, i % 2
        here = pl.ds(pl.multiple_of(half * rows, rows), rows)
        for head in range(HALF):
            def put(target):
                pltpu.make_async_copy(sources[head], target, sem_of(head)).start()

            if not first:
                put(terms[head].at[at_block, here])
                continue

            @pl.when(i >= 2)
            def _():
                put(terms[head].at[at_block, here])

            @pl.when(i == 0)
            def _():
                put(ups[head])

            @pl.when(i == 1)
            def _():
                put(downs[head])

    def sent(sem_of):
        for head in range(HALF):
            pltpu.make_async_copy(zero_ref, terms[head].at[0, :rows], sem_of(head)).wait()

    def send_zeros(i, carry):
        @pl.when(jnp.logical_not(seen(i)))
        def _():
            send(i, [zero_ref] * HALF, lambda head: zero_sems.at[i, head])

        return carry

    lax.fori_loop(0, 2 * len(offsets), send_zeros, 0)
    dqt_ref[...] = jnp.zeros_like(dqt_ref) if first else carried[...]
    for copy in copies:
        copy.wait()
    if first:
        for head in range(HALF):
            top_ref, total_ref = lse_out[head], sum_ref.at[head]
            top_ref[...] = shared[head][5][...]
            total_ref[...] = shared[head][6][...]
            measure_blocks(plan, [far], kv_ref.at[:, head], shared[head][0], top_ref, total_ref)
            top_ref[...] = top_ref[...] * EXP_SCALE + jnp.log2(total_ref[...])

    def visit(i, done):
        at_block, half = i // 2, i % 2
        here = pl.ds(pl.multiple_of(half * rows, rows), rows)

        if len(offsets) > first:
            @pl.when((half == 0) & (offset_ref[at_block] != far))
            def _():
                for head in range(HALF):
                    pltpu.make_async_copy(
                        blocks[head][-1], kv_ref.at[at_block, head], kv_sems.at[at_block, head]
                    ).wait()

        def look(side, carry):
            def look_tiles(tiles):
                live = slice(0, tiles * rows)
                for head in range(HALF):
                    qt_ref, gt_ref, gm_ref, qm_ref, delta_ref = shared[head][:5]
                    k = kv_ref[at_block, head, here, :DH]
                    v = kv_ref[at_block, head, here, DH:]
                    for tile in range(tiles):
                        lanes = slice(tile * rows, (tile + 1) * rows)
                        part = (side, slice(None), lanes)
                        s = dot(k, qt_ref[part]) * EXP_SCALE - lse_ref[head][part]
                        p = jnp.where(seen_keys(rows, sees(side, i), tile), jnp.exp2(s), 0.0)
                        ds = p * (dot(v, gt_ref[part]) - delta_ref[part])
                        p_ref[head, :, lanes] = p.astype(p_ref.dtype)
                        ds_ref[head, :, lanes] = ds.astype(ds_ref.dtype)
                    acc_ref[head, :, DH:] += dot(p_ref[head, :, live], gm_ref[side, live, :])
                    acc_ref[head, :, :DH] += dot(ds_ref[head, :, live], qm_ref[side, live, :])
                    dqt_ref[head, side, :, live] += dot(k.T, ds_ref[head, :, live])

            for tiles in range(FEWEST, PER + 1):
                @pl.when((sees(side, i) > 0) & (plan[4 * chips + side] == tiles))
                def _():
                    look_tiles(tiles)

            return carry

        @pl.when(seen(i))
        def _():
            slot = done % slots

            @pl.when(done >= slots)
            def _():
                sent(lambda head: out_sems.at[slot, head])

            acc_ref[...] = jnp.zeros_like(acc_ref)
            lax.fori_loop(0, 2, look, 0)
            for head in range(HALF):
                stage_ref[slot, head, :, :DH] = (acc_ref[head, :, :DH] * SCALE).astype(stage_ref.dtype)
                stage_ref[slot, head, :, DH:] = acc_ref[head, :, DH:].astype(stage_ref.dtype)
            send(i, [stage_ref.at[slot, head] for head in range(HALF)], lambda head: out_sems.at[slot, head])

        return done + seen(i).astype(jnp.int32)

    done = lax.fori_loop(0, 2 * len(offsets), visit, jnp.int32(0))
    if last:
        chunk = rows // CHUNKS
        for side, dq_ref in enumerate(outs):
            for head in range(HALF):
                for tile in range(PER):
                    dq = dqt_ref[head, side, :, tile * rows:(tile + 1) * rows] * SCALE
                    dq = dq.T.astype(dq_ref.dtype)
                    for piece in range(CHUNKS):
                        at, h = divmod(tile * CHUNKS + piece, PER)
                        cols = slice((head * PER + h) * DH, (head * PER + h + 1) * DH)
                        dq_ref[at * chunk:(at + 1) * chunk, cols] = dq[piece * chunk:(piece + 1) * chunk]

    def zeros_sent(i, carry):
        @pl.when(jnp.logical_not(seen(i)))
        def _():
            sent(lambda head: zero_sems.at[i, head])

        return carry

    lax.fori_loop(0, 2 * len(offsets), zeros_sent, 0)
    for slot in range(slots):
        @pl.when(done > slot)
        def _():
            sent(lambda head: out_sems.at[slot, head])


def gradients(prepared, stats, offsets, blocks, carried, last):
    plan = prepared[0][0]
    chips = chips_of(plan)
    rows = prepared[0][3].shape[1] // PER
    first = carried is None
    bf16, f32 = jnp.bfloat16, jnp.float32
    shared = [(*prepared[head][1:6], *stats[head]) for head in range(HALF)]
    arrays = [a for head in shared for a in head] + [a for head in blocks for a in head]
    arrays += [] if first else [carried]
    dense = jax.ShapeDtypeStruct((len(offsets), 2 * rows, 2 * DH), bf16)
    piece = jax.ShapeDtypeStruct((rows, 2 * DH), bf16)
    query = jax.ShapeDtypeStruct((rows, HALF * WIDE), bf16)
    sums = jax.ShapeDtypeStruct((HALF, 2, DH, PER * rows), f32)
    out_shape, out_specs = [dense] * HALF, [HBM] * HALF
    if first:
        out_shape += [piece] * (2 * HALF) + [row_stats(rows)] * HALF
        out_specs += [HBM] * (2 * HALF) + [VMEM] * HALF
    out_shape += [query] * 2 if last else [sums]
    out_specs += [VMEM] * (2 if last else 1)
    flat = sum(len(head) for head in shared)
    in_specs = [SMEM] + [VMEM] * flat + [HBM] * (len(arrays) - flat)
    if not first:
        in_specs[-1] = VMEM
    return pl.pallas_call(
        functools.partial(grads_kernel, chips, tuple(offsets), first, last),
        in_specs=in_specs,
        out_specs=out_specs,
        out_shape=out_shape,
        scratch_shapes=[
            pltpu.VMEM((len(offsets), HALF, 2 * rows, 2 * DH), bf16),
            pltpu.VMEM((HALF, rows, 2 * DH), f32),
            pltpu.VMEM((4, HALF, rows, 2 * DH), bf16),
            pltpu.VMEM((rows, 2 * DH), bf16),
            pltpu.VMEM((HALF, rows, PER * rows), bf16),
            pltpu.VMEM((HALF, rows, PER * rows), bf16),
            pltpu.VMEM((HALF, 2, 1, PER * rows), f32),
            pltpu.VMEM((HALF, 2, DH, PER * rows) if last else (8, DH), f32),
            pltpu.SMEM((len(offsets),), jnp.int32),
            pltpu.SemaphoreType.DMA((2 * HALF,)),
            pltpu.SemaphoreType.DMA((len(offsets), HALF)),
            pltpu.SemaphoreType.DMA((4, HALF)),
            pltpu.SemaphoreType.DMA((2 * len(offsets), HALF)),
        ],
        compiler_params=pltpu.CompilerParams(vmem_limit_bytes=(13 << 20) + (len(offsets) << 19)),
        cost_estimate=pl.CostEstimate(flops=8 << 30, bytes_accessed=16 << 20, transcendentals=0),
    )(plan, *arrays)


def wide(x):
    return x.astype(jnp.float32)


def assemble_kernel(me_ref, *refs):
    ours, theirs, refs = refs[0], refs[1], refs[2:]
    kept, got, refs = refs[:HALF], refs[HALF:2 * HALF], refs[2 * HALF:]
    query_grad, key_grad, value_grad, sems = refs
    rows = ours.shape[0]
    core = me_ref[0] % 2
    pairs = []
    for which, query, sums in ((core, ours, kept), (1 - core, theirs, got)):
        column = pl.multiple_of(which * (HALF * WIDE), HALF * WIDE)
        pairs.append((query, query_grad.at[:, pl.ds(column, HALF * WIDE)]))
        for head in range(HALF):
            column = pl.multiple_of((which * HALF + head) * DH, DH)
            for first, out in ((0, key_grad), (DH, value_grad)):
                pairs.append((sums[head].at[:rows, first:first + DH], out.at[:, pl.ds(column, DH)]))
    for copy in run_copies(pairs, sems):
        copy.wait()


def assemble(me, ours, theirs, kept, got):
    rows = ours.shape[0]
    return pl.pallas_call(
        assemble_kernel,
        in_specs=[SMEM] + [HBM] * (2 + 2 * HALF),
        out_specs=[HBM] * 3,
        out_shape=[
            jax.ShapeDtypeStruct((rows, 2 * HALF * WIDE), jnp.bfloat16),
            jax.ShapeDtypeStruct((rows, 2 * HALF * DH), jnp.bfloat16),
            jax.ShapeDtypeStruct((rows, 2 * HALF * DH), jnp.bfloat16),
        ],
        scratch_shapes=[pltpu.SemaphoreType.DMA((2 + 4 * HALF,))],
        compiler_params=pltpu.CompilerParams(vmem_limit_bytes=2 << 20),
        cost_estimate=pl.CostEstimate(flops=0, bytes_accessed=4 << 20, transcendentals=0),
    )(me, ours, theirs, *kept, *got)


def local(queries, keys, values, saved_out, grad_out, parents, assignment, lengths):
    rows = keys.shape[0]
    chips = lax.axis_size("leaf") // 2
    order = ring_order(chips)
    ahead = [(order[i], order[(i + 1) % chips]) for i in range(chips)]
    right = [(2 * a + c, 2 * b + c) for a, b in ahead for c in range(2)]
    left = [(b, a) for a, b in right]
    swap = [(2 * a + c, 2 * a + 1 - c) for a in range(chips) for c in range(2)]
    places = jnp.asarray([order.index(chip) for chip in range(chips)], jnp.int32)
    index = lax.axis_index("leaf").astype(jnp.int32)
    core = index % 2
    me = index.reshape(1)
    tables = (me, places, parents, assignment, lengths)

    def part(array, which, width):
        return lax.dynamic_slice(array, (0, which * width), (rows, width))

    def heads_of(which):
        pieces = [part(array, which * HALF + head, DH) for head in range(HALF) for array in (keys, values)]
        return jnp.concatenate(pieces, axis=1)

    kept = heads_of(core)
    got = lax.ppermute(heads_of(1 - core), "leaf", swap)
    own = []
    for head in range(HALF):
        cols = slice(head * 2 * DH, (head + 1) * 2 * DH)
        own.append(jnp.concatenate([kept[:, cols], got[:, cols]], axis=0))
    mine = (queries, grad_out, saved_out)
    late = lax.optimization_barrier((*mine, got))[:3]
    other = jnp.concatenate([part(array, 1 - core, HALF * WIDE) for array in late], axis=1)
    other = lax.ppermute(other, "leaf", swap)

    def shift(arrays, ring):
        return [lax.ppermute(array, "leaf", ring) for array in arrays]

    far = chips // 2
    prepared, stats = [None] * HALF, [None] * HALF
    blocks, halves = [], []
    streams = [(block, block) for block in own]
    blocks = [{0: block} for block in own]
    for step in range(1, far):
        for head in range(HALF):
            up, down = streams[head]
            up, down = lax.ppermute(up, "leaf", right), lax.ppermute(down, "leaf", left)
            blocks[head][chips - step], blocks[head][step] = up, down
            if step == 1:
                prepared[head] = prepare(head, tables, mine, other, own[head])
                stats[head] = prepared[head][6:]
            else:
                met = (step - 1, chips - step + 1)
                stats[head] = measure(met, prepared[head], stats[head], [blocks[head][at] for at in met])
            stats[head], streams[head] = lax.optimization_barrier((stats[head], (up, down)))
    for head in range(HALF):
        up, down = streams[head]
        halves.append([lax.ppermute(up[:rows], "leaf", right), lax.ppermute(down[rows:], "leaf", left)])
        met = (far - 1, far + 1)
        stats[head] = measure(met, prepared[head], stats[head], [blocks[head][at] for at in met])

    offsets = [far]
    for step in range(1, far - 3):
        offsets += [far + step, far - step]
    arrays = [halves[head] + [blocks[head][at] for at in offsets[1:]] for head in range(HALF)]
    *terms, carried = gradients(prepared, stats, offsets, arrays, None, False)
    lse = [[a] for a in terms[3 * HALF:]]
    by_offset = {at: [terms[head][slot] for head in range(HALF)] for slot, at in enumerate(offsets)}
    ups, downs = terms[HALF:2 * HALF], terms[2 * HALF:3 * HALF]

    def add(sums, at):
        return [(wide(a) + wide(b)).astype(jnp.bfloat16) for a, b in zip(sums, by_offset[at])]

    later = {4: [chips - 3, 3], 3: [chips - 2, 2], 2: [chips - 1, 1], 1: [0]}
    ours = theirs = None
    for step in range(far, 0, -1):
        if step < far:
            ups, downs = add(ups, step), add(downs, chips - step)
        if step in later:
            last = 0 in later[step]
            (lse, carried), held = lax.optimization_barrier(((lse, carried), (ups[1:], downs[1:])))
            ups, downs = ups[:1] + held[0], downs[:1] + held[1]
            arrays = [[blocks[head][at] for at in later[step]] for head in range(HALF)]
            *terms, lead = gradients(prepared, lse, later[step], arrays, carried, last)
            for slot, at in enumerate(later[step]):
                by_offset[at] = [terms[head][slot] for head in range(HALF)]
            if last:
                ours, theirs = terms[HALF], lead
            else:
                carried = lead
        ups, downs = shift(ups, right), shift(downs, left)
        if step == far:
            ups = [jnp.pad(a, ((0, rows), (0, 0))) for a in ups]
            downs = [jnp.pad(a, ((rows, 0), (0, 0))) for a in downs]
    theirs, ups, downs = lax.optimization_barrier((theirs, ups, downs))
    theirs = lax.ppermute(theirs, "leaf", swap)
    kept, got = [], []
    for head in range(HALF):
        summed = (wide(by_offset[0][head]) + wide(ups[head]) + wide(downs[head])).astype(jnp.bfloat16)
        kept.append(summed)
        got.append(lax.ppermute(summed[rows:], "leaf", swap))

    return tuple(assemble(me, ours, theirs, kept, got))


def solution(mesh):
    tokens = P(("groups", "leaf"), None)
    tables = P("groups")
    return jax.shard_map(
        local,
        mesh=mesh,
        in_specs=(tokens,) * 5 + (tables,) * 3,
        out_specs=(tokens,) * 3,
        check_vma=False,
    )
```

```python
import functools
import math

import jax
import jax.numpy as jnp
from jax import lax
from jax.experimental import pallas as pl
from jax.experimental.pallas import tpu as pltpu
from jax.sharding import PartitionSpec as P

HQ = 20
HK = 4
DH = 128
PER = HQ // HK
HALF = HK // 2
WIDE = PER * DH
ANCESTORS = 5
SLOTS = ANCESTORS + 1
OWN = 1 << 20
CHUNKS = 4
ALWAYS = 4
TAIL = 8
SCALE = 1.0 / math.sqrt(DH)
EXP_SCALE = SCALE / math.log(2.0)
NN = (((1,), (0,)), ((), ()))
SMEM = pl.BlockSpec(memory_space=pltpu.SMEM)
HBM = pl.BlockSpec(memory_space=pl.ANY)
VMEM = pl.BlockSpec(memory_space=pltpu.VMEM)


def dot(a, b):
    return lax.dot_general(a, b, NN, preferred_element_type=jnp.float32)


def ring_order(chips):
    if chips == 8:
        return [0, 2, 4, 6, 7, 5, 3, 1]
    return list(range(chips))


def walk(device, me, places, parents, assignment, lengths, owner, plan, side, rows):
    chips = places.shape[0]
    here = places[me // 2]

    def place(held):
        at = places[held // 2] - here
        at = jnp.where(at < 0, at + chips, at)
        return side * 2 * chips + at * 2 + jnp.where(held % 2 == me % 2, 0, 1)

    def clear(at, carry):
        plan[side * 2 * chips + at] = 0
        return carry

    lax.fori_loop(0, 2 * chips, clear, 0)
    segment = assignment[device]
    plan[place(device)] = OWN
    chunk = rows // CHUNKS
    live = (lengths[segment] + chunk - 1) // chunk
    plan[4 * chips + side] = (live * PER + CHUNKS - 1) // CHUNKS
    up = parents[segment]
    for _ in range(ANCESTORS):
        at = jnp.maximum(up, 0)

        @pl.when(up >= 0)
        def _():
            plan[place(owner[at])] = lengths[at]

        up = jnp.where(up >= 0, parents[at], -1)


def run_copies(pairs, sems):
    copies = [pltpu.make_async_copy(a, b, sems.at[i]) for i, (a, b) in enumerate(pairs)]
    for copy in copies:
        copy.start()
    return copies


def column_of(me, head, h):
    return pl.multiple_of(((me % 2 * HALF + head) * PER + h) * DH, DH)


def chips_of(plan):
    return (plan.shape[0] - TAIL) // 4


def seen_keys(rows, sees, tile):
    chunk = rows // CHUNKS
    packed = lax.broadcasted_iota(jnp.int32, (1, rows), 1) + tile * rows
    row_at = packed & (chunk - 1)
    for at in range(1, CHUNKS):
        row_at = row_at + jnp.where(packed >= at * PER * chunk, chunk, 0)
    key_at = lax.broadcasted_iota(jnp.int32, (rows, 1), 0)
    return key_at <= jnp.where(sees == OWN, row_at, sees - 1)


def measure_blocks(plan, offsets, kv_ref, qt_ref, top_ref, sum_ref):
    rows = kv_ref.shape[1] // 2
    chips = chips_of(plan)
    for slot, offset in enumerate(offsets):
        def visit(i, carry):
            half, side = i // 2, i % 2
            sees = plan[side * 2 * chips + offset * 2 + half]

            def measure_tile(tile):
                keys = kv_ref[slot, pl.ds(pl.multiple_of(half * rows, rows), rows), :DH]
                at = (side, slice(None), slice(tile * rows, (tile + 1) * rows))
                s = jnp.where(seen_keys(rows, sees, tile), dot(keys, qt_ref[at]), -1e30)
                old = top_ref[at]
                top = jnp.maximum(old, jnp.max(s, axis=0, keepdims=True))
                total = jnp.sum(jnp.exp2((s - top) * EXP_SCALE), axis=0, keepdims=True)
                top_ref[at] = top
                sum_ref[at] = sum_ref[at] * jnp.exp2((old - top) * EXP_SCALE) + total

            @pl.when(sees > 0)
            def _():
                for tile in range(ALWAYS):
                    measure_tile(tile)

            for tile in range(ALWAYS, PER):
                @pl.when((sees > 0) & (plan[4 * chips + side] > tile))
                def _():
                    measure_tile(tile)

            return carry

        lax.fori_loop(0, 4, visit, 0)


def prepare_kernel(head, me_ref, places, parents, assignment, lengths, queries, grads, saved, other, block, *refs):
    (plan, qt_ref, gt_ref, gm_ref, qm_ref, delta_ref, top_ref, sum_ref,
     owner, q_ref, g_ref, o_ref, terms_ref, kv_ref, sems) = refs
    rows = queries.shape[0]
    chunk = rows // CHUNKS
    me = me_ref[0]
    column = pl.multiple_of((me % 2 * HALF + head) * WIDE, WIDE)
    pairs = [(block, kv_ref.at[0])]
    for at, (array, held) in enumerate(zip((queries, grads, saved), (q_ref, g_ref, o_ref))):
        pairs.append((array.at[:, pl.ds(column, WIDE)], held.at[0]))
        first = (at * HALF + head) * WIDE
        pairs.append((other.at[:, first:first + WIDE], held.at[1]))
    copies = run_copies(pairs, sems)

    def invert(d, carry):
        owner[assignment[d]] = d
        return carry

    lax.fori_loop(0, assignment.shape[0], invert, 0)
    walk(me, me, places, parents, assignment, lengths, owner, plan, 0, rows)
    walk(me + 1 - me % 2 * 2, me, places, parents, assignment, lengths, owner, plan, 1, rows)
    row_at = lax.broadcasted_iota(jnp.int32, (rows, 1), 0)
    top_ref[...] = jnp.full(top_ref.shape, -1e30, top_ref.dtype)
    sum_ref[...] = jnp.zeros_like(sum_ref)
    for copy in copies:
        copy.wait()
    for side, device in enumerate((me, me + 1 - me % 2 * 2)):
        live = row_at < lengths[assignment[device]]
        for h in range(PER):
            cols = slice(h * DH, (h + 1) * DH)
            masked = jnp.where(live, g_ref[side, :, cols], jnp.zeros((), g_ref.dtype))
            query = q_ref[side, :, cols]
            terms = masked.astype(jnp.float32) * o_ref[side, :, cols].astype(jnp.float32)
            for at in range(CHUNKS):
                here = slice(at * chunk, (at + 1) * chunk)
                there = slice((at * PER + h) * chunk, (at * PER + h + 1) * chunk)
                gm_ref[side, there, :] = masked[here]
                qm_ref[side, there, :] = query[here]
                terms_ref[there, :] = terms[here]
        for tile in range(PER):
            lanes = slice(tile * rows, (tile + 1) * rows)
            gt_ref[side, :, lanes] = gm_ref[side, lanes, :].T
            qt_ref[side, :, lanes] = qm_ref[side, lanes, :].T
            delta_ref[side, :, lanes] = jnp.sum(terms_ref[lanes, :].T, axis=0, keepdims=True)
    measure_blocks(plan, [0], kv_ref, qt_ref, top_ref, sum_ref)


def row_stats(rows):
    return jax.ShapeDtypeStruct((2, 1, PER * rows), jnp.float32)


def prepare(head, tables, mine, other, block):
    rows = other.shape[0]
    chips = tables[1].shape[0]
    bf16 = jnp.bfloat16
    return pl.pallas_call(
        functools.partial(prepare_kernel, head),
        in_specs=[SMEM] * 5 + [HBM] * 5,
        out_specs=[SMEM] + [VMEM] * 7,
        out_shape=[
            jax.ShapeDtypeStruct((4 * chips + TAIL,), jnp.int32),
            jax.ShapeDtypeStruct((2, DH, PER * rows), bf16),
            jax.ShapeDtypeStruct((2, DH, PER * rows), bf16),
            jax.ShapeDtypeStruct((2, PER * rows, DH), bf16),
            jax.ShapeDtypeStruct((2, PER * rows, DH), bf16),
            row_stats(rows),
            row_stats(rows),
            row_stats(rows),
        ],
        scratch_shapes=[pltpu.SMEM(tables[3].shape, jnp.int32)]
        + [pltpu.VMEM((2, rows, WIDE), bf16)] * 3
        + [pltpu.VMEM((PER * rows, DH), jnp.float32)]
        + [pltpu.VMEM((1, 2 * rows, 2 * DH), bf16), pltpu.SemaphoreType.DMA((7,))],
        compiler_params=pltpu.CompilerParams(vmem_limit_bytes=8 << 20),
        cost_estimate=pl.CostEstimate(flops=0, bytes_accessed=12 << 20, transcendentals=0),
    )(*tables, *mine, other, block)


def measure_kernel(offsets, plan, qt_ref, top_in, sum_in, *refs):
    count = len(offsets)
    blocks, (top_ref, sum_ref, kv_ref, sems) = refs[:count], refs[count:]
    copies = run_copies([(held, kv_ref.at[i]) for i, held in enumerate(blocks)], sems)
    top_ref[...] = top_in[...]
    sum_ref[...] = sum_in[...]
    for copy in copies:
        copy.wait()
    measure_blocks(plan, offsets, kv_ref, qt_ref, top_ref, sum_ref)


def measure(offsets, prepared, stats, blocks):
    rows = blocks[0].shape[0] // 2
    plan, qt = prepared[:2]
    return pl.pallas_call(
        functools.partial(measure_kernel, offsets),
        in_specs=[SMEM] + [VMEM] * 3 + [HBM] * len(blocks),
        out_specs=[VMEM] * 2,
        out_shape=[row_stats(rows)] * 2,
        scratch_shapes=[
            pltpu.VMEM((len(offsets), 2 * rows, 2 * DH), jnp.bfloat16),
            pltpu.SemaphoreType.DMA((len(blocks),)),
        ],
        compiler_params=pltpu.CompilerParams(vmem_limit_bytes=6 << 20),
        cost_estimate=pl.CostEstimate(flops=0, bytes_accessed=8 << 20, transcendentals=0),
    )(plan, qt, *stats, *blocks)


def grads_kernel(chips, offsets, first, last, plan, *refs):
    far = chips // 2
    shared = []
    for head in range(HALF):
        shared.append(refs[:6 + first])
        refs = refs[6 + first:]
    blocks = []
    for head in range(HALF):
        blocks.append(refs[:len(offsets) + first])
        refs = refs[len(offsets) + first:]
    carried = None
    if not first:
        carried, refs = refs[0], refs[1:]
    terms, refs = refs[:HALF], refs[HALF:]
    if first:
        ups, downs, refs = refs[:HALF], refs[HALF:2 * HALF], refs[2 * HALF:]
        lse_out, refs = refs[:HALF], refs[HALF:]
    outs, refs = refs[:2 if last else 1], refs[2 if last else 1:]
    (kv_ref, acc_ref, stage_ref, zero_ref, p_ref, ds_ref, sum_ref, dqt_ref, offset_ref,
     sems, kv_sems, out_sems, zero_sems) = refs
    lse_ref = lse_out if first else [head[5] for head in shared]
    if not last:
        dqt_ref = outs[0]
    rows = acc_ref.shape[1]
    slots = stage_ref.shape[0]

    pairs = []
    for head in range(HALF):
        for slot, offset in enumerate(offsets):
            offset_ref[slot] = offset
            if offset == far:
                pairs.append((blocks[head][0], kv_ref.at[slot, head, :rows]))
                pairs.append((blocks[head][1], kv_ref.at[slot, head, rows:]))
            else:
                pltpu.make_async_copy(
                    blocks[head][slot + first], kv_ref.at[slot, head], kv_sems.at[slot, head]
                ).start()
    copies = run_copies(pairs, sems)
    zero_ref[...] = jnp.zeros_like(zero_ref)

    def sees(side, i):
        return plan[side * 2 * chips + offset_ref[i // 2] * 2 + i % 2]

    def seen(i):
        return (sees(0, i) > 0) | (sees(1, i) > 0)

    def send(i, sources, sem_of):
        at_block, half = i // 2, i % 2
        here = pl.ds(pl.multiple_of(half * rows, rows), rows)
        for head in range(HALF):
            def put(target):
                pltpu.make_async_copy(sources[head], target, sem_of(head)).start()

            if not first:
                put(terms[head].at[at_block, here])
                continue

            @pl.when(i >= 2)
            def _():
                put(terms[head].at[at_block, here])

            @pl.when(i == 0)
            def _():
                put(ups[head])

            @pl.when(i == 1)
            def _():
                put(downs[head])

    def sent(sem_of):
        for head in range(HALF):
            pltpu.make_async_copy(zero_ref, terms[head].at[0, :rows], sem_of(head)).wait()

    def send_zeros(i, carry):
        @pl.when(jnp.logical_not(seen(i)))
        def _():
            send(i, [zero_ref] * HALF, lambda head: zero_sems.at[i, head])

        return carry

    lax.fori_loop(0, 2 * len(offsets), send_zeros, 0)
    dqt_ref[...] = jnp.zeros_like(dqt_ref) if first else carried[...]
    for copy in copies:
        copy.wait()
    if first:
        for head in range(HALF):
            top_ref, total_ref = lse_out[head], sum_ref.at[head]
            top_ref[...] = shared[head][5][...]
            total_ref[...] = shared[head][6][...]
            measure_blocks(plan, [far], kv_ref.at[:, head], shared[head][0], top_ref, total_ref)
            top_ref[...] = top_ref[...] * EXP_SCALE + jnp.log2(total_ref[...])

    def visit(i, done):
        at_block, half = i // 2, i % 2
        here = pl.ds(pl.multiple_of(half * rows, rows), rows)

        if len(offsets) > first:
            @pl.when((half == 0) & (offset_ref[at_block] != far))
            def _():
                for head in range(HALF):
                    pltpu.make_async_copy(
                        blocks[head][-1], kv_ref.at[at_block, head], kv_sems.at[at_block, head]
                    ).wait()

        def look(side, carry):
            def look_tiles(first_tile, last_tile):
                live = slice(first_tile * rows, last_tile * rows)
                for head in range(HALF):
                    qt_ref, gt_ref, gm_ref, qm_ref, delta_ref = shared[head][:5]
                    k = kv_ref[at_block, head, here, :DH]
                    v = kv_ref[at_block, head, here, DH:]
                    for tile in range(first_tile, last_tile):
                        lanes = slice(tile * rows, (tile + 1) * rows)
                        part = (side, slice(None), lanes)
                        s = dot(k, qt_ref[part]) * EXP_SCALE - lse_ref[head][part]
                        p = jnp.where(seen_keys(rows, sees(side, i), tile), jnp.exp2(s), 0.0)
                        ds = p * (dot(v, gt_ref[part]) - delta_ref[part])
                        p_ref[head, :, lanes] = p.astype(p_ref.dtype)
                        ds_ref[head, :, lanes] = ds.astype(ds_ref.dtype)
                    acc_ref[head, :, DH:] += dot(p_ref[head, :, live], gm_ref[side, live, :])
                    acc_ref[head, :, :DH] += dot(ds_ref[head, :, live], qm_ref[side, live, :])
                    dqt_ref[head, side, :, live] += dot(k.T, ds_ref[head, :, live])

            @pl.when(sees(side, i) > 0)
            def _():
                look_tiles(0, ALWAYS)

            @pl.when((sees(side, i) > 0) & (plan[4 * chips + side] > ALWAYS))
            def _():
                look_tiles(ALWAYS, PER)

            return carry

        @pl.when(seen(i))
        def _():
            slot = done % slots

            @pl.when(done >= slots)
            def _():
                sent(lambda head: out_sems.at[slot, head])

            acc_ref[...] = jnp.zeros_like(acc_ref)
            lax.fori_loop(0, 2, look, 0)
            for head in range(HALF):
                stage_ref[slot, head, :, :DH] = (acc_ref[head, :, :DH] * SCALE).astype(stage_ref.dtype)
                stage_ref[slot, head, :, DH:] = acc_ref[head, :, DH:].astype(stage_ref.dtype)
            send(i, [stage_ref.at[slot, head] for head in range(HALF)], lambda head: out_sems.at[slot, head])

        return done + seen(i).astype(jnp.int32)

    done = lax.fori_loop(0, 2 * len(offsets), visit, jnp.int32(0))
    if last:
        chunk = rows // CHUNKS
        for side, dq_ref in enumerate(outs):
            for head in range(HALF):
                for tile in range(PER):
                    dq = dqt_ref[head, side, :, tile * rows:(tile + 1) * rows] * SCALE
                    dq = dq.T.astype(dq_ref.dtype)
                    for piece in range(CHUNKS):
                        at, h = divmod(tile * CHUNKS + piece, PER)
                        cols = slice((head * PER + h) * DH, (head * PER + h + 1) * DH)
                        dq_ref[at * chunk:(at + 1) * chunk, cols] = dq[piece * chunk:(piece + 1) * chunk]

    def zeros_sent(i, carry):
        @pl.when(jnp.logical_not(seen(i)))
        def _():
            sent(lambda head: zero_sems.at[i, head])

        return carry

    lax.fori_loop(0, 2 * len(offsets), zeros_sent, 0)
    for slot in range(slots):
        @pl.when(done > slot)
        def _():
            sent(lambda head: out_sems.at[slot, head])


def gradients(prepared, stats, offsets, blocks, carried, last):
    plan = prepared[0][0]
    chips = chips_of(plan)
    rows = prepared[0][3].shape[1] // PER
    first = carried is None
    bf16, f32 = jnp.bfloat16, jnp.float32
    shared = [(*prepared[head][1:6], *stats[head]) for head in range(HALF)]
    arrays = [a for head in shared for a in head] + [a for head in blocks for a in head]
    arrays += [] if first else [carried]
    dense = jax.ShapeDtypeStruct((len(offsets), 2 * rows, 2 * DH), bf16)
    piece = jax.ShapeDtypeStruct((rows, 2 * DH), bf16)
    query = jax.ShapeDtypeStruct((rows, HALF * WIDE), bf16)
    sums = jax.ShapeDtypeStruct((HALF, 2, DH, PER * rows), f32)
    out_shape, out_specs = [dense] * HALF, [HBM] * HALF
    if first:
        out_shape += [piece] * (2 * HALF) + [row_stats(rows)] * HALF
        out_specs += [HBM] * (2 * HALF) + [VMEM] * HALF
    out_shape += [query] * 2 if last else [sums]
    out_specs += [VMEM] * (2 if last else 1)
    flat = sum(len(head) for head in shared)
    in_specs = [SMEM] + [VMEM] * flat + [HBM] * (len(arrays) - flat)
    if not first:
        in_specs[-1] = VMEM
    return pl.pallas_call(
        functools.partial(grads_kernel, chips, tuple(offsets), first, last),
        in_specs=in_specs,
        out_specs=out_specs,
        out_shape=out_shape,
        scratch_shapes=[
            pltpu.VMEM((len(offsets), HALF, 2 * rows, 2 * DH), bf16),
            pltpu.VMEM((HALF, rows, 2 * DH), f32),
            pltpu.VMEM((4, HALF, rows, 2 * DH), bf16),
            pltpu.VMEM((rows, 2 * DH), bf16),
            pltpu.VMEM((HALF, rows, PER * rows), bf16),
            pltpu.VMEM((HALF, rows, PER * rows), bf16),
            pltpu.VMEM((HALF, 2, 1, PER * rows), f32),
            pltpu.VMEM((HALF, 2, DH, PER * rows) if last else (8, DH), f32),
            pltpu.SMEM((len(offsets),), jnp.int32),
            pltpu.SemaphoreType.DMA((2 * HALF,)),
            pltpu.SemaphoreType.DMA((len(offsets), HALF)),
            pltpu.SemaphoreType.DMA((4, HALF)),
            pltpu.SemaphoreType.DMA((2 * len(offsets), HALF)),
        ],
        compiler_params=pltpu.CompilerParams(vmem_limit_bytes=(13 << 20) + (len(offsets) << 19)),
        cost_estimate=pl.CostEstimate(flops=8 << 30, bytes_accessed=16 << 20, transcendentals=0),
    )(plan, *arrays)


def wide(x):
    return x.astype(jnp.float32)


def assemble_kernel(me_ref, *refs):
    ours, theirs, refs = refs[0], refs[1], refs[2:]
    kept, got, refs = refs[:HALF], refs[HALF:2 * HALF], refs[2 * HALF:]
    query_grad, key_grad, value_grad, sems = refs
    rows = ours.shape[0]
    core = me_ref[0] % 2
    pairs = []
    for which, query, sums in ((core, ours, kept), (1 - core, theirs, got)):
        column = pl.multiple_of(which * (HALF * WIDE), HALF * WIDE)
        pairs.append((query, query_grad.at[:, pl.ds(column, HALF * WIDE)]))
        for head in range(HALF):
            column = pl.multiple_of((which * HALF + head) * DH, DH)
            for first, out in ((0, key_grad), (DH, value_grad)):
                pairs.append((sums[head].at[:rows, first:first + DH], out.at[:, pl.ds(column, DH)]))
    for copy in run_copies(pairs, sems):
        copy.wait()


def assemble(me, ours, theirs, kept, got):
    rows = ours.shape[0]
    return pl.pallas_call(
        assemble_kernel,
        in_specs=[SMEM] + [HBM] * (2 + 2 * HALF),
        out_specs=[HBM] * 3,
        out_shape=[
            jax.ShapeDtypeStruct((rows, 2 * HALF * WIDE), jnp.bfloat16),
            jax.ShapeDtypeStruct((rows, 2 * HALF * DH), jnp.bfloat16),
            jax.ShapeDtypeStruct((rows, 2 * HALF * DH), jnp.bfloat16),
        ],
        scratch_shapes=[pltpu.SemaphoreType.DMA((2 + 4 * HALF,))],
        compiler_params=pltpu.CompilerParams(vmem_limit_bytes=2 << 20),
        cost_estimate=pl.CostEstimate(flops=0, bytes_accessed=4 << 20, transcendentals=0),
    )(me, ours, theirs, *kept, *got)


def local(queries, keys, values, saved_out, grad_out, parents, assignment, lengths):
    rows = keys.shape[0]
    chips = lax.axis_size("leaf") // 2
    order = ring_order(chips)
    ahead = [(order[i], order[(i + 1) % chips]) for i in range(chips)]
    right = [(2 * a + c, 2 * b + c) for a, b in ahead for c in range(2)]
    left = [(b, a) for a, b in right]
    swap = [(2 * a + c, 2 * a + 1 - c) for a in range(chips) for c in range(2)]
    places = jnp.asarray([order.index(chip) for chip in range(chips)], jnp.int32)
    index = lax.axis_index("leaf").astype(jnp.int32)
    core = index % 2
    me = index.reshape(1)
    tables = (me, places, parents, assignment, lengths)

    def part(array, which, width):
        return lax.dynamic_slice(array, (0, which * width), (rows, width))

    def heads_of(which):
        pieces = [part(array, which * HALF + head, DH) for head in range(HALF) for array in (keys, values)]
        return jnp.concatenate(pieces, axis=1)

    kept = heads_of(core)
    got = lax.ppermute(heads_of(1 - core), "leaf", swap)
    own = []
    for head in range(HALF):
        cols = slice(head * 2 * DH, (head + 1) * 2 * DH)
        own.append(jnp.concatenate([kept[:, cols], got[:, cols]], axis=0))
    mine = (queries, grad_out, saved_out)
    late = lax.optimization_barrier((*mine, got))[:3]
    other = jnp.concatenate([part(array, 1 - core, HALF * WIDE) for array in late], axis=1)
    other = lax.ppermute(other, "leaf", swap)

    def shift(arrays, ring):
        return [lax.ppermute(array, "leaf", ring) for array in arrays]

    far = chips // 2
    prepared, stats = [None] * HALF, [None] * HALF
    blocks, halves = [], []
    streams = [(block, block) for block in own]
    blocks = [{0: block} for block in own]
    for step in range(1, far):
        for head in range(HALF):
            up, down = streams[head]
            up, down = lax.ppermute(up, "leaf", right), lax.ppermute(down, "leaf", left)
            blocks[head][chips - step], blocks[head][step] = up, down
            if step == 1:
                prepared[head] = prepare(head, tables, mine, other, own[head])
                stats[head] = prepared[head][6:]
            else:
                met = (step - 1, chips - step + 1)
                stats[head] = measure(met, prepared[head], stats[head], [blocks[head][at] for at in met])
            stats[head], streams[head] = lax.optimization_barrier((stats[head], (up, down)))
    for head in range(HALF):
        up, down = streams[head]
        halves.append([lax.ppermute(up[:rows], "leaf", right), lax.ppermute(down[rows:], "leaf", left)])
        met = (far - 1, far + 1)
        stats[head] = measure(met, prepared[head], stats[head], [blocks[head][at] for at in met])

    offsets = [far]
    for step in range(1, far - 3):
        offsets += [far + step, far - step]
    arrays = [halves[head] + [blocks[head][at] for at in offsets[1:]] for head in range(HALF)]
    *terms, carried = gradients(prepared, stats, offsets, arrays, None, False)
    lse = [[a] for a in terms[3 * HALF:]]
    by_offset = {at: [terms[head][slot] for head in range(HALF)] for slot, at in enumerate(offsets)}
    ups, downs = terms[HALF:2 * HALF], terms[2 * HALF:3 * HALF]

    def add(sums, at):
        return [(wide(a) + wide(b)).astype(jnp.bfloat16) for a, b in zip(sums, by_offset[at])]

    later = {4: [chips - 3, 3], 3: [chips - 2, 2], 2: [chips - 1, 1], 1: [0]}
    ours = theirs = None
    for step in range(far, 0, -1):
        if step < far:
            ups, downs = add(ups, step), add(downs, chips - step)
        if step in later:
            last = 0 in later[step]
            (lse, carried), held = lax.optimization_barrier(((lse, carried), (ups[1:], downs[1:])))
            ups, downs = ups[:1] + held[0], downs[:1] + held[1]
            arrays = [[blocks[head][at] for at in later[step]] for head in range(HALF)]
            *terms, lead = gradients(prepared, lse, later[step], arrays, carried, last)
            for slot, at in enumerate(later[step]):
                by_offset[at] = [terms[head][slot] for head in range(HALF)]
            if last:
                ours, theirs = terms[HALF], lead
            else:
                carried = lead
        ups, downs = shift(ups, right), shift(downs, left)
        if step == far:
            ups = [jnp.pad(a, ((0, rows), (0, 0))) for a in ups]
            downs = [jnp.pad(a, ((rows, 0), (0, 0))) for a in downs]
    theirs, ups, downs = lax.optimization_barrier((theirs, ups, downs))
    theirs = lax.ppermute(theirs, "leaf", swap)
    kept, got = [], []
    for head in range(HALF):
        summed = (wide(by_offset[0][head]) + wide(ups[head]) + wide(downs[head])).astype(jnp.bfloat16)
        kept.append(summed)
        got.append(lax.ppermute(summed[rows:], "leaf", swap))

    return tuple(assemble(me, ours, theirs, kept, got))


def solution(mesh):
    tokens = P(("groups", "leaf"), None)
    tables = P("groups")
    return jax.shard_map(
        local,
        mesh=mesh,
        in_specs=(tokens,) * 5 + (tables,) * 3,
        out_specs=(tokens,) * 3,
        check_vma=False,
    )
```

```python
import functools
import math

import jax
import jax.numpy as jnp
from jax import lax
from jax.experimental import pallas as pl
from jax.experimental.pallas import tpu as pltpu
from jax.sharding import PartitionSpec as P

HQ = 20
HK = 4
DH = 128
PER = HQ // HK
HALF = HK // 2
WIDE = PER * DH
ANCESTORS = 5
SLOTS = ANCESTORS + 1
OWN = 1 << 20
SCALE = 1.0 / math.sqrt(DH)
EXP_SCALE = SCALE / math.log(2.0)
NN = (((1,), (0,)), ((), ()))
SMEM = pl.BlockSpec(memory_space=pltpu.SMEM)
HBM = pl.BlockSpec(memory_space=pl.ANY)
VMEM = pl.BlockSpec(memory_space=pltpu.VMEM)


def dot(a, b):
    return lax.dot_general(a, b, NN, preferred_element_type=jnp.float32)


def ring_order(chips):
    if chips == 8:
        return [0, 2, 4, 6, 7, 5, 3, 1]
    return list(range(chips))


def walk(device, me, places, parents, assignment, lengths, owner, plan, side):
    chips = places.shape[0]
    here = places[me // 2]

    def place(held):
        at = places[held // 2] - here
        at = jnp.where(at < 0, at + chips, at)
        return side * 2 * chips + at * 2 + jnp.where(held % 2 == me % 2, 0, 1)

    def clear(at, carry):
        plan[side * 2 * chips + at] = 0
        return carry

    lax.fori_loop(0, 2 * chips, clear, 0)
    segment = assignment[device]
    plan[place(device)] = OWN
    up = parents[segment]
    for _ in range(ANCESTORS):
        at = jnp.maximum(up, 0)

        @pl.when(up >= 0)
        def _():
            plan[place(owner[at])] = lengths[at]

        up = jnp.where(up >= 0, parents[at], -1)


def run_copies(pairs, sems):
    copies = [pltpu.make_async_copy(a, b, sems.at[i]) for i, (a, b) in enumerate(pairs)]
    for copy in copies:
        copy.start()
    return copies


def column_of(me, head, h):
    return pl.multiple_of(((me % 2 * HALF + head) * PER + h) * DH, DH)


def seen_keys(rows, sees):
    lane_at = lax.broadcasted_iota(jnp.int32, (1, rows), 1)
    key_at = lax.broadcasted_iota(jnp.int32, (rows, 1), 0)
    return key_at <= jnp.where(sees == OWN, lane_at, sees - 1)


def measure_blocks(plan, offsets, kv_ref, qt_ref, top_ref, sum_ref):
    rows = kv_ref.shape[1] // 2
    chips = plan.shape[0] // 4
    for slot, offset in enumerate(offsets):
        def visit(i, carry):
            half, side = i // 2, i % 2
            sees = plan[side * 2 * chips + offset * 2 + half]

            @pl.when(sees > 0)
            def _():
                seen = seen_keys(rows, sees)
                keys = kv_ref[slot, pl.ds(pl.multiple_of(half * rows, rows), rows), :DH]
                for h in range(PER):
                    at = (side, slice(None), slice(h * rows, (h + 1) * rows))
                    s = jnp.where(seen, dot(keys, qt_ref[at]), -1e30)
                    old = top_ref[at]
                    top = jnp.maximum(old, jnp.max(s, axis=0, keepdims=True))
                    total = jnp.sum(jnp.exp2((s - top) * EXP_SCALE), axis=0, keepdims=True)
                    top_ref[at] = top
                    sum_ref[at] = sum_ref[at] * jnp.exp2((old - top) * EXP_SCALE) + total

            return carry

        lax.fori_loop(0, 4, visit, 0)


def prepare_kernel(head, me_ref, places, parents, assignment, lengths, queries, grads, saved, other, block, *refs):
    (plan, qt_ref, gt_ref, gm_ref, qm_ref, delta_ref, top_ref, sum_ref,
     owner, q_ref, g_ref, o_ref, kv_ref, sems) = refs
    rows = queries.shape[0]
    me = me_ref[0]
    column = pl.multiple_of((me % 2 * HALF + head) * WIDE, WIDE)
    pairs = [(block, kv_ref.at[0])]
    for at, (array, held) in enumerate(zip((queries, grads, saved), (q_ref, g_ref, o_ref))):
        pairs.append((array.at[:, pl.ds(column, WIDE)], held.at[0]))
        first = (at * HALF + head) * WIDE
        pairs.append((other.at[:, first:first + WIDE], held.at[1]))
    copies = run_copies(pairs, sems)

    def invert(d, carry):
        owner[assignment[d]] = d
        return carry

    lax.fori_loop(0, assignment.shape[0], invert, 0)
    walk(me, me, places, parents, assignment, lengths, owner, plan, 0)
    walk(me + 1 - me % 2 * 2, me, places, parents, assignment, lengths, owner, plan, 1)
    row_at = lax.broadcasted_iota(jnp.int32, (rows, 1), 0)
    top_ref[...] = jnp.full(top_ref.shape, -1e30, top_ref.dtype)
    sum_ref[...] = jnp.zeros_like(sum_ref)
    for copy in copies:
        copy.wait()
    for side, device in enumerate((me, me + 1 - me % 2 * 2)):
        live = row_at < lengths[assignment[device]]
        for h in range(PER):
            lanes = slice(h * rows, (h + 1) * rows)
            cols = slice(h * DH, (h + 1) * DH)
            masked = jnp.where(live, g_ref[side, :, cols], jnp.zeros((), g_ref.dtype))
            query = q_ref[side, :, cols]
            gm_ref[side, lanes, :] = masked
            qm_ref[side, lanes, :] = query
            gt_ref[side, :, lanes] = masked.T
            qt_ref[side, :, lanes] = query.T
            terms = masked.astype(jnp.float32) * o_ref[side, :, cols].astype(jnp.float32)
            delta_ref[side, :, lanes] = jnp.sum(terms.T, axis=0, keepdims=True)
    measure_blocks(plan, [0], kv_ref, qt_ref, top_ref, sum_ref)


def row_stats(rows):
    return jax.ShapeDtypeStruct((2, 1, PER * rows), jnp.float32)


def prepare(head, tables, mine, other, block):
    rows = other.shape[0]
    chips = tables[1].shape[0]
    bf16 = jnp.bfloat16
    return pl.pallas_call(
        functools.partial(prepare_kernel, head),
        in_specs=[SMEM] * 5 + [HBM] * 5,
        out_specs=[SMEM] + [VMEM] * 7,
        out_shape=[
            jax.ShapeDtypeStruct((4 * chips,), jnp.int32),
            jax.ShapeDtypeStruct((2, DH, PER * rows), bf16),
            jax.ShapeDtypeStruct((2, DH, PER * rows), bf16),
            jax.ShapeDtypeStruct((2, PER * rows, DH), bf16),
            jax.ShapeDtypeStruct((2, PER * rows, DH), bf16),
            row_stats(rows),
            row_stats(rows),
            row_stats(rows),
        ],
        scratch_shapes=[pltpu.SMEM(tables[3].shape, jnp.int32)]
        + [pltpu.VMEM((2, rows, WIDE), bf16)] * 3
        + [pltpu.VMEM((1, 2 * rows, 2 * DH), bf16), pltpu.SemaphoreType.DMA((7,))],
        compiler_params=pltpu.CompilerParams(vmem_limit_bytes=8 << 20),
        cost_estimate=pl.CostEstimate(flops=0, bytes_accessed=12 << 20, transcendentals=0),
    )(*tables, *mine, other, block)


def measure_kernel(offsets, plan, qt_ref, top_in, sum_in, *refs):
    count = len(offsets)
    blocks, (top_ref, sum_ref, kv_ref, sems) = refs[:count], refs[count:]
    copies = run_copies([(held, kv_ref.at[i]) for i, held in enumerate(blocks)], sems)
    top_ref[...] = top_in[...]
    sum_ref[...] = sum_in[...]
    for copy in copies:
        copy.wait()
    measure_blocks(plan, offsets, kv_ref, qt_ref, top_ref, sum_ref)


def measure(offsets, prepared, stats, blocks):
    rows = blocks[0].shape[0] // 2
    plan, qt = prepared[:2]
    return pl.pallas_call(
        functools.partial(measure_kernel, offsets),
        in_specs=[SMEM] + [VMEM] * 3 + [HBM] * len(blocks),
        out_specs=[VMEM] * 2,
        out_shape=[row_stats(rows)] * 2,
        scratch_shapes=[
            pltpu.VMEM((len(offsets), 2 * rows, 2 * DH), jnp.bfloat16),
            pltpu.SemaphoreType.DMA((len(blocks),)),
        ],
        compiler_params=pltpu.CompilerParams(vmem_limit_bytes=6 << 20),
        cost_estimate=pl.CostEstimate(flops=0, bytes_accessed=8 << 20, transcendentals=0),
    )(plan, qt, *stats, *blocks)


def grads_kernel(chips, offsets, first, last, plan, *refs):
    far = chips // 2
    shared = []
    for head in range(HALF):
        shared.append(refs[:6 + first])
        refs = refs[6 + first:]
    blocks = []
    for head in range(HALF):
        blocks.append(refs[:len(offsets) + first])
        refs = refs[len(offsets) + first:]
    carried = None
    if not first:
        carried, refs = refs[0], refs[1:]
    terms, refs = refs[:HALF], refs[HALF:]
    if first:
        up_ref, down_ref, refs = refs[0], refs[1], refs[2:]
        lse_out, refs = refs[:HALF], refs[HALF:]
    outs, refs = refs[:2 if last else 1], refs[2 if last else 1:]
    (kv_ref, acc_ref, stage_ref, zero_ref, p_ref, ds_ref, sum_ref, dqt_ref, offset_ref,
     sems, kv_sems, out_sems, zero_sems) = refs
    lse_ref = lse_out if first else [head[5] for head in shared]
    if not last:
        dqt_ref = outs[0]
    rows = acc_ref.shape[1]
    slots = stage_ref.shape[0]

    pairs = []
    for head in range(HALF):
        for slot, offset in enumerate(offsets):
            offset_ref[slot] = offset
            if offset == far:
                pairs.append((blocks[head][0], kv_ref.at[slot, head, :rows]))
                pairs.append((blocks[head][1], kv_ref.at[slot, head, rows:]))
            else:
                pltpu.make_async_copy(
                    blocks[head][slot + first], kv_ref.at[slot, head], kv_sems.at[slot, head]
                ).start()
    copies = run_copies(pairs, sems)
    zero_ref[...] = jnp.zeros_like(zero_ref)

    def sees(side, i):
        return plan[side * 2 * chips + offset_ref[i // 2] * 2 + i % 2]

    def seen(i):
        return (sees(0, i) > 0) | (sees(1, i) > 0)

    def send(i, sources, sem_of):
        at_block, half = i // 2, i % 2
        here = pl.ds(pl.multiple_of(half * rows, rows), rows)
        for head in range(HALF):
            def put(target):
                pltpu.make_async_copy(sources[head], target, sem_of(head)).start()

            if not first:
                put(terms[head].at[at_block, here])
                continue

            @pl.when(i >= 2)
            def _():
                put(terms[head].at[at_block, here])

            @pl.when(i == 0)
            def _():
                put(up_ref.at[head])

            @pl.when(i == 1)
            def _():
                put(down_ref.at[head])

    def sent(sem_of):
        for head in range(HALF):
            pltpu.make_async_copy(zero_ref, terms[head].at[0, :rows], sem_of(head)).wait()

    def send_zeros(i, carry):
        @pl.when(jnp.logical_not(seen(i)))
        def _():
            send(i, [zero_ref] * HALF, lambda head: zero_sems.at[i, head])

        return carry

    lax.fori_loop(0, 2 * len(offsets), send_zeros, 0)
    dqt_ref[...] = jnp.zeros_like(dqt_ref) if first else carried[...]
    for copy in copies:
        copy.wait()
    if first:
        for head in range(HALF):
            top_ref, total_ref = lse_out[head], sum_ref.at[head]
            top_ref[...] = shared[head][5][...]
            total_ref[...] = shared[head][6][...]
            measure_blocks(plan, [far], kv_ref.at[:, head], shared[head][0], top_ref, total_ref)
            top_ref[...] = top_ref[...] * EXP_SCALE + jnp.log2(total_ref[...])

    def visit(i, done):
        at_block, half = i // 2, i % 2
        here = pl.ds(pl.multiple_of(half * rows, rows), rows)

        if len(offsets) > first:
            @pl.when((half == 0) & (offset_ref[at_block] != far))
            def _():
                for head in range(HALF):
                    pltpu.make_async_copy(
                        blocks[head][-1], kv_ref.at[at_block, head], kv_sems.at[at_block, head]
                    ).wait()

        def look(side, carry):
            @pl.when(sees(side, i) > 0)
            def _():
                allowed = seen_keys(rows, sees(side, i))
                for head in range(HALF):
                    qt_ref, gt_ref, gm_ref, qm_ref, delta_ref = shared[head][:5]
                    k = kv_ref[at_block, head, here, :DH]
                    v = kv_ref[at_block, head, here, DH:]
                    for h in range(PER):
                        lanes = slice(h * rows, (h + 1) * rows)
                        part = (side, slice(None), lanes)
                        s = dot(k, qt_ref[part]) * EXP_SCALE - lse_ref[head][part]
                        p = jnp.where(allowed, jnp.exp2(s), 0.0)
                        ds = p * (dot(v, gt_ref[part]) - delta_ref[part])
                        p_ref[head, :, lanes] = p.astype(p_ref.dtype)
                        ds_ref[head, :, lanes] = ds.astype(ds_ref.dtype)
                    acc_ref[head, :, DH:] += dot(p_ref[head], gm_ref[side])
                    acc_ref[head, :, :DH] += dot(ds_ref[head], qm_ref[side])
                    dqt_ref[head, side] += dot(k.T, ds_ref[head])

            return carry

        @pl.when(seen(i))
        def _():
            slot = done % slots

            @pl.when(done >= slots)
            def _():
                sent(lambda head: out_sems.at[slot, head])

            acc_ref[...] = jnp.zeros_like(acc_ref)
            lax.fori_loop(0, 2, look, 0)
            for head in range(HALF):
                stage_ref[slot, head, :, :DH] = (acc_ref[head, :, :DH] * SCALE).astype(stage_ref.dtype)
                stage_ref[slot, head, :, DH:] = acc_ref[head, :, DH:].astype(stage_ref.dtype)
            send(i, [stage_ref.at[slot, head] for head in range(HALF)], lambda head: out_sems.at[slot, head])

        return done + seen(i).astype(jnp.int32)

    done = lax.fori_loop(0, 2 * len(offsets), visit, jnp.int32(0))
    if last:
        for side, dq_ref in enumerate(outs):
            for head in range(HALF):
                for h in range(PER):
                    dq = (dqt_ref[head, side, :, h * rows:(h + 1) * rows] * SCALE).astype(dq_ref.dtype)
                    dq_ref[:, (head * PER + h) * DH:(head * PER + h + 1) * DH] = dq.T

    def zeros_sent(i, carry):
        @pl.when(jnp.logical_not(seen(i)))
        def _():
            sent(lambda head: zero_sems.at[i, head])

        return carry

    lax.fori_loop(0, 2 * len(offsets), zeros_sent, 0)
    for slot in range(slots):
        @pl.when(done > slot)
        def _():
            sent(lambda head: out_sems.at[slot, head])


def gradients(prepared, stats, offsets, blocks, carried, last):
    plan = prepared[0][0]
    chips = plan.shape[0] // 4
    rows = prepared[0][3].shape[1] // PER
    first = carried is None
    bf16, f32 = jnp.bfloat16, jnp.float32
    shared = [(*prepared[head][1:6], *stats[head]) for head in range(HALF)]
    arrays = [a for head in shared for a in head] + [a for head in blocks for a in head]
    arrays += [] if first else [carried]
    dense = jax.ShapeDtypeStruct((len(offsets), 2 * rows, 2 * DH), bf16)
    piece = jax.ShapeDtypeStruct((HALF, rows, 2 * DH), bf16)
    query = jax.ShapeDtypeStruct((rows, HALF * WIDE), bf16)
    sums = jax.ShapeDtypeStruct((HALF, 2, DH, PER * rows), f32)
    out_shape, out_specs = [dense] * HALF, [HBM] * HALF
    if first:
        out_shape += [piece] * 2 + [row_stats(rows)] * HALF
        out_specs += [HBM] * 2 + [VMEM] * HALF
    out_shape += [query] * 2 if last else [sums]
    out_specs += [VMEM] * (2 if last else 1)
    flat = sum(len(head) for head in shared)
    in_specs = [SMEM] + [VMEM] * flat + [HBM] * (len(arrays) - flat)
    if not first:
        in_specs[-1] = VMEM
    return pl.pallas_call(
        functools.partial(grads_kernel, chips, tuple(offsets), first, last),
        in_specs=in_specs,
        out_specs=out_specs,
        out_shape=out_shape,
        scratch_shapes=[
            pltpu.VMEM((len(offsets), HALF, 2 * rows, 2 * DH), bf16),
            pltpu.VMEM((HALF, rows, 2 * DH), f32),
            pltpu.VMEM((4, HALF, rows, 2 * DH), bf16),
            pltpu.VMEM((rows, 2 * DH), bf16),
            pltpu.VMEM((HALF, rows, PER * rows), bf16),
            pltpu.VMEM((HALF, rows, PER * rows), bf16),
            pltpu.VMEM((HALF, 2, 1, PER * rows), f32),
            pltpu.VMEM((HALF, 2, DH, PER * rows) if last else (8, DH), f32),
            pltpu.SMEM((len(offsets),), jnp.int32),
            pltpu.SemaphoreType.DMA((2 * HALF,)),
            pltpu.SemaphoreType.DMA((len(offsets), HALF)),
            pltpu.SemaphoreType.DMA((4, HALF)),
            pltpu.SemaphoreType.DMA((2 * len(offsets), HALF)),
        ],
        compiler_params=pltpu.CompilerParams(vmem_limit_bytes=(13 << 20) + (len(offsets) << 19)),
        cost_estimate=pl.CostEstimate(flops=8 << 30, bytes_accessed=16 << 20, transcendentals=0),
    )(plan, *arrays)


def wide(x):
    return x.astype(jnp.float32)


def assemble_kernel(me_ref, *refs):
    ours, theirs, refs = refs[0], refs[1], refs[2:]
    kept, got, refs = refs[:HALF], refs[HALF:2 * HALF], refs[2 * HALF:]
    query_grad, key_grad, value_grad, sems = refs
    rows = ours.shape[0]
    core = me_ref[0] % 2
    pairs = []
    for which, query, sums in ((core, ours, kept), (1 - core, theirs, got)):
        column = pl.multiple_of(which * (HALF * WIDE), HALF * WIDE)
        pairs.append((query, query_grad.at[:, pl.ds(column, HALF * WIDE)]))
        for head in range(HALF):
            column = pl.multiple_of((which * HALF + head) * DH, DH)
            for first, out in ((0, key_grad), (DH, value_grad)):
                pairs.append((sums[head].at[:rows, first:first + DH], out.at[:, pl.ds(column, DH)]))
    for copy in run_copies(pairs, sems):
        copy.wait()


def assemble(me, ours, theirs, kept, got):
    rows = ours.shape[0]
    return pl.pallas_call(
        assemble_kernel,
        in_specs=[SMEM] + [HBM] * (2 + 2 * HALF),
        out_specs=[HBM] * 3,
        out_shape=[
            jax.ShapeDtypeStruct((rows, 2 * HALF * WIDE), jnp.bfloat16),
            jax.ShapeDtypeStruct((rows, 2 * HALF * DH), jnp.bfloat16),
            jax.ShapeDtypeStruct((rows, 2 * HALF * DH), jnp.bfloat16),
        ],
        scratch_shapes=[pltpu.SemaphoreType.DMA((2 + 4 * HALF,))],
        compiler_params=pltpu.CompilerParams(vmem_limit_bytes=2 << 20),
        cost_estimate=pl.CostEstimate(flops=0, bytes_accessed=4 << 20, transcendentals=0),
    )(me, ours, theirs, *kept, *got)


def local(queries, keys, values, saved_out, grad_out, parents, assignment, lengths):
    rows = keys.shape[0]
    chips = lax.axis_size("leaf") // 2
    order = ring_order(chips)
    ahead = [(order[i], order[(i + 1) % chips]) for i in range(chips)]
    right = [(2 * a + c, 2 * b + c) for a, b in ahead for c in range(2)]
    left = [(b, a) for a, b in right]
    swap = [(2 * a + c, 2 * a + 1 - c) for a in range(chips) for c in range(2)]
    places = jnp.asarray([order.index(chip) for chip in range(chips)], jnp.int32)
    index = lax.axis_index("leaf").astype(jnp.int32)
    core = index % 2
    me = index.reshape(1)
    tables = (me, places, parents, assignment, lengths)

    def part(array, which, width):
        return lax.dynamic_slice(array, (0, which * width), (rows, width))

    def heads_of(which):
        pieces = [part(array, which * HALF + head, DH) for head in range(HALF) for array in (keys, values)]
        return jnp.concatenate(pieces, axis=1)

    kept = heads_of(core)
    got = lax.ppermute(heads_of(1 - core), "leaf", swap)
    own = []
    for head in range(HALF):
        cols = slice(head * 2 * DH, (head + 1) * 2 * DH)
        own.append(jnp.concatenate([kept[:, cols], got[:, cols]], axis=0))
    mine = (queries, grad_out, saved_out)
    late = lax.optimization_barrier((*mine, got))[:3]
    other = jnp.concatenate([part(array, 1 - core, HALF * WIDE) for array in late], axis=1)
    other = lax.ppermute(other, "leaf", swap)

    def shift(arrays, ring):
        return [lax.ppermute(array, "leaf", ring) for array in arrays]

    far = chips // 2
    prepared, stats = [None] * HALF, [None] * HALF
    blocks, halves = [], []
    streams = [(block, block) for block in own]
    blocks = [{0: block} for block in own]
    for step in range(1, far):
        for head in range(HALF):
            up, down = streams[head]
            up, down = lax.ppermute(up, "leaf", right), lax.ppermute(down, "leaf", left)
            blocks[head][chips - step], blocks[head][step] = up, down
            if step == 1:
                prepared[head] = prepare(head, tables, mine, other, own[head])
                stats[head] = prepared[head][6:]
            else:
                met = (step - 1, chips - step + 1)
                stats[head] = measure(met, prepared[head], stats[head], [blocks[head][at] for at in met])
            stats[head], streams[head] = lax.optimization_barrier((stats[head], (up, down)))
    for head in range(HALF):
        up, down = streams[head]
        halves.append([lax.ppermute(up[:rows], "leaf", right), lax.ppermute(down[rows:], "leaf", left)])
        met = (far - 1, far + 1)
        stats[head] = measure(met, prepared[head], stats[head], [blocks[head][at] for at in met])

    offsets = [far]
    for step in range(1, far - 3):
        offsets += [far + step, far - step]
    arrays = [halves[head] + [blocks[head][at] for at in offsets[1:]] for head in range(HALF)]
    *terms, carried = gradients(prepared, stats, offsets, arrays, None, False)
    lse = [[a] for a in terms[HALF + 2:]]
    by_offset = {at: [terms[head][slot] for head in range(HALF)] for slot, at in enumerate(offsets)}
    ups, downs = terms[HALF:HALF + 1], terms[HALF + 1:HALF + 2]

    def add(sums, at):
        return [(wide(a) + wide(b)).astype(jnp.bfloat16) for a, b in zip(sums, by_offset[at])]

    later = {4: [chips - 3, 3], 3: [chips - 2, 2], 2: [chips - 1, 1], 1: [0]}
    ours = theirs = None
    for step in range(far, 0, -1):
        if step < far:
            ups, downs = add(ups, step), add(downs, chips - step)
        if step in later:
            last = 0 in later[step]
            (lse, carried), held = lax.optimization_barrier(((lse, carried), (ups[-1:], downs[-1:])))
            ups, downs = ups[:-1] + held[0], downs[:-1] + held[1]
            arrays = [[blocks[head][at] for at in later[step]] for head in range(HALF)]
            *terms, lead = gradients(prepared, lse, later[step], arrays, carried, last)
            for slot, at in enumerate(later[step]):
                by_offset[at] = [terms[head][slot] for head in range(HALF)]
            if last:
                ours, theirs = terms[HALF], lead
            else:
                carried = lead
        ups, downs = shift(ups, right), shift(downs, left)
        if step == far:
            ups = [jnp.pad(a, ((0, rows), (0, 0))) for a in ups[0]]
            downs = [jnp.pad(a, ((rows, 0), (0, 0))) for a in downs[0]]
    theirs, ups, downs = lax.optimization_barrier((theirs, ups, downs))
    theirs = lax.ppermute(theirs, "leaf", swap)
    kept, got = [], []
    for head in range(HALF):
        summed = (wide(by_offset[0][head]) + wide(ups[head]) + wide(downs[head])).astype(jnp.bfloat16)
        kept.append(summed)
        got.append(lax.ppermute(summed[rows:], "leaf", swap))

    return tuple(assemble(me, ours, theirs, kept, got))


def solution(mesh):
    tokens = P(("groups", "leaf"), None)
    tables = P("groups")
    return jax.shard_map(
        local,
        mesh=mesh,
        in_specs=(tokens,) * 5 + (tables,) * 3,
        out_specs=(tokens,) * 3,
        check_vma=False,
    )
```

```python
import functools
import math

import jax
import jax.numpy as jnp
from jax import lax
from jax.experimental import pallas as pl
from jax.experimental.pallas import tpu as pltpu
from jax.sharding import PartitionSpec as P

HQ = 20
HK = 4
DH = 128
PER = HQ // HK
HALF = HK // 2
WIDE = PER * DH
ANCESTORS = 5
SLOTS = ANCESTORS + 1
OWN = 1 << 20
SCALE = 1.0 / math.sqrt(DH)
EXP_SCALE = SCALE / math.log(2.0)
NN = (((1,), (0,)), ((), ()))
SMEM = pl.BlockSpec(memory_space=pltpu.SMEM)
HBM = pl.BlockSpec(memory_space=pl.ANY)
VMEM = pl.BlockSpec(memory_space=pltpu.VMEM)


def dot(a, b):
    return lax.dot_general(a, b, NN, preferred_element_type=jnp.float32)


def ring_order(chips):
    if chips == 8:
        return [0, 2, 4, 6, 7, 5, 3, 1]
    return list(range(chips))


def walk(device, me, places, parents, assignment, lengths, owner, plan, side):
    chips = places.shape[0]
    here = places[me // 2]

    def place(held):
        at = places[held // 2] - here
        at = jnp.where(at < 0, at + chips, at)
        return side * 2 * chips + at * 2 + jnp.where(held % 2 == me % 2, 0, 1)

    def clear(at, carry):
        plan[side * 2 * chips + at] = 0
        return carry

    lax.fori_loop(0, 2 * chips, clear, 0)
    segment = assignment[device]
    plan[place(device)] = OWN
    up = parents[segment]
    for _ in range(ANCESTORS):
        at = jnp.maximum(up, 0)

        @pl.when(up >= 0)
        def _():
            plan[place(owner[at])] = lengths[at]

        up = jnp.where(up >= 0, parents[at], -1)


def run_copies(pairs, sems):
    copies = [pltpu.make_async_copy(a, b, sems.at[i]) for i, (a, b) in enumerate(pairs)]
    for copy in copies:
        copy.start()
    return copies


def column_of(me, head, h):
    return pl.multiple_of(((me % 2 * HALF + head) * PER + h) * DH, DH)


def seen_keys(rows, sees):
    lane_at = lax.broadcasted_iota(jnp.int32, (1, rows), 1)
    key_at = lax.broadcasted_iota(jnp.int32, (rows, 1), 0)
    return key_at <= jnp.where(sees == OWN, lane_at, sees - 1)


def measure_blocks(plan, offsets, kv_ref, qt_ref, top_ref, sum_ref):
    rows = kv_ref.shape[1] // 2
    chips = plan.shape[0] // 4
    for slot, offset in enumerate(offsets):
        def visit(i, carry):
            half, side = i // 2, i % 2
            sees = plan[side * 2 * chips + offset * 2 + half]

            @pl.when(sees > 0)
            def _():
                seen = seen_keys(rows, sees)
                keys = kv_ref[slot, pl.ds(pl.multiple_of(half * rows, rows), rows), :DH]
                for h in range(PER):
                    at = (side, slice(None), slice(h * rows, (h + 1) * rows))
                    s = jnp.where(seen, dot(keys, qt_ref[at]), -1e30)
                    old = top_ref[at]
                    top = jnp.maximum(old, jnp.max(s, axis=0, keepdims=True))
                    total = jnp.sum(jnp.exp2((s - top) * EXP_SCALE), axis=0, keepdims=True)
                    top_ref[at] = top
                    sum_ref[at] = sum_ref[at] * jnp.exp2((old - top) * EXP_SCALE) + total

            return carry

        lax.fori_loop(0, 4, visit, 0)


def prepare_kernel(head, me_ref, places, parents, assignment, lengths, queries, grads, saved, other, block, *refs):
    (plan, qt_ref, gt_ref, gm_ref, qm_ref, delta_ref, top_ref, sum_ref,
     owner, q_ref, g_ref, o_ref, kv_ref, sems) = refs
    rows = queries.shape[0]
    me = me_ref[0]
    column = pl.multiple_of((me % 2 * HALF + head) * WIDE, WIDE)
    pairs = [(block, kv_ref.at[0])]
    for at, (array, held) in enumerate(zip((queries, grads, saved), (q_ref, g_ref, o_ref))):
        pairs.append((array.at[:, pl.ds(column, WIDE)], held.at[0]))
        first = (at * HALF + head) * WIDE
        pairs.append((other.at[:, first:first + WIDE], held.at[1]))
    copies = run_copies(pairs, sems)

    def invert(d, carry):
        owner[assignment[d]] = d
        return carry

    lax.fori_loop(0, assignment.shape[0], invert, 0)
    walk(me, me, places, parents, assignment, lengths, owner, plan, 0)
    walk(me + 1 - me % 2 * 2, me, places, parents, assignment, lengths, owner, plan, 1)
    row_at = lax.broadcasted_iota(jnp.int32, (rows, 1), 0)
    top_ref[...] = jnp.full(top_ref.shape, -1e30, top_ref.dtype)
    sum_ref[...] = jnp.zeros_like(sum_ref)
    for copy in copies:
        copy.wait()
    for side, device in enumerate((me, me + 1 - me % 2 * 2)):
        live = row_at < lengths[assignment[device]]
        for h in range(PER):
            lanes = slice(h * rows, (h + 1) * rows)
            cols = slice(h * DH, (h + 1) * DH)
            masked = jnp.where(live, g_ref[side, :, cols], jnp.zeros((), g_ref.dtype))
            query = q_ref[side, :, cols]
            gm_ref[side, lanes, :] = masked
            qm_ref[side, lanes, :] = query
            gt_ref[side, :, lanes] = masked.T
            qt_ref[side, :, lanes] = query.T
            terms = masked.astype(jnp.float32) * o_ref[side, :, cols].astype(jnp.float32)
            delta_ref[side, :, lanes] = jnp.sum(terms.T, axis=0, keepdims=True)
    measure_blocks(plan, [0], kv_ref, qt_ref, top_ref, sum_ref)


def row_stats(rows):
    return jax.ShapeDtypeStruct((2, 1, PER * rows), jnp.float32)


def prepare(head, tables, mine, other, block):
    rows = other.shape[0]
    chips = tables[1].shape[0]
    bf16 = jnp.bfloat16
    return pl.pallas_call(
        functools.partial(prepare_kernel, head),
        in_specs=[SMEM] * 5 + [HBM] * 5,
        out_specs=[SMEM] + [VMEM] * 7,
        out_shape=[
            jax.ShapeDtypeStruct((4 * chips,), jnp.int32),
            jax.ShapeDtypeStruct((2, DH, PER * rows), bf16),
            jax.ShapeDtypeStruct((2, DH, PER * rows), bf16),
            jax.ShapeDtypeStruct((2, PER * rows, DH), bf16),
            jax.ShapeDtypeStruct((2, PER * rows, DH), bf16),
            row_stats(rows),
            row_stats(rows),
            row_stats(rows),
        ],
        scratch_shapes=[pltpu.SMEM(tables[3].shape, jnp.int32)]
        + [pltpu.VMEM((2, rows, WIDE), bf16)] * 3
        + [pltpu.VMEM((1, 2 * rows, 2 * DH), bf16), pltpu.SemaphoreType.DMA((7,))],
        compiler_params=pltpu.CompilerParams(vmem_limit_bytes=8 << 20),
        cost_estimate=pl.CostEstimate(flops=0, bytes_accessed=12 << 20, transcendentals=0),
    )(*tables, *mine, other, block)


def measure_kernel(offsets, plan, qt_ref, top_in, sum_in, *refs):
    count = len(offsets)
    blocks, (top_ref, sum_ref, kv_ref, sems) = refs[:count], refs[count:]
    copies = run_copies([(held, kv_ref.at[i]) for i, held in enumerate(blocks)], sems)
    top_ref[...] = top_in[...]
    sum_ref[...] = sum_in[...]
    for copy in copies:
        copy.wait()
    measure_blocks(plan, offsets, kv_ref, qt_ref, top_ref, sum_ref)


def measure(offsets, prepared, stats, blocks):
    rows = blocks[0].shape[0] // 2
    plan, qt = prepared[:2]
    return pl.pallas_call(
        functools.partial(measure_kernel, offsets),
        in_specs=[SMEM] + [VMEM] * 3 + [HBM] * len(blocks),
        out_specs=[VMEM] * 2,
        out_shape=[row_stats(rows)] * 2,
        scratch_shapes=[
            pltpu.VMEM((len(offsets), 2 * rows, 2 * DH), jnp.bfloat16),
            pltpu.SemaphoreType.DMA((len(blocks),)),
        ],
        compiler_params=pltpu.CompilerParams(vmem_limit_bytes=6 << 20),
        cost_estimate=pl.CostEstimate(flops=0, bytes_accessed=8 << 20, transcendentals=0),
    )(plan, qt, *stats, *blocks)


def grads_kernel(chips, offsets, first, last, plan, *refs):
    far = chips // 2
    shared = []
    for head in range(HALF):
        shared.append(refs[:6 + first])
        refs = refs[6 + first:]
    blocks = []
    for head in range(HALF):
        blocks.append(refs[:len(offsets) + first])
        refs = refs[len(offsets) + first:]
    carried = None
    if not first:
        carried, refs = refs[0], refs[1:]
    terms, refs = refs[:HALF], refs[HALF:]
    if first:
        up_ref, down_ref, refs = refs[0], refs[1], refs[2:]
        lse_out, refs = refs[:HALF], refs[HALF:]
    outs, refs = refs[:2 if last else 1], refs[2 if last else 1:]
    (kv_ref, acc_ref, stage_ref, zero_ref, p_ref, ds_ref, sum_ref, dqt_ref, offset_ref,
     sems, kv_sems, out_sems, zero_sems) = refs
    lse_ref = lse_out if first else [head[5] for head in shared]
    if not last:
        dqt_ref = outs[0]
    rows = acc_ref.shape[1]
    slots = stage_ref.shape[0]

    for slot, offset in enumerate(offsets):
        offset_ref[slot] = offset

    def sees(side, i):
        return plan[side * 2 * chips + offset_ref[i // 2] * 2 + i % 2]

    def seen(i):
        return (sees(0, i) > 0) | (sees(1, i) > 0)

    pairs = []
    for slot, offset in enumerate(offsets):
        if offset == far:
            for head in range(HALF):
                pairs.append((blocks[head][0], kv_ref.at[slot, head, :rows]))
                pairs.append((blocks[head][1], kv_ref.at[slot, head, rows:]))
            continue

        @pl.when(seen(2 * slot) | seen(2 * slot + 1))
        def _():
            for head in range(HALF):
                pltpu.make_async_copy(
                    blocks[head][slot + first], kv_ref.at[slot, head], kv_sems.at[slot, head]
                ).start()

    copies = run_copies(pairs, sems)
    zero_ref[...] = jnp.zeros_like(zero_ref)

    def send(i, sources, sem_of):
        at_block, half = i // 2, i % 2
        here = pl.ds(pl.multiple_of(half * rows, rows), rows)
        for head in range(HALF):
            def put(target):
                pltpu.make_async_copy(sources[head], target, sem_of(head)).start()

            if not first:
                put(terms[head].at[at_block, here])
                continue

            @pl.when(i >= 2)
            def _():
                put(terms[head].at[at_block, here])

            @pl.when(i == 0)
            def _():
                put(up_ref.at[head])

            @pl.when(i == 1)
            def _():
                put(down_ref.at[head])

    def sent(sem_of):
        for head in range(HALF):
            pltpu.make_async_copy(zero_ref, terms[head].at[0, :rows], sem_of(head)).wait()

    def send_zeros(i, carry):
        @pl.when(jnp.logical_not(seen(i)))
        def _():
            send(i, [zero_ref] * HALF, lambda head: zero_sems.at[i, head])

        return carry

    lax.fori_loop(0, 2 * len(offsets), send_zeros, 0)
    dqt_ref[...] = jnp.zeros_like(dqt_ref) if first else carried[...]
    for copy in copies:
        copy.wait()
    if first:
        for head in range(HALF):
            top_ref, total_ref = lse_out[head], sum_ref.at[head]
            top_ref[...] = shared[head][5][...]
            total_ref[...] = shared[head][6][...]
            measure_blocks(plan, [far], kv_ref.at[:, head], shared[head][0], top_ref, total_ref)
            top_ref[...] = top_ref[...] * EXP_SCALE + jnp.log2(total_ref[...])

    def visit(i, done):
        at_block, half = i // 2, i % 2
        here = pl.ds(pl.multiple_of(half * rows, rows), rows)

        if len(offsets) > first:
            either = seen(2 * at_block) | seen(2 * at_block + 1)

            @pl.when((half == 0) & (offset_ref[at_block] != far) & either)
            def _():
                for head in range(HALF):
                    pltpu.make_async_copy(
                        blocks[head][-1], kv_ref.at[at_block, head], kv_sems.at[at_block, head]
                    ).wait()

        def look(side, carry):
            @pl.when(sees(side, i) > 0)
            def _():
                allowed = seen_keys(rows, sees(side, i))
                for head in range(HALF):
                    qt_ref, gt_ref, gm_ref, qm_ref, delta_ref = shared[head][:5]
                    k = kv_ref[at_block, head, here, :DH]
                    v = kv_ref[at_block, head, here, DH:]
                    for h in range(PER):
                        lanes = slice(h * rows, (h + 1) * rows)
                        part = (side, slice(None), lanes)
                        s = dot(k, qt_ref[part]) * EXP_SCALE - lse_ref[head][part]
                        p = jnp.where(allowed, jnp.exp2(s), 0.0)
                        ds = p * (dot(v, gt_ref[part]) - delta_ref[part])
                        p_ref[head, :, lanes] = p.astype(p_ref.dtype)
                        ds_ref[head, :, lanes] = ds.astype(ds_ref.dtype)
                    acc_ref[head, :, DH:] += dot(p_ref[head], gm_ref[side])
                    acc_ref[head, :, :DH] += dot(ds_ref[head], qm_ref[side])
                    dqt_ref[head, side] += dot(k.T, ds_ref[head])

            return carry

        @pl.when(seen(i))
        def _():
            slot = done % slots

            @pl.when(done >= slots)
            def _():
                sent(lambda head: out_sems.at[slot, head])

            acc_ref[...] = jnp.zeros_like(acc_ref)
            lax.fori_loop(0, 2, look, 0)
            for head in range(HALF):
                stage_ref[slot, head, :, :DH] = (acc_ref[head, :, :DH] * SCALE).astype(stage_ref.dtype)
                stage_ref[slot, head, :, DH:] = acc_ref[head, :, DH:].astype(stage_ref.dtype)
            send(i, [stage_ref.at[slot, head] for head in range(HALF)], lambda head: out_sems.at[slot, head])

        return done + seen(i).astype(jnp.int32)

    done = lax.fori_loop(0, 2 * len(offsets), visit, jnp.int32(0))
    if last:
        for side, dq_ref in enumerate(outs):
            for head in range(HALF):
                for h in range(PER):
                    dq = (dqt_ref[head, side, :, h * rows:(h + 1) * rows] * SCALE).astype(dq_ref.dtype)
                    dq_ref[:, (head * PER + h) * DH:(head * PER + h + 1) * DH] = dq.T

    def zeros_sent(i, carry):
        @pl.when(jnp.logical_not(seen(i)))
        def _():
            sent(lambda head: zero_sems.at[i, head])

        return carry

    lax.fori_loop(0, 2 * len(offsets), zeros_sent, 0)
    for slot in range(slots):
        @pl.when(done > slot)
        def _():
            sent(lambda head: out_sems.at[slot, head])


def gradients(prepared, stats, offsets, blocks, carried, last):
    plan = prepared[0][0]
    chips = plan.shape[0] // 4
    rows = prepared[0][3].shape[1] // PER
    first = carried is None
    bf16, f32 = jnp.bfloat16, jnp.float32
    shared = [(*prepared[head][1:6], *stats[head]) for head in range(HALF)]
    arrays = [a for head in shared for a in head] + [a for head in blocks for a in head]
    arrays += [] if first else [carried]
    dense = jax.ShapeDtypeStruct((len(offsets), 2 * rows, 2 * DH), bf16)
    piece = jax.ShapeDtypeStruct((HALF, rows, 2 * DH), bf16)
    query = jax.ShapeDtypeStruct((rows, HALF * WIDE), bf16)
    sums = jax.ShapeDtypeStruct((HALF, 2, DH, PER * rows), f32)
    out_shape, out_specs = [dense] * HALF, [HBM] * HALF
    if first:
        out_shape += [piece] * 2 + [row_stats(rows)] * HALF
        out_specs += [HBM] * 2 + [VMEM] * HALF
    out_shape += [query] * 2 if last else [sums]
    out_specs += [VMEM] * (2 if last else 1)
    flat = sum(len(head) for head in shared)
    in_specs = [SMEM] + [VMEM] * flat + [HBM] * (len(arrays) - flat)
    if not first:
        in_specs[-1] = VMEM
    return pl.pallas_call(
        functools.partial(grads_kernel, chips, tuple(offsets), first, last),
        in_specs=in_specs,
        out_specs=out_specs,
        out_shape=out_shape,
        scratch_shapes=[
            pltpu.VMEM((len(offsets), HALF, 2 * rows, 2 * DH), bf16),
            pltpu.VMEM((HALF, rows, 2 * DH), f32),
            pltpu.VMEM((4, HALF, rows, 2 * DH), bf16),
            pltpu.VMEM((rows, 2 * DH), bf16),
            pltpu.VMEM((HALF, rows, PER * rows), bf16),
            pltpu.VMEM((HALF, rows, PER * rows), bf16),
            pltpu.VMEM((HALF, 2, 1, PER * rows), f32),
            pltpu.VMEM((HALF, 2, DH, PER * rows) if last else (8, DH), f32),
            pltpu.SMEM((len(offsets),), jnp.int32),
            pltpu.SemaphoreType.DMA((2 * HALF,)),
            pltpu.SemaphoreType.DMA((len(offsets), HALF)),
            pltpu.SemaphoreType.DMA((4, HALF)),
            pltpu.SemaphoreType.DMA((2 * len(offsets), HALF)),
        ],
        compiler_params=pltpu.CompilerParams(vmem_limit_bytes=(13 << 20) + (len(offsets) << 19)),
        cost_estimate=pl.CostEstimate(flops=8 << 30, bytes_accessed=16 << 20, transcendentals=0),
    )(plan, *arrays)


def wide(x):
    return x.astype(jnp.float32)


def assemble_kernel(me_ref, *refs):
    ours, theirs, refs = refs[0], refs[1], refs[2:]
    kept, got, refs = refs[:HALF], refs[HALF:2 * HALF], refs[2 * HALF:]
    query_grad, key_grad, value_grad, sems = refs
    rows = ours.shape[0]
    core = me_ref[0] % 2
    pairs = []
    for which, query, sums in ((core, ours, kept), (1 - core, theirs, got)):
        column = pl.multiple_of(which * (HALF * WIDE), HALF * WIDE)
        pairs.append((query, query_grad.at[:, pl.ds(column, HALF * WIDE)]))
        for head in range(HALF):
            column = pl.multiple_of((which * HALF + head) * DH, DH)
            for first, out in ((0, key_grad), (DH, value_grad)):
                pairs.append((sums[head].at[:rows, first:first + DH], out.at[:, pl.ds(column, DH)]))
    for copy in run_copies(pairs, sems):
        copy.wait()


def assemble(me, ours, theirs, kept, got):
    rows = ours.shape[0]
    return pl.pallas_call(
        assemble_kernel,
        in_specs=[SMEM] + [HBM] * (2 + 2 * HALF),
        out_specs=[HBM] * 3,
        out_shape=[
            jax.ShapeDtypeStruct((rows, 2 * HALF * WIDE), jnp.bfloat16),
            jax.ShapeDtypeStruct((rows, 2 * HALF * DH), jnp.bfloat16),
            jax.ShapeDtypeStruct((rows, 2 * HALF * DH), jnp.bfloat16),
        ],
        scratch_shapes=[pltpu.SemaphoreType.DMA((2 + 4 * HALF,))],
        compiler_params=pltpu.CompilerParams(vmem_limit_bytes=2 << 20),
        cost_estimate=pl.CostEstimate(flops=0, bytes_accessed=4 << 20, transcendentals=0),
    )(me, ours, theirs, *kept, *got)


def local(queries, keys, values, saved_out, grad_out, parents, assignment, lengths):
    rows = keys.shape[0]
    chips = lax.axis_size("leaf") // 2
    order = ring_order(chips)
    ahead = [(order[i], order[(i + 1) % chips]) for i in range(chips)]
    right = [(2 * a + c, 2 * b + c) for a, b in ahead for c in range(2)]
    left = [(b, a) for a, b in right]
    swap = [(2 * a + c, 2 * a + 1 - c) for a in range(chips) for c in range(2)]
    places = jnp.asarray([order.index(chip) for chip in range(chips)], jnp.int32)
    index = lax.axis_index("leaf").astype(jnp.int32)
    core = index % 2
    me = index.reshape(1)
    tables = (me, places, parents, assignment, lengths)

    def part(array, which, width):
        return lax.dynamic_slice(array, (0, which * width), (rows, width))

    def heads_of(which):
        pieces = [part(array, which * HALF + head, DH) for head in range(HALF) for array in (keys, values)]
        return jnp.concatenate(pieces, axis=1)

    kept = heads_of(core)
    got = lax.ppermute(heads_of(1 - core), "leaf", swap)
    own = []
    for head in range(HALF):
        cols = slice(head * 2 * DH, (head + 1) * 2 * DH)
        own.append(jnp.concatenate([kept[:, cols], got[:, cols]], axis=0))
    mine = (queries, grad_out, saved_out)
    late = lax.optimization_barrier((*mine, got))[:3]
    other = jnp.concatenate([part(array, 1 - core, HALF * WIDE) for array in late], axis=1)
    other = lax.ppermute(other, "leaf", swap)

    def shift(arrays, ring):
        return [lax.ppermute(array, "leaf", ring) for array in arrays]

    far = chips // 2
    prepared, stats = [None] * HALF, [None] * HALF
    blocks, halves = [], []
    streams = [(block, block) for block in own]
    blocks = [{0: block} for block in own]
    for step in range(1, far):
        for head in range(HALF):
            up, down = streams[head]
            up, down = lax.ppermute(up, "leaf", right), lax.ppermute(down, "leaf", left)
            blocks[head][chips - step], blocks[head][step] = up, down
            if step == 1:
                prepared[head] = prepare(head, tables, mine, other, own[head])
                stats[head] = prepared[head][6:]
            else:
                met = (step - 1, chips - step + 1)
                stats[head] = measure(met, prepared[head], stats[head], [blocks[head][at] for at in met])
            stats[head], streams[head] = lax.optimization_barrier((stats[head], (up, down)))
    for head in range(HALF):
        up, down = streams[head]
        halves.append([lax.ppermute(up[:rows], "leaf", right), lax.ppermute(down[rows:], "leaf", left)])
        met = (far - 1, far + 1)
        stats[head] = measure(met, prepared[head], stats[head], [blocks[head][at] for at in met])

    offsets = [far]
    for step in range(1, far - 3):
        offsets += [far + step, far - step]
    arrays = [halves[head] + [blocks[head][at] for at in offsets[1:]] for head in range(HALF)]
    *terms, carried = gradients(prepared, stats, offsets, arrays, None, False)
    lse = [[a] for a in terms[HALF + 2:]]
    by_offset = {at: [terms[head][slot] for head in range(HALF)] for slot, at in enumerate(offsets)}
    ups, downs = terms[HALF:HALF + 1], terms[HALF + 1:HALF + 2]

    def add(sums, at):
        return [(wide(a) + wide(b)).astype(jnp.bfloat16) for a, b in zip(sums, by_offset[at])]

    later = {4: [chips - 3, 3], 3: [chips - 2, 2], 2: [chips - 1, 1], 1: [0]}
    ours = theirs = None
    for step in range(far, 0, -1):
        if step < far:
            ups, downs = add(ups, step), add(downs, chips - step)
        if step in later:
            last = 0 in later[step]
            (lse, carried), held = lax.optimization_barrier(((lse, carried), (ups[-1:], downs[-1:])))
            ups, downs = ups[:-1] + held[0], downs[:-1] + held[1]
            arrays = [[blocks[head][at] for at in later[step]] for head in range(HALF)]
            *terms, lead = gradients(prepared, lse, later[step], arrays, carried, last)
            for slot, at in enumerate(later[step]):
                by_offset[at] = [terms[head][slot] for head in range(HALF)]
            if last:
                ours, theirs = terms[HALF], lead
            else:
                carried = lead
        ups, downs = shift(ups, right), shift(downs, left)
        if step == far:
            ups = [jnp.pad(a, ((0, rows), (0, 0))) for a in ups[0]]
            downs = [jnp.pad(a, ((rows, 0), (0, 0))) for a in downs[0]]
    theirs, ups, downs = lax.optimization_barrier((theirs, ups, downs))
    theirs = lax.ppermute(theirs, "leaf", swap)
    kept, got = [], []
    for head in range(HALF):
        summed = (wide(by_offset[0][head]) + wide(ups[head]) + wide(downs[head])).astype(jnp.bfloat16)
        kept.append(summed)
        got.append(lax.ppermute(summed[rows:], "leaf", swap))

    return tuple(assemble(me, ours, theirs, kept, got))


def solution(mesh):
    tokens = P(("groups", "leaf"), None)
    tables = P("groups")
    return jax.shard_map(
        local,
        mesh=mesh,
        in_specs=(tokens,) * 5 + (tables,) * 3,
        out_specs=(tokens,) * 3,
        check_vma=False,
    )
```
